32 devices in a mesh: dp: 8 (over y, x, core), tensor: 4 (over z).
Axes of the slice: x: 2, y: 2, z: 4, core: 2. Of those that a mesh axis runs over, the one named last changes fastest.
Arguments:
- tokens: bfloat16 [8, 2048, 2048], P('dp', 'tensor'), may hold values from -6 to 6
- cotangent: bfloat16 [8, 2048, 2048], P('dp', 'tensor'), may hold values from -6 to 6
- lengths: int32 [8], P('dp'), may hold values from 512 to 2048, as said below
- adapter_ids: int32 [8], P('dp'), may hold values from 0 to 7, as said below
- pre_gain: float32 [2048], replicated, may hold values from 0.1 to 1.9
- in_inner: bfloat16 [2048, 2, 4096], P('dp', None, 'tensor'), may hold values from -0.125 to 0.125
- in_maps: bfloat16 [2048, 256], P('dp'), may hold values from -0.125 to 0.125
- in_steps: bfloat16 [2048, 64], P('dp', 'tensor'), may hold values from -0.125 to 0.125
- conv_inner: float32 [4, 4096], P(None, 'tensor'), may hold values from -3 to 3
- conv_maps: float32 [4, 256], replicated, may hold values from -3 to 3
- step_bias: float32 [64], P('tensor'), may hold values from -8 to -3
- decay_log: float32 [64], P('tensor'), may hold values from 0 to 2.77
- skip_gain: float32 [64], P('tensor'), may hold values from 0.5 to 1.5
- norm_gain: float32 [4096], P('tensor'), may hold values from 0.1 to 1.9
- out_weight: bfloat16 [4096, 2048], P('tensor', 'dp'), may hold values from -0.09375 to 0.09375
- adapter_in_down: bfloat16 [8, 2048, 16], replicated, may hold values from -0.125 to 0.125
- adapter_in_up: bfloat16 [8, 16, 2, 4096], P(None, None, None, 'tensor'), may hold values from -0.75 to 0.75
- adapter_out_down: bfloat16 [8, 4096, 16], P(None, 'tensor'), may hold values from -0.09375 to 0.09375
- adapter_out_up: bfloat16 [8, 16, 2048], replicated, may hold values from -0.75 to 0.75
Outputs:
- mixed: bfloat16 [8, 2048, 2048], P('dp', 'tensor')
- tokens_grad: bfloat16 [8, 2048, 2048], P('dp', 'tensor')
- adapter_in_down_grad: float32 [8, 2048, 16], replicated
- adapter_in_up_grad: float32 [8, 16, 2, 4096], P(None, None, None, 'tensor')
- adapter_out_down_grad: float32 [8, 4096, 16], P(None, 'tensor')
- adapter_out_up_grad: float32 [8, 16, 2048], replicated
The draws below stay inside these ranges and needn't reach their ends.
Inputs may be any that keep to these rules, and one draw needn't show every extreme that they name: `lengths`: the valid positions of a sequence come first; the rest of its slot is padding. `adapter_ids`: every adapter is used by at least one sequence.
All inputs are finite; a program needn't handle non-finite values.
Results may differ from the reference program's by a relative error of at most 0.0072.
Values may be sent and summed in bfloat16 or wider, within the bound.
No kernel may reach another device: no remote copies, remote signals or barrier semaphores. Data moves between devices by JAX's collectives and lax.ppermute only.
A program may use at most 320 MiB of HBM per device.

```python
import jax
import jax.numpy as jnp
from jax import lax

D = 2048
HEADS = 64
STATE = 128
INNER = 4096
CONV = 4
BLOCK = 256
RANK = 16
ADAPTERS = 8
SEQ_LEN = 2048
SLOTS = 8


def draw_lengths(key, part):
    key = jax.random.fold_in(key, 7)
    key_base, key_order = jax.random.split(key)
    drawn = jax.random.randint(key_base, (SLOTS,), SEQ_LEN // 4, SEQ_LEN + 1)
    order = jax.random.permutation(key_order, SLOTS)
    slot_index = jnp.arange(SLOTS)
    drawn = jnp.where(slot_index == order[0], SEQ_LEN, drawn)
    drawn = jnp.where(slot_index == order[1], SEQ_LEN // 4, drawn)
    return drawn.astype(jnp.int32)


def draw_adapter_ids(key, part):
    key = jax.random.fold_in(key, 13)
    key_rank, key_fill = jax.random.split(key)
    order = jax.random.permutation(key_rank, SLOTS)
    ranked = jnp.argsort(order, stable=True)
    filler = jax.random.randint(key_fill, (SLOTS,), 0, ADAPTERS)
    return jnp.where(ranked < ADAPTERS, ranked, filler).astype(jnp.int32)


def shard_levels(stream_key, extent, cuts, low, high):
    def one(axis_at, shards_of):
        heights = jax.random.uniform(jax.random.fold_in(jax.random.fold_in(stream_key, 6), axis_at), (shards_of,), jnp.float32, low / len(cuts), high / len(cuts))
        return jnp.repeat(jnp.exp(heights), extent[axis_at] // shards_of).reshape((-1,) + (1,) * (len(extent) - axis_at - 1))

    factor_of = one(*cuts[0])
    for cut in cuts[1:]:
        factor_of = factor_of * one(*cut)
    return factor_of


def normal_values(own_key, extent, width, limit, cuts=(), kind=jnp.bfloat16):
    gain = shard_levels(own_key, extent, cuts, -0.22, 0.18) if cuts else 1.0
    values = jax.random.normal(own_key, extent, jnp.float32) * width * gain
    return jnp.minimum(jnp.maximum(values, -limit), limit).astype(kind)


def setup_inputs(seed: int = 0) -> dict:
    key_of = jax.random.split(jax.random.key(seed), 20)
    return {
        "tokens": normal_values(key_of[0], (SLOTS, SEQ_LEN, D), 1.0, 6.0, ((0, 8), (1, 4))),
        "cotangent": normal_values(key_of[1], (SLOTS, SEQ_LEN, D), 1.0, 6.0, ((0, 8), (1, 4))),
        "lengths": draw_lengths(jax.random.fold_in(key_of[19], 71), 0),
        "adapter_ids": draw_adapter_ids(jax.random.fold_in(key_of[19], 71), 0),
        "pre_gain": jnp.clip(1.0 + 0.18 * jax.random.normal(key_of[4], (D,), jnp.float32), 0.1, 1.9),
        "in_inner": normal_values(key_of[5], (D, 2, INNER), D ** -0.5, 0.125, ((0, 8), (2, 4))),
        "in_maps": normal_values(key_of[6], (D, 2 * STATE), D ** -0.5, 0.125, ((0, 8),)),
        "in_steps": normal_values(key_of[7], (D, HEADS), D ** -0.5, 0.125, ((0, 8), (1, 4))),
        "conv_inner": normal_values(key_of[8], (CONV, INNER), CONV ** -0.5, 3.0, ((1, 4),), jnp.float32),
        "conv_maps": normal_values(key_of[9], (CONV, 2 * STATE), CONV ** -0.5, 3.0, (), jnp.float32),
        "step_bias": jnp.clip(-8.0 + 5.0 * jax.random.uniform(key_of[10], (HEADS,), jnp.float32) ** shard_levels(key_of[10], (HEADS,), ((0, 4),), -0.2, 0.2), -8.0, -3.0),
        "decay_log": jnp.clip(2.77 * jax.random.uniform(key_of[11], (HEADS,), jnp.float32) ** shard_levels(key_of[11], (HEADS,), ((0, 4),), -0.2, 0.2), 0.0, 2.77),
        "skip_gain": jnp.clip(0.5 + 1.0 * jax.random.uniform(key_of[12], (HEADS,), jnp.float32) ** shard_levels(key_of[12], (HEADS,), ((0, 4),), -0.2, 0.2), 0.5, 1.5),
        "norm_gain": jnp.clip(1.0 + 0.18 * jax.random.normal(key_of[13], (INNER,), jnp.float32), 0.1, 1.9),
        "out_weight": normal_values(key_of[14], (INNER, D), INNER ** -0.5, 0.09375, ((0, 4), (1, 8))),
        "adapter_in_down": normal_values(key_of[15], (ADAPTERS, D, RANK), D ** -0.5, 0.125),
        "adapter_in_up": normal_values(key_of[16], (ADAPTERS, RANK, 2, INNER), (4 * RANK) ** -0.5, 0.75, ((3, 4),)),
        "adapter_out_down": normal_values(key_of[17], (ADAPTERS, INNER, RANK), INNER ** -0.5, 0.09375, ((1, 4),)),
        "adapter_out_up": normal_values(key_of[18], (ADAPTERS, RANK, D), (4 * RANK) ** -0.5, 0.75),
    }


epsilon = 1e-05
highest = lax.Precision.HIGHEST

@jax.custom_vjp
def low(v):
    return lax.optimization_barrier(v.astype(jnp.bfloat16)).astype(jnp.float32)

@jax.custom_vjp
def low_back(v):
    return v

def low_keep(v):
    return (low(v), None)

def low_pass(kept, grad):
    return (grad,)

def back_keep(v):
    return (v, None)

def back_low(kept, grad):
    return (low(grad),)
low.defvjp(low_keep, low_pass)
low_back.defvjp(back_keep, back_low)

def causal_conv(values, kernel):
    tap_count = kernel.shape[0]
    row_count = values.shape[0]
    padded = jnp.pad(values, ((tap_count - 1, 0), (0, 0)))
    running = padded[0:row_count] * kernel[0]
    for tap_index in range(1, tap_count):
        running = running + padded[tap_index:tap_index + row_count] * kernel[tap_index]
    return running

def block_terms(pieces):
    values, b_block, c_block, log_decay = pieces
    cumulative = jnp.cumsum(log_decay, axis=0)
    cum_heads = cumulative.T
    gap_log = cum_heads[:, :, None] - cum_heads[:, None, :]
    block_size = log_decay.shape[0]
    causal_mask = jnp.arange(block_size)[:, None] >= jnp.arange(block_size)[None, :]
    decay_mask = jnp.where(causal_mask, jnp.exp(jnp.where(causal_mask, gap_log, 0.0)), 0.0)
    inner_terms = jnp.dot(c_block, b_block.T, precision=highest)
    weighting = decay_mask * inner_terms
    within = jnp.einsum('hij,jhp->ihp', weighting, values, precision=highest)
    to_end = jnp.exp(cumulative[-1][None, :] - cumulative)
    block_state = jnp.einsum('jh,jhp,js->hps', to_end, values, b_block, precision=highest)
    return (within, block_state, cumulative)

def mix_heads(inner_raw, maps_raw, steps_raw, conv_inner, conv_maps, step_bias, decay_log, skip_gain, block_len):
    row_count = inner_raw.shape[0]
    head_count = steps_raw.shape[1]
    head_width = inner_raw.shape[1] // head_count
    state_width = maps_raw.shape[1] // 2
    inner_conv = jax.nn.silu(causal_conv(inner_raw, conv_inner))
    maps_conv = jax.nn.silu(causal_conv(maps_raw, conv_maps))
    delta = jax.nn.softplus(steps_raw + step_bias)
    rates = -delta * jnp.exp(decay_log)
    blocks = row_count // block_len
    scaled = inner_conv.reshape(row_count, head_count, head_width) * delta[:, :, None]
    pieces = (scaled.reshape(blocks, block_len, head_count, head_width), maps_conv[:, :state_width].reshape(blocks, block_len, state_width), maps_conv[:, state_width:].reshape(blocks, block_len, state_width), rates.reshape(blocks, block_len, head_count))
    within, states, cumulative = lax.map(jax.checkpoint(block_terms), pieces)

    def carry_step(carried, inputs):
        state_here, totals = inputs
        return (carried * jnp.exp(totals)[:, None, None] + state_here, carried)
    initial = jnp.zeros((head_count, head_width, state_width), jnp.float32)
    _, entering = lax.scan(carry_step, initial, (states, cumulative[:, -1, :]))
    carried_out = jnp.einsum('cis,chps,cih->cihp', pieces[2], entering, jnp.exp(cumulative), precision=highest)
    mixed_inner = (within + carried_out).reshape(row_count, head_count * head_width)
    return mixed_inner + inner_conv * jnp.repeat(skip_gain, head_width)

def reference(tokens, cotangent, lengths, adapter_ids, pre_gain, in_inner, in_maps, in_steps, conv_inner, conv_maps, step_bias, decay_log, skip_gain, norm_gain, out_weight, adapter_in_down, adapter_in_up, adapter_out_down, adapter_out_up):
    whole_in = in_inner.astype(jnp.float32).reshape(D, 2 * INNER)
    maps_weight = in_maps.astype(jnp.float32)
    steps_weight = in_steps.astype(jnp.float32)
    out_wide = out_weight.astype(jnp.float32)
    positions = jnp.arange(SEQ_LEN)

    def one_slot(adapters, row_values, length, pick):
        in_down, in_up, out_down, out_up = adapters
        down_in = lax.dynamic_index_in_dim(in_down, pick, 0, keepdims=False)
        up_in = lax.dynamic_index_in_dim(in_up, pick, 0, keepdims=False).reshape(RANK, 2 * INNER)
        down_out = lax.dynamic_index_in_dim(out_down, pick, 0, keepdims=False)
        up_out = lax.dynamic_index_in_dim(out_up, pick, 0, keepdims=False)
        stat = lax.optimization_barrier(jnp.mean(row_values * row_values, axis=-1, keepdims=True))
        normed = low(row_values * lax.rsqrt(stat + epsilon) * pre_gain)
        low_in = jnp.dot(normed, down_in, precision=highest)
        gate_inner = low_back(jnp.dot(normed, whole_in, precision=highest) + jnp.dot(low_in, up_in, precision=highest))
        paired = gate_inner.reshape(SEQ_LEN, 2, INNER)
        gate_part = paired[:, 0]
        inner_raw = paired[:, 1]
        maps_raw = jnp.dot(normed, maps_weight, precision=highest)
        steps_raw = low_back(jnp.dot(normed, steps_weight, precision=highest))
        mixed_inner = mix_heads(inner_raw, maps_raw, steps_raw, conv_inner, conv_maps, step_bias, decay_log, skip_gain, BLOCK)
        gated = mixed_inner * jax.nn.silu(gate_part)
        squares = lax.optimization_barrier(jnp.sum(gated * gated, axis=-1, keepdims=True))
        normed_out = low(gated * lax.rsqrt(squares / INNER + epsilon) * norm_gain)
        out_hidden = jnp.dot(normed_out, down_out, precision=highest)
        branch = jnp.dot(normed_out, out_wide, precision=highest) + jnp.dot(out_hidden, up_out, precision=highest)
        valid = (positions < length).astype(jnp.float32)[:, None]
        return valid * (row_values + branch)

    def forward(token_values, in_down, in_up, out_down, out_up):
        adapters = (in_down, in_up, out_down, out_up)

        def slot_apply(inputs):
            row_values, length, pick = inputs
            return jax.checkpoint(one_slot)(adapters, row_values, length, pick)
        return lax.map(slot_apply, (token_values, lengths, adapter_ids))
    outputs, pullback = jax.vjp(forward, tokens.astype(jnp.float32), adapter_in_down.astype(jnp.float32), adapter_in_up.astype(jnp.float32), adapter_out_down.astype(jnp.float32), adapter_out_up.astype(jnp.float32))
    grads = pullback(cotangent.astype(jnp.float32))
    return (outputs.astype(jnp.bfloat16), grads[0].astype(jnp.bfloat16), grads[1], grads[2], grads[3], grads[4])
```

```python
import functools

import jax
import jax.numpy as jnp
from jax import lax
from jax.experimental import pallas as pl
from jax.experimental.pallas import tpu as pltpu
from jax.sharding import PartitionSpec as P

f32 = jnp.float32
bf16 = jnp.bfloat16
epsilon = 1e-05
highest = lax.Precision.HIGHEST
LOG2E = 1.4426950408889634
HEAD = 64
HALO = 128
SUB = 256
CB = 256

NN = ((1,), (0,))
NT = ((1,), (1,))
TN = ((0,), (0,))


def dot(a, b, dims=NN):
    return lax.dot_general(a, b, (dims, ((), ())), preferred_element_type=f32)


def compiler_params(grid_rank):
    return pltpu.CompilerParams(
        dimension_semantics=("arbitrary",) * grid_rank, vmem_limit_bytes=60 * 2**20
    )


def cost(flops, size):
    return pl.CostEstimate(flops=int(flops), bytes_accessed=int(size), transcendentals=0)


def sigmoid(v):
    return 0.5 + 0.5 * jnp.tanh(0.5 * v)


def conv_values(raw, chan):
    out = raw * chan[:, 3:4]
    for k in range(3):
        out = out + pltpu.roll(raw, 3 - k, 1) * chan[:, k : k + 1]
    return out[:, HALO:]


def per_head(values, rows):
    hb = rows.shape[0]
    parts = [values[h * HEAD : (h + 1) * HEAD] * rows[h : h + 1] for h in range(hb)]
    return jnp.concatenate(parts, axis=0)


def head_sums(values, hb):
    parts = [
        jnp.sum(values[h * HEAD : (h + 1) * HEAD], axis=0, keepdims=True) for h in range(hb)
    ]
    return jnp.concatenate(parts, axis=0)


def weight_dots(refs, orders, right, width):
    acc = None
    for ref, offsets in zip(refs, orders):
        for b, off in enumerate(offsets):
            term = dot(ref[b], right[off : off + width])
            acc = term if acc is None else acc + term
    return acc


def fwd_kernel(zo, xo, kb, hb, sub, *refs):
    nz, nx = len(zo), len(xo)
    zrefs, xrefs = refs[:nz], refs[nz : nz + nx]
    (nt, low, upz, upx, chan_r, hp_r, cumn_r, ct, bn, cbt) = refs[nz + nx : nz + nx + 10]
    z_out, xr_out, mix_out, ent_out, st_out = refs[-5:]
    chan = chan_r[...]
    hp = hp_r[...]
    length = ct.shape[1]
    z = weight_dots(zrefs, zo, nt[:, HALO:], kb) + dot(upz[...], low[:, HALO:])
    z_out[...] = z.astype(bf16)
    xr = weight_dots(xrefs, xo, nt, kb) + dot(upx[...], low[...])
    xr_out[...] = xr.astype(bf16)
    xc = conv_values(xr, chan)
    x = xc * sigmoid(xc)
    xs = per_head(x, hp[2 * hb : 3 * hb])
    xs_low = xs.astype(bf16)
    state = None
    for s in range(length // sub):
        cols = slice(s * sub, (s + 1) * sub)
        cum = hp[:hb, cols]
        rows_n = cumn_r[cols, :]
        within = []
        for h in range(hb):
            gap = jnp.minimum(cum[h : h + 1] - rows_n[:, h : h + 1], 0.0)
            weight = (jnp.exp2(gap) * cbt[s]).astype(bf16)
            within.append(dot(xs_low[h * HEAD : (h + 1) * HEAD, cols], weight))
        y = jnp.concatenate(within, axis=0)
        last = cum[:, sub - 1 : sub]
        ends = jnp.exp2(last - cum)
        add = dot(per_head(xs[:, cols], ends).astype(bf16), bn[cols, :])
        if s > 0:
            ent_out[s - 1] = state
            y = y + per_head(dot(state.astype(bf16), ct[:, cols]), jnp.exp2(cum))
            state = per_head(state, jnp.exp2(last)) + add
        else:
            state = add
        mix_out[:, cols] = y + x[:, cols] * chan[:, 4:5]
    if length // sub == 1:
        ent_out[0] = state
    st_out[...] = state


def forward_slot(j, zw, xw, zo, xo, nt, low, upz, upx, chan, hp, cumn, ct, bn, cbt, bufs):
    slots, ch = upz.shape[0], upz.shape[1]
    length = ct.shape[1]
    ext = nt.shape[1]
    hb = CB // HEAD
    ncb = ch // CB
    kb = zw[0].shape[2]
    nsub = length // SUB
    full = lambda a: pl.BlockSpec(a.shape, lambda i: (0,) * a.ndim)
    wspec = lambda a: pl.BlockSpec((a.shape[0], CB, a.shape[2]), lambda i: (0, i, 0))
    per_chan = lambda a: pl.BlockSpec((None, CB, a.shape[2]), lambda i: (j, i, 0))
    per_blk = lambda a: pl.BlockSpec((None,) + a.shape[1:], lambda i: (j * ncb + i, 0, 0))
    ops = list(zw) + list(xw) + [nt, low, upz, upx, chan, hp, cumn, ct, bn, cbt]
    specs = (
        [wspec(a) for a in list(zw) + list(xw)]
        + [full(nt), full(low), per_chan(upz), per_chan(upx), per_chan(chan)]
        + [per_blk(hp), per_blk(cumn), full(ct), full(bn), full(cbt)]
    )
    shapes = [
        jax.ShapeDtypeStruct((slots, ch, length), bf16),
        jax.ShapeDtypeStruct((slots, ch, ext), bf16),
        jax.ShapeDtypeStruct((slots, ch, length), f32),
        jax.ShapeDtypeStruct((slots, max(nsub - 1, 1), ch, 128), f32),
        jax.ShapeDtypeStruct((slots, ch, 128), f32),
    ]
    outs = [
        pl.BlockSpec((None, CB, length), lambda i: (j, i, 0)),
        pl.BlockSpec((None, CB, ext), lambda i: (j, i, 0)),
        pl.BlockSpec((None, CB, length), lambda i: (j, i, 0)),
        pl.BlockSpec((None, max(nsub - 1, 1), CB, 128), lambda i: (j, 0, i, 0)),
        pl.BlockSpec((None, CB, 128), lambda i: (j, i, 0)),
    ]
    aliases = {}
    if bufs is not None:
        aliases = {len(ops) + k: k for k in range(5)}
        ops += list(bufs)
        specs += [pl.BlockSpec(memory_space=pl.ANY)] * 5
    return pl.pallas_call(
        functools.partial(fwd_kernel, zo, xo, kb, hb, SUB),
        grid=(ncb,),
        in_specs=specs,
        out_specs=outs,
        out_shape=shapes,
        input_output_aliases=aliases,
        compiler_params=compiler_params(1),
        cost_estimate=cost(2 * ch * 2048 * (length + ext), 2 * ch * 2048 * 2 + ch * length * 10),
        name="forward_slot",
    )(*ops)


def gate_kernel(sets, kb, hb, inner, *refs):
    n_w = sum(len(orders) for _, orders in sets)
    wrefs = refs[:n_w]
    (gt, bh, dn, chan_r, hp_r, mix_r, z_r, ent_r, ct, cn) = refs[n_w : n_w + 10]
    nout_o, dmix_o, dz_o, sl_o = refs[n_w + 10 : n_w + 14]
    dsc, wsc, msc, sq_sc, dot_sc = refs[n_w + 14 :]
    phase, slot, c = pl.program_id(0), pl.program_id(1), pl.program_id(2)
    blk = slot * pl.num_programs(2) + c
    length = gt.shape[1]
    z = z_r[...].astype(f32)
    sig = sigmoid(z)
    silu = z * sig
    chan = chan_r[...]
    gain = chan[:, 5:6]
    hp = hp_r[...]
    cum_all = hp[hb : 2 * hb]

    @pl.when((phase == 0) & (blk == 0))
    def _():
        sq_sc[...] = jnp.zeros_like(sq_sc)
        dot_sc[...] = jnp.zeros_like(dot_sc)

    at = 0
    for (lo, hi), orders in sets:
        mine = wrefs[at : at + len(orders)]
        at += len(orders)

        @pl.when((phase == 0) & (slot >= lo) & (slot < hi))
        def _(mine=mine, orders=orders):
            dsc[...] = weight_dots(mine, orders, gt, kb)

    @pl.when(phase == 0)
    def _():
        weighted = (dsc[...] + dot(dn[...], bh[...])) * gain
        mix = mix_r[...] + per_head(dot(ent_r[...], ct[...]), jnp.exp2(cum_all))
        gated = mix * silu
        wsc[blk] = weighted
        msc[blk] = mix
        sq_sc[...] += jnp.sum((gated * gated).reshape(CB // 8, 8, length), axis=0)
        dot_sc[...] += jnp.sum((gated * weighted).reshape(CB // 8, 8, length), axis=0)

    @pl.when(phase == 1)
    def _():
        r = lax.rsqrt(jnp.sum(sq_sc[...], axis=0, keepdims=True) * (1.0 / inner) + epsilon)
        coef = r * r * r * (jnp.sum(dot_sc[...], axis=0, keepdims=True) * (1.0 / inner))
        mix = msc[blk]
        gated = mix * silu
        nout_o[...] = (gated * r * gain).astype(bf16)
        d_gated = r * wsc[blk] - gated * coef
        d_mix = d_gated * silu
        dmix_o[...] = d_mix.astype(bf16)
        dz_o[...] = (d_gated * mix * (sig + silu * (1.0 - sig))).astype(bf16)
        sl_o[...] = dot(per_head(d_mix, jnp.exp2(cum_all)).astype(bf16), cn[...])


def gate_call(ow, oo, gt, bh, dn, chan, hp, mix, z, ent, ct, cn, inner):
    slots, ch, length = mix.shape
    ncb = ch // CB
    hb = CB // HEAD
    kb = ow[0][1][0].shape[3]
    full = lambda a: pl.BlockSpec(a.shape, lambda p, s, c: (0,) * a.ndim)
    per_chan = lambda a: pl.BlockSpec((None, CB, a.shape[2]), lambda p, s, c: (s, c, 0))
    first = lambda a: pl.BlockSpec(
        (None, CB, a.shape[2]),
        lambda p, s, c: (jnp.where(p == 0, s, slots - 1), jnp.where(p == 0, c, ncb - 1), 0),
    )
    per_blk = lambda a: pl.BlockSpec((None,) + a.shape[1:], lambda p, s, c: (s * ncb + c, 0, 0))
    later = lambda w: pl.BlockSpec(
        (None, CB, w), lambda p, s, c: (jnp.where(p == 1, s, 0), jnp.where(p == 1, c, 0), 0)
    )
    ops, specs, sets = [], [], []
    for ((lo, hi), arrays), orders in zip(ow, oo):
        sets.append(((lo, hi), orders))
        for a in arrays:
            ops.append(a)

            def index(p, s, c, lo=lo, hi=hi):
                t = jnp.where(p == 0, s, slots)
                cc = jnp.where(t < lo, 0, jnp.where(t >= hi, ncb - 1, c))
                return (0, jnp.clip(t, lo, hi - 1) - lo, cc, 0)

            specs.append(pl.BlockSpec((a.shape[0], None, CB, a.shape[3]), index))
    ops += [gt, bh, dn, chan, hp, mix, z, ent, ct, cn]
    specs += [full(gt), full(bh), first(dn), per_chan(chan), per_blk(hp), first(mix)]
    specs += [per_chan(z), first(ent), full(ct), full(cn)]
    blocks = slots * ncb
    return pl.pallas_call(
        functools.partial(gate_kernel, sets, kb, hb, inner),
        grid=(2, slots, ncb),
        in_specs=specs,
        out_specs=[later(length), later(length), later(length), later(128)],
        out_shape=[
            jax.ShapeDtypeStruct((slots, ch, length), bf16),
            jax.ShapeDtypeStruct((slots, ch, length), bf16),
            jax.ShapeDtypeStruct((slots, ch, length), bf16),
            jax.ShapeDtypeStruct((slots, ch, 128), f32),
        ],
        scratch_shapes=[
            pltpu.VMEM((CB, length), f32),
            pltpu.VMEM((blocks, CB, length), f32),
            pltpu.VMEM((blocks, CB, length), f32),
            pltpu.VMEM((8, length), f32),
            pltpu.VMEM((8, length), f32),
        ],
        compiler_params=compiler_params(3),
        cost_estimate=cost(2 * slots * ch * 2048 * length, slots * ch * (4096 + length * 18)),
        name="gate",
    )(*ops)


def back_kernel(hb, sub, *refs):
    (dy_r, xr_r, chan_r, hp_r, cumn_r, ent_r, loc_r, ct, cn, bt, cbt) = refs[:11]
    dxs_o, u1_o, u2_o, kl_o, dcb_o, db_o, dc_o = refs[11:]
    blk = pl.program_id(0) * pl.num_programs(1) + pl.program_id(1)
    chan = chan_r[...]
    hp = hp_r[...]
    length = ct.shape[1]
    nsub = length // sub

    @pl.when(blk == 0)
    def _():
        dcb_o[...] = jnp.zeros_like(dcb_o)
        db_o[...] = jnp.zeros_like(db_o)
        dc_o[...] = jnp.zeros_like(dc_o)

    xc = conv_values(xr_r[...].astype(f32), chan)
    x = xc * sigmoid(xc)
    xs = per_head(x, hp[2 * hb : 3 * hb])
    xs_low = xs.astype(bf16)
    adj = None
    kl = []
    for s in reversed(range(nsub)):
        cols = slice(s * sub, (s + 1) * sub)
        cum = hp[:hb, cols]
        rows_n = cumn_r[cols, :]
        ecum = jnp.exp2(cum)
        last = cum[:, sub - 1 : sub]
        state = ent_r[...].astype(f32)
        if s > 0:
            before = hp[hb : 2 * hb, s * sub - 1 : s * sub]
            state = loc_r[s - 1] + per_head(state, jnp.exp2(before))
        state_low = state.astype(bf16)
        dy_low = dy_r[:, cols]
        dy = dy_low.astype(f32)
        y_in = per_head(dot(state_low, ct[:, cols]), ecum)
        ed = per_head(dy, ecum).astype(bf16)
        dc_o[:, cols] += dot(state_low, ed, TN)
        dxw, yw = [], []
        for h in range(hb):
            hs = slice(h * HEAD, (h + 1) * HEAD)
            gap = jnp.minimum(cum[h : h + 1] - rows_n[:, h : h + 1], 0.0)
            decay = jnp.exp2(gap)
            weight = (decay * cbt[s]).astype(bf16)
            yw.append(dot(xs_low[hs, cols], weight))
            dxw.append(dot(dy_low[hs], weight, NT))
            dcb_o[s] += decay * dot(xs_low[hs, cols], dy_low[hs], TN)
        yw = jnp.concatenate(yw, axis=0)
        dxs = jnp.concatenate(dxw, axis=0)
        u1_o[:, cols] = head_sums(dy * (yw + y_in) - xs_low[:, cols].astype(f32) * dxs, hb)
        add = dot(ed, cn[cols, :])
        if adj is None:
            u2_o[:, cols] = jnp.zeros((hb, sub), f32)
            kl.append(jnp.zeros((hb, 128), f32))
            adj = add
        else:
            ends = jnp.exp2(last - cum)
            adj_low = adj.astype(bf16)
            dxi = per_head(dot(adj_low, bt[:, cols]), ends)
            xs_s = xs[:, cols]
            u2_o[:, cols] = head_sums(xs_s * dxi, hb)
            kl.append(head_sums(adj * state, hb) * jnp.exp2(last))
            db_o[:, cols] += dot(adj_low, per_head(xs_s, ends).astype(bf16), TN)
            dxs = dxs + dxi
            adj = per_head(adj, jnp.exp2(last)) + add
        dxs_o[:, cols] = dxs
    for s in range(nsub):
        kl_o[:, s * 128 : (s + 1) * 128] = kl[nsub - 1 - s]


def back_call(dy, xr, chan, hp, cumn, ent, loc, ct, cn, bt, cbt):
    slots, ch, length = dy.shape
    ncb = ch // CB
    hb = CB // HEAD
    nsub = length // SUB
    full = lambda a: pl.BlockSpec(a.shape, lambda s, c: (0,) * a.ndim)
    per_chan = lambda a: pl.BlockSpec((None, CB, a.shape[2]), lambda s, c: (s, c, 0))
    per_blk = lambda a: pl.BlockSpec((None,) + a.shape[1:], lambda s, c: (s * ncb + c, 0, 0))
    blk_out = lambda w: pl.BlockSpec((None, hb, w), lambda s, c: (s * ncb + c, 0, 0))
    loc_spec = pl.BlockSpec((None, loc.shape[1], CB, 128), lambda s, c: (s, 0, c, 0))
    blocks = slots * ncb
    return pl.pallas_call(
        functools.partial(back_kernel, hb, SUB),
        grid=(slots, ncb),
        in_specs=[per_chan(dy), per_chan(xr), per_chan(chan), per_blk(hp), per_blk(cumn)]
        + [per_chan(ent), loc_spec, full(ct), full(cn), full(bt), full(cbt)],
        out_specs=[
            pl.BlockSpec((None, CB, length), lambda s, c: (s, c, 0)),
            blk_out(length),
            blk_out(length),
            blk_out(128 * nsub),
            pl.BlockSpec((nsub, SUB, SUB), lambda s, c: (0, 0, 0)),
            pl.BlockSpec((128, length), lambda s, c: (0, 0)),
            pl.BlockSpec((128, length), lambda s, c: (0, 0)),
        ],
        out_shape=[
            jax.ShapeDtypeStruct((slots, ch, length), f32),
            jax.ShapeDtypeStruct((blocks, hb, length), f32),
            jax.ShapeDtypeStruct((blocks, hb, length), f32),
            jax.ShapeDtypeStruct((blocks, hb, 128 * nsub), f32),
            jax.ShapeDtypeStruct((nsub, SUB, SUB), f32),
            jax.ShapeDtypeStruct((128, length), f32),
            jax.ShapeDtypeStruct((128, length), f32),
        ],
        compiler_params=compiler_params(2),
        cost_estimate=cost(slots * ch * length * SUB * 40, slots * ch * length * 12),
        name="state_back",
    )(dy, xr, chan, hp, cumn, ent, loc, ct, cn, bt, cbt)


def finish_kernel(hb, *refs):
    (dxs_r, dy_r, xr_r, chan_r, hp_r, ent_r, adj_r, bt) = refs[:8]
    dconv_o, dd_o, u2_o, kf_o, db_o = refs[8:]
    blk = pl.program_id(0) * pl.num_programs(1) + pl.program_id(1)
    chan = chan_r[...]
    hp = hp_r[...]
    length = bt.shape[1]

    @pl.when(blk == 0)
    def _():
        db_o[...] = jnp.zeros_like(db_o)

    xc = conv_values(xr_r[...].astype(f32), chan)
    sig = sigmoid(xc)
    x = xc * sig
    delta = hp[2 * hb : 3 * hb]
    xs = per_head(x, delta)
    total = hp[hb : 2 * hb]
    last = total[:, length - 1 : length]
    ends = jnp.exp2(last - total)
    adj_low = adj_r[...]
    extra = per_head(dot(adj_low, bt[...]), ends)
    u2_o[...] = head_sums(xs * extra, hb)
    kf_o[...] = head_sums(adj_low.astype(f32) * ent_r[...].astype(f32), hb) * jnp.exp2(last)
    db_o[...] += dot(adj_low, per_head(xs, ends).astype(bf16), TN)
    dxs = dxs_r[...] + extra
    dd_o[...] = head_sums(x * dxs, hb)
    dx = per_head(dxs, delta) + dy_r[...].astype(f32) * chan[:, 4:5]
    dconv_o[...] = dx * (sig + x * (1.0 - sig))


def finish_call(dxs, dy, xr, chan, hp, ent, adj, bt):
    slots, ch, length = dy.shape
    ncb = ch // CB
    hb = CB // HEAD
    full = lambda a: pl.BlockSpec(a.shape, lambda s, c: (0,) * a.ndim)
    per_chan = lambda a: pl.BlockSpec((None, CB, a.shape[2]), lambda s, c: (s, c, 0))
    per_blk = lambda a: pl.BlockSpec((None,) + a.shape[1:], lambda s, c: (s * ncb + c, 0, 0))
    blk_out = lambda w: pl.BlockSpec((None, hb, w), lambda s, c: (s * ncb + c, 0, 0))
    blocks = slots * ncb
    return pl.pallas_call(
        functools.partial(finish_kernel, hb),
        grid=(slots, ncb),
        in_specs=[per_chan(dxs), per_chan(dy), per_chan(xr), per_chan(chan), per_blk(hp)]
        + [per_chan(ent), per_chan(adj), full(bt)],
        out_specs=[
            pl.BlockSpec((None, CB, length), lambda s, c: (s, c, 0)),
            blk_out(length),
            blk_out(length),
            blk_out(128),
            pl.BlockSpec((128, length), lambda s, c: (0, 0)),
        ],
        out_shape=[
            jax.ShapeDtypeStruct((slots, ch, length), f32),
            jax.ShapeDtypeStruct((blocks, hb, length), f32),
            jax.ShapeDtypeStruct((blocks, hb, length), f32),
            jax.ShapeDtypeStruct((blocks, hb, 128), f32),
            jax.ShapeDtypeStruct((128, length), f32),
        ],
        compiler_params=compiler_params(2),
        cost_estimate=cost(slots * ch * length * 512, slots * ch * length * 14),
        name="finish_back",
    )(dxs, dy, xr, chan, hp, ent, adj, bt)


def pair_kernel(*refs):
    (dconv_r, halo_r, dz_r, chan_r, upz, upx, low) = refs[:7]
    dx_o, gz_o, gx_o, dl_o = refs[7:]
    blk = pl.program_id(0) * pl.num_programs(1) + pl.program_id(1)
    chan = chan_r[...]

    @pl.when(blk == 0)
    def _():
        dl_o[...] = jnp.zeros_like(dl_o)

    ext = jnp.concatenate([dconv_r[...], halo_r[...]], axis=1)
    width = ext.shape[1]
    out = ext * chan[:, 3:4]
    for k in range(3):
        out = out + pltpu.roll(ext, width - (3 - k), 1) * chan[:, k : k + 1]
    dx = out[:, : width - HALO].astype(bf16)
    dx_o[...] = dx
    dz = dz_r[...]
    gz_o[...] = dot(dz, low[...], NT)
    gx_o[...] = dot(dx, low[...], NT)
    dl_o[...] += dot(upz[...], dz, TN) + dot(upx[...], dx, TN)


def pair_call(dconv, halo, dz, chan, upz, upx, low):
    slots, ch, length = dz.shape
    ncb = ch // CB
    rank2 = low.shape[0]
    full = lambda a: pl.BlockSpec(a.shape, lambda s, c: (0,) * a.ndim)
    per_chan = lambda a: pl.BlockSpec((None, CB, a.shape[2]), lambda s, c: (s, c, 0))
    return pl.pallas_call(
        pair_kernel,
        grid=(slots, ncb),
        in_specs=[per_chan(a) for a in (dconv, halo, dz, chan, upz, upx)] + [full(low)],
        out_specs=[
            pl.BlockSpec((None, CB, length), lambda s, c: (s, c, 0)),
            pl.BlockSpec((None, CB, rank2), lambda s, c: (s, c, 0)),
            pl.BlockSpec((None, CB, rank2), lambda s, c: (s, c, 0)),
            pl.BlockSpec((rank2, length), lambda s, c: (0, 0)),
        ],
        out_shape=[
            jax.ShapeDtypeStruct((slots, ch, length), bf16),
            jax.ShapeDtypeStruct((slots, ch, rank2), f32),
            jax.ShapeDtypeStruct((slots, ch, rank2), f32),
            jax.ShapeDtypeStruct((rank2, length), f32),
        ],
        compiler_params=compiler_params(2),
        cost_estimate=cost(slots * ch * length * 256, slots * ch * length * 8),
        name="pair",
    )(dconv, halo, dz, chan, upz, upx, low)


def project_kernel(sets, kb, *refs):
    n_left = len({left for _, left, _ in sets})
    lefts = refs[:n_left]
    n_w = sum(len(orders) for _, _, orders in sets)
    wrefs = refs[n_left : n_left + n_w]
    out = refs[-2]
    acc = refs[-1]
    slot, c = pl.program_id(0), pl.program_id(1)

    @pl.when((slot == 0) & (c == 0))
    def _():
        acc[...] = jnp.zeros_like(acc)

    turned = [jnp.transpose(ref[...]) for ref in lefts]
    at = 0
    for (lo, hi), left, orders in sets:
        mine = wrefs[at : at + len(orders)]
        at += len(orders)

        @pl.when((slot >= lo) & (slot < hi))
        def _(mine=mine, orders=orders, left=left):
            for ref, offsets in zip(mine, orders):
                for b, off in enumerate(offsets):
                    acc[:, off : off + kb] += dot(turned[left], ref[b])

    @pl.when((slot == pl.num_programs(0) - 1) & (c == pl.num_programs(1) - 1))
    def _():
        out[...] = acc[...]


def project_call(lefts, weights, orders, width, name):
    slots, ch, length = lefts[0].shape
    ncb = ch // CB
    ops = list(lefts)
    specs = [pl.BlockSpec((None, CB, length), lambda s, c: (s, c, 0)) for _ in lefts]
    sets = []
    for ((lo, hi), left, arrays), order in zip(weights, orders):
        sets.append(((lo, hi), left, order))
        for a in arrays:
            ops.append(a)

            def index(s, c, lo=lo, hi=hi, nd=a.ndim):
                cc = jnp.where(s < lo, 0, jnp.where(s >= hi, ncb - 1, c))
                if nd == 3:
                    return (0, cc, 0)
                return (0, jnp.clip(s, lo, hi - 1) - lo, cc, 0)

            shape = (a.shape[0], CB, a.shape[2]) if a.ndim == 3 else (
                a.shape[0], None, CB, a.shape[3])
            specs.append(pl.BlockSpec(shape, index))
    kb = weights[0][2][0].shape[-1]
    n_l = len(lefts)
    return pl.pallas_call(
        functools.partial(project_kernel, sets, kb),
        grid=(slots, ncb),
        in_specs=specs,
        out_specs=pl.BlockSpec((length, width), lambda s, c: (0, 0)),
        out_shape=jax.ShapeDtypeStruct((length, width), f32),
        scratch_shapes=[pltpu.VMEM((length, width), f32)],
        compiler_params=compiler_params(2),
        cost_estimate=cost(2 * n_l * slots * ch * length * width, n_l * slots * ch * width * 2),
        name=name,
    )(*ops)


def body(
    tokens,
    cotangent,
    lengths,
    adapter_ids,
    pre_gain,
    in_inner,
    in_maps,
    in_steps,
    conv_inner,
    conv_maps,
    step_bias,
    decay_log,
    skip_gain,
    norm_gain,
    out_weight,
    adapter_in_down,
    adapter_in_up,
    adapter_out_down,
    adapter_out_up,
):
    planes = lax.axis_size("tensor")
    seqs = lax.axis_size("dp")
    place = lax.axis_index("tensor")
    mine = lax.axis_index("dp")
    length = tokens.shape[1]
    width = tokens.shape[2]
    rows_here = in_inner.shape[0]
    ch = in_inner.shape[2]
    inner = ch * planes
    hs = in_steps.shape[1]
    heads = hs * planes
    rank = adapter_in_down.shape[2]
    adapters = adapter_in_down.shape[0]
    state_w = in_maps.shape[1] // 2
    hb = CB // HEAD
    ncb = ch // CB
    nblk = planes * ncb
    nsub = length // SUB
    quick = seqs == 8 and planes == 4

    def from_plane(v, j):
        return lax.ppermute(v, "tensor", [((s + j) % planes, s) for s in range(planes)])

    def flip(v, bit):
        return lax.ppermute(v, "dp", [(i, i ^ bit) for i in range(seqs)])

    def slot_order(v):
        twice = jnp.concatenate([v, v], axis=0)
        return lax.dynamic_slice_in_dim(twice, place, planes, 0)

    def rel(v):
        if not quick:
            return v
        parts = [
            lax.dynamic_slice_in_dim(v, (mine ^ m) * rows_here, rows_here, 1) for m in range(8)
        ]
        return jnp.concatenate(parts, axis=1)

    wt = jnp.transpose(in_inner, (1, 2, 0))
    if quick:

        def plane_gather(a, b):
            ax, by = flip(a, 2), flip(b, 4)
            a1, b1 = jnp.stack([a, ax]), jnp.stack([b, by])
            a2, b2 = flip(a1, 4), flip(b1, 2)
            return (
                [a1, a2, flip(a1, 1), flip(a2, 1)],
                [b1, b2, flip(b1, 1), flip(b2, 1)],
            )

        k = rows_here
        order_a = [[0, 2 * k], [4 * k, 6 * k], [1 * k, 3 * k], [5 * k, 7 * k]]
        order_b = [[0, 4 * k], [2 * k, 6 * k], [1 * k, 5 * k], [3 * k, 7 * k]]
        slot_w = []
        for j in range(planes):
            w = wt if j == 0 else from_plane(wt, j)
            slot_w.append(plane_gather(w[0], w[1]))
        outs = [out_weight] + [from_plane(out_weight, j) for j in range(1, planes)]
        half = planes // 2
        oa, ob = plane_gather(jnp.stack(outs[:half]), jnp.stack(outs[half:]))
        ow = [((0, half), oa), ((half, planes), ob)]
        oo = [order_a, order_b]
    else:
        order_a = order_b = [[0]]
        w = lax.all_gather(in_inner, "dp", axis=0, tiled=True)
        w = slot_order(lax.all_gather(jnp.transpose(w, (1, 2, 0)), "tensor", axis=0))
        slot_w = [([w[j, 0][None]], [w[j, 1][None]]) for j in range(planes)]
        o = lax.all_gather(out_weight, "dp", axis=1, tiled=True)
        ow = [((0, planes), [slot_order(lax.all_gather(o, "tensor", axis=0))[None]])]
        oo = [[[0]]]

    pick = adapter_ids[0]
    down_in = lax.dynamic_index_in_dim(adapter_in_down, pick, 0, keepdims=False)
    up_here = lax.dynamic_index_in_dim(adapter_in_up, pick, 0, keepdims=False)
    down_here = lax.dynamic_index_in_dim(adapter_out_down, pick, 0, keepdims=False)
    up_out = lax.dynamic_index_in_dim(adapter_out_up, pick, 0, keepdims=False)
    packed = jnp.concatenate(
        [
            jnp.transpose(up_here, (1, 0, 2)).reshape(2 * rank, ch).astype(f32),
            down_here.T.astype(f32),
            conv_inner,
            jnp.repeat(skip_gain, HEAD)[None],
            norm_gain[None],
            jnp.pad(jnp.stack([step_bias, decay_log]), ((0, 0), (0, ch - hs))),
        ],
        axis=0,
    )
    packed = slot_order(lax.all_gather(packed, "tensor", axis=0))
    up_z = jnp.swapaxes(packed[:, :rank], 1, 2).astype(bf16)
    up_x = jnp.swapaxes(packed[:, rank : 2 * rank], 1, 2).astype(bf16)
    down_out = jnp.swapaxes(packed[:, 2 * rank : 3 * rank], 1, 2).astype(bf16)
    chan = jnp.swapaxes(packed[:, 3 * rank : 3 * rank + 6], 1, 2)
    chan = jnp.pad(chan, ((0, 0), (0, 0), (0, 2)))
    bias = packed[:, 3 * rank + 6, :hs].reshape(heads)
    speed = jnp.exp(packed[:, 3 * rank + 7, :hs].reshape(heads))
    up_z2 = jnp.concatenate([up_z, up_z], axis=2)
    up_x2 = jnp.concatenate([up_x, up_x], axis=2)
    down_out2 = jnp.concatenate([down_out, down_out], axis=2)
    steps_all = slot_order(lax.all_gather(in_steps, "tensor", axis=0))
    steps_all = jnp.swapaxes(steps_all, 0, 1).reshape(rows_here, heads)
    small_w = lax.all_gather(
        jnp.concatenate([in_maps, steps_all], axis=1), "dp", axis=0, tiled=True
    )
    ids = lax.all_gather(adapter_ids, "dp", axis=0, tiled=True)

    residual = tokens[0].astype(f32)
    stat = jnp.mean(residual * residual, axis=-1, keepdims=True)
    root = lax.rsqrt(stat + epsilon)
    normed = (residual * root * pre_gain).astype(bf16)
    before = lax.ppermute(normed[-16:], "tensor", [(s, s + 1) for s in range(planes - 1)])
    ext = jnp.concatenate([before, normed], axis=0)
    wide = jnp.concatenate([jnp.zeros((HALO - 16, width), bf16), ext], axis=0)
    nt = jnp.transpose(rel(wide))
    low_t = dot(down_in, wide, ((0,), (1,)))
    low_hi = low_t.astype(bf16)
    low2 = jnp.concatenate([low_hi, (low_t - low_hi.astype(f32)).astype(bf16)], axis=0)

    small = dot(ext, small_w)
    maps_ext = small[:, : 2 * state_w]
    steps = small[16:, 2 * state_w :] + bias
    maps_pre = sum(maps_ext[13 + k : 13 + k + length] * conv_maps[k] for k in range(4))
    maps_sig = jax.nn.sigmoid(maps_pre)
    maps = (maps_pre * maps_sig).astype(bf16)
    b_low, c_low = maps[:, :state_w], maps[:, state_w:]
    bt, ct = b_low.T, c_low.T
    delta = jax.nn.softplus(steps)
    rates = -delta * speed
    upto = (jnp.arange(SUB)[:, None] >= jnp.arange(SUB)[None, :]).astype(f32)
    cum = jnp.einsum(
        "ij,sjh->sih", upto, rates.reshape(nsub, SUB, heads), precision=highest
    )
    ends_before = jnp.concatenate(
        [jnp.zeros((1, heads), f32), jnp.cumsum(cum[:-1, -1], axis=0)], axis=0
    ) if nsub > 1 else jnp.zeros((1, heads), f32)
    cum_all = (cum + ends_before[:, None, :]).reshape(length, heads) * LOG2E
    cum = cum.reshape(length, heads) * LOG2E
    cumn = jnp.transpose(cum.reshape(length, nblk, hb), (1, 0, 2))
    lanes = lambda v: v.T.reshape(nblk, hb, length)
    hp = jnp.concatenate([lanes(cum), lanes(cum_all), lanes(delta)], axis=1)
    by_sub = lambda v: v.reshape(nsub, SUB, state_w)
    keep = upto.T[None]
    cbt = keep * jnp.einsum(
        "sjn,sin->sji", by_sub(b_low), by_sub(c_low), preferred_element_type=f32
    )

    positions = place * length + jnp.arange(length)
    valid = (positions < lengths[0]).astype(f32)[:, None]
    masked = (cotangent[0].astype(f32) * valid).astype(bf16)
    gt = jnp.transpose(rel(masked))
    back_t = dot(up_out, masked, NT)
    back_hi = back_t.astype(bf16)
    back2 = jnp.concatenate([back_hi, (back_t - back_hi.astype(f32)).astype(bf16)], axis=0)

    bufs = None
    for j in range(planes):
        zw, xw = slot_w[j]
        bufs = forward_slot(
            j, zw, xw, order_a, order_b, nt, low2, up_z2, up_x2, chan, hp, cumn, ct, b_low, cbt,
            bufs,
        )
    z, xr, mix, loc, s_end = bufs

    total = jnp.exp2(jnp.repeat(cum_all[-1].reshape(planes, hs), HEAD, axis=1))[:, :, None]
    ent = jnp.zeros((planes, ch, state_w), bf16)
    for _ in range(planes - 1):
        send = (ent.astype(f32) * total + s_end).astype(bf16)
        got = lax.ppermute(send, "tensor", [(s, s + 1) for s in range(planes - 1)])
        ent = jnp.roll(got, -1, axis=0)

    nout, dy, dz, sl = gate_call(
        ow, oo, gt, back2, down_out2, chan, hp, mix, z, ent, ct, c_low, inner
    )

    adj = jnp.zeros((planes, ch, state_w), bf16)
    for _ in range(planes - 1):
        send = (adj.astype(f32) * total + sl).astype(bf16)
        got = lax.ppermute(send, "tensor", [(s + 1, s) for s in range(planes - 1)])
        adj = jnp.roll(got, 1, axis=0)

    dxs, u1, u2, kl, dcb, db1, dc1 = back_call(
        dy, xr, chan, hp, cumn, ent, loc, ct, c_low, bt, cbt
    )
    dconv, ddelta, u2f, kf, db2 = finish_call(dxs, dy, xr, chan, hp, ent, adj, bt)

    dcb = (dcb * keep).astype(bf16)
    d_b = (db1 + db2).T + jnp.einsum(
        "sji,sin->sjn", dcb, by_sub(c_low), preferred_element_type=f32
    ).reshape(length, state_w)
    d_c = dc1.T + jnp.einsum(
        "sji,sjn->sin", dcb, by_sub(b_low), preferred_element_type=f32
    ).reshape(length, state_w)
    d_maps_pre = jnp.concatenate([d_b, d_c], axis=1) * (
        maps_sig * (1.0 + maps_pre * (1.0 - maps_sig))
    )
    flat = lambda v: v.reshape(heads, length)
    rate_in = jnp.einsum(
        "hst,tu->hsu", flat(u1).reshape(heads, nsub, SUB), upto, precision=highest
    )
    rate_in += jnp.einsum(
        "hst,tu->hsu", flat(u2).reshape(heads, nsub, SUB), 1.0 - upto, precision=highest
    )
    rate_in += jnp.sum(kl.reshape(heads, nsub, 128), axis=-1, keepdims=True)
    after = (jnp.arange(length)[:, None] < jnp.arange(length)[None, :]).astype(f32)
    d_rate = rate_in.reshape(heads, length) + jnp.dot(flat(u2f), after, precision=highest)
    d_rate += jnp.sum(kf.reshape(heads, 128), axis=-1, keepdims=True)
    d_delta = flat(ddelta) - speed[:, None] * d_rate
    d_steps = (d_delta * jax.nn.sigmoid(steps.T)).astype(bf16)

    near = lax.ppermute(
        jnp.concatenate(
            [jnp.swapaxes(dconv[:, :, :4], 1, 2).reshape(planes * 4 * ch),
             d_maps_pre[:4].reshape(8 * state_w)]
        ),
        "tensor",
        [(s + 1, s) for s in range(planes - 1)],
    )
    near_x = jnp.swapaxes(near[: planes * 4 * ch].reshape(planes, 4, ch), 1, 2)
    near_x = jnp.pad(jnp.roll(near_x, 1, axis=0), ((0, 0), (0, 0), (0, HALO - 4)))
    near_maps = near[planes * 4 * ch :].reshape(4, 2 * state_w)
    maps_more = jnp.concatenate([d_maps_pre, near_maps], axis=0)
    d_maps = sum(maps_more[3 - k : 3 - k + length] * conv_maps[k] for k in range(4))

    dx, grad_z, grad_x, d_low2 = pair_call(
        dconv, near_x, dz, chan, up_z2, up_x2, low2[:, HALO:]
    )
    d_low = d_low2[:rank]

    weights = []
    orders = []
    for j in range(planes):
        for left in range(2):
            weights.append(((j, j + 1), left, slot_w[j][left]))
            orders.append((order_a, order_b)[left])
    d_normed = project_call([dz, dx], weights, orders, width, "input_back")
    left = jnp.concatenate([d_maps.astype(bf16), d_steps.T, d_low.T.astype(bf16)], axis=1)
    right = jnp.concatenate([small_w, down_in], axis=1)
    d_normed = rel(d_normed) + dot(left, right, NT)
    d_scaled = d_normed * pre_gain
    d_resid = root * d_scaled - residual * root * root * root * jnp.mean(
        d_scaled * residual, axis=-1, keepdims=True
    )
    tokens_grad = (masked.astype(f32) + d_resid).astype(bf16)[None]

    branch = rel(
        project_call(
            [nout], [(span, 0, arrays) for span, arrays in ow], oo, width, "output"
        )
    )
    hidden_t = jnp.einsum("jkr,jkt->rt", down_out, nout, preferred_element_type=f32)
    branch = branch + dot(hidden_t.astype(bf16), up_out, TN)
    mixed = (valid * (residual + branch)).astype(bf16)[None]

    grad_up = jnp.stack(
        [grad_z[..., :rank] + grad_z[..., rank:], grad_x[..., :rank] + grad_x[..., rank:]], axis=1
    )
    grad_down_out = jnp.einsum("jkt,rt->jkr", nout, back_hi, preferred_element_type=f32)
    grad_down = dot(normed, d_low.T.astype(bf16), TN)
    grad_up_out = dot(hidden_t.astype(bf16), masked)
    to_planes = jnp.concatenate(
        [
            grad_up.reshape(planes, 2 * ch * rank),
            grad_down_out.reshape(planes, ch * rank),
            slot_order(grad_down.reshape(planes, width * rank // planes)),
            slot_order(grad_up_out.reshape(planes, width * rank // planes)),
        ],
        axis=1,
    )
    summed = to_planes[0]
    for j in range(1, planes):
        part = to_planes[j].astype(bf16)
        summed += lax.ppermute(
            part, "tensor", [(s, (s + j) % planes) for s in range(planes)]
        ).astype(f32)
    chosen = (ids[None, :] == jnp.arange(adapters)[:, None]).astype(bf16)
    head_part = 3 * ch * rank
    by_seq = lax.all_gather(summed.astype(bf16), "dp", axis=0)
    headwise = dot(chosen, by_seq[:, :head_part])
    shared = lax.all_gather(
        dot(chosen, by_seq[:, head_part:]).astype(bf16), "tensor", axis=0
    ).astype(f32)
    shared = jnp.transpose(shared.reshape(planes, adapters, 2, -1), (2, 1, 0, 3))
    g_down = shared[0].reshape(adapters, width, rank)
    g_up_out = shared[1].reshape(adapters, rank, width)
    g_up = jnp.transpose(
        headwise[:, : 2 * ch * rank].reshape(adapters, 2, ch, rank), (0, 3, 1, 2)
    )
    g_down_out = headwise[:, 2 * ch * rank :].reshape(adapters, ch, rank)
    return (mixed, tokens_grad, g_down, g_up, g_down_out, g_up_out)


def solution(mesh):
    placed = (
        P("dp", "tensor", None),
        P("dp", "tensor", None),
        P("dp"),
        P("dp"),
        P(),
        P("dp", None, "tensor"),
        P("dp", None),
        P("dp", "tensor"),
        P(None, "tensor"),
        P(),
        P("tensor"),
        P("tensor"),
        P("tensor"),
        P("tensor"),
        P("tensor", "dp"),
        P(),
        P(None, None, None, "tensor"),
        P(None, "tensor", None),
        P(),
    )
    return jax.shard_map(
        body,
        mesh=mesh,
        in_specs=placed,
        out_specs=(
            P("dp", "tensor", None),
            P("dp", "tensor", None),
            P(),
            P(None, None, None, "tensor"),
            P(None, "tensor", None),
            P(),
        ),
        check_vma=False,
    )
```

```python
import functools

import jax
import jax.numpy as jnp
from jax import lax
from jax.experimental import pallas as pl
from jax.experimental.pallas import tpu as pltpu
from jax.sharding import PartitionSpec as P

f32 = jnp.float32
bf16 = jnp.bfloat16
epsilon = 1e-05
highest = lax.Precision.HIGHEST
LOG2E = 1.4426950408889634
HEAD = 64
HALO = 128
SUB = 256
CB = 256

NN = ((1,), (0,))
NT = ((1,), (1,))
TN = ((0,), (0,))


def dot(a, b, dims=NN):
    return lax.dot_general(a, b, (dims, ((), ())), preferred_element_type=f32)


def compiler_params(grid_rank):
    return pltpu.CompilerParams(
        dimension_semantics=("arbitrary",) * grid_rank, vmem_limit_bytes=60 * 2**20
    )


def cost(flops, size):
    return pl.CostEstimate(
        flops=int(flops) // 8, bytes_accessed=int(size) // 8, transcendentals=0
    )


def sigmoid(v):
    return 0.5 + 0.5 * jnp.tanh(0.5 * v)


def conv_values(raw, chan):
    out = raw * chan[:, 3:4]
    for k in range(3):
        out = out + pltpu.roll(raw, 3 - k, 1) * chan[:, k : k + 1]
    return out[:, HALO:]


def per_head(values, rows):
    hb = rows.shape[0]
    parts = [values[h * HEAD : (h + 1) * HEAD] * rows[h : h + 1] for h in range(hb)]
    return jnp.concatenate(parts, axis=0)


def head_sums(values, hb):
    parts = [
        jnp.sum(values[h * HEAD : (h + 1) * HEAD], axis=0, keepdims=True) for h in range(hb)
    ]
    return jnp.concatenate(parts, axis=0)


def joined(refs, picks):
    parts = [refs[k][b] for k, b in picks]
    return parts[0] if len(parts) == 1 else jnp.concatenate(parts, axis=1)


def block_at(mine, m, quick):
    return pl.multiple_of((mine ^ m) * CB, CB) if quick else m * CB


def turn_kernel(flat, quick, *refs):
    (sc, tok_r, bef_r, cot_r, gain, down, up) = refs[:7]
    normed_o, masked_o, root_o, low_o, back_o, nt_o, gt_o, tok_o, halo_sc = refs[-9:]
    tok_o[...] = jnp.zeros_like(tok_o)
    width = tok_r.shape[1]
    length = tok_r.shape[0]

    def norm(v):
        v = v.astype(f32)
        root = lax.rsqrt(jnp.sum(v * v, axis=1, keepdims=True) * (1.0 / width) + epsilon)
        return (v * root * gain[...]).astype(bf16), root

    normed, root = norm(tok_r[...])
    normed_o[...] = normed
    root_o[...] = root
    halo_sc[...] = jnp.zeros_like(halo_sc)
    halo_sc[HALO - 16 :, :] = norm(bef_r[...])[0]
    rows = lax.broadcasted_iota(jnp.int32, (length, 1), 0)
    masked_o[...] = jnp.where(rows < sc[1], cot_r[...].astype(f32), 0.0).astype(bf16)
    low = back = None
    for i, m in enumerate(flat):
        at = pl.ds(block_at(sc[0], m, quick), CB)
        nt = jnp.concatenate(
            [jnp.transpose(halo_sc[:, at]), jnp.transpose(normed_o[:, at])], axis=1
        )
        gt = jnp.transpose(masked_o[:, at])
        nt_o[i * CB : (i + 1) * CB, :] = nt
        gt_o[i * CB : (i + 1) * CB, :] = gt
        low_m = dot(down[at, :], nt, TN)
        back_m = dot(up[:, at], gt)
        low = low_m if low is None else low + low_m
        back = back_m if back is None else back + back_m
    for out, v in ((low_o, low), (back_o, back)):
        hi = v.astype(bf16)
        out[...] = jnp.concatenate([hi, (v - hi.astype(f32)).astype(bf16)], axis=0)


def turn_call(sc, tokens, before, cot, gain, down, up, flat, quick, later):
    length, width = tokens.shape
    rank = up.shape[0]
    ext = length + HALO
    vm = pl.BlockSpec(memory_space=pltpu.VMEM)
    return pl.pallas_call(
        functools.partial(turn_kernel, flat, quick),
        in_specs=[pl.BlockSpec(memory_space=pltpu.SMEM)] + [vm] * 6
        + [pl.BlockSpec(memory_space=pl.ANY)] * len(later),
        out_specs=[vm] * 8,
        out_shape=[
            jax.ShapeDtypeStruct((length, width), bf16),
            jax.ShapeDtypeStruct((length, width), bf16),
            jax.ShapeDtypeStruct((length, 1), f32),
            jax.ShapeDtypeStruct((2 * rank, ext), bf16),
            jax.ShapeDtypeStruct((2 * rank, length), bf16),
            jax.ShapeDtypeStruct((width, ext), bf16),
            jax.ShapeDtypeStruct((width, length), bf16),
            jax.ShapeDtypeStruct((8, 128), f32),
        ],
        scratch_shapes=[pltpu.VMEM((HALO, width), bf16)],
        compiler_params=compiler_params(0),
        cost_estimate=cost(length * width * 200, length * width * 16),
        name="turn",
    )(sc, tokens, before, cot, gain, down, up, *later)


def row_specs(paths, first, rows):
    ops, specs = [], []
    for arrays in paths:
        for a in arrays:
            ops.append(a)
            specs.append(
                pl.BlockSpec((a.shape[0], rows, a.shape[2]), lambda i: (0, first // rows, 0))
            )
    return ops, specs


def maps_kernel(n_w, picks, sub, *refs):
    nt, taps = refs[n_w : n_w + 2]
    bt_o, ct_o, bn_o, cn_o, cbt_o, pre_o, w_o = refs[-7:]
    length = bt_o.shape[1]
    state_w = bt_o.shape[0]
    per = n_w // len(picks)
    w = jnp.concatenate(
        [joined(refs[p * per : (p + 1) * per], order) for p, order in enumerate(picks)], axis=0
    )
    w_o[...] = w
    maps_pre = conv_values(dot(w, nt[...]), taps[...])
    pre_o[...] = maps_pre
    maps = (maps_pre * sigmoid(maps_pre)).astype(bf16)
    bt, ct = maps[:state_w], maps[state_w:]
    bt_o[...] = bt
    ct_o[...] = ct
    bn = jnp.transpose(bt)
    bn_o[...] = bn
    cn_o[...] = jnp.transpose(ct)
    row = lax.broadcasted_iota(jnp.int32, (sub, sub), 0)
    col = lax.broadcasted_iota(jnp.int32, (sub, sub), 1)
    upto = jnp.where(row <= col, 1.0, 0.0)
    for s in range(length // sub):
        cols = slice(s * sub, (s + 1) * sub)
        cbt_o[s] = upto * dot(bn[cols, :], ct[:, cols])


def maps_call(paths, first, rows, picks, nt, taps, length, later):
    ops, specs = row_specs(paths, first, rows)
    state_w = rows * len(picks) // 2
    vm = pl.BlockSpec(memory_space=pltpu.VMEM)
    n_w = len(ops)
    return pl.pallas_call(
        functools.partial(maps_kernel, n_w, picks, SUB),
        grid=(1,),
        in_specs=specs + [vm, vm] + [pl.BlockSpec(memory_space=pl.ANY)] * len(later),
        out_specs=[vm] * 7,
        out_shape=[
            jax.ShapeDtypeStruct((state_w, length), bf16),
            jax.ShapeDtypeStruct((state_w, length), bf16),
            jax.ShapeDtypeStruct((length, state_w), bf16),
            jax.ShapeDtypeStruct((length, state_w), bf16),
            jax.ShapeDtypeStruct((length // SUB, SUB, SUB), f32),
            jax.ShapeDtypeStruct((2 * state_w, length), f32),
            jax.ShapeDtypeStruct((2 * state_w, nt.shape[0]), bf16),
        ],
        compiler_params=compiler_params(1),
        cost_estimate=cost(nt.shape[0] * nt.shape[1] * 512, nt.size * 2 + nt.shape[0] * 1024),
        name="maps",
    )(*ops, nt, taps, *later)


def steps_kernel(n_w, order, hb, sub, *refs):
    nt, bias, speed = refs[n_w : n_w + 3]
    hp_o, sig_o, w_o = refs[-3:]
    length = sig_o.shape[1]
    heads = sig_o.shape[0]
    w = joined(refs[:n_w], order)
    w_o[...] = w
    steps = dot(w, nt[:, HALO:]) + bias[...]
    sig_o[...] = sigmoid(steps)
    delta = jnp.maximum(steps, 0.0) + jnp.log1p(jnp.exp(-jnp.abs(steps)))
    rates = -delta * speed[...]
    row = lax.broadcasted_iota(jnp.int32, (sub, sub), 0)
    col = lax.broadcasted_iota(jnp.int32, (sub, sub), 1)
    upto = jnp.where(row <= col, 1.0, 0.0)
    before = None
    for s in range(length // sub):
        cols = slice(s * sub, (s + 1) * sub)
        cum = (
            lax.dot_general(
                rates[:, cols], upto, (NN, ((), ())), precision=highest,
                preferred_element_type=f32,
            )
            * LOG2E
        )
        cum_all = cum if before is None else cum + before
        before = cum_all[:, sub - 1 : sub]
        for b in range(heads // hb):
            mine = slice(b * hb, (b + 1) * hb)
            hp_o[b, :hb, cols] = cum[mine]
            hp_o[b, hb : 2 * hb, cols] = cum_all[mine]
            hp_o[b, 2 * hb :, cols] = delta[mine, cols]


def steps_call(arrays, first, order, nt, bias, speed, length, later):
    heads = bias.shape[0]
    hb = CB // HEAD
    ops, specs = row_specs([arrays], first, heads)
    vm = pl.BlockSpec(memory_space=pltpu.VMEM)
    return pl.pallas_call(
        functools.partial(steps_kernel, len(ops), order, hb, SUB),
        grid=(1,),
        in_specs=specs + [vm] * 3 + [pl.BlockSpec(memory_space=pl.ANY)] * len(later),
        out_specs=[vm] * 3,
        out_shape=[
            jax.ShapeDtypeStruct((heads // hb, 3 * hb, length), f32),
            jax.ShapeDtypeStruct((heads, length), f32),
            jax.ShapeDtypeStruct((heads, nt.shape[0]), bf16),
        ],
        compiler_params=compiler_params(1),
        cost_estimate=cost(nt.shape[0] * nt.shape[1] * 128, nt.size * 2),
        name="steps",
    )(*ops, nt, bias, speed, *later)


def hop_kernel(hb, ncb, got, own, hp, *rest):
    out = rest[-1]
    length = hp.shape[2]
    for c in range(ncb):
        rows = slice(c * CB, (c + 1) * CB)
        total = jnp.exp2(hp[c, hb : 2 * hb, length - 1 : length])
        out[rows, :] = (per_head(got[rows, :].astype(f32), total) + own[rows, :]).astype(bf16)


def hop_call(got, shift, own, hp, later=()):
    slots, ch, state_w = own.shape
    ncb = ch // CB
    return pl.pallas_call(
        functools.partial(hop_kernel, CB // HEAD, ncb),
        grid=(slots,),
        in_specs=[
            pl.BlockSpec((None, ch, state_w), lambda s: ((s + shift) % slots, 0, 0)),
            pl.BlockSpec((None, ch, state_w), lambda s: (s, 0, 0)),
            pl.BlockSpec((ncb,) + hp.shape[1:], lambda s: (s, 0, 0)),
        ]
        + [pl.BlockSpec(memory_space=pl.ANY)] * len(later),
        out_specs=pl.BlockSpec((None, ch, state_w), lambda s: (s, 0, 0)),
        out_shape=jax.ShapeDtypeStruct((slots, ch, state_w), bf16),
        compiler_params=compiler_params(1),
        cost_estimate=cost(own.size * 4, own.size * 8),
        name="hop",
    )(got, own, hp, *later)


def hold_kernel(*refs):
    refs[-1][...] = jnp.zeros_like(refs[-1])


def hold(deps, passed=()):
    anywhere = pl.BlockSpec(memory_space=pl.ANY)
    deps, passed = list(deps), list(passed)
    out = pl.pallas_call(
        hold_kernel,
        in_specs=[anywhere] * (len(deps) + len(passed)),
        out_specs=[anywhere] * len(passed) + [pl.BlockSpec(memory_space=pltpu.VMEM)],
        out_shape=[jax.ShapeDtypeStruct(v.shape, v.dtype) for v in passed]
        + [jax.ShapeDtypeStruct((8, 128), f32)],
        input_output_aliases={len(deps) + k: k for k in range(len(passed))},
        cost_estimate=cost(8, 8),
        name="hold",
    )(*deps, *passed)
    return out[-1][0, 0].astype(bf16), out[-1], list(out[:-1])


def path_dots(out, refs, picks, right, step, blocks):
    per = len(refs) // len(picks)
    for p, order in enumerate(picks):
        mine = refs[p * per : (p + 1) * per]

        @pl.when(step // (blocks // len(picks)) == p)
        def _(mine=mine, order=order):
            out[...] = dot(joined(mine, order), right)


def scan_kernel(nx, picks, ncb, hb, sub, *refs):
    xrefs = refs[:nx]
    (nt, low, upx, chan_r, hp_r, ct, bn, cbt) = refs[nx : nx + 8]
    xc_out, mix_out, ent_out, st_out, sent_out, tok_out, raw_sc = refs[-7:]
    tok_out[...] = jnp.zeros_like(tok_out)
    chan = chan_r[...]
    hp = hp_r[...]
    length = ct.shape[1]
    path_dots(raw_sc, xrefs, picks, nt[...], pl.program_id(1), ncb)
    xr = raw_sc[...] + dot(upx[...], low[...])
    xc = conv_values(xr, chan)
    xc_out[...] = xc.astype(bf16)
    x = xc * sigmoid(xc)
    xs = per_head(x, hp[2 * hb : 3 * hb])
    xs_low = xs.astype(bf16)
    state = None
    for s in range(length // sub):
        cols = slice(s * sub, (s + 1) * sub)
        cum = hp[:hb, cols]
        rows_n = jnp.transpose(jnp.concatenate([cum, cum], axis=0))
        within = []
        for h in range(hb):
            gap = jnp.minimum(cum[h : h + 1] - rows_n[:, h : h + 1], 0.0)
            weight = (jnp.exp2(gap) * cbt[s]).astype(bf16)
            within.append(dot(xs_low[h * HEAD : (h + 1) * HEAD, cols], weight))
        y = jnp.concatenate(within, axis=0)
        last = cum[:, sub - 1 : sub]
        ends = jnp.exp2(last - cum)
        add = dot(per_head(xs[:, cols], ends).astype(bf16), bn[cols, :])
        if s > 0:
            ent_out[s - 1] = state
            y = y + per_head(dot(state.astype(bf16), ct[:, cols]), jnp.exp2(cum))
            state = per_head(state, jnp.exp2(last)) + add
        else:
            state = add
        mix_out[:, cols] = y + x[:, cols] * chan[:, 4:5]
    if length // sub == 1:
        ent_out[0] = state
    st_out[...] = state
    sent_out[...] = state.astype(bf16)


def range_specs(lo, ncb):
    full = lambda a: pl.BlockSpec(a.shape, lambda s, c: (0,) * a.ndim)
    per_chan = lambda a: pl.BlockSpec((None, CB, a.shape[2]), lambda s, c: (s + lo, c, 0))
    per_blk = lambda a: pl.BlockSpec(
        (None,) + a.shape[1:], lambda s, c: ((s + lo) * ncb + c, 0, 0)
    )
    return full, per_chan, per_blk


def weight_specs(weight, ncb):
    paths, base = weight
    per = ncb // len(paths)
    ops, specs = [], []
    for p, arrays in enumerate(paths):
        for a in arrays:
            ops.append(a)
            index = lambda s, c, p=p: (0, (s + base) * per + jnp.clip(c - p * per, 0, per - 1), 0)
            specs.append(pl.BlockSpec((a.shape[0], CB, a.shape[2]), index))
    return ops, specs


def scan_call(lo, hi, xw, picks, nt, low, upx, chan, hp, ct, bn, cbt, bufs, later=()):
    slots, ch = upx.shape[0], upx.shape[1]
    length = ct.shape[1]
    ext = low.shape[1]
    hb = CB // HEAD
    ncb = ch // CB
    nsub = length // SUB
    full, per_chan, per_blk = range_specs(lo, ncb)
    ops, specs = weight_specs(xw, ncb)
    nx = len(ops)
    ops += [nt, low, upx, chan, hp, ct, bn, cbt]
    specs += [full(nt), full(low), per_chan(upx), per_chan(chan)]
    specs += [per_blk(hp), full(ct), full(bn), full(cbt)]
    inner_states = max(nsub - 1, 1)
    shapes = [
        jax.ShapeDtypeStruct((slots, ch, length), bf16),
        jax.ShapeDtypeStruct((slots, ch, length), f32),
        jax.ShapeDtypeStruct((slots, inner_states, ch, 128), f32),
        jax.ShapeDtypeStruct((slots, ch, 128), f32),
        jax.ShapeDtypeStruct((slots, ch, 128), bf16),
        jax.ShapeDtypeStruct((8, 128), f32),
    ]
    chan_out = lambda w: pl.BlockSpec((None, CB, w), lambda s, c: (s + lo, c, 0))
    outs = [
        chan_out(length),
        chan_out(length),
        pl.BlockSpec((None, inner_states, CB, 128), lambda s, c: (s + lo, 0, c, 0)),
        chan_out(128),
        chan_out(128),
        pl.BlockSpec((8, 128), lambda s, c: (0, 0)),
    ]
    aliases = {}
    if bufs is not None:
        aliases = {len(ops) + k: k for k in range(5)}
        ops += list(bufs)
        specs += [pl.BlockSpec(memory_space=pl.ANY)] * 5
    ops += list(later)
    specs += [pl.BlockSpec(memory_space=pl.ANY)] * len(later)
    n = hi - lo
    out = pl.pallas_call(
        functools.partial(scan_kernel, nx, picks, ncb, hb, SUB),
        grid=(n, ncb),
        in_specs=specs,
        out_specs=outs,
        out_shape=shapes,
        scratch_shapes=[pltpu.VMEM((CB, ext), f32)],
        input_output_aliases=aliases,
        compiler_params=compiler_params(2),
        cost_estimate=cost(4 * n * ch * 2048 * ext, n * ch * (4096 + length * 8)),
        name="scan_slots",
    )(*ops)
    return out[:5], out[5]


def proj_kernel(n, picks, ncb, cut, gain, *refs):
    (right, low, up) = refs[n : n + 3]
    chan_r = refs[n + 3]
    out, tok_o, sc = refs[-3:]
    tok_o[...] = jnp.zeros_like(tok_o)
    path_dots(sc, refs[:n], picks, right[:, cut:], pl.program_id(1), ncb)
    value = sc[...] + dot(up[...], low[:, cut:])
    if gain:
        value = value * chan_r[:, 5:6]
    out[...] = value.astype(bf16)


def proj_call(lo, hi, weight, picks, right, low, up, chan, cut, gain, buf, later=()):
    slots, ch = up.shape[0], up.shape[1]
    length = right.shape[1] - cut
    ncb = ch // CB
    full, per_chan, _ = range_specs(lo, ncb)
    ops, specs = weight_specs(weight, ncb)
    n_w = len(ops)
    ops += [right, low, up, chan]
    specs += [full(right), full(low), per_chan(up), per_chan(chan)]
    aliases = {}
    if buf is not None:
        aliases = {len(ops): 0}
        ops.append(buf)
        specs.append(pl.BlockSpec(memory_space=pl.ANY))
    ops += list(later)
    specs += [pl.BlockSpec(memory_space=pl.ANY)] * len(later)
    n = hi - lo
    return pl.pallas_call(
        functools.partial(proj_kernel, n_w, picks, ncb, cut, gain),
        grid=(n, ncb),
        in_specs=specs,
        out_specs=[
            pl.BlockSpec((None, CB, length), lambda s, c: (s + lo, c, 0)),
            pl.BlockSpec((8, 128), lambda s, c: (0, 0)),
        ],
        out_shape=[
            jax.ShapeDtypeStruct((slots, ch, length), bf16),
            jax.ShapeDtypeStruct((8, 128), f32),
        ],
        scratch_shapes=[pltpu.VMEM((CB, length), f32)],
        input_output_aliases=aliases,
        compiler_params=compiler_params(2),
        cost_estimate=cost(2 * n * ch * 2048 * length, n * ch * (4096 + length * 2)),
        name="proj_slots",
    )(*ops)


def gate_kernel(hb, inner, *refs):
    (z_r, mix_r, wgt_r, ent_r, chan_r, hp_r, ct, cn) = refs[:8]
    nout_o, dmix_o, dz_o, sl_o, sent_o = refs[8:13]
    mix_sc, sq_sc, dot_sc = refs[13:]
    phase = pl.program_id(0)
    blk = pl.program_id(1) * pl.num_programs(2) + pl.program_id(2)
    length = ct.shape[1]
    z = z_r[...].astype(f32)
    sig = sigmoid(z)
    silu = z * sig
    weighted = wgt_r[...].astype(f32)
    cum = jnp.exp2(hp_r[hb : 2 * hb])

    @pl.when((phase == 0) & (blk == 0))
    def _():
        sq_sc[...] = jnp.zeros_like(sq_sc)
        dot_sc[...] = jnp.zeros_like(dot_sc)

    @pl.when(phase == 0)
    def _():
        mix = mix_r[...] + per_head(dot(ent_r[...], ct[...]), cum)
        mix_sc[blk] = mix
        gated = mix * silu
        sq_sc[...] += jnp.sum((gated * gated).reshape(CB // 8, 8, length), axis=0)
        dot_sc[...] += jnp.sum((gated * weighted).reshape(CB // 8, 8, length), axis=0)

    @pl.when(phase == 1)
    def _():
        r = lax.rsqrt(jnp.sum(sq_sc[...], axis=0, keepdims=True) * (1.0 / inner) + epsilon)
        coef = r * r * r * (jnp.sum(dot_sc[...], axis=0, keepdims=True) * (1.0 / inner))
        mix = mix_sc[blk]
        gated = mix * silu
        nout_o[...] = (gated * (r * chan_r[:, 5:6])).astype(bf16)
        d_gated = r * weighted - gated * coef
        d_mix = d_gated * silu
        dmix_o[...] = d_mix.astype(bf16)
        dz_o[...] = (d_gated * mix * (sig + silu * (1.0 - sig))).astype(bf16)
        adj = dot(per_head(d_mix, cum).astype(bf16), cn[...])
        sl_o[...] = adj
        sent_o[...] = adj.astype(bf16)


def gate_call(z, mix, wgt, ent, chan, hp, ct, cn, inner):
    slots, ch, length = mix.shape
    ncb = ch // CB
    hb = CB // HEAD
    full = lambda a: pl.BlockSpec(a.shape, lambda p, s, c: (0,) * a.ndim)
    per_chan = lambda a: pl.BlockSpec((None, CB, a.shape[2]), lambda p, s, c: (s, c, 0))
    per_blk = lambda a: pl.BlockSpec((None,) + a.shape[1:], lambda p, s, c: (s * ncb + c, 0, 0))
    held = lambda p, s, c, k: (
        jnp.where(p == 0, (s + k) % slots, (slots - 1 + k) % slots),
        jnp.where(p == 0, c, ncb - 1),
        0,
    )
    first = lambda a, k: pl.BlockSpec((None, CB, a.shape[2]), lambda p, s, c: held(p, s, c, k))
    later = lambda w: pl.BlockSpec(
        (None, CB, w), lambda p, s, c: (jnp.where(p == 1, s, 0), jnp.where(p == 1, c, 0), 0)
    )
    return pl.pallas_call(
        functools.partial(gate_kernel, hb, inner),
        grid=(2, slots, ncb),
        in_specs=[per_chan(z), first(mix, 0), per_chan(wgt), first(ent, 1), per_chan(chan)]
        + [per_blk(hp), full(ct), full(cn)],
        out_specs=[later(length), later(length), later(length), later(128), later(128)],
        out_shape=[
            jax.ShapeDtypeStruct((slots, ch, length), bf16),
            jax.ShapeDtypeStruct((slots, ch, length), bf16),
            jax.ShapeDtypeStruct((slots, ch, length), bf16),
            jax.ShapeDtypeStruct((slots, ch, 128), f32),
            jax.ShapeDtypeStruct((slots, ch, 128), bf16),
        ],
        scratch_shapes=[
            pltpu.VMEM((slots * ncb, CB, length), f32),
            pltpu.VMEM((8, length), f32),
            pltpu.VMEM((8, length), f32),
        ],
        compiler_params=compiler_params(3),
        cost_estimate=cost(slots * ch * length * 600, slots * ch * length * 22),
        name="gate",
    )(z, mix, wgt, ent, chan, hp, ct, cn)


def grid_specs(ncb):
    full = lambda a: pl.BlockSpec(a.shape, lambda s, c: (0,) * a.ndim)
    per_chan = lambda a: pl.BlockSpec((None, CB, a.shape[2]), lambda s, c: (s, c, 0))
    per_blk = lambda a: pl.BlockSpec((None,) + a.shape[1:], lambda s, c: (s * ncb + c, 0, 0))
    return full, per_chan, per_blk


def back_kernel(hb, sub, *refs):
    (dy_r, xc_r, hp_r, ent_r, loc_r, ct, cn, bt, cbt) = refs[:9]
    dxs_o, u1_o, u2_o, kl_o, dcb_o, db_o, dc_o = refs[-7:]
    blk = pl.program_id(0) * pl.num_programs(1) + pl.program_id(1)
    hp = hp_r[...]
    length = ct.shape[1]
    nsub = length // sub

    @pl.when(blk == 0)
    def _():
        dcb_o[...] = jnp.zeros_like(dcb_o)
        db_o[...] = jnp.zeros_like(db_o)
        dc_o[...] = jnp.zeros_like(dc_o)

    xc = xc_r[...].astype(f32)
    x = xc * sigmoid(xc)
    xs = per_head(x, hp[2 * hb : 3 * hb])
    xs_low = xs.astype(bf16)
    adj = None
    kl = []
    for s in reversed(range(nsub)):
        cols = slice(s * sub, (s + 1) * sub)
        cum = hp[:hb, cols]
        rows_n = jnp.transpose(jnp.concatenate([cum, cum], axis=0))
        ecum = jnp.exp2(cum)
        last = cum[:, sub - 1 : sub]
        state = ent_r[...].astype(f32)
        if s > 0:
            before = hp[hb : 2 * hb, s * sub - 1 : s * sub]
            state = loc_r[s - 1] + per_head(state, jnp.exp2(before))
        state_low = state.astype(bf16)
        dy_low = dy_r[:, cols]
        dy = dy_low.astype(f32)
        y_in = per_head(dot(state_low, ct[:, cols]), ecum)
        ed = per_head(dy, ecum).astype(bf16)
        dc_o[:, cols] += dot(state_low, ed, TN)
        dxw, yw = [], []
        for h in range(hb):
            hs = slice(h * HEAD, (h + 1) * HEAD)
            gap = jnp.minimum(cum[h : h + 1] - rows_n[:, h : h + 1], 0.0)
            decay = jnp.exp2(gap)
            weight = (decay * cbt[s]).astype(bf16)
            yw.append(dot(xs_low[hs, cols], weight))
            dxw.append(dot(dy_low[hs], weight, NT))
            dcb_o[s] += decay * dot(xs_low[hs, cols], dy_low[hs], TN)
        yw = jnp.concatenate(yw, axis=0)
        dxs = jnp.concatenate(dxw, axis=0)
        u1_o[:, cols] = head_sums(dy * (yw + y_in) - xs_low[:, cols].astype(f32) * dxs, hb)
        add = dot(ed, cn[cols, :])
        if adj is None:
            u2_o[:, cols] = jnp.zeros((hb, sub), f32)
            kl.append(jnp.zeros((hb, 128), f32))
            adj = add
        else:
            ends = jnp.exp2(last - cum)
            adj_low = adj.astype(bf16)
            dxi = per_head(dot(adj_low, bt[:, cols]), ends)
            xs_s = xs[:, cols]
            u2_o[:, cols] = head_sums(xs_s * dxi, hb)
            kl.append(head_sums(adj * state, hb) * jnp.exp2(last))
            db_o[:, cols] += dot(adj_low, per_head(xs_s, ends).astype(bf16), TN)
            dxs = dxs + dxi
            adj = per_head(adj, jnp.exp2(last)) + add
        dxs_o[:, cols] = dxs
    for s in range(nsub):
        kl_o[:, s * 128 : (s + 1) * 128] = kl[nsub - 1 - s]


def back_call(lo, hi, dy, xc, hp, ent, loc, ct, cn, bt, cbt, bufs, later=()):
    slots, ch, length = dy.shape
    ncb = ch // CB
    hb = CB // HEAD
    nsub = length // SUB
    full = lambda a: pl.BlockSpec(a.shape, lambda s, c: (0,) * a.ndim)
    per_chan = lambda a: pl.BlockSpec((None, CB, a.shape[2]), lambda s, c: (s + lo, c, 0))
    per_blk = lambda a: pl.BlockSpec(
        (None,) + a.shape[1:], lambda s, c: ((s + lo) * ncb + c, 0, 0)
    )
    blk_out = lambda w: pl.BlockSpec((None, hb, w), lambda s, c: ((s + lo) * ncb + c, 0, 0))
    loc_spec = pl.BlockSpec((None, loc.shape[1], CB, 128), lambda s, c: (s + lo, 0, c, 0))
    blocks = slots * ncb
    ops = [dy, xc, hp, ent, loc, ct, cn, bt, cbt]
    entered = pl.BlockSpec((None, CB, 128), lambda s, c: ((s + lo + 1) % slots, c, 0))
    specs = [per_chan(dy), per_chan(xc), per_blk(hp), entered, loc_spec]
    specs += [full(ct), full(cn), full(bt), full(cbt)]
    aliases = {}
    if bufs is not None:
        aliases = {len(ops) + k: k for k in range(4)}
        ops += list(bufs)
        specs += [pl.BlockSpec(memory_space=pl.ANY)] * 4
    ops += list(later)
    specs += [pl.BlockSpec(memory_space=pl.ANY)] * len(later)
    return pl.pallas_call(
        functools.partial(back_kernel, hb, SUB),
        grid=(hi - lo, ncb),
        in_specs=specs,
        out_specs=[
            pl.BlockSpec((None, CB, length), lambda s, c: (s + lo, c, 0)),
            blk_out(length),
            blk_out(length),
            blk_out(128 * nsub),
            pl.BlockSpec((nsub, SUB, SUB), lambda s, c: (0, 0, 0)),
            pl.BlockSpec((128, length), lambda s, c: (0, 0)),
            pl.BlockSpec((128, length), lambda s, c: (0, 0)),
        ],
        out_shape=[
            jax.ShapeDtypeStruct((slots, ch, length), f32),
            jax.ShapeDtypeStruct((blocks, hb, length), f32),
            jax.ShapeDtypeStruct((blocks, hb, length), f32),
            jax.ShapeDtypeStruct((blocks, hb, 128 * nsub), f32),
            jax.ShapeDtypeStruct((nsub, SUB, SUB), f32),
            jax.ShapeDtypeStruct((128, length), f32),
            jax.ShapeDtypeStruct((128, length), f32),
        ],
        input_output_aliases=aliases,
        compiler_params=compiler_params(2),
        cost_estimate=cost((hi - lo) * ch * length * SUB * 20, (hi - lo) * ch * length * 8),
        name="state_back",
    )(*ops)


def finish_kernel(hb, *refs):
    (dxs_r, dy_r, xc_r, dz_r, chan_r, hp_r, ent_r, adj_r, bt, upz, upx, low) = refs[:12]
    dx_o, tail_o, head_o, gz_o, gx_o, dl_o, dd_o, u2_o, kf_o, db_o = refs[-10:]
    blk = pl.program_id(0) * pl.num_programs(1) + pl.program_id(1)
    chan = chan_r[...]
    hp = hp_r[...]
    length = bt.shape[1]

    @pl.when(blk == 0)
    def _():
        db_o[...] = jnp.zeros_like(db_o)
        dl_o[...] = jnp.zeros_like(dl_o)

    xc = xc_r[...].astype(f32)
    sig = sigmoid(xc)
    x = xc * sig
    delta = hp[2 * hb : 3 * hb]
    xs = per_head(x, delta)
    total = hp[hb : 2 * hb]
    last = total[:, length - 1 : length]
    ends = jnp.exp2(last - total)
    adj_low = adj_r[...]
    extra = per_head(dot(adj_low, bt[...]), ends)
    u2_o[...] = head_sums(xs * extra, hb)
    kf_o[...] = head_sums(adj_low.astype(f32) * ent_r[...].astype(f32), hb) * jnp.exp2(last)
    db_o[...] += dot(adj_low, per_head(xs, ends).astype(bf16), TN)
    dxs = dxs_r[...] + extra
    dd_o[...] = head_sums(x * dxs, hb)
    dx = per_head(dxs, delta) + dy_r[...].astype(f32) * chan[:, 4:5]
    dconv = dx * (sig + x * (1.0 - sig))
    head_o[...] = jnp.transpose(dconv[:, :HALO])[:8]
    ext = jnp.concatenate([dconv, jnp.zeros((CB, HALO), f32)], axis=1)
    width = ext.shape[1]
    out = ext * chan[:, 3:4]
    for k in range(3):
        out = out + pltpu.roll(ext, width - (3 - k), 1) * chan[:, k : k + 1]
    out = out[:, :length]
    tail_o[...] = out[:, length - HALO :]
    dx_low = out.astype(bf16)
    dx_o[...] = dx_low
    dz = dz_r[...]
    gz_o[...] = dot(low[...], dz, NT)
    gx_o[...] = dot(low[...], dx_low, NT)
    dl_o[...] += dot(upz[...], dz, TN) + dot(upx[...], dx_low, TN)


def finish_call(dxs, dy, xc, dz, chan, hp, ent, adj, bt, upz, upx, low, later):
    slots, ch, length = dy.shape
    ncb = ch // CB
    hb = CB // HEAD
    rank2 = low.shape[0]
    full, per_chan, per_blk = grid_specs(ncb)
    blk_out = lambda w: pl.BlockSpec((None, hb, w), lambda s, c: (s * ncb + c, 0, 0))
    chan_out = lambda w: pl.BlockSpec((None, CB, w), lambda s, c: (s, c, 0))
    turned = lambda w: pl.BlockSpec((None, w, CB), lambda s, c: (s, 0, c))
    moved = lambda k: pl.BlockSpec((None, CB, 128), lambda s, c: ((s + k) % slots, c, 0))
    blocks = slots * ncb
    return pl.pallas_call(
        functools.partial(finish_kernel, hb),
        grid=(slots, ncb),
        in_specs=[per_chan(dxs), per_chan(dy), per_chan(xc), per_chan(dz), per_chan(chan)]
        + [per_blk(hp), moved(1), moved(slots - 1), full(bt), per_chan(upz), per_chan(upx)]
        + [full(low)] + [pl.BlockSpec(memory_space=pl.ANY)] * len(later),
        out_specs=[
            chan_out(length),
            chan_out(HALO),
            turned(8),
            turned(rank2),
            turned(rank2),
            pl.BlockSpec((rank2, length), lambda s, c: (0, 0)),
            blk_out(length),
            blk_out(length),
            blk_out(128),
            pl.BlockSpec((128, length), lambda s, c: (0, 0)),
        ],
        out_shape=[
            jax.ShapeDtypeStruct((slots, ch, length), bf16),
            jax.ShapeDtypeStruct((slots, ch, HALO), f32),
            jax.ShapeDtypeStruct((slots, 8, ch), f32),
            jax.ShapeDtypeStruct((slots, rank2, ch), f32),
            jax.ShapeDtypeStruct((slots, rank2, ch), f32),
            jax.ShapeDtypeStruct((rank2, length), f32),
            jax.ShapeDtypeStruct((blocks, hb, length), f32),
            jax.ShapeDtypeStruct((blocks, hb, length), f32),
            jax.ShapeDtypeStruct((blocks, hb, 128), f32),
            jax.ShapeDtypeStruct((128, length), f32),
        ],
        compiler_params=compiler_params(2),
        cost_estimate=cost(slots * ch * length * 700, slots * ch * length * 14),
        name="finish_back",
    )(dxs, dy, xc, dz, chan, hp, ent, adj, bt, upz, upx, low, *later)


def glue_kernel(hb, sub, *refs):
    (dcb_r, db1, db2, dc1, bt, ct, pre_r, u1, u2, kl, dd, u2f, kf) = refs[:13]
    (sig_r, speed, taps) = refs[13:16]
    left_o, tail_o, head_o = refs[16:]
    state_w, length = bt.shape
    nsub = length // sub
    blocks = u1.shape[0]
    row = lax.broadcasted_iota(jnp.int32, (sub, sub), 0)
    col = lax.broadcasted_iota(jnp.int32, (sub, sub), 1)
    below = jnp.where(row >= col, 1.0, 0.0)
    keep = jnp.where(row <= col, 1.0, 0.0)

    def exact(p, q):
        return lax.dot_general(
            p, q, (NN, ((), ())), precision=highest, preferred_element_type=f32
        )

    def flat(ref, cols=slice(None)):
        return jnp.concatenate([ref[b, :, cols] for b in range(blocks)], axis=0)

    d_b, d_c, rate_in = [], [], []
    for s in range(nsub):
        cols = slice(s * sub, (s + 1) * sub)
        dcb = (dcb_r[s] * keep).astype(bf16)
        d_b.append(dot(ct[:, cols], dcb, NT))
        d_c.append(dot(bt[:, cols], dcb))
        lane = slice(s * 128, (s + 1) * 128)
        rate_in.append(
            exact(flat(u1, cols), below)
            + exact(flat(u2, cols), 1.0 - below)
            + jnp.sum(flat(kl, lane), axis=1, keepdims=True)
        )
    d_b = jnp.concatenate(d_b, axis=1) + db1[...] + db2[...]
    d_c = jnp.concatenate(d_c, axis=1) + dc1[...]
    pre = pre_r[...]
    sig = sigmoid(pre)
    d_pre = jnp.concatenate([d_b, d_c], axis=0) * (sig + pre * sig * (1.0 - sig))
    head_o[...] = jnp.transpose(d_pre[:, :HALO])[:8]
    ext = jnp.concatenate([d_pre, jnp.zeros((2 * state_w, HALO), f32)], axis=1)
    out = ext * taps[:, 3:4]
    for k in range(3):
        out = out + pltpu.roll(ext, ext.shape[1] - (3 - k), 1) * taps[:, k : k + 1]
    tail_o[...] = out[:, length - HALO : length]
    left_o[: 2 * state_w, :] = out[:, :length].astype(bf16)
    rate = jnp.concatenate(rate_in, axis=1) + jnp.sum(flat(kf), axis=1, keepdims=True)
    first = flat(u2f)
    run = None
    parts = []
    for s in range(nsub):
        piece = first[:, s * sub : (s + 1) * sub]
        here = exact(piece, 1.0 - below)
        parts.append(here if run is None else here + run)
        ends = jnp.sum(piece, axis=1, keepdims=True)
        run = ends if run is None else run + ends
    rate = rate + jnp.concatenate(parts, axis=1)
    left_o[2 * state_w :, :] = ((flat(dd) - speed[...] * rate) * sig_r[...]).astype(bf16)


def glue_call(args, state_w, length, heads):
    vm = pl.BlockSpec(memory_space=pltpu.VMEM)
    return pl.pallas_call(
        functools.partial(glue_kernel, CB // HEAD, SUB),
        in_specs=[vm] * len(args),
        out_specs=[vm] * 3,
        out_shape=[
            jax.ShapeDtypeStruct((2 * state_w + heads, length), bf16),
            jax.ShapeDtypeStruct((2 * state_w, HALO), f32),
            jax.ShapeDtypeStruct((8, 2 * state_w), f32),
        ],
        compiler_params=compiler_params(0),
        cost_estimate=cost(1e8, 4e6),
        name="glue",
    )(*args)


def add_products(acc, turned, sets, picks, n_left, refs, slot, c):
    at = 0
    for lo, hi, per in sets:
        for p, order in enumerate(picks):
            groups = [refs[at + g * per : at + (g + 1) * per] for g in range(n_left)]
            at += n_left * per

            @pl.when((slot >= lo) & (slot < hi) & (c == p))
            def _(groups=groups, order=order):
                off = 0
                for k, b in order:
                    parts = [g[k][b] for g in groups]
                    w = parts[0] if n_left == 1 else jnp.concatenate(parts, axis=0)
                    acc[:, off : off + w.shape[1]] += dot(turned, w)
                    off += w.shape[1]


def product_specs(weights, paths, block):
    ops, specs, sets = [], [], []
    for (lo, hi), groups in weights:
        sets.append((lo, hi, len(groups[0][0][0])))
        for p in range(paths):
            for arrays, base in groups:
                for a in arrays[p]:
                    ops.append(a)

                    def index(s, c, lo=lo, hi=hi, base=base):
                        return (0, base + jnp.clip(s, lo, hi - 1) - lo, 0)

                    specs.append(pl.BlockSpec((a.shape[0], block, a.shape[2]), index))
    return ops, specs, sets


def output_kernel(sets, picks, flat, quick, n_w, *refs):
    (sc, nout, dn, bh, up, tok, masked) = refs[:7]
    wrefs = refs[7 : 7 + n_w]
    mixed_o, gdo_o, guo_o, acc, hid = refs[-5:]
    slot, c = pl.program_id(0), pl.program_id(1)
    rank = up.shape[0]
    length, width = tok.shape

    @pl.when((slot == 0) & (c == 0))
    def _():
        acc[...] = jnp.zeros_like(acc)
        hid[...] = jnp.zeros_like(hid)

    values = nout[...]
    gdo_o[...] = dot(bh[:rank, :], values, NT)
    hid[...] += dot(dn[:, :rank], values, TN)
    add_products(acc, jnp.transpose(values), sets, picks, 1, wrefs, slot, c)

    @pl.when((slot == pl.num_programs(0) - 1) & (c == pl.num_programs(1) - 1))
    def _():
        low = hid[...].astype(bf16)
        guo_o[...] = dot(low, masked[...])
        rows = lax.broadcasted_iota(jnp.int32, (length, 1), 0) < sc[1]
        for i, m in enumerate(flat):
            at = pl.ds(block_at(sc[0], m, quick), CB)
            total = acc[:, i * CB : (i + 1) * CB] + dot(low, up[:, at], TN)
            total = total + tok[:, at].astype(f32)
            mixed_o[:, at] = jnp.where(rows, total, 0.0).astype(bf16)


def output_call(sc, nout, dn, bh, up, tok, masked, weights, picks, flat, quick):
    slots, ch, length = nout.shape
    rank, width = up.shape
    paths = len(picks)
    block = ch // paths
    full = lambda a: pl.BlockSpec(a.shape, lambda s, c: (0,) * a.ndim)
    chan = lambda a: pl.BlockSpec((None, block, a.shape[2]), lambda s, c: (s, c, 0))
    w_ops, w_specs, sets = product_specs(weights, paths, block)
    return pl.pallas_call(
        functools.partial(output_kernel, sets, picks, flat, quick, len(w_ops)),
        grid=(slots, paths),
        in_specs=[pl.BlockSpec(memory_space=pltpu.SMEM), chan(nout), chan(dn), full(bh)]
        + [full(up), full(tok), full(masked)] + w_specs,
        out_specs=[
            pl.BlockSpec((length, width), lambda s, c: (0, 0)),
            pl.BlockSpec((None, rank, block), lambda s, c: (s, 0, c)),
            pl.BlockSpec((rank, width), lambda s, c: (0, 0)),
        ],
        out_shape=[
            jax.ShapeDtypeStruct((length, width), bf16),
            jax.ShapeDtypeStruct((slots, rank, ch), f32),
            jax.ShapeDtypeStruct((rank, width), f32),
        ],
        scratch_shapes=[pltpu.VMEM((length, width), f32), pltpu.VMEM((rank, length), f32)],
        compiler_params=compiler_params(2),
        cost_estimate=cost(2 * slots * ch * length * width, slots * ch * width * 2),
        name="output",
    )(sc, nout, dn, bh, up, tok, masked, *w_ops)


def gate_back_kernel(sets, picks, n_w, *refs):
    dz = refs[0]
    acc = refs[-1]
    slot, c = pl.program_id(0), pl.program_id(1)

    @pl.when((slot == 0) & (c == 0))
    def _():
        acc[...] = jnp.zeros_like(acc)

    add_products(acc, jnp.transpose(dz[...]), sets, picks, 1, refs[1 : 1 + n_w], slot, c)


def gate_back_call(dz, weights, picks, width, later=()):
    slots, ch, length = dz.shape
    paths = len(picks)
    block = ch // paths
    w_ops, w_specs, sets = product_specs(weights, paths, block)
    return pl.pallas_call(
        functools.partial(gate_back_kernel, sets, picks, len(w_ops)),
        grid=(slots, paths),
        in_specs=[pl.BlockSpec((None, block, length), lambda s, c: (s, c, 0))] + w_specs
        + [pl.BlockSpec(memory_space=pl.ANY)] * len(later),
        out_specs=pl.BlockSpec((length, width), lambda s, c: (0, 0)),
        out_shape=jax.ShapeDtypeStruct((length, width), f32),
        compiler_params=compiler_params(2),
        cost_estimate=cost(2 * slots * ch * length * width, 2 * slots * ch * width),
        name="gate_back",
    )(dz, *w_ops, *later)


def input_kernel(sets, picks, flat, quick, n_w, n_small, *refs):
    (sc, dx, tail, left, d_low, down, root_r, gain, tok, masked, start) = refs[:11]
    smalls = refs[11 : 11 + n_small]
    wrefs = refs[11 + n_small : 11 + n_small + n_w]
    out, acc = refs[-2:]
    slot, c = pl.program_id(0), pl.program_id(1)
    length, width = tok.shape

    @pl.when((slot == 0) & (c == 0))
    def _():
        low = jnp.transpose(d_low[...])
        total = start[...]
        row = 0
        for w in smalls:
            total = total + dot(left[row : row + w.shape[0], :], w[...], TN)
            row += w.shape[0]
        acc[...] = total
        for i, m in enumerate(flat):
            at = pl.ds(block_at(sc[0], m, quick), CB)
            acc[:, i * CB : (i + 1) * CB] += dot(low, down[at, :], NT)

    dx_all = jnp.concatenate([dx[:, : length - HALO], tail[...]], axis=1)
    add_products(acc, jnp.transpose(dx_all), sets, picks, 1, wrefs, slot, c)

    @pl.when((slot == pl.num_programs(0) - 1) & (c == pl.num_programs(1) - 1))
    def _():
        root = root_r[...]
        mean = None
        for i, m in enumerate(flat):
            at = pl.ds(block_at(sc[0], m, quick), CB)
            cols = slice(i * CB, (i + 1) * CB)
            scaled = acc[:, cols] * gain[:, at]
            acc[:, cols] = scaled
            part = jnp.sum(scaled * tok[:, at].astype(f32), axis=1, keepdims=True)
            mean = part if mean is None else mean + part
        coef = root * root * root * (mean * (1.0 / width))
        for i, m in enumerate(flat):
            at = pl.ds(block_at(sc[0], m, quick), CB)
            d_resid = root * acc[:, i * CB : (i + 1) * CB] - tok[:, at].astype(f32) * coef
            out[:, at] = (masked[:, at].astype(f32) + d_resid).astype(bf16)


def input_call(
    sc, dx, tail, left, d_low, down, root, gain, tok, masked, start, smalls, weights, picks,
    flat, quick,
):
    slots, ch, length = dx.shape
    width = tok.shape[1]
    paths = len(picks)
    block = ch // paths
    once = pl.Buffered(1)
    full = lambda a: pl.BlockSpec(a.shape, lambda s, c: (0,) * a.ndim, pipeline_mode=once)
    chan = lambda a: pl.BlockSpec((None, block, a.shape[2]), lambda s, c: (s, c, 0))
    w_ops, w_specs, sets = product_specs(weights, paths, block)
    return pl.pallas_call(
        functools.partial(input_kernel, sets, picks, flat, quick, len(w_ops), len(smalls)),
        grid=(slots, paths),
        in_specs=[pl.BlockSpec(memory_space=pltpu.SMEM), chan(dx), chan(tail)]
        + [full(a) for a in [left, d_low, down, root, gain, tok, masked, start] + list(smalls)]
        + w_specs,
        out_specs=pl.BlockSpec((length, width), lambda s, c: (0, 0)),
        out_shape=jax.ShapeDtypeStruct((length, width), bf16),
        scratch_shapes=[pltpu.VMEM((length, width), f32)],
        compiler_params=compiler_params(2),
        cost_estimate=cost(2 * slots * ch * length * width, 2 * slots * ch * width),
        name="input_back",
    )(sc, dx, tail, left, d_low, down, root, gain, tok, masked, start, *smalls, *w_ops)


def body(
    tokens,
    cotangent,
    lengths,
    adapter_ids,
    pre_gain,
    in_inner,
    in_maps,
    in_steps,
    conv_inner,
    conv_maps,
    step_bias,
    decay_log,
    skip_gain,
    norm_gain,
    out_weight,
    adapter_in_down,
    adapter_in_up,
    adapter_out_down,
    adapter_out_up,
):
    planes = lax.axis_size("tensor")
    seqs = lax.axis_size("dp")
    place = lax.axis_index("tensor")
    mine = lax.axis_index("dp")
    length = tokens.shape[1]
    width = tokens.shape[2]
    rows_here = in_inner.shape[0]
    ch = in_inner.shape[2]
    inner = ch * planes
    hs = in_steps.shape[1]
    heads = hs * planes
    rank = adapter_in_down.shape[2]
    adapters = adapter_in_down.shape[0]
    state_w = in_maps.shape[1] // 2
    hb = CB // HEAD
    ncb = ch // CB
    nblk = planes * ncb
    nsub = length // SUB
    quick = seqs == 8 and planes == 4

    def from_plane(v, j):
        return lax.ppermute(v, "tensor", [((s + j) % planes, s) for s in range(planes)])

    def flip(v, bit):
        return lax.ppermute(v, "dp", [(i, i ^ bit) for i in range(seqs)])

    def slot_order(v, first=0):
        return jnp.stack(
            [
                lax.dynamic_index_in_dim(v, (place + j) % planes, 0, keepdims=False)
                for j in range(first, planes)
            ]
        )

    def by_slot(v):
        return slot_order(lax.all_gather(v, "tensor", axis=0))

    def to_slots(v):
        total = v[0]
        for j in range(1, planes):
            total = total + lax.ppermute(
                v[j].astype(bf16), "tensor", [(s, (s + j) % planes) for s in range(planes)]
            ).astype(f32)
        return total

    flat = [0, 2, 4, 6, 1, 3, 5, 7] if quick else list(range(width // CB))
    if quick:
        picks = [
            [(0, 0), (0, 1), (1, 0), (1, 1), (2, 0), (2, 1), (3, 0), (3, 1)],
            [(0, 0), (1, 0), (0, 1), (1, 1), (2, 0), (3, 0), (2, 1), (3, 1)],
        ]
    else:
        picks = [[(0, 0)]]
    half = planes // 2

    def halves(parts, more=((), ())):
        cut = ch // 2
        return [
            jnp.concatenate([v[:cut] for v in parts] + list(more[0]), axis=0),
            jnp.concatenate([v[cut:] for v in parts] + list(more[1]), axis=0),
        ]

    def pass_one(ab):
        return [flip(ab[0], 2), flip(ab[1], 4)]

    def with_first(ab, got, token):
        return [jnp.stack([v, w]) + token for v, w in zip(ab, got)]

    def pass_two(ab):
        return [flip(ab[0], 4), flip(ab[1], 2)]

    def pass_core(arrays):
        return [flip(v, 1) for v in arrays]

    def as_paths(arrays, swapped):
        return [[arrays[k], arrays[k + 2], swapped[k], swapped[k + 2]] for k in range(2)]

    pick = adapter_ids[0]
    down_in = lax.dynamic_index_in_dim(adapter_in_down, pick, 0, keepdims=False)
    up_here = lax.dynamic_index_in_dim(adapter_in_up, pick, 0, keepdims=False)
    down_here = lax.dynamic_index_in_dim(adapter_out_down, pick, 0, keepdims=False)
    up_out = lax.dynamic_index_in_dim(adapter_out_up, pick, 0, keepdims=False)
    step_rows = rows_here * hs // ch
    halo_rows = 16 * width // ch
    numbers = jnp.concatenate(
        [
            conv_inner,
            jnp.repeat(skip_gain, HEAD)[None],
            norm_gain[None],
            jnp.pad(jnp.stack([step_bias, decay_log]), ((0, 0), (0, ch - hs))),
        ],
        axis=0,
    )
    coarse = lax.optimization_barrier(numbers.astype(bf16))
    fine = lax.optimization_barrier((numbers - coarse.astype(f32)).astype(bf16))
    packed = jnp.concatenate(
        [
            jnp.transpose(up_here, (1, 0, 2)).reshape(2 * rank, ch),
            down_here.T,
            in_steps.T.reshape(step_rows, ch),
            tokens[0, -16:].reshape(halo_rows, ch),
            coarse,
            fine,
        ],
        axis=0,
    )
    halo = [(s, s + 1) for s in range(planes - 1)]
    wt = jnp.transpose(in_inner, (1, 2, 0))
    maps_w = in_maps.T
    own_rows = 3 * ch // 2
    if quick:
        own = halves(
            [wt[0], wt[1], out_weight],
            ([maps_w[:state_w], in_steps.T], [maps_w[state_w:]]),
        )
        got = pass_one(own)
        packed = jnp.stack([packed] + [from_plane(packed, j) for j in range(1, planes)])
        all_x = lax.all_gather(wt[1], "tensor", axis=0)
        all_z = lax.all_gather(wt[0], "tensor", axis=0)
        all_o = lax.all_gather(out_weight, "tensor", axis=0)
    else:
        packed = by_slot(packed)
    step_at, halo_at = 3 * rank, 3 * rank + step_rows
    number_at = halo_at + halo_rows
    before = packed[planes - 1, halo_at:number_at].reshape(16, width)
    before = jnp.where(place > 0, before, jnp.zeros_like(before))
    numbers = packed[:, number_at : number_at + 8].astype(f32) + packed[
        :, number_at + 8 :
    ].astype(f32)
    steps_w = packed[:, step_at:halo_at].reshape(planes, hs, rows_here)
    held = []
    if quick:
        token, held, _ = hold(got + [before])
        own = with_first(own, got, token)
        two = pass_two(own)
        swapped = pass_core(own)
        far_x = halves(slot_order(all_x, 1), ([steps_w[1:].reshape(-1, rows_here)], ()))
        held = [held]

    up_z = jnp.swapaxes(packed[:, :rank], 1, 2)
    up_x = jnp.swapaxes(packed[:, rank : 2 * rank], 1, 2)
    down_out = jnp.swapaxes(packed[:, 2 * rank : 3 * rank], 1, 2)
    taps = numbers[:, :4]
    chan = jnp.swapaxes(jnp.pad(numbers[:, :6], ((0, 0), (0, 2), (0, 0))), 1, 2)
    bias = numbers[:, 6, :hs].reshape(heads)
    speed = jnp.exp(numbers[:, 7, :hs].reshape(heads))
    up_z2 = jnp.concatenate([up_z, up_z], axis=2)
    up_x2 = jnp.concatenate([up_x, up_x], axis=2)
    down_out2 = jnp.concatenate([down_out, down_out], axis=2)

    sc = jnp.stack([mine, lengths[0] - place * length]).astype(jnp.int32)
    normed, masked, root, low2, back2, nt, gt, turned = turn_call(
        sc, tokens[0], before, cotangent[0], pre_gain[None], down_in, up_out, flat, quick, held
    )
    map_taps = jnp.pad(conv_maps.T, ((0, 0), (0, 4)))
    if quick:
        token, held, passed = hold([turned] + swapped, two + far_x)
        two, far_x = passed[:2], passed[2:]
        own = own + two
        swapped = swapped + pass_core(two)
        got = pass_one(far_x)
        own = as_paths(own, swapped)
        token, held, _ = hold(got + own[0] + own[1])
        held = [held]
        all_maps, all_steps = own, own[0]
        maps_at, maps_rows = own_rows, state_w
        steps_at, mine_heads = own_rows + state_w, hs
    else:
        all_maps = [[lax.all_gather(maps_w, "dp", axis=1, tiled=True)[None]]]
        all_steps = steps_w.reshape(heads, rows_here)
        all_steps = [lax.all_gather(all_steps, "dp", axis=1, tiled=True)[None]]
        maps_at, maps_rows = 0, 2 * state_w
        steps_at, mine_heads = 0, heads
    bt, ct, b_low, c_low, cbt, maps_pre, maps_w = maps_call(
        all_maps, maps_at, maps_rows, picks, nt, map_taps, length, held
    )
    hp, step_sig, mine_w = steps_call(
        all_steps, steps_at, picks[0], nt, bias[:mine_heads, None], speed[:mine_heads, None],
        length, held,
    )
    small_w = [maps_w, mine_w]

    x_args = (picks, nt, low2, up_x2, chan)
    z_args = (picks, nt, low2, up_z2, chan, HALO, False)
    o_args = (picks, gt, back2, down_out2, chan, 0, True)
    if quick:
        far_x = with_first(far_x, got, token)
        two = pass_two(far_x)
        swapped = pass_core(far_x)
        far_z = halves(slot_order(all_z, 1))
        bufs, done = scan_call(0, 1, (own, 1), *x_args, hp, ct, b_low, cbt, None, held)

        token, held, passed = hold([done] + swapped, two + far_z)
        two, far_z = passed[:2], passed[2:]
        far_x = as_paths(far_x + two, swapped + pass_core(two))
        got = pass_one(far_z)
        z, done = proj_call(0, 1, (own, 0), *z_args, None, [held])
        wgt, beside = proj_call(0, 1, (own, 2), *o_args, None, [done])

        token, held, _ = hold(got + far_x[0] + far_x[1] + [beside])
        far_z = with_first(far_z, got, token)
        two = pass_two(far_z)
        swapped = pass_core(far_z)
        far_o = halves(slot_order(all_o, 1))
        hp_far, sig_far, far_w = steps_call(
            far_x[0], own_rows, picks[0], nt, bias[hs:, None], speed[hs:, None], length, [held]
        )
        hp = jnp.concatenate([hp, hp_far], axis=0)
        step_sig = jnp.concatenate([step_sig, sig_far], axis=0)
        small_w.append(far_w)
        bufs, done = scan_call(
            1, planes, (far_x, 0), *x_args, hp, ct, b_low, cbt, bufs, [held]
        )

        token, held, passed = hold([done] + swapped, two + far_o)
        two, far_o = passed[:2], passed[2:]
        far_z = as_paths(far_z + two, swapped + pass_core(two))
        got = pass_one(far_o)
        ent = lax.ppermute(bufs[4], "tensor", halo)

        token, held, (ent,) = hold(got + far_z[0] + far_z[1], [ent])
        far_o = with_first(far_o, got, token)
        two = pass_two(far_o)
        swapped = pass_core(far_o)
        ent = lax.ppermute(hop_call(ent, 1, bufs[3], hp), "tensor", halo)
        z, done = proj_call(1, planes, (far_z, 0), *z_args, z, [held])

        token, held, passed = hold([done] + swapped, two + [ent])
        two, ent = passed[:2], passed[2]
        far_o = as_paths(far_o + two, swapped + pass_core(two))
        ent = lax.ppermute(hop_call(ent, 1, bufs[3], hp), "tensor", halo)
        wgt, _ = proj_call(1, planes, (far_o, 0), *o_args, wgt, [held])
        z_sets = [((0, 1), [(own, 0)]), ((1, planes), [(far_z, 0)])]
        x_sets = [((0, 1), [(own, 1)]), ((1, planes), [(far_x, 0)])]
        o_sets = [((0, 1), [(own, 2)]), ((1, planes), [(far_o, 0)])]
    else:
        w = lax.all_gather(wt, "dp", axis=2, tiled=True)
        w = slot_order(lax.all_gather(w, "tensor", axis=0))
        o = lax.all_gather(out_weight, "dp", axis=1, tiled=True)
        flat_rows = lambda v: [[v.reshape(1, inner, width)]]
        wz, wx = flat_rows(w[:, 0]), flat_rows(w[:, 1])
        o = flat_rows(slot_order(lax.all_gather(o, "tensor", axis=0)))
        bufs, _ = scan_call(0, planes, (wx, 0), *x_args, hp, ct, b_low, cbt, None)
        z, _ = proj_call(0, planes, (wz, 0), *z_args, None)
        wgt, _ = proj_call(0, planes, (o, 0), *o_args, None)
        ent = lax.ppermute(bufs[4], "tensor", halo)
        for _ in range(planes - 2):
            ent = lax.ppermute(hop_call(ent, 1, bufs[3], hp), "tensor", halo)
        z_sets = [((0, planes), [(wz, 0)])]
        x_sets = [((0, planes), [(wx, 0)])]
        o_sets = [((0, planes), [(o, 0)])]
    xc, mix, loc, s_end, _ = bufs
    left = [(s + 1, s) for s in range(planes - 1)]

    nout, dy, dz, sl, sl_sent = gate_call(z, mix, wgt, ent, chan, hp, ct, c_low, inner)

    adj = lax.ppermute(sl_sent, "tensor", left)
    mixed, grad_down_out, grad_up_out = output_call(
        sc, nout, down_out2, back2, up_out, tokens[0], masked, o_sets, picks, flat, quick
    )
    adj = lax.ppermute(hop_call(adj, planes - 1, sl, hp, [mixed]), "tensor", left)
    d_normed = gate_back_call(dz, z_sets, picks, width, [mixed])
    adj = lax.ppermute(hop_call(adj, planes - 1, sl, hp, [d_normed]), "tensor", left)
    for _ in range(planes - 4):
        adj = lax.ppermute(hop_call(adj, planes - 1, sl, hp), "tensor", left)
    dxs, u1, u2, kl, dcb, db1, dc1 = back_call(
        0, planes, dy, xc, hp, ent, loc, ct, c_low, bt, cbt, None, [d_normed]
    )

    (dx, tail, head, grad_z, grad_x, d_low2, ddelta, u2f, kf, db3) = finish_call(
        dxs, dy, xc, dz, chan, hp, ent, adj, bt, up_z2, up_x2, low2[:, HALO:], [mixed]
    )
    small_left, maps_tail, maps_head = glue_call(
        [dcb, db1, db3, dc1, bt, ct, maps_pre]
        + [u1, u2, kl, ddelta, u2f, kf, step_sig, speed[:, None], map_taps],
        state_w, length, heads,
    )

    near = lax.ppermute(
        jnp.concatenate(
            [head[:, :4].reshape(planes * 4 * ch), maps_head[:4].reshape(8 * state_w)]
        ),
        "tensor",
        left,
    )

    def beyond(values, taps_of):
        return [sum(taps_of(k) * values(i - k) for k in range(i + 1)) for i in range(3)]

    near_x = jnp.roll(near[: planes * 4 * ch].reshape(planes, 4, ch), 1, axis=0)
    more = jnp.stack(beyond(lambda n: near_x[:, n], lambda k: taps[:, k]), axis=1)
    tail = (
        tail + jnp.pad(jnp.swapaxes(more, 1, 2), ((0, 0), (0, 0), (HALO - 3, 0)))
    ).astype(bf16)
    low_last = low2[:rank, -3:].astype(f32)
    grad_x = grad_x[:, :rank] + grad_x[:, rank:]
    grad_x += sum(low_last[None, :, i, None] * more[:, i, None, :] for i in range(3))
    grad_z = grad_z[:, :rank] + grad_z[:, rank:]
    d_low_more = jnp.einsum("jrk,jik->ri", packed[:, rank : 2 * rank].astype(f32), more)
    d_low = d_low2[:rank] + jnp.pad(d_low_more, ((0, 0), (length - 3, 0)))
    d_low = d_low.astype(bf16)
    near_maps = near[planes * 4 * ch :].reshape(4, 2 * state_w)
    maps_more = jnp.stack(beyond(lambda n: near_maps[n], lambda k: conv_maps[k]), axis=1)
    maps_tail = maps_tail + jnp.pad(maps_more, ((0, 0), (HALO - 3, 0)))
    small_left = lax.dynamic_update_slice(
        small_left, maps_tail.astype(bf16), (0, length - HALO)
    )

    grad_down = dot(d_low, normed)
    quarters = lambda v: slot_order(
        jnp.swapaxes(v.reshape(rank, planes, width // planes), 0, 1)
    )
    mine_sum = to_slots(
        jnp.concatenate(
            [grad_z, grad_x, grad_down_out, quarters(grad_down), quarters(grad_up_out)], axis=2
        )
    ).astype(bf16)
    head_part = 3 * ch
    shared = by_slot(mine_sum[:, head_part:])
    sent = jnp.concatenate(
        [
            mine_sum[:, :head_part],
            jnp.swapaxes(shared, 0, 1).reshape(rank, -1),
            jnp.full((rank, 128), pick).astype(bf16),
        ],
        axis=1,
    )
    if quick:
        by_seq = sent[None]
        for bit in (2, 4, 1):
            by_seq = jnp.concatenate([by_seq, flip(by_seq, bit)], axis=0)
    else:
        by_seq = lax.all_gather(sent, "dp", axis=0)
    ids = by_seq[:, 0, -1].astype(jnp.int32)
    chosen = (ids[None, :] == jnp.arange(adapters)[:, None]).astype(bf16)
    grads = jnp.einsum("as,srk->ark", chosen, by_seq[..., :-128], preferred_element_type=f32)
    g_up = grads[:, :, : 2 * ch].reshape(adapters, rank, 2, ch)
    g_down_out = jnp.swapaxes(grads[:, :, 2 * ch : 3 * ch], 1, 2)
    common = grads[:, :, 3 * ch :].reshape(adapters, rank, planes, 2, width // planes)
    twice = jnp.concatenate([common, common], axis=2)
    common = lax.dynamic_slice_in_dim(twice, (planes - place) % planes, planes, 2)
    g_down = jnp.swapaxes(common[:, :, :, 0].reshape(adapters, rank, width), 1, 2)
    g_up_out = common[:, :, :, 1].reshape(adapters, rank, width)

    tokens_grad = input_call(
        sc, dx, tail, small_left, d_low, down_in, root, pre_gain[None], tokens[0], masked,
        d_normed, small_w, x_sets, picks, flat, quick,
    )
    return (mixed[None], tokens_grad[None], g_down, g_up, g_down_out, g_up_out)


def solution(mesh):
    placed = (
        P("dp", "tensor", None),
        P("dp", "tensor", None),
        P("dp"),
        P("dp"),
        P(),
        P("dp", None, "tensor"),
        P("dp", None),
        P("dp", "tensor"),
        P(None, "tensor"),
        P(),
        P("tensor"),
        P("tensor"),
        P("tensor"),
        P("tensor"),
        P("tensor", "dp"),
        P(),
        P(None, None, None, "tensor"),
        P(None, "tensor", None),
        P(),
    )
    return jax.shard_map(
        body,
        mesh=mesh,
        in_specs=placed,
        out_specs=(
            P("dp", "tensor", None),
            P("dp", "tensor", None),
            P(),
            P(None, None, None, "tensor"),
            P(None, "tensor", None),
            P(),
        ),
        check_vma=False,
    )
```

```python
import functools

import jax
import jax.numpy as jnp
from jax import lax
from jax.experimental import pallas as pl
from jax.experimental.pallas import tpu as pltpu
from jax.sharding import PartitionSpec as P

f32 = jnp.float32
bf16 = jnp.bfloat16
epsilon = 1e-05
highest = lax.Precision.HIGHEST
LOG2E = 1.4426950408889634
HEAD = 64
HALO = 128
SUB = 256
CB = 256

NN = ((1,), (0,))
NT = ((1,), (1,))
TN = ((0,), (0,))


def dot(a, b, dims=NN):
    return lax.dot_general(a, b, (dims, ((), ())), preferred_element_type=f32)


def compiler_params(grid_rank):
    return pltpu.CompilerParams(
        dimension_semantics=("arbitrary",) * grid_rank, vmem_limit_bytes=60 * 2**20
    )


def cost(flops, size):
    return pl.CostEstimate(
        flops=int(flops) // 8, bytes_accessed=int(size) // 8, transcendentals=0
    )


def packed_spec(kind, index):
    def where(*grid):
        slot, c = index(*grid)
        return (slot, c * 4 + kind, 0)

    return pl.BlockSpec((None, 16, CB), where)


def sigmoid(v):
    return 0.5 + 0.5 * jnp.tanh(0.5 * v)


def columns(numbers):
    v = numbers[...].astype(f32)
    return jnp.transpose(v[:8] + v[8:])


def tall(rows):
    return jnp.transpose(jnp.concatenate([rows, rows], axis=0))


def conv_values(raw, chan):
    out = raw * chan[:, 3:4]
    for k in range(3):
        out = out + pltpu.roll(raw, 3 - k, 1) * chan[:, k : k + 1]
    return out[:, HALO:]


def per_head(values, rows):
    hb = rows.shape[0]
    parts = [values[h * HEAD : (h + 1) * HEAD] * rows[h : h + 1] for h in range(hb)]
    return jnp.concatenate(parts, axis=0)


def head_sums(values, hb):
    parts = [
        jnp.sum(values[h * HEAD : (h + 1) * HEAD], axis=0, keepdims=True) for h in range(hb)
    ]
    return jnp.concatenate(parts, axis=0)


def joined(refs, picks):
    parts = [refs[k][b] for k, b in picks]
    return parts[0] if len(parts) == 1 else jnp.concatenate(parts, axis=1)


def block_at(mine, m, quick):
    return pl.multiple_of((mine ^ m) * CB, CB) if quick else m * CB


def turn_kernel(flat, quick, *refs):
    (sc, tok_r, bef_r, cot_r, gain, down, up) = refs[:7]
    normed_o, masked_o, root_o, low_o, back_o, nt_o, gt_o, halo_sc = refs[-8:]
    width = tok_r.shape[1]
    length = tok_r.shape[0]

    def norm(v):
        v = v.astype(f32)
        root = lax.rsqrt(jnp.sum(v * v, axis=1, keepdims=True) * (1.0 / width) + epsilon)
        return (v * root * gain[...]).astype(bf16), root

    normed, root = norm(tok_r[...])
    normed_o[...] = normed
    root_o[...] = root
    halo_sc[...] = jnp.zeros_like(halo_sc)
    halo_sc[HALO - 16 :, :] = norm(bef_r[...])[0]
    rows = lax.broadcasted_iota(jnp.int32, (length, 1), 0)
    masked_o[...] = jnp.where(rows < sc[1], cot_r[...].astype(f32), 0.0).astype(bf16)
    low = back = None
    for i, m in enumerate(flat):
        at = pl.ds(block_at(sc[0], m, quick), CB)
        nt = jnp.concatenate(
            [jnp.transpose(halo_sc[:, at]), jnp.transpose(normed_o[:, at])], axis=1
        )
        gt = jnp.transpose(masked_o[:, at])
        nt_o[i * CB : (i + 1) * CB, :] = nt
        gt_o[i * CB : (i + 1) * CB, :] = gt
        low_m = dot(down[at, :], nt, TN)
        back_m = dot(up[:, at], gt)
        low = low_m if low is None else low + low_m
        back = back_m if back is None else back + back_m
    low_o[...] = low.astype(bf16)
    back_o[...] = back.astype(bf16)


def turn_call(sc, tokens, before, cot, gain, down, up, flat, quick, later):
    length, width = tokens.shape
    rank = up.shape[0]
    ext = length + HALO
    vm = pl.BlockSpec(memory_space=pltpu.VMEM)
    return pl.pallas_call(
        functools.partial(turn_kernel, flat, quick),
        in_specs=[pl.BlockSpec(memory_space=pltpu.SMEM)] + [vm] * 6
        + [pl.BlockSpec(memory_space=pl.ANY)] * len(later),
        out_specs=[vm] * 7,
        out_shape=[
            jax.ShapeDtypeStruct((length, width), bf16),
            jax.ShapeDtypeStruct((length, width), bf16),
            jax.ShapeDtypeStruct((length, 1), f32),
            jax.ShapeDtypeStruct((rank, ext), bf16),
            jax.ShapeDtypeStruct((rank, length), bf16),
            jax.ShapeDtypeStruct((width, ext), bf16),
            jax.ShapeDtypeStruct((width, length), bf16),
        ],
        scratch_shapes=[pltpu.VMEM((HALO, width), bf16)],
        compiler_params=compiler_params(0),
        cost_estimate=cost(length * width * 200, length * width * 16),
        name="turn",
    )(sc, tokens, before, cot, gain, down, up, *later)


def row_specs(paths, first, rows):
    ops, specs = [], []
    for arrays in paths:
        for a in arrays:
            ops.append(a)
            specs.append(
                pl.BlockSpec((a.shape[0], rows, a.shape[2]), lambda i: (0, first // rows, 0))
            )
    return ops, specs


def maps_kernel(n_w, picks, sub, *refs):
    nt, taps = refs[n_w : n_w + 2]
    bt_o, ct_o, bn_o, cn_o, cbt_o, pre_o, w_o = refs[-7:]
    length = bt_o.shape[1]
    state_w = bt_o.shape[0]
    per = n_w // len(picks)
    w = jnp.concatenate(
        [joined(refs[p * per : (p + 1) * per], order) for p, order in enumerate(picks)], axis=0
    )
    w_o[...] = w
    maps_pre = conv_values(dot(w, nt[...]), tall(taps[...]))
    pre_o[...] = maps_pre
    maps = (maps_pre * sigmoid(maps_pre)).astype(bf16)
    bt, ct = maps[:state_w], maps[state_w:]
    bt_o[...] = bt
    ct_o[...] = ct
    bn = jnp.transpose(bt)
    bn_o[...] = bn
    cn_o[...] = jnp.transpose(ct)
    row = lax.broadcasted_iota(jnp.int32, (sub, sub), 0)
    col = lax.broadcasted_iota(jnp.int32, (sub, sub), 1)
    upto = jnp.where(row <= col, 1.0, 0.0)
    for s in range(length // sub):
        cols = slice(s * sub, (s + 1) * sub)
        cbt_o[s] = upto * dot(bn[cols, :], ct[:, cols])


def maps_call(paths, first, rows, picks, nt, taps, length, later):
    ops, specs = row_specs(paths, first, rows)
    state_w = rows * len(picks) // 2
    vm = pl.BlockSpec(memory_space=pltpu.VMEM)
    n_w = len(ops)
    return pl.pallas_call(
        functools.partial(maps_kernel, n_w, picks, SUB),
        grid=(1,),
        in_specs=specs + [vm, vm] + [pl.BlockSpec(memory_space=pl.ANY)] * len(later),
        out_specs=[vm] * 7,
        out_shape=[
            jax.ShapeDtypeStruct((state_w, length), bf16),
            jax.ShapeDtypeStruct((state_w, length), bf16),
            jax.ShapeDtypeStruct((length, state_w), bf16),
            jax.ShapeDtypeStruct((length, state_w), bf16),
            jax.ShapeDtypeStruct((length // SUB, SUB, SUB), f32),
            jax.ShapeDtypeStruct((2 * state_w, length), f32),
            jax.ShapeDtypeStruct((2 * state_w, nt.shape[0]), bf16),
        ],
        compiler_params=compiler_params(1),
        cost_estimate=cost(nt.shape[0] * nt.shape[1] * 512, nt.size * 2 + nt.shape[0] * 1024),
        name="maps",
    )(*ops, nt, taps, *later)


def steps_kernel(n_w, order, hb, sub, lo, hi, hs, *refs):
    nt, numbers = refs[n_w : n_w + 2]
    hp_o, sig_o, speed_o, w_o = refs[-4:]
    length = sig_o.shape[1]
    heads = sig_o.shape[0]
    w = joined(refs[:n_w], order)
    w_o[...] = w
    cols = [columns(numbers.at[j])[:hs] for j in range(lo, hi)]
    bias = jnp.concatenate([v[:, 6:7] for v in cols], axis=0)
    speed = jnp.exp(jnp.concatenate([v[:, 7:8] for v in cols], axis=0))
    speed_o[...] = jnp.broadcast_to(speed, (heads, 128))
    steps = dot(w, nt[:, HALO:]) + bias
    sig_o[...] = sigmoid(steps)
    delta = jnp.maximum(steps, 0.0) + jnp.log1p(jnp.exp(-jnp.abs(steps)))
    rates = -delta * speed
    row = lax.broadcasted_iota(jnp.int32, (sub, sub), 0)
    col = lax.broadcasted_iota(jnp.int32, (sub, sub), 1)
    upto = jnp.where(row <= col, 1.0, 0.0)
    before = None
    for s in range(length // sub):
        cols = slice(s * sub, (s + 1) * sub)
        cum = (
            lax.dot_general(
                rates[:, cols], upto, (NN, ((), ())), precision=highest,
                preferred_element_type=f32,
            )
            * LOG2E
        )
        cum_all = cum if before is None else cum + before
        before = cum_all[:, sub - 1 : sub]
        for b in range(heads // hb):
            mine = slice(b * hb, (b + 1) * hb)
            hp_o[b, :hb, cols] = cum[mine]
            hp_o[b, hb : 2 * hb, cols] = cum_all[mine]
            hp_o[b, 2 * hb :, cols] = delta[mine, cols]


def steps_call(arrays, first, order, nt, pk, lo, hi, hs, length, later):
    heads = (hi - lo) * hs
    hb = CB // HEAD
    ops, specs = row_specs([arrays], first, heads)
    vm = pl.BlockSpec(memory_space=pltpu.VMEM)
    return pl.pallas_call(
        functools.partial(steps_kernel, len(ops), order, hb, SUB, lo, hi, hs),
        grid=(1,),
        in_specs=specs
        + [vm, pl.BlockSpec((pk.shape[0], 16, CB), lambda i: (0, 3, 0))]
        + [pl.BlockSpec(memory_space=pl.ANY)] * len(later),
        out_specs=[vm] * 4,
        out_shape=[
            jax.ShapeDtypeStruct((heads // hb, 3 * hb, length), f32),
            jax.ShapeDtypeStruct((heads, length), f32),
            jax.ShapeDtypeStruct((heads, 128), f32),
            jax.ShapeDtypeStruct((heads, nt.shape[0]), bf16),
        ],
        compiler_params=compiler_params(1),
        cost_estimate=cost(nt.shape[0] * nt.shape[1] * 128, nt.size * 2),
        name="steps",
    )(*ops, nt, pk, *later)


def hop_kernel(hb, got, own, hp, *rest):
    out = rest[-1]
    length = hp.shape[2]
    for c in range(hp.shape[0]):
        rows = slice(c * CB, (c + 1) * CB)
        total = jnp.exp2(hp[c, hb : 2 * hb, length - 1 : length])
        out[rows, :] = (per_head(got[rows, :].astype(f32), total) + own[rows, :]).astype(bf16)


def hop_call(got, shift, own, hp, part=0, later=()):
    slots, rows, state_w = got.shape
    parts = own.shape[1] // rows
    return pl.pallas_call(
        functools.partial(hop_kernel, CB // HEAD),
        grid=(slots,),
        in_specs=[
            pl.BlockSpec((None, rows, state_w), lambda s: ((s + shift) % slots, 0, 0)),
            pl.BlockSpec((None, rows, state_w), lambda s: (s, part, 0)),
            pl.BlockSpec((rows // CB,) + hp.shape[1:], lambda s: (s * parts + part, 0, 0)),
        ]
        + [pl.BlockSpec(memory_space=pl.ANY)] * len(later),
        out_specs=pl.BlockSpec((None, rows, state_w), lambda s: (s, 0, 0)),
        out_shape=jax.ShapeDtypeStruct((slots, rows, state_w), bf16),
        compiler_params=compiler_params(1),
        cost_estimate=cost(got.size * 4, got.size * 8),
        name="hop",
    )(got, own, hp, *later)


def hold_kernel(n_joined, *refs):
    parts = refs[:n_joined]
    outs = refs[-1 - n_joined :]
    for part, out in zip(parts, outs):
        out[...] = part[...]
    outs[-1][...] = jnp.zeros((1, 1), bf16)


def hold(deps, passed=(), joined_to=(), parts=()):
    anywhere = pl.BlockSpec(memory_space=pl.ANY)
    deps, passed, joined_to, parts = list(deps), list(passed), list(joined_to), list(parts)
    kept = passed + joined_to
    whole = lambda a: pl.BlockSpec(a.shape, lambda i: (0, 0))
    second = lambda a: pl.BlockSpec((None,) + a.shape[1:], lambda i: (1, 0, 0))
    first = len(parts) + len(deps)
    out = pl.pallas_call(
        functools.partial(hold_kernel, len(parts)),
        grid=(1,),
        in_specs=[whole(a) for a in parts] + [anywhere] * (len(deps) + len(kept)),
        out_specs=[anywhere] * len(passed)
        + [second(a) for a in joined_to]
        + [pl.BlockSpec((1, 1), lambda i: (0, 0))],
        out_shape=[jax.ShapeDtypeStruct(v.shape, v.dtype) for v in kept]
        + [jax.ShapeDtypeStruct((1, 1), bf16)],
        input_output_aliases={first + k: k for k in range(len(kept))},
        compiler_params=compiler_params(1),
        cost_estimate=cost(8, 8),
        name="hold",
    )(*parts, *deps, *kept)
    n = len(passed)
    return out[-1], list(out[:n]), list(out[n:-1])


def path_dots(out, refs, picks, right, step, blocks):
    per = len(refs) // len(picks)
    for p, order in enumerate(picks):
        mine = refs[p * per : (p + 1) * per]

        @pl.when(step // (blocks // len(picks)) == p)
        def _(mine=mine, order=order):
            out[...] = dot(joined(mine, order), right)


def scan_kernel(nx, order, hb, sub, *refs):
    xrefs = refs[:nx]
    (nt, low, upx, num_r, hp_r, ct, bn, cbt) = refs[nx : nx + 8]
    xc_out, mix_out, ent_out, st_out, sent_out, tok_out = refs[-6:]
    tok_out[...] = jnp.zeros_like(tok_out)
    chan = columns(num_r)
    hp = hp_r[...]
    length = ct.shape[1]
    xr = dot(joined(xrefs, order), nt[...]) + dot(upx[...], low[...], TN)
    xc = conv_values(xr, chan)
    xc_out[...] = xc.astype(bf16)
    x = xc * sigmoid(xc)
    xs = per_head(x, hp[2 * hb : 3 * hb])
    xs_low = xs.astype(bf16)
    state = None
    for s in range(length // sub):
        cols = slice(s * sub, (s + 1) * sub)
        cum = hp[:hb, cols]
        rows_n = jnp.transpose(jnp.concatenate([cum, cum], axis=0))
        within = []
        for h in range(hb):
            gap = jnp.minimum(cum[h : h + 1] - rows_n[:, h : h + 1], 0.0)
            weight = (jnp.exp2(gap) * cbt[s]).astype(bf16)
            within.append(dot(xs_low[h * HEAD : (h + 1) * HEAD, cols], weight))
        y = jnp.concatenate(within, axis=0)
        last = cum[:, sub - 1 : sub]
        ends = jnp.exp2(last - cum)
        add = dot(per_head(xs[:, cols], ends).astype(bf16), bn[cols, :])
        if s > 0:
            ent_out[s - 1] = state
            y = y + per_head(dot(state.astype(bf16), ct[:, cols]), jnp.exp2(cum))
            state = per_head(state, jnp.exp2(last)) + add
        else:
            state = add
        mix_out[:, cols] = y + x[:, cols] * chan[:, 4:5]
    if length // sub == 1:
        ent_out[0] = state
    st_out[...] = state
    sent_out[...] = state.astype(bf16)


def range_specs(lo, ncb):
    full = lambda a: pl.BlockSpec(a.shape, lambda s, c: (0,) * a.ndim)
    per_chan = lambda a: pl.BlockSpec((None, CB, a.shape[2]), lambda s, c: (s + lo, c, 0))
    per_blk = lambda a: pl.BlockSpec(
        (None,) + a.shape[1:], lambda s, c: ((s + lo) * ncb + c, 0, 0)
    )
    return full, per_chan, per_blk


def weight_specs(weight, ncb):
    paths, base = weight
    per = ncb // len(paths)
    ops, specs = [], []
    for p, arrays in enumerate(paths):
        for a in arrays:
            ops.append(a)
            index = lambda s, c, p=p: (0, (s + base) * per + jnp.clip(c - p * per, 0, per - 1), 0)
            specs.append(pl.BlockSpec((a.shape[0], CB, a.shape[2]), index))
    return ops, specs


def scan_call(lo, hi, xw, part, picks, nt, low, pk, ch, hp, ct, bn, cbt, bufs, later=()):
    slots = pk.shape[0]
    length = ct.shape[1]
    hb = CB // HEAD
    paths, base = xw
    ncb = ch // CB
    per = ncb // len(paths)
    off = part * per
    nsub = length // SUB
    full = lambda a: pl.BlockSpec(a.shape, lambda s, c: (0,) * a.ndim)
    per_chan = lambda w: pl.BlockSpec((None, CB, w), lambda s, c: (s + lo, c + off, 0))
    ops = list(paths[part])
    specs = [
        pl.BlockSpec((a.shape[0], CB, a.shape[2]), lambda s, c: (0, (s + base) * per + c, 0))
        for a in ops
    ]
    nx = len(ops)
    ops += [nt, low, pk, pk, hp, ct, bn, cbt]
    here = lambda s, c: (s + lo, c + off)
    specs += [full(nt), full(low), packed_spec(1, here), packed_spec(3, here)]
    specs += [
        pl.BlockSpec((None,) + hp.shape[1:], lambda s, c: ((s + lo) * ncb + c + off, 0, 0)),
        full(ct), full(bn), full(cbt),
    ]
    inner_states = max(nsub - 1, 1)
    shapes = [
        jax.ShapeDtypeStruct((slots, ch, length), bf16),
        jax.ShapeDtypeStruct((slots, ch, length), f32),
        jax.ShapeDtypeStruct((slots, inner_states, ch, 128), f32),
        jax.ShapeDtypeStruct((slots, ch, 128), f32),
        jax.ShapeDtypeStruct((slots, per * CB, 128), bf16),
        jax.ShapeDtypeStruct((1, 1), bf16),
    ]
    outs = [
        per_chan(length),
        per_chan(length),
        pl.BlockSpec((None, inner_states, CB, 128), lambda s, c: (s + lo, 0, c + off, 0)),
        per_chan(128),
        pl.BlockSpec((None, CB, 128), lambda s, c: (s + lo, c, 0)),
        pl.BlockSpec((1, 1), lambda s, c: (0, 0)),
    ]
    aliases = {len(ops) + k: k for k in range(5) if bufs[k] is not None}
    given = [v for v in bufs if v is not None]
    aliases = {len(ops) + i: k for i, k in enumerate(k for k in range(5) if bufs[k] is not None)}
    ops += given + list(later)
    specs += [pl.BlockSpec(memory_space=pl.ANY)] * (len(given) + len(later))
    n = hi - lo
    out = pl.pallas_call(
        functools.partial(scan_kernel, nx, picks[part], hb, SUB),
        grid=(n, per),
        in_specs=specs,
        out_specs=outs,
        out_shape=shapes,
        input_output_aliases=aliases,
        compiler_params=compiler_params(2),
        cost_estimate=cost(
            4 * n * per * CB * 2048 * length, n * per * CB * (4096 + length * 8)
        ),
        name="scan_slots",
    )(*ops)
    return list(out[:5]), out[5]


def proj_kernel(n, picks, ncb, cut, gain, *refs):
    (right, low, up) = refs[n : n + 3]
    num_r = refs[n + 3]
    out, tok_o, sc = refs[-3:]
    tok_o[...] = jnp.zeros_like(tok_o)
    path_dots(sc, refs[:n], picks, right[:, cut:], pl.program_id(1), ncb)
    value = sc[...] + dot(up[...], low[:, cut:], TN)
    if gain:
        value = value * columns(num_r)[:, 5:6]
    out[...] = value.astype(bf16)


def proj_call(lo, hi, weight, picks, right, low, pk, ch, cut, gain, buf, later=()):
    slots = pk.shape[0]
    length = right.shape[1] - cut
    ncb = ch // CB
    full, per_chan, _ = range_specs(lo, ncb)
    ops, specs = weight_specs(weight, ncb)
    n_w = len(ops)
    ops += [right, low, pk, pk]
    here = lambda s, c: (s + lo, c)
    specs += [full(right), full(low), packed_spec(2 if gain else 0, here), packed_spec(3, here)]
    aliases = {}
    if buf is not None:
        aliases = {len(ops): 0}
        ops.append(buf)
        specs.append(pl.BlockSpec(memory_space=pl.ANY))
    ops += list(later)
    specs += [pl.BlockSpec(memory_space=pl.ANY)] * len(later)
    n = hi - lo
    return pl.pallas_call(
        functools.partial(proj_kernel, n_w, picks, ncb, cut, gain),
        grid=(n, ncb),
        in_specs=specs,
        out_specs=[
            pl.BlockSpec((None, CB, length), lambda s, c: (s + lo, c, 0)),
            pl.BlockSpec((1, 1), lambda s, c: (0, 0)),
        ],
        out_shape=[
            jax.ShapeDtypeStruct((slots, ch, length), bf16),
            jax.ShapeDtypeStruct((1, 1), bf16),
        ],
        scratch_shapes=[pltpu.VMEM((CB, length), f32)],
        input_output_aliases=aliases,
        compiler_params=compiler_params(2),
        cost_estimate=cost(2 * n * ch * 2048 * length, n * ch * (4096 + length * 2)),
        name="proj_slots",
    )(*ops)


def gate_kernel(hb, inner, *refs):
    (z_r, mix_r, wgt_r, ent_r, num_r, hp_r, ct, cn) = refs[:8]
    nout_o, dmix_o, dz_o, sl_o, sent_o = refs[8:13]
    mix_sc, sq_sc, dot_sc = refs[13:]
    phase = pl.program_id(0)
    blk = pl.program_id(1) * pl.num_programs(2) + pl.program_id(2)
    length = ct.shape[1]
    z = z_r[...].astype(f32)
    sig = sigmoid(z)
    silu = z * sig
    weighted = wgt_r[...].astype(f32)
    cum = jnp.exp2(hp_r[hb : 2 * hb])

    @pl.when((phase == 0) & (blk == 0))
    def _():
        sq_sc[...] = jnp.zeros_like(sq_sc)
        dot_sc[...] = jnp.zeros_like(dot_sc)

    @pl.when(phase == 0)
    def _():
        mix = mix_r[...] + per_head(dot(ent_r[...], ct[...]), cum)
        mix_sc[blk] = mix
        gated = mix * silu
        sq_sc[...] += jnp.sum((gated * gated).reshape(CB // 8, 8, length), axis=0)
        dot_sc[...] += jnp.sum((gated * weighted).reshape(CB // 8, 8, length), axis=0)

    @pl.when(phase == 1)
    def _():
        r = lax.rsqrt(jnp.sum(sq_sc[...], axis=0, keepdims=True) * (1.0 / inner) + epsilon)
        coef = r * r * r * (jnp.sum(dot_sc[...], axis=0, keepdims=True) * (1.0 / inner))
        mix = mix_sc[blk]
        gated = mix * silu
        nout_o[...] = (gated * (r * columns(num_r)[:, 5:6])).astype(bf16)
        d_gated = r * weighted - gated * coef
        d_mix = d_gated * silu
        dmix_o[...] = d_mix.astype(bf16)
        dz_o[...] = (d_gated * mix * (sig + silu * (1.0 - sig))).astype(bf16)
        adj = dot(per_head(d_mix, cum).astype(bf16), cn[...])
        sl_o[...] = adj
        sent_o[...] = adj.astype(bf16)


def gate_call(z, mix, wgt, ent, pk, hp, ct, cn, inner):
    slots, ch, length = mix.shape
    ncb = ch // CB
    hb = CB // HEAD
    full = lambda a: pl.BlockSpec(a.shape, lambda p, s, c: (0,) * a.ndim)
    per_chan = lambda a: pl.BlockSpec((None, CB, a.shape[2]), lambda p, s, c: (s, c, 0))
    per_blk = lambda a: pl.BlockSpec((None,) + a.shape[1:], lambda p, s, c: (s * ncb + c, 0, 0))
    held = lambda p, s, c, k: (
        jnp.where(p == 0, (s + k) % slots, (slots - 1 + k) % slots),
        jnp.where(p == 0, c, ncb - 1),
        0,
    )
    first = lambda a, k: pl.BlockSpec((None, CB, a.shape[2]), lambda p, s, c: held(p, s, c, k))
    per = ncb // ent.shape[0]

    def entered(p, s, c):
        slot, block, _ = held(p, s, c, 1)
        return (block // per, slot, block % per, 0)

    later = lambda w: pl.BlockSpec(
        (None, CB, w), lambda p, s, c: (jnp.where(p == 1, s, 0), jnp.where(p == 1, c, 0), 0)
    )
    return pl.pallas_call(
        functools.partial(gate_kernel, hb, inner),
        grid=(2, slots, ncb),
        in_specs=[per_chan(z), first(mix, 0), per_chan(wgt)]
        + [pl.BlockSpec((None, None, CB, 128), entered), packed_spec(3, lambda p, s, c: (s, c))]
        + [per_blk(hp), full(ct), full(cn)],
        out_specs=[later(length), later(length), later(length), later(128), later(128)],
        out_shape=[
            jax.ShapeDtypeStruct((slots, ch, length), bf16),
            jax.ShapeDtypeStruct((slots, ch, length), bf16),
            jax.ShapeDtypeStruct((slots, ch, length), bf16),
            jax.ShapeDtypeStruct((slots, ch, 128), f32),
            jax.ShapeDtypeStruct((slots, ch, 128), bf16),
        ],
        scratch_shapes=[
            pltpu.VMEM((slots * ncb, CB, length), f32),
            pltpu.VMEM((8, length), f32),
            pltpu.VMEM((8, length), f32),
        ],
        compiler_params=compiler_params(3),
        cost_estimate=cost(slots * ch * length * 600, slots * ch * length * 22),
        name="gate",
    )(z, mix, wgt, ent, pk, hp, ct, cn)


def grid_specs(ncb):
    full = lambda a: pl.BlockSpec(a.shape, lambda s, c: (0,) * a.ndim)
    per_chan = lambda a: pl.BlockSpec((None, CB, a.shape[2]), lambda s, c: (s, c, 0))
    per_blk = lambda a: pl.BlockSpec((None,) + a.shape[1:], lambda s, c: (s * ncb + c, 0, 0))
    return full, per_chan, per_blk


def back_kernel(hb, sub, *refs):
    (dy_r, xc_r, hp_r, ent_r, loc_r, ct, cn, bt, cbt) = refs[:9]
    dxs_o, u1_o, u2_o, kl_o, dcb_o, db_o, dc_o = refs[-7:]
    blk = pl.program_id(0) * pl.num_programs(1) + pl.program_id(1)
    hp = hp_r[...]
    length = ct.shape[1]
    nsub = length // sub

    @pl.when(blk == 0)
    def _():
        dcb_o[...] = jnp.zeros_like(dcb_o)
        db_o[...] = jnp.zeros_like(db_o)
        dc_o[...] = jnp.zeros_like(dc_o)

    xc = xc_r[...].astype(f32)
    x = xc * sigmoid(xc)
    xs = per_head(x, hp[2 * hb : 3 * hb])
    xs_low = xs.astype(bf16)
    adj = None
    kl = []
    for s in reversed(range(nsub)):
        cols = slice(s * sub, (s + 1) * sub)
        cum = hp[:hb, cols]
        rows_n = jnp.transpose(jnp.concatenate([cum, cum], axis=0))
        ecum = jnp.exp2(cum)
        last = cum[:, sub - 1 : sub]
        state = ent_r[...].astype(f32)
        if s > 0:
            before = hp[hb : 2 * hb, s * sub - 1 : s * sub]
            state = loc_r[s - 1] + per_head(state, jnp.exp2(before))
        state_low = state.astype(bf16)
        dy_low = dy_r[:, cols]
        dy = dy_low.astype(f32)
        y_in = per_head(dot(state_low, ct[:, cols]), ecum)
        ed = per_head(dy, ecum).astype(bf16)
        dc_o[:, cols] += dot(state_low, ed, TN)
        dxw, yw = [], []
        for h in range(hb):
            hs = slice(h * HEAD, (h + 1) * HEAD)
            gap = jnp.minimum(cum[h : h + 1] - rows_n[:, h : h + 1], 0.0)
            decay = jnp.exp2(gap)
            weight = (decay * cbt[s]).astype(bf16)
            yw.append(dot(xs_low[hs, cols], weight))
            dxw.append(dot(dy_low[hs], weight, NT))
            dcb_o[s] += decay * dot(xs_low[hs, cols], dy_low[hs], TN)
        yw = jnp.concatenate(yw, axis=0)
        dxs = jnp.concatenate(dxw, axis=0)
        u1_o[:, cols] = head_sums(dy * (yw + y_in) - xs_low[:, cols].astype(f32) * dxs, hb)
        add = dot(ed, cn[cols, :])
        if adj is None:
            u2_o[:, cols] = jnp.zeros((hb, sub), f32)
            kl.append(jnp.zeros((hb, 128), f32))
            adj = add
        else:
            ends = jnp.exp2(last - cum)
            adj_low = adj.astype(bf16)
            dxi = per_head(dot(adj_low, bt[:, cols]), ends)
            xs_s = xs[:, cols]
            u2_o[:, cols] = head_sums(xs_s * dxi, hb)
            kl.append(head_sums(adj * state, hb) * jnp.exp2(last))
            db_o[:, cols] += dot(adj_low, per_head(xs_s, ends).astype(bf16), TN)
            dxs = dxs + dxi
            adj = per_head(adj, jnp.exp2(last)) + add
        dxs_o[:, cols] = dxs
    for s in range(nsub):
        kl_o[:, s * 128 : (s + 1) * 128] = kl[nsub - 1 - s]


def back_call(lo, hi, dy, xc, hp, ent, loc, ct, cn, bt, cbt, bufs, later=()):
    slots, ch, length = dy.shape
    ncb = ch // CB
    hb = CB // HEAD
    nsub = length // SUB
    full = lambda a: pl.BlockSpec(a.shape, lambda s, c: (0,) * a.ndim)
    per_chan = lambda a: pl.BlockSpec((None, CB, a.shape[2]), lambda s, c: (s + lo, c, 0))
    per_blk = lambda a: pl.BlockSpec(
        (None,) + a.shape[1:], lambda s, c: ((s + lo) * ncb + c, 0, 0)
    )
    blk_out = lambda w: pl.BlockSpec((None, hb, w), lambda s, c: ((s + lo) * ncb + c, 0, 0))
    loc_spec = pl.BlockSpec((None, loc.shape[1], CB, 128), lambda s, c: (s + lo, 0, c, 0))
    blocks = slots * ncb
    ops = [dy, xc, hp, ent, loc, ct, cn, bt, cbt]
    per = ncb // ent.shape[0]
    entered = pl.BlockSpec(
        (None, None, CB, 128), lambda s, c: (c // per, (s + lo + 1) % slots, c % per, 0)
    )
    specs = [per_chan(dy), per_chan(xc), per_blk(hp), entered, loc_spec]
    specs += [full(ct), full(cn), full(bt), full(cbt)]
    aliases = {}
    if bufs is not None:
        aliases = {len(ops) + k: k for k in range(4)}
        ops += list(bufs)
        specs += [pl.BlockSpec(memory_space=pl.ANY)] * 4
    ops += list(later)
    specs += [pl.BlockSpec(memory_space=pl.ANY)] * len(later)
    return pl.pallas_call(
        functools.partial(back_kernel, hb, SUB),
        grid=(hi - lo, ncb),
        in_specs=specs,
        out_specs=[
            pl.BlockSpec((None, CB, length), lambda s, c: (s + lo, c, 0)),
            blk_out(length),
            blk_out(length),
            blk_out(128 * nsub),
            pl.BlockSpec((nsub, SUB, SUB), lambda s, c: (0, 0, 0)),
            pl.BlockSpec((128, length), lambda s, c: (0, 0)),
            pl.BlockSpec((128, length), lambda s, c: (0, 0)),
        ],
        out_shape=[
            jax.ShapeDtypeStruct((slots, ch, length), f32),
            jax.ShapeDtypeStruct((blocks, hb, length), f32),
            jax.ShapeDtypeStruct((blocks, hb, length), f32),
            jax.ShapeDtypeStruct((blocks, hb, 128 * nsub), f32),
            jax.ShapeDtypeStruct((nsub, SUB, SUB), f32),
            jax.ShapeDtypeStruct((128, length), f32),
            jax.ShapeDtypeStruct((128, length), f32),
        ],
        input_output_aliases=aliases,
        compiler_params=compiler_params(2),
        cost_estimate=cost((hi - lo) * ch * length * SUB * 20, (hi - lo) * ch * length * 8),
        name="state_back",
    )(*ops)


def finish_kernel(hb, *refs):
    (dxs_r, dy_r, xc_r, dz_r, num_r, hp_r, ent_r, adj_r, bt, upz, upx, low) = refs[:12]
    dx_o, tail_o, head_o, gx_o, dl_o, dd_o, u2_o, kf_o, db_o = refs[-9:]
    blk = pl.program_id(0) * pl.num_programs(1) + pl.program_id(1)
    chan = columns(num_r)
    hp = hp_r[...]
    length = bt.shape[1]

    @pl.when(blk == 0)
    def _():
        db_o[...] = jnp.zeros_like(db_o)
        dl_o[...] = jnp.zeros_like(dl_o)

    xc = xc_r[...].astype(f32)
    sig = sigmoid(xc)
    x = xc * sig
    delta = hp[2 * hb : 3 * hb]
    xs = per_head(x, delta)
    total = hp[hb : 2 * hb]
    last = total[:, length - 1 : length]
    ends = jnp.exp2(last - total)
    adj_low = adj_r[...]
    extra = per_head(dot(adj_low, bt[...]), ends)
    u2_o[...] = head_sums(xs * extra, hb)
    kf_o[...] = head_sums(adj_low.astype(f32) * ent_r[...].astype(f32), hb) * jnp.exp2(last)
    db_o[...] += dot(adj_low, per_head(xs, ends).astype(bf16), TN)
    dxs = dxs_r[...] + extra
    dd_o[...] = head_sums(x * dxs, hb)
    dx = per_head(dxs, delta) + dy_r[...].astype(f32) * chan[:, 4:5]
    dconv = dx * (sig + x * (1.0 - sig))
    head_o[...] = jnp.transpose(dconv[:, :HALO])[:8]
    none = jnp.zeros((CB, HALO), f32)
    ext = jnp.concatenate([none, dconv, none], axis=1)
    width = ext.shape[1]
    out = ext * chan[:, 3:4]
    for k in range(3):
        out = out + pltpu.roll(ext, width - (3 - k), 1) * chan[:, k : k + 1]
    out = out[:, : HALO + length]
    tail_o[...] = out[:, length:]
    all_low = out.astype(bf16)
    dx_o[...] = all_low[:, HALO:]
    gx_o[...] = dot(low[...], all_low, NT)
    dl_o[...] += dot(upx[...], all_low)
    dl_o[:, HALO:] += dot(upz[...], dz_r[...])


def finish_call(dxs, dy, xc, dz, pk, hp, ent, adj, bt, low, later):
    slots, ch, length = dy.shape
    ncb = ch // CB
    hb = CB // HEAD
    rank = low.shape[0]
    full, per_chan, per_blk = grid_specs(ncb)
    blk_out = lambda w: pl.BlockSpec((None, hb, w), lambda s, c: (s * ncb + c, 0, 0))
    chan_out = lambda w: pl.BlockSpec((None, CB, w), lambda s, c: (s, c, 0))
    turned = lambda w: pl.BlockSpec((None, w, CB), lambda s, c: (s, 0, c))
    moved = lambda k: pl.BlockSpec((None, CB, 128), lambda s, c: ((s + k) % slots, c, 0))
    per = ncb // ent.shape[0]
    entered = pl.BlockSpec(
        (None, None, CB, 128), lambda s, c: (c // per, (s + 1) % slots, c % per, 0)
    )
    here = lambda s, c: (s, c)
    blocks = slots * ncb
    return pl.pallas_call(
        functools.partial(finish_kernel, hb),
        grid=(slots, ncb),
        in_specs=[per_chan(dxs), per_chan(dy), per_chan(xc), per_chan(dz), packed_spec(3, here)]
        + [per_blk(hp), entered, moved(slots - 1), full(bt)]
        + [packed_spec(0, here), packed_spec(1, here), full(low)]
        + [pl.BlockSpec(memory_space=pl.ANY)] * len(later),
        out_specs=[
            chan_out(length),
            chan_out(HALO),
            turned(8),
            turned(rank),
            pl.BlockSpec((rank, HALO + length), lambda s, c: (0, 0)),
            blk_out(length),
            blk_out(length),
            blk_out(128),
            pl.BlockSpec((128, length), lambda s, c: (0, 0)),
        ],
        out_shape=[
            jax.ShapeDtypeStruct((slots, ch, length), bf16),
            jax.ShapeDtypeStruct((slots, ch, HALO), f32),
            jax.ShapeDtypeStruct((slots, 8, ch), f32),
            jax.ShapeDtypeStruct((slots, rank, ch), f32),
            jax.ShapeDtypeStruct((rank, HALO + length), f32),
            jax.ShapeDtypeStruct((blocks, hb, length), f32),
            jax.ShapeDtypeStruct((blocks, hb, length), f32),
            jax.ShapeDtypeStruct((blocks, hb, 128), f32),
            jax.ShapeDtypeStruct((128, length), f32),
        ],
        compiler_params=compiler_params(2),
        cost_estimate=cost(slots * ch * length * 700, slots * ch * length * 14),
        name="finish_back",
    )(dxs, dy, xc, dz, pk, hp, ent, adj, bt, pk, pk, low, *later)


def glue_kernel(flat_order, quick, sub, *refs):
    (dcb_r, db1, db2, dc1, bt, ct, pre_r, u1, u2, kl, dd, u2f, kf) = refs[:13]
    (sig_r, speed, taps_r, sc, dl, nt) = refs[13:19]
    left_o, tail_o, head_o, gd_o = refs[19:]
    taps = tall(taps_r[...])
    low = dl[...].astype(bf16)
    for i, m in enumerate(flat_order):
        at = pl.ds(block_at(sc[0], m, quick), CB)
        gd_o[:, at] = dot(low, nt[i * CB : (i + 1) * CB, :], NT)
    state_w, length = bt.shape
    nsub = length // sub
    blocks = u1.shape[0]
    row = lax.broadcasted_iota(jnp.int32, (sub, sub), 0)
    col = lax.broadcasted_iota(jnp.int32, (sub, sub), 1)
    below = jnp.where(row >= col, 1.0, 0.0)
    keep = jnp.where(row <= col, 1.0, 0.0)

    def exact(p, q):
        return lax.dot_general(
            p, q, (NN, ((), ())), precision=highest, preferred_element_type=f32
        )

    def flat(ref, cols=slice(None)):
        return jnp.concatenate([ref[b, :, cols] for b in range(blocks)], axis=0)

    d_b, d_c, rate_in = [], [], []
    for s in range(nsub):
        cols = slice(s * sub, (s + 1) * sub)
        dcb = (dcb_r[s] * keep).astype(bf16)
        d_b.append(dot(ct[:, cols], dcb, NT))
        d_c.append(dot(bt[:, cols], dcb))
        lane = slice(s * 128, (s + 1) * 128)
        rate_in.append(
            exact(flat(u1, cols), below)
            + exact(flat(u2, cols), 1.0 - below)
            + jnp.sum(flat(kl, lane), axis=1, keepdims=True)
        )
    d_b = jnp.concatenate(d_b, axis=1) + db1[...] + db2[...]
    d_c = jnp.concatenate(d_c, axis=1) + dc1[...]
    pre = pre_r[...]
    sig = sigmoid(pre)
    d_pre = jnp.concatenate([d_b, d_c], axis=0) * (sig + pre * sig * (1.0 - sig))
    head_o[...] = jnp.transpose(d_pre[:, :HALO])[:8]
    ext = jnp.concatenate([d_pre, jnp.zeros((2 * state_w, HALO), f32)], axis=1)
    out = ext * taps[:, 3:4]
    for k in range(3):
        out = out + pltpu.roll(ext, ext.shape[1] - (3 - k), 1) * taps[:, k : k + 1]
    tail_o[...] = out[:, length - HALO : length]
    left_o[: 2 * state_w, :] = out[:, :length].astype(bf16)
    rate = jnp.concatenate(rate_in, axis=1) + jnp.sum(flat(kf), axis=1, keepdims=True)
    first = flat(u2f)
    run = None
    parts = []
    for s in range(nsub):
        piece = first[:, s * sub : (s + 1) * sub]
        here = exact(piece, 1.0 - below)
        parts.append(here if run is None else here + run)
        ends = jnp.sum(piece, axis=1, keepdims=True)
        run = ends if run is None else run + ends
    rate = rate + jnp.concatenate(parts, axis=1)
    left_o[2 * state_w :, :] = ((flat(dd) - speed[:, :1] * rate) * sig_r[...]).astype(bf16)


def glue_call(args, sc, dl, nt, state_w, length, heads, flat, quick):
    vm = pl.BlockSpec(memory_space=pltpu.VMEM)
    return pl.pallas_call(
        functools.partial(glue_kernel, flat, quick, SUB),
        in_specs=[vm] * len(args) + [pl.BlockSpec(memory_space=pltpu.SMEM), vm, vm],
        out_specs=[vm] * 4,
        out_shape=[
            jax.ShapeDtypeStruct((2 * state_w + heads, length), bf16),
            jax.ShapeDtypeStruct((2 * state_w, HALO), f32),
            jax.ShapeDtypeStruct((8, 2 * state_w), f32),
            jax.ShapeDtypeStruct((dl.shape[0], nt.shape[0]), f32),
        ],
        compiler_params=compiler_params(0),
        cost_estimate=cost(1e8, 4e6),
        name="glue",
    )(*args, sc, dl, nt)


def add_products(acc, turned, sets, picks, n_left, refs, slot, c):
    at = 0
    for lo, hi, per in sets:
        for p, order in enumerate(picks):
            groups = [refs[at + g * per : at + (g + 1) * per] for g in range(n_left)]
            at += n_left * per

            @pl.when((slot >= lo) & (slot < hi) & (c == p))
            def _(groups=groups, order=order):
                off = 0
                for k, b in order:
                    parts = [g[k][b] for g in groups]
                    w = parts[0] if n_left == 1 else jnp.concatenate(parts, axis=0)
                    acc[:, off : off + w.shape[1]] += dot(turned, w)
                    off += w.shape[1]


def product_specs(weights, paths, block):
    ops, specs, sets = [], [], []
    for (lo, hi), groups in weights:
        sets.append((lo, hi, len(groups[0][0][0])))
        for p in range(paths):
            for arrays, base in groups:
                for a in arrays[p]:
                    ops.append(a)

                    def index(s, c, lo=lo, hi=hi, base=base):
                        return (0, base + jnp.clip(s, lo, hi - 1) - lo, 0)

                    specs.append(pl.BlockSpec((a.shape[0], block, a.shape[2]), index))
    return ops, specs, sets


def output_kernel(sets, picks, flat, quick, n_w, *refs):
    (sc, nout, dn, bh, up, tok, masked) = refs[:7]
    wrefs = refs[7 : 7 + n_w]
    mixed_o, gdo_o, guo_o, acc, hid = refs[-5:]
    slot, c = pl.program_id(0), pl.program_id(1)
    rank = up.shape[0]
    length, width = tok.shape

    @pl.when((slot == 0) & (c == 0))
    def _():
        acc[...] = jnp.zeros_like(acc)
        hid[...] = jnp.zeros_like(hid)

    values = nout[...]
    gdo_o[...] = dot(bh[...], values, NT)
    for part in range(dn.shape[0] // 64):
        mine = slice(part * CB, (part + 1) * CB)
        hid[...] += dot(dn[part * 64 + 32 : part * 64 + 48, :], values[mine])
    add_products(acc, jnp.transpose(values), sets, picks, 1, wrefs, slot, c)

    @pl.when((slot == pl.num_programs(0) - 1) & (c == pl.num_programs(1) - 1))
    def _():
        low = hid[...].astype(bf16)
        guo_o[...] = dot(low, masked[...])
        rows = lax.broadcasted_iota(jnp.int32, (length, 1), 0) < sc[1]
        for i, m in enumerate(flat):
            at = pl.ds(block_at(sc[0], m, quick), CB)
            total = acc[:, i * CB : (i + 1) * CB] + dot(low, up[:, at], TN)
            total = total + tok[:, at].astype(f32)
            mixed_o[:, at] = jnp.where(rows, total, 0.0).astype(bf16)


def output_call(sc, nout, pk, bh, up, tok, masked, weights, picks, flat, quick):
    slots, ch, length = nout.shape
    rank, width = up.shape
    paths = len(picks)
    block = ch // paths
    full = lambda a: pl.BlockSpec(a.shape, lambda s, c: (0,) * a.ndim)
    chan = lambda a: pl.BlockSpec((None, block, a.shape[2]), lambda s, c: (s, c, 0))
    w_ops, w_specs, sets = product_specs(weights, paths, block)
    return pl.pallas_call(
        functools.partial(output_kernel, sets, picks, flat, quick, len(w_ops)),
        grid=(slots, paths),
        in_specs=[pl.BlockSpec(memory_space=pltpu.SMEM), chan(nout)]
        + [pl.BlockSpec((None, block // 4, CB), lambda s, c: (s, c, 0)), full(bh)]
        + [full(up), full(tok), full(masked)] + w_specs,
        out_specs=[
            pl.BlockSpec((length, width), lambda s, c: (0, 0)),
            pl.BlockSpec((None, rank, block), lambda s, c: (s, 0, c)),
            pl.BlockSpec((rank, width), lambda s, c: (0, 0)),
        ],
        out_shape=[
            jax.ShapeDtypeStruct((length, width), bf16),
            jax.ShapeDtypeStruct((slots, rank, ch), f32),
            jax.ShapeDtypeStruct((rank, width), f32),
        ],
        scratch_shapes=[pltpu.VMEM((length, width), f32), pltpu.VMEM((rank, length), f32)],
        compiler_params=compiler_params(2),
        cost_estimate=cost(2 * slots * ch * length * width, slots * ch * width * 2),
        name="output",
    )(sc, nout, pk, bh, up, tok, masked, *w_ops)


def gate_back_kernel(sets, picks, n_w, *refs):
    dz, low = refs[:2]
    acc, gz_o = refs[-2:]
    slot, c = pl.program_id(0), pl.program_id(1)

    @pl.when((slot == 0) & (c == 0))
    def _():
        acc[...] = jnp.zeros_like(acc)

    gz_o[...] = dot(low[:, HALO:], dz[...], NT)
    add_products(acc, jnp.transpose(dz[...]), sets, picks, 1, refs[2 : 2 + n_w], slot, c)


def gate_back_call(dz, low, weights, picks, width, later=()):
    slots, ch, length = dz.shape
    rank = low.shape[0]
    paths = len(picks)
    block = ch // paths
    w_ops, w_specs, sets = product_specs(weights, paths, block)
    return pl.pallas_call(
        functools.partial(gate_back_kernel, sets, picks, len(w_ops)),
        grid=(slots, paths),
        in_specs=[
            pl.BlockSpec((None, block, length), lambda s, c: (s, c, 0)),
            pl.BlockSpec(low.shape, lambda s, c: (0, 0)),
        ]
        + w_specs
        + [pl.BlockSpec(memory_space=pl.ANY)] * len(later),
        out_specs=[
            pl.BlockSpec((length, width), lambda s, c: (0, 0)),
            pl.BlockSpec((None, rank, block), lambda s, c: (s, 0, c)),
        ],
        out_shape=[
            jax.ShapeDtypeStruct((length, width), f32),
            jax.ShapeDtypeStruct((slots, rank, ch), f32),
        ],
        compiler_params=compiler_params(2),
        cost_estimate=cost(2 * slots * ch * length * width, 2 * slots * ch * width),
        name="gate_back",
    )(dz, low, *w_ops, *later)


def beyond(near, taps, rows):
    parts = [jnp.zeros((HALO - 3, rows), f32)]
    for i in range(3):
        total = near[i : i + 1] * taps[0:1]
        for k in range(1, i + 1):
            total = total + near[i - k : i - k + 1] * taps[k : k + 1]
        parts.append(total)
    return jnp.transpose(jnp.concatenate(parts, axis=0))


def input_kernel(sets, picks, flat, quick, n_w, n_small, *refs):
    (sc, dx, tail, near, num, left, maps_tail, maps_near, maps_taps) = refs[:9]
    (dl, near_dl, down, root_r, gain, tok, masked, start) = refs[9:17]
    smalls = refs[17 : 17 + n_small]
    wrefs = refs[17 + n_small : 17 + n_small + n_w]
    out, acc = refs[-2:]
    slot, c = pl.program_id(0), pl.program_id(1)
    length, width = tok.shape
    cut = length - HALO

    @pl.when((slot == 0) & (c == 0))
    def _():
        d_low = jnp.concatenate(
            [dl[:, HALO:length], dl[:, length:] + near_dl[:, :HALO]], axis=1
        ).astype(bf16)
        low = jnp.transpose(d_low)
        n_maps = maps_tail.shape[0]
        maps_last = maps_tail[...] + beyond(maps_near[:, :n_maps], maps_taps, n_maps)
        maps_left = jnp.concatenate([left[:n_maps, :cut], maps_last.astype(bf16)], axis=1)
        total = start[...] + dot(maps_left, smalls[0][...], TN)
        row = n_maps
        for w in smalls[1:]:
            total = total + dot(left[row : row + w.shape[0], :], w[...], TN)
            row += w.shape[0]
        acc[...] = total
        for i, m in enumerate(flat):
            at = pl.ds(block_at(sc[0], m, quick), CB)
            acc[:, i * CB : (i + 1) * CB] += dot(low, down[at, :], NT)

    block = dx.shape[0]
    taps = jnp.concatenate(
        [
            num[b * 64 + 48 : b * 64 + 56, :].astype(f32)
            + num[b * 64 + 56 : b * 64 + 64, :].astype(f32)
            for b in range(block // CB)
        ],
        axis=1,
    )
    last = tail[...] + beyond(near[...], taps, block)
    dx_all = jnp.concatenate([dx[:, :cut], last.astype(bf16)], axis=1)
    add_products(acc, jnp.transpose(dx_all), sets, picks, 1, wrefs, slot, c)

    @pl.when((slot == pl.num_programs(0) - 1) & (c == pl.num_programs(1) - 1))
    def _():
        root = root_r[...]
        mean = None
        for i, m in enumerate(flat):
            at = pl.ds(block_at(sc[0], m, quick), CB)
            cols = slice(i * CB, (i + 1) * CB)
            scaled = acc[:, cols] * gain[:, at]
            acc[:, cols] = scaled
            part = jnp.sum(scaled * tok[:, at].astype(f32), axis=1, keepdims=True)
            mean = part if mean is None else mean + part
        coef = root * root * root * (mean * (1.0 / width))
        for i, m in enumerate(flat):
            at = pl.ds(block_at(sc[0], m, quick), CB)
            d_resid = root * acc[:, i * CB : (i + 1) * CB] - tok[:, at].astype(f32) * coef
            out[:, at] = (masked[:, at].astype(f32) + d_resid).astype(bf16)


def input_call(
    sc, dx, tail, near, pk, left, maps_tail, maps_taps, dl, down, root, gain, tok, masked, start,
    smalls, weights, picks, flat, quick, later=(),
):
    slots, ch, length = dx.shape
    width = tok.shape[1]
    paths = len(picks)
    block = ch // paths
    rank = dl.shape[0]
    once = pl.Buffered(1)
    full = lambda a: pl.BlockSpec(a.shape, lambda s, c: (0,) * a.ndim, pipeline_mode=once)
    chan = lambda a: pl.BlockSpec((None, block, a.shape[2]), lambda s, c: (s, c, 0))
    w_ops, w_specs, sets = product_specs(weights, paths, block)
    near_rows = pl.BlockSpec((8, block), lambda s, c: ((s + slots - 1) % slots, c))
    near_maps = pl.BlockSpec((8, ch), lambda s, c: (slots, 0), pipeline_mode=once)
    near_low = pl.BlockSpec(
        (rank, ch), lambda s, c: (((slots + 1) * 8 + rank - 1) // rank, 0), pipeline_mode=once
    )
    return pl.pallas_call(
        functools.partial(input_kernel, sets, picks, flat, quick, len(w_ops), len(smalls)),
        grid=(slots, paths),
        in_specs=[pl.BlockSpec(memory_space=pltpu.SMEM), chan(dx), chan(tail), near_rows]
        + [pl.BlockSpec((None, block // 4, CB), lambda s, c: (s, c, 0))]
        + [full(left), full(maps_tail), near_maps, full(maps_taps), full(dl), near_low]
        + [full(a) for a in [down, root, gain, tok, masked, start] + list(smalls)]
        + w_specs
        + [pl.BlockSpec(memory_space=pl.ANY)] * len(later),
        out_specs=pl.BlockSpec((length, width), lambda s, c: (0, 0)),
        out_shape=jax.ShapeDtypeStruct((length, width), bf16),
        scratch_shapes=[pltpu.VMEM((length, width), f32)],
        compiler_params=compiler_params(2),
        cost_estimate=cost(2 * slots * ch * length * width, 2 * slots * ch * width),
        name="input_back",
    )(
        sc, dx, tail, near, pk, left, maps_tail, near, maps_taps, dl, near, down, root, gain, tok,
        masked, start, *smalls, *w_ops, *later
    )


def assemble_kernel(n, planes, ch, *refs):
    parts = refs[:n]
    down_o, up_o, down_out_o, up_out_o = refs[n:]
    which = pl.program_id(0).astype(f32)
    total = None
    for ref in parts:
        for b in range(ref.shape[0]):
            chosen = jnp.where(ref[b, :, -1:].astype(f32) == which, 1.0, 0.0)
            term = ref[b, :, :-128].astype(f32) * chosen
            total = term if total is None else total + term
    up_o[:, 0, :] = total[:, :ch]
    up_o[:, 1, :] = total[:, ch : 2 * ch]
    down_out_o[...] = total[:, 2 * ch : 3 * ch]
    width = down_o.shape[1]
    down_o[...] = total[:, 3 * ch : 3 * ch + width]
    up_out_o[...] = total[:, 3 * ch + width :]


def assemble_call(parts, adapters, planes, ch, width):
    rank = parts[0].shape[1]
    return pl.pallas_call(
        functools.partial(assemble_kernel, len(parts), planes, ch),
        grid=(adapters,),
        in_specs=[pl.BlockSpec(a.shape, lambda i: (0, 0, 0)) for a in parts],
        out_specs=[
            pl.BlockSpec((None, rank, width), lambda i: (i, 0, 0)),
            pl.BlockSpec((None, rank, 2, ch), lambda i: (i, 0, 0, 0)),
            pl.BlockSpec((None, rank, ch), lambda i: (i, 0, 0)),
            pl.BlockSpec((None, rank, width), lambda i: (i, 0, 0)),
        ],
        out_shape=[
            jax.ShapeDtypeStruct((adapters, rank, width), f32),
            jax.ShapeDtypeStruct((adapters, rank, 2, ch), f32),
            jax.ShapeDtypeStruct((adapters, rank, ch), f32),
            jax.ShapeDtypeStruct((adapters, rank, width), f32),
        ],
        compiler_params=compiler_params(1),
        cost_estimate=cost(1e7, 2e7),
        name="assemble",
    )(*parts)


def body(
    tokens,
    cotangent,
    lengths,
    adapter_ids,
    pre_gain,
    in_inner,
    in_maps,
    in_steps,
    conv_inner,
    conv_maps,
    step_bias,
    decay_log,
    skip_gain,
    norm_gain,
    out_weight,
    adapter_in_down,
    adapter_in_up,
    adapter_out_down,
    adapter_out_up,
):
    planes = lax.axis_size("tensor")
    seqs = lax.axis_size("dp")
    place = lax.axis_index("tensor")
    mine = lax.axis_index("dp")
    length = tokens.shape[1]
    width = tokens.shape[2]
    rows_here = in_inner.shape[0]
    ch = in_inner.shape[2]
    inner = ch * planes
    hs = in_steps.shape[1]
    heads = hs * planes
    rank = adapter_in_down.shape[2]
    adapters = adapter_in_down.shape[0]
    state_w = in_maps.shape[1] // 2
    hb = CB // HEAD
    ncb = ch // CB
    nblk = planes * ncb
    nsub = length // SUB
    quick = seqs == 8 and planes == 4

    def from_plane(v, j):
        return lax.ppermute(v, "tensor", [((s + j) % planes, s) for s in range(planes)])

    def flip(v, bit):
        return lax.ppermute(v, "dp", [(i, i ^ bit) for i in range(seqs)])

    def slot_order(v, first=0, at=place):
        return [
            lax.dynamic_index_in_dim(v, (at + j) % planes, 0, keepdims=False)
            for j in range(first, planes)
        ]

    def by_slot(v):
        return jnp.stack(slot_order(lax.all_gather(v, "tensor", axis=0)))

    def to_slots(rows, whole):
        total = jnp.concatenate([rows[0], whole], axis=1)
        for j in range(1, planes):
            part = jnp.concatenate([rows[j], whole], axis=1).astype(bf16)
            total = total + lax.ppermute(
                part, "tensor", [(s, (s + j) % planes) for s in range(planes)]
            ).astype(f32)
        return total

    flat = [0, 2, 4, 6, 1, 3, 5, 7] if quick else list(range(width // CB))
    if quick:
        picks = [
            [(0, 0), (0, 1), (1, 0), (1, 1), (2, 0), (2, 1), (3, 0), (3, 1)],
            [(0, 0), (1, 0), (0, 1), (1, 1), (2, 0), (3, 0), (2, 1), (3, 1)],
        ]
    else:
        picks = [[(0, 0)]]
    half = planes // 2

    def halves(parts, more=((), ())):
        cut = ch // 2
        return [
            jnp.concatenate([v[:cut] for v in parts] + list(more[0]), axis=0),
            jnp.concatenate([v[cut:] for v in parts] + list(more[1]), axis=0),
        ]

    def pass_one(ab):
        return [flip(ab[0], 2), flip(ab[1], 4)]

    def room(ab):
        return [jnp.stack([v, jnp.zeros_like(v)]) for v in ab]

    def pass_two(ab):
        return [flip(ab[0], 4), flip(ab[1], 2)]

    def pass_core(arrays):
        return [flip(v, 1) for v in arrays]

    def as_paths(arrays, swapped):
        return [[arrays[k], arrays[k + 2], swapped[k], swapped[k + 2]] for k in range(2)]

    pick = adapter_ids[0]
    down_in = lax.dynamic_index_in_dim(adapter_in_down, pick, 0, keepdims=False)
    up_here = lax.dynamic_index_in_dim(adapter_in_up, pick, 0, keepdims=False)
    down_here = lax.dynamic_index_in_dim(adapter_out_down, pick, 0, keepdims=False)
    up_out = lax.dynamic_index_in_dim(adapter_out_up, pick, 0, keepdims=False)
    numbers = jnp.concatenate(
        [
            conv_inner,
            jnp.repeat(skip_gain, HEAD)[None],
            norm_gain[None],
            jnp.pad(jnp.stack([step_bias, decay_log]), ((0, 0), (0, ch - hs))),
        ],
        axis=0,
    )
    coarse = lax.optimization_barrier(numbers.astype(bf16))
    fine = lax.optimization_barrier((numbers - coarse.astype(f32)).astype(bf16))
    packed = jnp.concatenate(
        [jnp.transpose(up_here, (1, 0, 2)).reshape(2 * rank, ch), down_here.T, coarse, fine],
        axis=0,
    )
    packed = jnp.swapaxes(packed.reshape(64, ncb, CB), 0, 1).reshape(64 * ncb, CB)
    last_rows = tokens[0, -16:].reshape(16 * width // CB, CB)
    halo = [(s, s + 1) for s in range(planes - 1)]
    wt = jnp.transpose(in_inner, (1, 2, 0))
    maps_w = in_maps.T
    steps_w = in_steps.T
    own_rows = 3 * ch // 2
    if quick:
        own = halves(
            [wt[0], wt[1], out_weight],
            ([maps_w[:state_w], steps_w], [maps_w[state_w:]]),
        )
        got = pass_one(own)
        all_x = lax.all_gather(
            jnp.concatenate([wt[1], packed, steps_w, last_rows], axis=0), "tensor", axis=0
        )
        all_z = lax.all_gather(wt[0], "tensor", axis=0)
        all_o = lax.all_gather(out_weight, "tensor", axis=0)
        token, _, own = hold([], [], room(own), got)
        two = pass_two(own)
        swapped = pass_core(own)
        marks = [ch, ch + 64 * ncb, ch + 64 * ncb + hs]
        all_x = slot_order(all_x)
        pk = jnp.stack([v[marks[0] : marks[1]] for v in all_x])
        last_rows = all_x[planes - 1][marks[2] :]
        far_x = halves(
            [v[:ch] for v in all_x[1:]], ([v[marks[1] : marks[2]] for v in all_x[1:]], ())
        )
        wide_x = room(far_x)
        token, passed, _ = hold(wide_x + swapped + [pk, last_rows], two + far_x)
        two, far_x = passed[:2], passed[2:]
        own = own + two
        swapped = swapped + pass_core(two)
        got = pass_one(far_x)
        held = [token]
    else:
        pk = by_slot(packed)
        last_rows = by_slot(last_rows)[planes - 1]
        steps_w = by_slot(steps_w)
        held = []
    before = last_rows.reshape(16, width)
    before = jnp.where(place > 0, before, jnp.zeros_like(before))
    sc = jnp.stack([mine, lengths[0] - place * length]).astype(jnp.int32)
    normed, masked, root, low2, back2, nt, gt = turn_call(
        sc, tokens[0], before, cotangent[0], pre_gain[None], down_in, up_out, flat, quick, held
    )
    if quick:
        own = as_paths(own, swapped)
        token, _, far_x = hold([nt] + own[0] + own[1], [], wide_x, got)
        two = pass_two(far_x)
        swapped = pass_core(far_x)
        held = [token]
        all_maps, all_steps = own, own[0]
        maps_at, maps_rows = own_rows, state_w
        steps_at, mine_slots = own_rows + state_w, 1
    else:
        all_maps = [[lax.all_gather(maps_w, "dp", axis=1, tiled=True)[None]]]
        all_steps = steps_w.reshape(heads, rows_here)
        all_steps = [lax.all_gather(all_steps, "dp", axis=1, tiled=True)[None]]
        maps_at, maps_rows = 0, 2 * state_w
        steps_at, mine_slots = 0, planes
    bt, ct, b_low, c_low, cbt, maps_pre, maps_w = maps_call(
        all_maps, maps_at, maps_rows, picks, nt, conv_maps, length, held
    )
    hp, step_sig, speed, mine_w = steps_call(
        all_steps, steps_at, picks[0], nt, pk, 0, mine_slots, hs, length, held
    )
    small_w = [maps_w, mine_w]

    x_args = (picks, nt, low2, pk, ch)
    z_args = (picks, nt, low2, pk, ch, HALO, False)
    o_args = (picks, gt, back2, pk, ch, 0, True)
    if quick:
        empty = [None] * 4
        bufs, _ = scan_call(
            0, 1, (own, 1), 0, *x_args, hp, ct, b_low, cbt, empty + [None], held
        )
        sent_a = bufs[4]
        bufs, done = scan_call(
            0, 1, (own, 1), 1, *x_args, hp, ct, b_low, cbt, bufs[:4] + [None], held
        )
        sent_b = bufs[4]
        far_z = halves(slot_order(all_z, 1, place + token[0, 0].astype(jnp.int32)))
        wide_z = room(far_z)

        token, passed, _ = hold([done] + wide_z + swapped, two + far_z)
        two, far_z = passed[:2], passed[2:]
        far_x = as_paths(far_x + two, swapped + pass_core(two))
        got = pass_one(far_z)
        far_o = halves(slot_order(all_o, 1, place + token[0, 0].astype(jnp.int32)))
        wide_o = room(far_o)
        z, beside = proj_call(0, 1, (own, 0), *z_args, None, [token])
        wgt, beside = proj_call(0, 1, (own, 2), *o_args, None, [beside])

        token, far_o, far_z = hold([beside] + far_x[0] + far_x[1] + wide_o, far_o, wide_z, got)
        two = pass_two(far_z)
        swapped = pass_core(far_z)
        hp_far, sig_far, speed_far, far_w = steps_call(
            far_x[0], own_rows, picks[0], nt, pk, 1, planes, hs, length, [token]
        )
        hp = jnp.concatenate([hp, hp_far], axis=0)
        step_sig = jnp.concatenate([step_sig, sig_far], axis=0)
        speed = jnp.concatenate([speed, speed_far], axis=0)
        small_w.append(far_w)
        bufs, _ = scan_call(
            1, planes, (far_x, 0), 0, *x_args, hp, ct, b_low, cbt, bufs[:4] + [sent_a], [token]
        )
        ent_a = lax.ppermute(bufs[4], "tensor", halo)
        bufs, done = scan_call(
            1, planes, (far_x, 0), 1, *x_args, hp, ct, b_low, cbt, bufs[:4] + [sent_b], [token]
        )
        sent_b = bufs[4]
        token, passed, _ = hold([done] + swapped, two + far_o + [ent_a, sent_b])
        two, far_o, (ent_a, sent_b) = passed[:2], passed[2:4], passed[4:]
        far_z = as_paths(far_z + two, swapped + pass_core(two))
        got = pass_one(far_o)
        ent_b = lax.ppermute(sent_b, "tensor", halo)

        token, passed, far_o = hold(far_z[0] + far_z[1], [ent_a, ent_b], wide_o, got)
        ent_a, ent_b = passed
        two = pass_two(far_o)
        swapped = pass_core(far_o)
        send = hop_call(ent_a, 1, bufs[3], hp, 0, [token])
        ent_a = lax.ppermute(send, "tensor", halo)
        z, done = proj_call(1, planes, (far_z, 0), *z_args, z, [send])
        ent_b = lax.ppermute(hop_call(ent_b, 1, bufs[3], hp, 1, [done]), "tensor", halo)
        send = hop_call(ent_a, 1, bufs[3], hp, 0, [done])

        token, two, _ = hold([done, ent_b] + swapped, two + [send])
        two, send = two[:2], two[2]
        ent_a = lax.ppermute(send, "tensor", halo)
        far_o = as_paths(far_o + two, swapped + pass_core(two))
        ent_b = lax.ppermute(hop_call(ent_b, 1, bufs[3], hp, 1, [token]), "tensor", halo)
        wgt, done = proj_call(1, planes, (far_o, 0), *o_args, wgt)
        _, ent, _ = hold([done], [ent_a, ent_b])
        ent = jnp.stack(ent)
        z_sets = [((0, 1), [(own, 0)]), ((1, planes), [(far_z, 0)])]
        x_sets = [((0, 1), [(own, 1)]), ((1, planes), [(far_x, 0)])]
        o_sets = [((0, 1), [(own, 2)]), ((1, planes), [(far_o, 0)])]
    else:
        w = lax.all_gather(wt, "dp", axis=2, tiled=True)
        w = by_slot(w)
        o = lax.all_gather(out_weight, "dp", axis=1, tiled=True)
        flat_rows = lambda v: [[v.reshape(1, inner, width)]]
        wz, wx = flat_rows(w[:, 0]), flat_rows(w[:, 1])
        o = flat_rows(by_slot(o))
        bufs, _ = scan_call(
            0, planes, (wx, 0), 0, *x_args, hp, ct, b_low, cbt, [None] * 5
        )
        z, _ = proj_call(0, planes, (wz, 0), *z_args, None)
        wgt, _ = proj_call(0, planes, (o, 0), *o_args, None)
        ent = lax.ppermute(bufs[4], "tensor", halo)
        for _ in range(planes - 2):
            ent = lax.ppermute(hop_call(ent, 1, bufs[3], hp), "tensor", halo)
        ent = ent[None]
        z_sets = [((0, planes), [(wz, 0)])]
        x_sets = [((0, planes), [(wx, 0)])]
        o_sets = [((0, planes), [(o, 0)])]
    xc, mix, loc, s_end, _ = bufs
    left = [(s + 1, s) for s in range(planes - 1)]

    nout, dy, dz, sl, sl_sent = gate_call(z, mix, wgt, ent, pk, hp, ct, c_low, inner)

    adj = lax.ppermute(sl_sent, "tensor", left)
    mixed, grad_down_out, grad_up_out = output_call(
        sc, nout, pk, back2, up_out, tokens[0], masked, o_sets, picks, flat, quick
    )
    send = hop_call(adj, planes - 1, sl, hp, 0, [mixed])
    adj = lax.ppermute(send, "tensor", left)
    d_normed, grad_z = gate_back_call(dz, low2, z_sets, picks, width, [send])
    send = hop_call(adj, planes - 1, sl, hp, 0, [d_normed])
    adj = lax.ppermute(send, "tensor", left)
    for _ in range(planes - 4):
        adj = lax.ppermute(hop_call(adj, planes - 1, sl, hp), "tensor", left)
    dxs, u1, u2, kl, dcb, db1, dc1 = back_call(
        0, planes, dy, xc, hp, ent, loc, ct, c_low, bt, cbt, None, [send]
    )

    early = to_slots(
        [jnp.concatenate([grad_z[j], grad_down_out[j]], axis=1) for j in range(planes)],
        grad_up_out,
    )
    (dx, tail, head, grad_x, d_low, ddelta, u2f, kf, db3) = finish_call(
        dxs, dy, xc, dz, pk, hp, ent, adj, bt, low2, [mixed, early]
    )
    small_left, maps_tail, maps_head, grad_down = glue_call(
        [dcb, db1, db3, dc1, bt, ct, maps_pre, u1, u2, kl, ddelta, u2f, kf, step_sig, speed]
        + [conv_maps],
        sc, d_low, nt, state_w, length, heads, flat, quick,
    )

    to_left = jnp.concatenate(
        [
            head.reshape(8 * planes, ch),
            jnp.pad(maps_head, ((0, 0), (0, ch - 2 * state_w))),
            jnp.zeros((-(8 * planes + 8) % rank, ch), f32),
            jnp.pad(d_low[:, :HALO], ((0, 0), (0, ch - HALO))),
        ],
        axis=0,
    )
    near = lax.ppermute(to_left, "tensor", left)
    late = to_slots([grad_x[j] for j in range(planes)], grad_down)
    sent = jnp.concatenate(
        [
            early[:, :ch],
            late[:, :ch],
            early[:, ch : 2 * ch],
            late[:, ch:],
            early[:, 2 * ch :],
            jnp.full((rank, 128), pick).astype(f32),
        ],
        axis=1,
    ).astype(bf16)[None]
    if quick:
        _, (sent,), _ = hold([near], [sent])
        by_seq = [sent] + [flip(sent, bit) for bit in (2, 4, 6)]
    else:
        by_seq = [lax.all_gather(sent[0], "dp", axis=0)]

    tokens_grad = input_call(
        sc, dx, tail, near, pk, small_left, maps_tail, conv_maps, d_low, down_in, root,
        pre_gain[None], tokens[0], masked, d_normed, small_w, x_sets, picks, flat, quick,
    )
    if quick:
        _, by_seq, _ = hold([tokens_grad], by_seq)
        by_seq = jnp.concatenate(by_seq, axis=0)
        by_seq = [by_seq, flip(by_seq, 1)]
    g_down, g_up, g_down_out, g_up_out = assemble_call(by_seq, adapters, planes, ch, width)
    g_down = jnp.swapaxes(g_down, 1, 2)
    g_down_out = jnp.swapaxes(g_down_out, 1, 2)
    return (mixed[None], tokens_grad[None], g_down, g_up, g_down_out, g_up_out)


def solution(mesh):
    placed = (
        P("dp", "tensor", None),
        P("dp", "tensor", None),
        P("dp"),
        P("dp"),
        P(),
        P("dp", None, "tensor"),
        P("dp", None),
        P("dp", "tensor"),
        P(None, "tensor"),
        P(),
        P("tensor"),
        P("tensor"),
        P("tensor"),
        P("tensor"),
        P("tensor", "dp"),
        P(),
        P(None, None, None, "tensor"),
        P(None, "tensor", None),
        P(),
    )
    return jax.shard_map(
        body,
        mesh=mesh,
        in_specs=placed,
        out_specs=(
            P("dp", "tensor", None),
            P("dp", "tensor", None),
            P(),
            P(None, None, None, "tensor"),
            P(None, "tensor", None),
            P(),
        ),
        check_vma=False,
    )
```

```python
import functools

import jax
import jax.numpy as jnp
from jax import lax
from jax.experimental import pallas as pl
from jax.experimental.pallas import tpu as pltpu
from jax.sharding import PartitionSpec as P

f32 = jnp.float32
bf16 = jnp.bfloat16
epsilon = 1e-05
highest = lax.Precision.HIGHEST
LOG2E = 1.4426950408889634
HEAD = 64
HALO = 128
SUB = 256
CB = 256
ROWS = 32

NN = ((1,), (0,))
NT = ((1,), (1,))
TN = ((0,), (0,))


def dot(a, b, dims=NN):
    return lax.dot_general(a, b, (dims, ((), ())), preferred_element_type=f32)


def compiler_params(grid_rank):
    return pltpu.CompilerParams(
        dimension_semantics=("arbitrary",) * grid_rank, vmem_limit_bytes=60 * 2**20
    )


def cost(flops, size):
    return pl.CostEstimate(
        flops=int(flops) // 8, bytes_accessed=int(size) // 8, transcendentals=0
    )


def kind_rows(packed, b, kind):
    return packed.at[pl.ds(pl.multiple_of(b * 64 + kind * 16, 16), 16)]


def block_rows(ref, b):
    return ref.at[pl.ds(pl.multiple_of(b * CB, CB), CB)]


def sigmoid(v):
    return 0.5 + 0.5 * jnp.tanh(0.5 * v)


def columns(numbers):
    v = numbers[...].astype(f32)
    return jnp.transpose(v[:8] + v[8:])


def spread(numbers, which):
    row = lax.broadcasted_iota(jnp.int32, (16, 128 * len(which)), 0) % 8
    col = lax.broadcasted_iota(jnp.int32, (16, 128 * len(which)), 1) // 128
    pick = jnp.zeros(row.shape, f32)
    for k, n in enumerate(which):
        pick = jnp.where((row == n) & (col == k), 1.0, pick)
    return dot(numbers[...], pick.astype(bf16), TN)


def lanes_of(values, width):
    return jnp.concatenate([values] * (width // 128), axis=1)


def tall(rows):
    return jnp.transpose(jnp.concatenate([rows, rows], axis=0))


def conv_values(raw, chan):
    out = raw * chan[:, 3:4]
    for k in range(3):
        out = out + pltpu.roll(raw, 3 - k, 1) * chan[:, k : k + 1]
    return out[:, HALO:]


def conv_rows(raw, taps, shift):
    width = raw.shape[1]
    out = raw * lanes_of(taps[3], width)
    for k in range(3):
        out = out + pltpu.roll(raw, shift(k), 1) * lanes_of(taps[k], width)
    return out


def per_head(values, rows):
    hb = rows.shape[0]
    parts = [values[h * HEAD : (h + 1) * HEAD] * rows[h : h + 1] for h in range(hb)]
    return jnp.concatenate(parts, axis=0)


def head_sums(values, hb):
    parts = [
        jnp.sum(values[h * HEAD : (h + 1) * HEAD], axis=0, keepdims=True) for h in range(hb)
    ]
    return jnp.concatenate(parts, axis=0)


def joined(refs, picks, rows=slice(None)):
    parts = [refs[k][b, rows] for k, b in picks]
    return parts[0] if len(parts) == 1 else jnp.concatenate(parts, axis=1)


def block_at(mine, m, quick):
    return pl.multiple_of((mine ^ m) * CB, CB) if quick else m * CB


def turn_kernel(flat, quick, *refs):
    (sc, tok_r, bef_r, cot_r, gain, down, up) = refs[:7]
    normed_o, masked_o, root_o, low_o, back_o, nt_o, gt_o, halo_sc = refs[-8:]
    width = tok_r.shape[1]
    length = tok_r.shape[0]

    def norm(v):
        v = v.astype(f32)
        root = lax.rsqrt(jnp.sum(v * v, axis=1, keepdims=True) * (1.0 / width) + epsilon)
        return (v * root * gain[...]).astype(bf16), root

    normed, root = norm(tok_r[...])
    normed_o[...] = normed
    root_o[...] = root
    halo_sc[...] = jnp.zeros_like(halo_sc)
    halo_sc[HALO - 16 :, :] = norm(bef_r[...])[0]
    rows = lax.broadcasted_iota(jnp.int32, (length, 1), 0)
    masked_o[...] = jnp.where(rows < sc[1], cot_r[...].astype(f32), 0.0).astype(bf16)
    low = back = None
    for i, m in enumerate(flat):
        at = pl.ds(block_at(sc[0], m, quick), CB)
        nt = jnp.concatenate(
            [jnp.transpose(halo_sc[:, at]), jnp.transpose(normed_o[:, at])], axis=1
        )
        gt = jnp.transpose(masked_o[:, at])
        nt_o[i * CB : (i + 1) * CB, :] = nt
        gt_o[i * CB : (i + 1) * CB, :] = gt
        low_m = dot(down[at, :], nt, TN)
        back_m = dot(up[:, at], gt)
        low = low_m if low is None else low + low_m
        back = back_m if back is None else back + back_m
    low_o[...] = low.astype(bf16)
    back_o[...] = back.astype(bf16)


def turn_call(sc, tokens, before, cot, gain, down, up, flat, quick, later):
    length, width = tokens.shape
    rank = up.shape[0]
    ext = length + HALO
    vm = pl.BlockSpec(memory_space=pltpu.VMEM)
    return pl.pallas_call(
        functools.partial(turn_kernel, flat, quick),
        in_specs=[pl.BlockSpec(memory_space=pltpu.SMEM)] + [vm] * 6
        + [pl.BlockSpec(memory_space=pl.ANY)] * len(later),
        out_specs=[vm] * 7,
        out_shape=[
            jax.ShapeDtypeStruct((length, width), bf16),
            jax.ShapeDtypeStruct((length, width), bf16),
            jax.ShapeDtypeStruct((length, 1), f32),
            jax.ShapeDtypeStruct((rank, ext), bf16),
            jax.ShapeDtypeStruct((rank, length), bf16),
            jax.ShapeDtypeStruct((width, ext), bf16),
            jax.ShapeDtypeStruct((width, length), bf16),
        ],
        scratch_shapes=[pltpu.VMEM((HALO, width), bf16)],
        compiler_params=compiler_params(0),
        cost_estimate=cost(length * width * 200, length * width * 16),
        name="turn",
    )(sc, tokens, before, cot, gain, down, up, *later)


def row_specs(paths, first, rows):
    ops, specs = [], []
    for arrays in paths:
        for a in arrays:
            ops.append(a)
            specs.append(
                pl.BlockSpec((a.shape[0], rows, a.shape[2]), lambda i: (0, first // rows, 0))
            )
    return ops, specs


def maps_kernel(n_w, picks, sub, *refs):
    nt, taps = refs[n_w : n_w + 2]
    bt_o, ct_o, bn_o, cn_o, cbt_o, pre_o, w_o = refs[-7:]
    length = bt_o.shape[1]
    state_w = bt_o.shape[0]
    per = n_w // len(picks)
    w = jnp.concatenate(
        [joined(refs[p * per : (p + 1) * per], order) for p, order in enumerate(picks)], axis=0
    )
    w_o[...] = w
    maps_pre = conv_values(dot(w, nt[...]), tall(taps[...]))
    pre_o[...] = maps_pre
    maps = (maps_pre * sigmoid(maps_pre)).astype(bf16)
    bt, ct = maps[:state_w], maps[state_w:]
    bt_o[...] = bt
    ct_o[...] = ct
    bn = jnp.transpose(bt)
    bn_o[...] = bn
    cn_o[...] = jnp.transpose(ct)
    row = lax.broadcasted_iota(jnp.int32, (sub, sub), 0)
    col = lax.broadcasted_iota(jnp.int32, (sub, sub), 1)
    upto = jnp.where(row <= col, 1.0, 0.0)
    for s in range(length // sub):
        cols = slice(s * sub, (s + 1) * sub)
        cbt_o[s] = upto * dot(bn[cols, :], ct[:, cols])


def maps_call(paths, first, rows, picks, nt, taps, length, later):
    ops, specs = row_specs(paths, first, rows)
    state_w = rows * len(picks) // 2
    vm = pl.BlockSpec(memory_space=pltpu.VMEM)
    n_w = len(ops)
    return pl.pallas_call(
        functools.partial(maps_kernel, n_w, picks, SUB),
        grid=(1,),
        in_specs=specs + [vm, vm] + [pl.BlockSpec(memory_space=pl.ANY)] * len(later),
        out_specs=[vm] * 7,
        out_shape=[
            jax.ShapeDtypeStruct((state_w, length), bf16),
            jax.ShapeDtypeStruct((state_w, length), bf16),
            jax.ShapeDtypeStruct((length, state_w), bf16),
            jax.ShapeDtypeStruct((length, state_w), bf16),
            jax.ShapeDtypeStruct((length // SUB, SUB, SUB), f32),
            jax.ShapeDtypeStruct((2 * state_w, length), f32),
            jax.ShapeDtypeStruct((2 * state_w, nt.shape[0]), bf16),
        ],
        compiler_params=compiler_params(1),
        cost_estimate=cost(nt.shape[0] * nt.shape[1] * 512, nt.size * 2 + nt.shape[0] * 1024),
        name="maps",
    )(*ops, nt, taps, *later)


def steps_kernel(n_w, order, hb, sub, lo, hi, hs, *refs):
    nt, numbers = refs[n_w : n_w + 2]
    hp_o, sig_o, speed_o, w_o = refs[-4:]
    length = sig_o.shape[1]
    heads = sig_o.shape[0]
    w = joined(refs[:n_w], order)
    w_o[...] = w
    cols = [columns(numbers.at[j])[:hs] for j in range(lo, hi)]
    bias = jnp.concatenate([v[:, 6:7] for v in cols], axis=0)
    speed = jnp.exp(jnp.concatenate([v[:, 7:8] for v in cols], axis=0))
    speed_o[...] = jnp.broadcast_to(speed, (heads, 128))
    steps = dot(w, nt[:, HALO:]) + bias
    sig_o[...] = sigmoid(steps)
    delta = jnp.maximum(steps, 0.0) + jnp.log1p(jnp.exp(-jnp.abs(steps)))
    rates = -delta * speed
    row = lax.broadcasted_iota(jnp.int32, (sub, sub), 0)
    col = lax.broadcasted_iota(jnp.int32, (sub, sub), 1)
    upto = jnp.where(row <= col, 1.0, 0.0)
    before = None
    for s in range(length // sub):
        cols = slice(s * sub, (s + 1) * sub)
        cum = (
            lax.dot_general(
                rates[:, cols], upto, (NN, ((), ())), precision=highest,
                preferred_element_type=f32,
            )
            * LOG2E
        )
        cum_all = cum if before is None else cum + before
        before = cum_all[:, sub - 1 : sub]
        for b in range(heads // hb):
            mine = slice(b * hb, (b + 1) * hb)
            hp_o[b, :hb, cols] = cum[mine]
            hp_o[b, hb : 2 * hb, cols] = cum_all[mine]
            hp_o[b, 2 * hb :, cols] = delta[mine, cols]


def steps_call(arrays, first, order, nt, pk, lo, hi, hs, length, later):
    heads = (hi - lo) * hs
    hb = CB // HEAD
    ops, specs = row_specs([arrays], first, heads)
    vm = pl.BlockSpec(memory_space=pltpu.VMEM)
    return pl.pallas_call(
        functools.partial(steps_kernel, len(ops), order, hb, SUB, lo, hi, hs),
        grid=(1,),
        in_specs=specs
        + [vm, pl.BlockSpec((pk.shape[0], 16, CB), lambda i: (0, 3, 0))]
        + [pl.BlockSpec(memory_space=pl.ANY)] * len(later),
        out_specs=[vm] * 4,
        out_shape=[
            jax.ShapeDtypeStruct((heads // hb, 3 * hb, length), f32),
            jax.ShapeDtypeStruct((heads, length), f32),
            jax.ShapeDtypeStruct((heads, 128), f32),
            jax.ShapeDtypeStruct((heads, nt.shape[0]), bf16),
        ],
        compiler_params=compiler_params(1),
        cost_estimate=cost(nt.shape[0] * nt.shape[1] * 128, nt.size * 2),
        name="steps",
    )(*ops, nt, pk, *later)


def hop_kernel(hb, got, own, hp, *rest):
    out = rest[-1]
    length = hp.shape[2]
    for c in range(hp.shape[0]):
        rows = slice(c * CB, (c + 1) * CB)
        total = jnp.exp2(hp[c, hb : 2 * hb, length - 1 : length])
        out[rows, :] = (per_head(got[rows, :].astype(f32), total) + own[rows, :]).astype(bf16)


def hop_call(got, shift, own, hp, part=0, later=()):
    slots, rows, state_w = got.shape
    parts = own.shape[1] // rows
    return pl.pallas_call(
        functools.partial(hop_kernel, CB // HEAD),
        grid=(slots,),
        in_specs=[
            pl.BlockSpec((None, rows, state_w), lambda s: ((s + shift) % slots, 0, 0)),
            pl.BlockSpec((None, rows, state_w), lambda s: (s, part, 0)),
            pl.BlockSpec((rows // CB,) + hp.shape[1:], lambda s: (s * parts + part, 0, 0)),
        ]
        + [pl.BlockSpec(memory_space=pl.ANY)] * len(later),
        out_specs=pl.BlockSpec((None, rows, state_w), lambda s: (s, 0, 0)),
        out_shape=jax.ShapeDtypeStruct((slots, rows, state_w), bf16),
        compiler_params=compiler_params(1),
        cost_estimate=cost(got.size * 4, got.size * 8),
        name="hop",
    )(got, own, hp, *later)


def hold_kernel(n_joined, *refs):
    outs = refs[-1 - n_joined :]
    for k in range(n_joined):
        outs[k][0] = refs[2 * k][...]
        outs[k][1] = refs[2 * k + 1][...]
    outs[-1][...] = jnp.zeros((1, 1), bf16)


def hold(deps, passed=(), pairs=()):
    anywhere = pl.BlockSpec(memory_space=pl.ANY)
    deps, passed, pairs = list(deps), list(passed), list(pairs)
    parts = [v for pair in pairs for v in pair]
    whole = lambda shape: pl.BlockSpec(shape, lambda i: (0,) * len(shape))
    first = len(parts) + len(deps)
    joined_shapes = [(2,) + pair[0].shape for pair in pairs]
    out = pl.pallas_call(
        functools.partial(hold_kernel, len(joined_shapes)),
        grid=(1,),
        in_specs=[whole(a.shape) for a in parts] + [anywhere] * (len(deps) + len(passed)),
        out_specs=[anywhere] * len(passed) + [whole(v) for v in joined_shapes] + [whole((1, 1))],
        out_shape=[jax.ShapeDtypeStruct(v.shape, v.dtype) for v in passed]
        + [jax.ShapeDtypeStruct(v, bf16) for v in joined_shapes]
        + [jax.ShapeDtypeStruct((1, 1), bf16)],
        input_output_aliases={first + k: k for k in range(len(passed))},
        compiler_params=compiler_params(1),
        cost_estimate=cost(8, 8),
        name="hold",
    )(*parts, *deps, *passed)
    n = len(passed)
    return out[-1], list(out[:n]), list(out[n:-1])


def decay_weights(out, cum, col, cbt, s, then=None):
    sub = out.shape[0]
    for r in range(0, sub, ROWS):
        part = slice(r, r + ROWS)
        first = r // 128 * 128
        decay = jnp.exp2(jnp.minimum(cum[:, first:] - col[part], 0.0))
        out[part, first:] = (decay * cbt[s, part, first:]).astype(bf16)
        if then is not None:
            then(part, first, decay)


def scan_kernel(nx, order, hb, sub, *refs):
    xrefs = refs[:nx]
    (nt, low, pk, hp_r, ct, bn, cbt) = refs[nx : nx + 7]
    xc_all, mix_all, ent_all, st_all, sent_all, tok_out = refs[-12:-6]
    raw_sc, x_sc, xs_sc, turn_sc, w_sc, tap_sc = refs[-6:]
    tok_out[...] = jnp.zeros_like(tok_out)
    length = ct.shape[1]
    w_sc[...] = jnp.zeros_like(w_sc)

    @pl.loop(0, xc_all.shape[0] // CB)
    def _(b):
        rows = pl.ds(pl.multiple_of(b * CB, CB), CB)
        mix_out = block_rows(mix_all, b)
        tap_sc[...] = spread(kind_rows(pk, b, 3), range(5))
        hp = hp_r[b]
        raw_sc[...] = dot(joined(xrefs, order, rows), nt[...]) + dot(
            kind_rows(pk, b, 1)[...], low[...], TN
        )
        for r in range(0, CB, ROWS):
            part = slice(r, r + ROWS)
            h = r // HEAD
            taps = [tap_sc[part, k * 128 : (k + 1) * 128] for k in range(4)]
            xc = conv_rows(raw_sc[part, :], taps, lambda k: 3 - k)[:, HALO:]
            xc_all[pl.ds(pl.multiple_of(b * CB + r, ROWS), ROWS), :] = xc.astype(bf16)
            x = xc * sigmoid(xc)
            x_sc[part, :] = x
            xs_sc[part, :] = (x * hp[2 * hb + h : 2 * hb + h + 1]).astype(bf16)
        state = None
        for s in range(length // sub):
            cols = slice(s * sub, (s + 1) * sub)
            cum = hp[:hb, cols]
            rows_n = jnp.transpose(jnp.concatenate([cum, cum], axis=0))
            last = cum[:, sub - 1 : sub]
            ends = jnp.exp2(last - cum)
            add = dot(per_head(xs_sc[:, cols].astype(f32), ends).astype(bf16), bn[cols, :])
            if s > 0:
                ent_all[s - 1, rows, :] = state
                grown = jnp.exp2(cum)
                turn_sc[...] = dot(state.astype(bf16), ct[:, cols])
            for h in range(hb):
                mine = slice(h * HEAD, (h + 1) * HEAD)
                decay_weights(w_sc, cum[h : h + 1], rows_n[:, h : h + 1], cbt, s)
                y = dot(xs_sc[mine, cols], w_sc[...])
                y = y + x_sc[mine, cols] * lanes_of(tap_sc[mine, 512:640], sub)
                if s > 0:
                    y = y + turn_sc[mine, :] * grown[h : h + 1]
                mix_out[mine, cols] = y
            state = add if state is None else per_head(state, jnp.exp2(last)) + add
        if length // sub == 1:
            ent_all[0, rows, :] = state
        st_all[rows, :] = state
        sent_all[rows, :] = state.astype(bf16)


def scan_call(lo, hi, xw, part, picks, nt, low, pk, ch, hp, ct, bn, cbt, bufs, later=()):
    slots = pk.shape[0]
    length = ct.shape[1]
    hb = CB // HEAD
    paths, base = xw
    n_paths = len(paths)
    per = ch // CB // n_paths
    width = per * CB
    nsub = length // SUB
    full = lambda a: pl.BlockSpec(a.shape, lambda s: (0,) * a.ndim)
    per_chan = lambda w: pl.BlockSpec((None, width, w), lambda s: (s + lo, part, 0))
    ops = list(paths[part])
    specs = [
        pl.BlockSpec((a.shape[0], width, a.shape[2]), lambda s: (0, s + base, 0)) for a in ops
    ]
    nx = len(ops)
    ops += [nt, low, pk, hp, ct, bn, cbt]
    specs += [full(nt), full(low)]
    specs += [pl.BlockSpec((None, per * 64, CB), lambda s: (s + lo, part, 0))]
    specs += [
        pl.BlockSpec((per,) + hp.shape[1:], lambda s: ((s + lo) * n_paths + part, 0, 0)),
        full(ct), full(bn), full(cbt),
    ]
    inner_states = max(nsub - 1, 1)
    shapes = [
        jax.ShapeDtypeStruct((slots, ch, length), bf16),
        jax.ShapeDtypeStruct((slots, ch, length), f32),
        jax.ShapeDtypeStruct((slots, inner_states, ch, 128), f32),
        jax.ShapeDtypeStruct((slots, ch, 128), f32),
        jax.ShapeDtypeStruct((slots, width, 128), bf16),
        jax.ShapeDtypeStruct((1, 1), bf16),
    ]
    outs = [
        per_chan(length),
        per_chan(length),
        pl.BlockSpec((None, inner_states, width, 128), lambda s: (s + lo, 0, part, 0)),
        per_chan(128),
        pl.BlockSpec((None, width, 128), lambda s: (s + lo, 0, 0)),
        pl.BlockSpec((1, 1), lambda s: (0, 0)),
    ]
    given = [v for v in bufs if v is not None]
    aliases = {len(ops) + i: k for i, k in enumerate(k for k in range(5) if bufs[k] is not None)}
    ops += given + list(later)
    specs += [pl.BlockSpec(memory_space=pl.ANY)] * (len(given) + len(later))
    n = hi - lo
    out = pl.pallas_call(
        functools.partial(scan_kernel, nx, picks[part], hb, SUB),
        grid=(n,),
        in_specs=specs,
        out_specs=outs,
        out_shape=shapes,
        scratch_shapes=[
            pltpu.VMEM((CB, HALO + length), f32),
            pltpu.VMEM((CB, length), f32),
            pltpu.VMEM((CB, length), bf16),
            pltpu.VMEM((CB, SUB), f32),
            pltpu.VMEM((SUB, SUB), bf16),
            pltpu.VMEM((CB, 640), f32),
        ],
        input_output_aliases=aliases,
        compiler_params=compiler_params(1),
        cost_estimate=cost(
            4 * n * per * CB * 2048 * length, n * per * CB * (4096 + length * 8)
        ),
        name="scan_slots",
    )(*ops)
    return list(out[:5]), out[5]


def proj_kernel(picks, n, cut, gain, *refs):
    (right, low, pk) = refs[n : n + 3]
    out, tok_o = refs[-2:]
    tok_o[...] = jnp.zeros_like(tok_o)
    per = n // len(picks)
    blocks = out.shape[0] // CB // len(picks)
    for p, order in enumerate(picks):
        mine = refs[p * per : (p + 1) * per]
        for k in range(blocks):
            b = p * blocks + k
            value = dot(joined(mine, order, slice(k * CB, (k + 1) * CB)), right[:, cut:])
            value = value + dot(kind_rows(pk, b, 2 if gain else 0)[...], low[:, cut:], TN)
            if gain:
                value = value * lanes_of(spread(kind_rows(pk, b, 3), [5]), value.shape[1])
            out[b * CB : (b + 1) * CB, :] = value.astype(bf16)


def proj_call(lo, hi, weight, picks, right, low, pk, ch, cut, gain, buf, later=()):
    slots = pk.shape[0]
    length = right.shape[1] - cut
    paths, base = weight
    share = ch // len(paths)
    full = lambda a: pl.BlockSpec(a.shape, lambda s: (0,) * a.ndim)
    ops = [a for arrays in paths for a in arrays]
    specs = [
        pl.BlockSpec((a.shape[0], share, a.shape[2]), lambda s: (0, s + base, 0)) for a in ops
    ]
    n_w = len(ops)
    ops += [right, low, pk]
    specs += [full(right), full(low)]
    specs += [pl.BlockSpec((None, ch // 4, CB), lambda s: (s + lo, 0, 0))]
    aliases = {}
    if buf is not None:
        aliases = {len(ops): 0}
        ops.append(buf)
        specs.append(pl.BlockSpec(memory_space=pl.ANY))
    ops += list(later)
    specs += [pl.BlockSpec(memory_space=pl.ANY)] * len(later)
    n = hi - lo
    return pl.pallas_call(
        functools.partial(proj_kernel, picks, n_w, cut, gain),
        grid=(n,),
        in_specs=specs,
        out_specs=[
            pl.BlockSpec((None, ch, length), lambda s: (s + lo, 0, 0)),
            pl.BlockSpec((1, 1), lambda s: (0, 0)),
        ],
        out_shape=[
            jax.ShapeDtypeStruct((slots, ch, length), bf16),
            jax.ShapeDtypeStruct((1, 1), bf16),
        ],
        input_output_aliases=aliases,
        compiler_params=compiler_params(1),
        cost_estimate=cost(2 * n * ch * 2048 * length, n * ch * (4096 + length * 2)),
        name="proj_slots",
    )(*ops)


def fold(values):
    total = values[:8]
    for r in range(8, values.shape[0], 8):
        total = total + values[r : r + 8]
    return total


def gate_kernel(hb, inner, *refs):
    (z_all, mix_all, wgt_all, ent_all, pk, hp_r, ct, cn) = refs[:8]
    nout_all, dmix_all, dz_all, sl_all, sent_all = refs[8:13]
    mix_sc, turn_sc, sq_sc, dot_sc, gain_sc = refs[13:]
    phase, slot = pl.program_id(0), pl.program_id(1)
    blocks = z_all.shape[0] // CB
    per = ent_all.shape[1] // CB

    def gates(ref, rows):
        z = ref[rows, :].astype(f32)
        sig = sigmoid(z)
        return sig, z * sig

    @pl.when((phase == 0) & (slot == 0))
    def _():
        sq_sc[...] = jnp.zeros_like(sq_sc)
        dot_sc[...] = jnp.zeros_like(dot_sc)

    @pl.when(phase == 0)
    def _():
        @pl.loop(0, blocks)
        def _(b):
            z_r, mix_r, wgt_r = [block_rows(v, b) for v in (z_all, mix_all, wgt_all)]
            cum = jnp.exp2(hp_r[b, hb : 2 * hb])
            ent = ent_all[b // per, pl.ds(pl.multiple_of(b % per * CB, CB), CB), :]
            turn_sc[...] = dot(ent, ct[...])
            sq, dots = sq_sc[...], dot_sc[...]
            for r in range(0, CB, ROWS):
                rows = slice(r, r + ROWS)
                h = r // HEAD
                _, silu = gates(z_r, rows)
                mix = mix_r[rows, :] + turn_sc[rows, :] * cum[h : h + 1]
                mix_sc[slot * blocks + b, rows, :] = mix
                gated = mix * silu
                sq = sq + fold(gated * gated)
                dots = dots + fold(gated * wgt_r[rows, :].astype(f32))
            sq_sc[...] = sq
            dot_sc[...] = dots

    @pl.when(phase == 1)
    def _():
        r_all = lax.rsqrt(jnp.sum(sq_sc[...], axis=0, keepdims=True) * (1.0 / inner) + epsilon)
        coef = r_all * r_all * r_all * (
            jnp.sum(dot_sc[...], axis=0, keepdims=True) * (1.0 / inner)
        )

        @pl.loop(0, blocks)
        def _(b):
            z_r, wgt_r = block_rows(z_all, b), block_rows(wgt_all, b)
            nout_o, dmix_o, dz_o = [block_rows(v, b) for v in (nout_all, dmix_all, dz_all)]
            cum = jnp.exp2(hp_r[b, hb : 2 * hb])
            gain_sc[...] = spread(kind_rows(pk, b, 3), [5])
            for r in range(0, CB, ROWS):
                rows = slice(r, r + ROWS)
                h = r // HEAD
                sig, silu = gates(z_r, rows)
                mix = mix_sc[slot * blocks + b, rows, :]
                gated = mix * silu
                gain = lanes_of(gain_sc[rows, :], gated.shape[1])
                nout_o[rows, :] = (gated * r_all * gain).astype(bf16)
                d_gated = r_all * wgt_r[rows, :].astype(f32) - gated * coef
                d_mix = d_gated * silu
                dmix_o[rows, :] = d_mix.astype(bf16)
                dz_o[rows, :] = (d_gated * mix * (sig + silu * (1.0 - sig))).astype(bf16)
                turn_sc[rows, :] = d_mix * cum[h : h + 1]
            adj = dot(turn_sc[...].astype(bf16), cn[...])
            here = pl.ds(pl.multiple_of(b * CB, CB), CB)
            sl_all[here, :] = adj
            sent_all[here, :] = adj.astype(bf16)


def gate_call(z, mix, wgt, ent, pk, hp, ct, cn, inner):
    slots, ch, length = mix.shape
    ncb = ch // CB
    hb = CB // HEAD
    full = lambda a: pl.BlockSpec(a.shape, lambda p, s: (0,) * a.ndim)
    per_chan = lambda a: pl.BlockSpec((None, ch, a.shape[2]), lambda p, s: (s, 0, 0))
    held = lambda p, s: jnp.where(p == 0, s, slots - 1)
    later = lambda w: pl.BlockSpec((None, ch, w), lambda p, s: (jnp.where(p == 1, s, 0), 0, 0))
    return pl.pallas_call(
        functools.partial(gate_kernel, hb, inner),
        grid=(2, slots),
        in_specs=[
            per_chan(z),
            pl.BlockSpec((None, ch, length), lambda p, s: (held(p, s), 0, 0)),
            per_chan(wgt),
            pl.BlockSpec(
                (ent.shape[0], None) + ent.shape[2:],
                lambda p, s: (0, (held(p, s) + 1) % slots, 0, 0),
            ),
            pl.BlockSpec((None, ch // 4, CB), lambda p, s: (s, 0, 0)),
            pl.BlockSpec((ncb,) + hp.shape[1:], lambda p, s: (s, 0, 0)),
            full(ct),
            full(cn),
        ],
        out_specs=[later(length), later(length), later(length), later(128), later(128)],
        out_shape=[
            jax.ShapeDtypeStruct((slots, ch, length), bf16),
            jax.ShapeDtypeStruct((slots, ch, length), bf16),
            jax.ShapeDtypeStruct((slots, ch, length), bf16),
            jax.ShapeDtypeStruct((slots, ch, 128), f32),
            jax.ShapeDtypeStruct((slots, ch, 128), bf16),
        ],
        scratch_shapes=[
            pltpu.VMEM((slots * ncb, CB, length), f32),
            pltpu.VMEM((CB, length), f32),
            pltpu.VMEM((8, length), f32),
            pltpu.VMEM((8, length), f32),
            pltpu.VMEM((CB, 128), f32),
        ],
        compiler_params=compiler_params(2),
        cost_estimate=cost(slots * ch * length * 600, slots * ch * length * 22),
        name="gate",
    )(z, mix, wgt, ent, pk, hp, ct, cn)


def back_kernel(hb, sub, *refs):
    (dy_all, xc_all, hp_r, ent_all, loc_all, ct, cn, bt, cbt) = refs[:9]
    dxs_all, u1_all, u2_all, kl_all, dcb_o, db_o, dc_o = refs[-12:-5]
    xs_sc, turn_sc, dxi_sc, dm_sc, w_sc = refs[-5:]
    w_sc[...] = jnp.zeros_like(w_sc)
    length = ct.shape[1]
    nsub = length // sub
    per = ent_all.shape[1] // CB

    @pl.when(pl.program_id(0) == 0)
    def _():
        dcb_o[...] = jnp.zeros_like(dcb_o)
        db_o[...] = jnp.zeros_like(db_o)
        dc_o[...] = jnp.zeros_like(dc_o)

    @pl.loop(0, dy_all.shape[0] // CB)
    def _(b):
        rows = pl.ds(pl.multiple_of(b * CB, CB), CB)
        dy_r, dxs_o = block_rows(dy_all, b), block_rows(dxs_all, b)
        u1_o, u2_o, kl_o = u1_all.at[b], u2_all.at[b], kl_all.at[b]
        hp = hp_r[b]
        for r in range(0, CB, ROWS):
            part = slice(r, r + ROWS)
            h = r // HEAD
            xc = xc_all[pl.ds(pl.multiple_of(b * CB + r, ROWS), ROWS), :].astype(f32)
            x = xc * sigmoid(xc)
            xs_sc[part, :] = (x * hp[2 * hb + h : 2 * hb + h + 1]).astype(bf16)
        adj = None
        kl = []
        for s in reversed(range(nsub)):
            cols = slice(s * sub, (s + 1) * sub)
            cum = hp[:hb, cols]
            rows_n = jnp.transpose(jnp.concatenate([cum, cum], axis=0))
            ecum = jnp.exp2(cum)
            last = cum[:, sub - 1 : sub]
            ends = jnp.exp2(last - cum)
            ent = ent_all[b // per, pl.ds(pl.multiple_of(b % per * CB, CB), CB), :]
            state = ent.astype(f32)
            if s > 0:
                before = hp[hb : 2 * hb, s * sub - 1 : s * sub]
                state = loc_all[s - 1, rows, :] + per_head(state, jnp.exp2(before))
            state_low = state.astype(bf16)
            turn_sc[...] = dot(state_low, ct[:, cols])
            ed = per_head(dy_r[:, cols].astype(f32), ecum).astype(bf16)
            dc_o[:, cols] += dot(state_low, ed, TN)
            add = dot(ed, cn[cols, :])
            if adj is not None:
                adj_low = adj.astype(bf16)
                dxi_sc[...] = dot(adj_low, bt[:, cols])
                db_o[:, cols] += dot(
                    adj_low, per_head(xs_sc[:, cols].astype(f32), ends).astype(bf16), TN
                )
            u1, u2 = [], []
            for h in range(hb):
                mine = slice(h * HEAD, (h + 1) * HEAD)
                dy_low, xs_low = dy_r[mine, cols], xs_sc[mine, cols]
                dm_sc[...] = dot(xs_low, dy_low, TN)

                def gather(part, first, decay):
                    dcb_o[s, part, first:] += decay * dm_sc[part, first:]

                decay_weights(w_sc, cum[h : h + 1], rows_n[:, h : h + 1], cbt, s, gather)
                xs = xs_low.astype(f32)
                y = dot(xs_low, w_sc[...]) + turn_sc[mine, :] * ecum[h : h + 1]
                dxs = dot(dy_low, w_sc[...], NT)
                u1.append(
                    jnp.sum(dy_low.astype(f32) * y - xs * dxs, axis=0, keepdims=True)
                )
                if adj is not None:
                    dxi = dxi_sc[mine, :] * ends[h : h + 1]
                    u2.append(jnp.sum(xs * dxi, axis=0, keepdims=True))
                    dxs = dxs + dxi
                dxs_o[mine, cols] = dxs
            u1_o[:, cols] = jnp.concatenate(u1, axis=0)
            if adj is None:
                u2_o[:, cols] = jnp.zeros((hb, sub), f32)
                kl.append(jnp.zeros((hb, 128), f32))
                adj = add
            else:
                u2_o[:, cols] = jnp.concatenate(u2, axis=0)
                kl.append(head_sums(adj * state, hb) * jnp.exp2(last))
                adj = per_head(adj, jnp.exp2(last)) + add
        for s in range(nsub):
            kl_o[:, s * 128 : (s + 1) * 128] = kl[nsub - 1 - s]


def back_call(dy, xc, hp, ent, loc, ct, cn, bt, cbt, later=()):
    slots, ch, length = dy.shape
    ncb = ch // CB
    hb = CB // HEAD
    nsub = length // SUB
    full = lambda a: pl.BlockSpec(a.shape, lambda s: (0,) * a.ndim)
    per_chan = lambda w: pl.BlockSpec((None, ch, w), lambda s: (s, 0, 0))
    blk_out = lambda w: pl.BlockSpec((ncb, hb, w), lambda s: (s, 0, 0))
    blocks = slots * ncb
    return pl.pallas_call(
        functools.partial(back_kernel, hb, SUB),
        grid=(slots,),
        in_specs=[
            per_chan(length),
            per_chan(length),
            pl.BlockSpec((ncb,) + hp.shape[1:], lambda s: (s, 0, 0)),
            pl.BlockSpec(
                (ent.shape[0], None) + ent.shape[2:], lambda s: (0, (s + 1) % slots, 0, 0)
            ),
            pl.BlockSpec((None,) + loc.shape[1:], lambda s: (s, 0, 0, 0)),
            full(ct),
            full(cn),
            full(bt),
            full(cbt),
        ]
        + [pl.BlockSpec(memory_space=pl.ANY)] * len(later),
        out_specs=[
            per_chan(length),
            blk_out(length),
            blk_out(length),
            blk_out(128 * nsub),
            pl.BlockSpec((nsub, SUB, SUB), lambda s: (0, 0, 0)),
            pl.BlockSpec((128, length), lambda s: (0, 0)),
            pl.BlockSpec((128, length), lambda s: (0, 0)),
        ],
        out_shape=[
            jax.ShapeDtypeStruct((slots, ch, length), f32),
            jax.ShapeDtypeStruct((blocks, hb, length), f32),
            jax.ShapeDtypeStruct((blocks, hb, length), f32),
            jax.ShapeDtypeStruct((blocks, hb, 128 * nsub), f32),
            jax.ShapeDtypeStruct((nsub, SUB, SUB), f32),
            jax.ShapeDtypeStruct((128, length), f32),
            jax.ShapeDtypeStruct((128, length), f32),
        ],
        scratch_shapes=[
            pltpu.VMEM((CB, length), bf16),
            pltpu.VMEM((CB, SUB), f32),
            pltpu.VMEM((CB, SUB), f32),
            pltpu.VMEM((SUB, SUB), f32),
            pltpu.VMEM((SUB, SUB), bf16),
        ],
        compiler_params=compiler_params(1),
        cost_estimate=cost(slots * ch * length * SUB * 20, slots * ch * length * 8),
        name="state_back",
    )(dy, xc, hp, ent, loc, ct, cn, bt, cbt, *later)


def finish_kernel(hb, *refs):
    (dxs_all, dy_all, xc_all, dz_all, pk, hp_r, ent_all, adj_all, bt, low) = refs[:10]
    dx_all, tail_all, head_all, gx_all, dl_o, dd_all, u2_all, kf_all, db_o = refs[-14:-5]
    turn_sc, xs_sc, head_sc, all_sc, tap_sc = refs[-5:]
    length = bt.shape[1]
    per = ent_all.shape[1] // CB

    @pl.when(pl.program_id(0) == 0)
    def _():
        db_o[...] = jnp.zeros_like(db_o)
        dl_o[...] = jnp.zeros_like(dl_o)

    for b in range(dx_all.shape[0] // CB):
        rows = slice(b * CB, (b + 1) * CB)
        tap_sc[...] = spread(kind_rows(pk, b, 3), range(5))
        hp = hp_r[b]
        delta = hp[2 * hb : 3 * hb]
        total = hp[hb : 2 * hb]
        last = total[:, length - 1 : length]
        ends = jnp.exp2(last - total)
        adj_low = adj_all[rows, :]
        ent = ent_all[b // per, b % per * CB : (b % per + 1) * CB, :]
        turn_sc[...] = dot(adj_low, bt[...])
        kf_all[b] = head_sums(adj_low.astype(f32) * ent.astype(f32), hb) * jnp.exp2(last)
        u2, dd = [], []
        for h in range(hb):
            u2_h = jnp.zeros((8, length), f32)
            dd_h = jnp.zeros((8, length), f32)
            for r in range(h * HEAD, (h + 1) * HEAD, ROWS):
                part = slice(r, r + ROWS)
                whole = slice(b * CB + r, b * CB + r + ROWS)
                xc = xc_all[whole, :].astype(f32)
                sig = sigmoid(xc)
                x = xc * sig
                xs = x * delta[h : h + 1]
                extra = turn_sc[part, :] * ends[h : h + 1]
                u2_h = u2_h + fold(xs * extra)
                xs_sc[part, :] = (xs * ends[h : h + 1]).astype(bf16)
                dxs = dxs_all[whole, :] + extra
                dd_h = dd_h + fold(x * dxs)
                skip = lanes_of(tap_sc[part, 512:640], length)
                dx = dxs * delta[h : h + 1] + dy_all[whole, :].astype(f32) * skip
                dconv = dx * (sig + x * (1.0 - sig))
                head_sc[part, :] = dconv[:, :HALO]
                none = jnp.zeros((ROWS, HALO), f32)
                ext = jnp.concatenate([none, dconv, none], axis=1)
                taps = [tap_sc[part, k * 128 : (k + 1) * 128] for k in range(4)]
                out = conv_rows(ext, taps, lambda k: ext.shape[1] - (3 - k))
                tail_all[whole, :] = out[:, length : HALO + length]
                all_low = out[:, : HALO + length].astype(bf16)
                all_sc[part, :] = all_low
                dx_all[whole, :] = all_low[:, HALO:]
            u2.append(jnp.sum(u2_h, axis=0, keepdims=True))
            dd.append(jnp.sum(dd_h, axis=0, keepdims=True))
        u2_all[b] = jnp.concatenate(u2, axis=0)
        dd_all[b] = jnp.concatenate(dd, axis=0)
        db_o[...] += dot(adj_low, xs_sc[...], TN)
        head_all[:, rows] = jnp.transpose(head_sc[...])[:8]
        all_low = all_sc[...]
        gx_all[:, rows] = dot(low[...], all_low, NT)
        dl_o[...] += dot(kind_rows(pk, b, 1)[...], all_low)
        dl_o[:, HALO:] += dot(kind_rows(pk, b, 0)[...], dz_all[rows, :])


def finish_call(dxs, dy, xc, dz, pk, hp, ent, adj, bt, low, later):
    slots, ch, length = dy.shape
    ncb = ch // CB
    hb = CB // HEAD
    rank = low.shape[0]
    full = lambda a: pl.BlockSpec(a.shape, lambda s: (0,) * a.ndim)
    chan = lambda w: pl.BlockSpec((None, ch, w), lambda s: (s, 0, 0))
    blk_out = lambda w: pl.BlockSpec((ncb, hb, w), lambda s: (s, 0, 0))
    turned = lambda w: pl.BlockSpec((None, w, ch), lambda s: (s, 0, 0))
    blocks = slots * ncb
    return pl.pallas_call(
        functools.partial(finish_kernel, hb),
        grid=(slots,),
        in_specs=[
            chan(length),
            chan(length),
            chan(length),
            chan(length),
            pl.BlockSpec((None, ch // 4, CB), lambda s: (s, 0, 0)),
            pl.BlockSpec((ncb,) + hp.shape[1:], lambda s: (s, 0, 0)),
            pl.BlockSpec(
                (ent.shape[0], None) + ent.shape[2:], lambda s: (0, (s + 1) % slots, 0, 0)
            ),
            pl.BlockSpec((None, ch, 128), lambda s: ((s + slots - 1) % slots, 0, 0)),
            full(bt),
            full(low),
        ]
        + [pl.BlockSpec(memory_space=pl.ANY)] * len(later),
        out_specs=[
            chan(length),
            chan(HALO),
            turned(8),
            turned(rank),
            pl.BlockSpec((rank, HALO + length), lambda s: (0, 0)),
            blk_out(length),
            blk_out(length),
            blk_out(128),
            pl.BlockSpec((128, length), lambda s: (0, 0)),
        ],
        out_shape=[
            jax.ShapeDtypeStruct((slots, ch, length), bf16),
            jax.ShapeDtypeStruct((slots, ch, HALO), f32),
            jax.ShapeDtypeStruct((slots, 8, ch), f32),
            jax.ShapeDtypeStruct((slots, rank, ch), f32),
            jax.ShapeDtypeStruct((rank, HALO + length), f32),
            jax.ShapeDtypeStruct((blocks, hb, length), f32),
            jax.ShapeDtypeStruct((blocks, hb, length), f32),
            jax.ShapeDtypeStruct((blocks, hb, 128), f32),
            jax.ShapeDtypeStruct((128, length), f32),
        ],
        scratch_shapes=[
            pltpu.VMEM((CB, length), f32),
            pltpu.VMEM((CB, length), bf16),
            pltpu.VMEM((CB, HALO), f32),
            pltpu.VMEM((CB, HALO + length), bf16),
            pltpu.VMEM((CB, 640), f32),
        ],
        compiler_params=compiler_params(1),
        cost_estimate=cost(slots * ch * length * 700, slots * ch * length * 14),
        name="finish_back",
    )(dxs, dy, xc, dz, pk, hp, ent, adj, bt, low, *later)


def glue_kernel(flat_order, quick, sub, *refs):
    (dcb_r, db1, db2, dc1, bt, ct, pre_r, u1, u2, kl, dd, u2f, kf) = refs[:13]
    (sig_r, speed, taps_r, sc, dl, nt) = refs[13:19]
    left_o, tail_o, head_o, gd_o = refs[19:]
    taps = tall(taps_r[...])
    low = dl[...].astype(bf16)
    for i, m in enumerate(flat_order):
        at = pl.ds(block_at(sc[0], m, quick), CB)
        gd_o[:, at] = dot(low, nt[i * CB : (i + 1) * CB, :], NT)
    state_w, length = bt.shape
    nsub = length // sub
    blocks = u1.shape[0]
    row = lax.broadcasted_iota(jnp.int32, (sub, sub), 0)
    col = lax.broadcasted_iota(jnp.int32, (sub, sub), 1)
    below = jnp.where(row >= col, 1.0, 0.0)
    keep = jnp.where(row <= col, 1.0, 0.0)

    def exact(p, q):
        return lax.dot_general(
            p, q, (NN, ((), ())), precision=highest, preferred_element_type=f32
        )

    def flat(ref, cols=slice(None)):
        return jnp.concatenate([ref[b, :, cols] for b in range(blocks)], axis=0)

    d_b, d_c, rate_in = [], [], []
    for s in range(nsub):
        cols = slice(s * sub, (s + 1) * sub)
        dcb = (dcb_r[s] * keep).astype(bf16)
        d_b.append(dot(ct[:, cols], dcb, NT))
        d_c.append(dot(bt[:, cols], dcb))
        lane = slice(s * 128, (s + 1) * 128)
        rate_in.append(
            exact(flat(u1, cols), below)
            + exact(flat(u2, cols), 1.0 - below)
            + jnp.sum(flat(kl, lane), axis=1, keepdims=True)
        )
    d_b = jnp.concatenate(d_b, axis=1) + db1[...] + db2[...]
    d_c = jnp.concatenate(d_c, axis=1) + dc1[...]
    pre = pre_r[...]
    sig = sigmoid(pre)
    d_pre = jnp.concatenate([d_b, d_c], axis=0) * (sig + pre * sig * (1.0 - sig))
    head_o[...] = jnp.transpose(d_pre[:, :HALO])[:8]
    ext = jnp.concatenate([d_pre, jnp.zeros((2 * state_w, HALO), f32)], axis=1)
    out = ext * taps[:, 3:4]
    for k in range(3):
        out = out + pltpu.roll(ext, ext.shape[1] - (3 - k), 1) * taps[:, k : k + 1]
    tail_o[...] = out[:, length - HALO : length]
    left_o[: 2 * state_w, :] = out[:, :length].astype(bf16)
    rate = jnp.concatenate(rate_in, axis=1) + jnp.sum(flat(kf), axis=1, keepdims=True)
    first = flat(u2f)
    run = None
    parts = []
    for s in range(nsub):
        piece = first[:, s * sub : (s + 1) * sub]
        here = exact(piece, 1.0 - below)
        parts.append(here if run is None else here + run)
        ends = jnp.sum(piece, axis=1, keepdims=True)
        run = ends if run is None else run + ends
    rate = rate + jnp.concatenate(parts, axis=1)
    left_o[2 * state_w :, :] = ((flat(dd) - speed[:, :1] * rate) * sig_r[...]).astype(bf16)


def glue_call(args, sc, dl, nt, state_w, length, heads, flat, quick):
    vm = pl.BlockSpec(memory_space=pltpu.VMEM)
    return pl.pallas_call(
        functools.partial(glue_kernel, flat, quick, SUB),
        in_specs=[vm] * len(args) + [pl.BlockSpec(memory_space=pltpu.SMEM), vm, vm],
        out_specs=[vm] * 4,
        out_shape=[
            jax.ShapeDtypeStruct((2 * state_w + heads, length), bf16),
            jax.ShapeDtypeStruct((2 * state_w, HALO), f32),
            jax.ShapeDtypeStruct((8, 2 * state_w), f32),
            jax.ShapeDtypeStruct((dl.shape[0], nt.shape[0]), f32),
        ],
        compiler_params=compiler_params(0),
        cost_estimate=cost(1e8, 4e6),
        name="glue",
    )(*args, sc, dl, nt)


def add_products(acc, turned, sets, picks, refs, slot):
    at = 0
    for lo, hi, per in sets:
        groups = [refs[at + p * per : at + (p + 1) * per] for p in range(len(picks))]
        at += len(picks) * per

        @pl.when((slot >= lo) & (slot < hi))
        def _(groups=groups):
            off = 0
            for i in range(len(picks[0])):
                parts = []
                for group, order in zip(groups, picks):
                    k, b = order[i]
                    parts.append(group[k][b])
                w = parts[0] if len(parts) == 1 else jnp.concatenate(parts, axis=0)
                acc[:, off : off + w.shape[1]] += dot(turned, w)
                off += w.shape[1]


def product_specs(weights, share):
    ops, specs, sets = [], [], []
    for (lo, hi), paths, base in weights:
        sets.append((lo, hi, len(paths[0])))
        for arrays in paths:
            for a in arrays:
                ops.append(a)
                index = lambda s, lo=lo, hi=hi, base=base: (0, base + jnp.clip(s, lo, hi - 1) - lo, 0)
                specs.append(pl.BlockSpec((a.shape[0], share, a.shape[2]), index))
    return ops, specs, sets


def output_kernel(sets, picks, flat, quick, n_w, *refs):
    (sc, nout, dn, bh, up, tok, masked) = refs[:7]
    wrefs = refs[7 : 7 + n_w]
    mixed_o, gdo_o, guo_o, acc, hid = refs[-5:]
    slot = pl.program_id(0)
    rank = up.shape[0]
    length, width = tok.shape

    @pl.when(slot == 0)
    def _():
        acc[...] = jnp.zeros_like(acc)
        hid[...] = jnp.zeros_like(hid)

    values = nout[...]
    gdo_o[...] = dot(bh[...], values, NT)
    for part in range(dn.shape[0] // 64):
        mine = slice(part * CB, (part + 1) * CB)
        hid[...] += dot(dn[part * 64 + 32 : part * 64 + 48, :], values[mine])
    add_products(acc, jnp.transpose(values), sets, picks, wrefs, slot)

    @pl.when(slot == pl.num_programs(0) - 1)
    def _():
        low = hid[...].astype(bf16)
        guo_o[...] = dot(low, masked[...])
        rows = lax.broadcasted_iota(jnp.int32, (length, 1), 0) < sc[1]
        for i, m in enumerate(flat):
            at = pl.ds(block_at(sc[0], m, quick), CB)
            total = acc[:, i * CB : (i + 1) * CB] + dot(low, up[:, at], TN)
            total = total + tok[:, at].astype(f32)
            mixed_o[:, at] = jnp.where(rows, total, 0.0).astype(bf16)


def output_call(sc, nout, pk, bh, up, tok, masked, weights, picks, flat, quick):
    slots, ch, length = nout.shape
    rank, width = up.shape
    block = ch
    full = lambda a: pl.BlockSpec(a.shape, lambda s: (0,) * a.ndim)
    chan = lambda a: pl.BlockSpec((None, block, a.shape[2]), lambda s: (s, 0, 0))
    w_ops, w_specs, sets = product_specs(weights, ch // len(picks))
    return pl.pallas_call(
        functools.partial(output_kernel, sets, picks, flat, quick, len(w_ops)),
        grid=(slots,),
        in_specs=[pl.BlockSpec(memory_space=pltpu.SMEM), chan(nout)]
        + [pl.BlockSpec((None, block // 4, CB), lambda s: (s, 0, 0)), full(bh)]
        + [full(up), full(tok), full(masked)] + w_specs,
        out_specs=[
            pl.BlockSpec((length, width), lambda s: (0, 0)),
            pl.BlockSpec((None, rank, block), lambda s: (s, 0, 0)),
            pl.BlockSpec((rank, width), lambda s: (0, 0)),
        ],
        out_shape=[
            jax.ShapeDtypeStruct((length, width), bf16),
            jax.ShapeDtypeStruct((slots, rank, ch), f32),
            jax.ShapeDtypeStruct((rank, width), f32),
        ],
        scratch_shapes=[pltpu.VMEM((length, width), f32), pltpu.VMEM((rank, length), f32)],
        compiler_params=compiler_params(1),
        cost_estimate=cost(2 * slots * ch * length * width, slots * ch * width * 2),
        name="output",
    )(sc, nout, pk, bh, up, tok, masked, *w_ops)


def gate_back_kernel(sets, picks, n_w, *refs):
    dz, low = refs[:2]
    acc, gz_o = refs[-2:]
    slot = pl.program_id(0)

    @pl.when(slot == 0)
    def _():
        acc[...] = jnp.zeros_like(acc)

    gz_o[...] = dot(low[:, HALO:], dz[...], NT)
    add_products(acc, jnp.transpose(dz[...]), sets, picks, refs[2 : 2 + n_w], slot)


def gate_back_call(dz, low, weights, picks, width, later=()):
    slots, ch, length = dz.shape
    rank = low.shape[0]
    block = ch
    w_ops, w_specs, sets = product_specs(weights, ch // len(picks))
    return pl.pallas_call(
        functools.partial(gate_back_kernel, sets, picks, len(w_ops)),
        grid=(slots,),
        in_specs=[
            pl.BlockSpec((None, block, length), lambda s: (s, 0, 0)),
            pl.BlockSpec(low.shape, lambda s: (0, 0)),
        ]
        + w_specs
        + [pl.BlockSpec(memory_space=pl.ANY)] * len(later),
        out_specs=[
            pl.BlockSpec((length, width), lambda s: (0, 0)),
            pl.BlockSpec((None, rank, block), lambda s: (s, 0, 0)),
        ],
        out_shape=[
            jax.ShapeDtypeStruct((length, width), f32),
            jax.ShapeDtypeStruct((slots, rank, ch), f32),
        ],
        compiler_params=compiler_params(1),
        cost_estimate=cost(2 * slots * ch * length * width, 2 * slots * ch * width),
        name="gate_back",
    )(dz, low, *w_ops, *later)


def beyond(near, taps, rows):
    parts = [jnp.zeros((HALO - 3, rows), f32)]
    for i in range(3):
        total = near[i : i + 1] * taps[0:1]
        for k in range(1, i + 1):
            total = total + near[i - k : i - k + 1] * taps[k : k + 1]
        parts.append(total)
    return jnp.transpose(jnp.concatenate(parts, axis=0))


def input_kernel(sets, picks, flat, quick, n_w, n_small, *refs):
    (sc, dx, tail, near, num, left, maps_tail, maps_near, maps_taps) = refs[:9]
    (dl, near_dl, down, root_r, gain, tok, masked, start) = refs[9:17]
    smalls = refs[17 : 17 + n_small]
    wrefs = refs[17 + n_small : 17 + n_small + n_w]
    out, acc = refs[-2:]
    slot = pl.program_id(0)
    length, width = tok.shape
    cut = length - HALO

    @pl.when(slot == 0)
    def _():
        d_low = jnp.concatenate(
            [dl[:, HALO:length], dl[:, length:] + near_dl[:, :HALO]], axis=1
        ).astype(bf16)
        low = jnp.transpose(d_low)
        n_maps = maps_tail.shape[0]
        maps_last = maps_tail[...] + beyond(maps_near[:, :n_maps], maps_taps, n_maps)
        maps_left = jnp.concatenate([left[:n_maps, :cut], maps_last.astype(bf16)], axis=1)
        total = start[...] + dot(maps_left, smalls[0][...], TN)
        row = n_maps
        for w in smalls[1:]:
            total = total + dot(left[row : row + w.shape[0], :], w[...], TN)
            row += w.shape[0]
        acc[...] = total
        for i, m in enumerate(flat):
            at = pl.ds(block_at(sc[0], m, quick), CB)
            acc[:, i * CB : (i + 1) * CB] += dot(low, down[at, :], NT)

    block = dx.shape[0]
    taps = jnp.concatenate(
        [
            num[b * 64 + 48 : b * 64 + 56, :].astype(f32)
            + num[b * 64 + 56 : b * 64 + 64, :].astype(f32)
            for b in range(block // CB)
        ],
        axis=1,
    )
    last = tail[...] + beyond(near[...], taps, block)
    dx_all = jnp.concatenate([dx[:, :cut], last.astype(bf16)], axis=1)
    add_products(acc, jnp.transpose(dx_all), sets, picks, wrefs, slot)

    @pl.when(slot == pl.num_programs(0) - 1)
    def _():
        root = root_r[...]
        mean = None
        for i, m in enumerate(flat):
            at = pl.ds(block_at(sc[0], m, quick), CB)
            cols = slice(i * CB, (i + 1) * CB)
            scaled = acc[:, cols] * gain[:, at]
            acc[:, cols] = scaled
            part = jnp.sum(scaled * tok[:, at].astype(f32), axis=1, keepdims=True)
            mean = part if mean is None else mean + part
        coef = root * root * root * (mean * (1.0 / width))
        for i, m in enumerate(flat):
            at = pl.ds(block_at(sc[0], m, quick), CB)
            d_resid = root * acc[:, i * CB : (i + 1) * CB] - tok[:, at].astype(f32) * coef
            out[:, at] = (masked[:, at].astype(f32) + d_resid).astype(bf16)


def input_call(
    sc, dx, tail, near, pk, left, maps_tail, maps_taps, dl, down, root, gain, tok, masked, start,
    smalls, weights, picks, flat, quick, later=(),
):
    slots, ch, length = dx.shape
    width = tok.shape[1]
    block = ch
    rank = dl.shape[0]
    once = pl.Buffered(1)
    full = lambda a: pl.BlockSpec(a.shape, lambda s: (0,) * a.ndim, pipeline_mode=once)
    chan = lambda a: pl.BlockSpec((None, block, a.shape[2]), lambda s: (s, 0, 0))
    w_ops, w_specs, sets = product_specs(weights, ch // len(picks))
    near_rows = pl.BlockSpec((8, block), lambda s: ((s + slots - 1) % slots, 0))
    near_maps = pl.BlockSpec((8, ch), lambda s: (slots, 0), pipeline_mode=once)
    near_low = pl.BlockSpec(
        (rank, ch), lambda s: (((slots + 1) * 8 + rank - 1) // rank, 0), pipeline_mode=once
    )
    return pl.pallas_call(
        functools.partial(input_kernel, sets, picks, flat, quick, len(w_ops), len(smalls)),
        grid=(slots,),
        in_specs=[pl.BlockSpec(memory_space=pltpu.SMEM), chan(dx), chan(tail), near_rows]
        + [pl.BlockSpec((None, block // 4, CB), lambda s: (s, 0, 0))]
        + [full(left), full(maps_tail), near_maps, full(maps_taps), full(dl), near_low]
        + [full(a) for a in [down, root, gain, tok, masked, start] + list(smalls)]
        + w_specs
        + [pl.BlockSpec(memory_space=pl.ANY)] * len(later),
        out_specs=pl.BlockSpec((length, width), lambda s: (0, 0)),
        out_shape=jax.ShapeDtypeStruct((length, width), bf16),
        scratch_shapes=[pltpu.VMEM((length, width), f32)],
        compiler_params=compiler_params(1),
        cost_estimate=cost(2 * slots * ch * length * width, 2 * slots * ch * width),
        name="input_back",
    )(
        sc, dx, tail, near, pk, left, maps_tail, near, maps_taps, dl, near, down, root, gain, tok,
        masked, start, *smalls, *w_ops, *later
    )


def assemble_kernel(n, planes, ch, *refs):
    parts = refs[:n]
    down_o, up_o, down_out_o, up_out_o = refs[n:]
    which = pl.program_id(0).astype(f32)
    total = None
    for ref in parts:
        for b in range(ref.shape[0]):
            chosen = jnp.where(ref[b, :, -1:].astype(f32) == which, 1.0, 0.0)
            term = ref[b, :, :-128].astype(f32) * chosen
            total = term if total is None else total + term
    up_o[:, 0, :] = total[:, :ch]
    up_o[:, 1, :] = total[:, ch : 2 * ch]
    down_out_o[...] = total[:, 2 * ch : 3 * ch]
    width = down_o.shape[1]
    down_o[...] = total[:, 3 * ch : 3 * ch + width]
    up_out_o[...] = total[:, 3 * ch + width :]


def assemble_call(parts, adapters, planes, ch, width):
    rank = parts[0].shape[1]
    return pl.pallas_call(
        functools.partial(assemble_kernel, len(parts), planes, ch),
        grid=(adapters,),
        in_specs=[pl.BlockSpec(a.shape, lambda i: (0, 0, 0)) for a in parts],
        out_specs=[
            pl.BlockSpec((None, rank, width), lambda i: (i, 0, 0)),
            pl.BlockSpec((None, rank, 2, ch), lambda i: (i, 0, 0, 0)),
            pl.BlockSpec((None, rank, ch), lambda i: (i, 0, 0)),
            pl.BlockSpec((None, rank, width), lambda i: (i, 0, 0)),
        ],
        out_shape=[
            jax.ShapeDtypeStruct((adapters, rank, width), f32),
            jax.ShapeDtypeStruct((adapters, rank, 2, ch), f32),
            jax.ShapeDtypeStruct((adapters, rank, ch), f32),
            jax.ShapeDtypeStruct((adapters, rank, width), f32),
        ],
        compiler_params=compiler_params(1),
        cost_estimate=cost(1e7, 2e7),
        name="assemble",
    )(*parts)


def body(
    tokens,
    cotangent,
    lengths,
    adapter_ids,
    pre_gain,
    in_inner,
    in_maps,
    in_steps,
    conv_inner,
    conv_maps,
    step_bias,
    decay_log,
    skip_gain,
    norm_gain,
    out_weight,
    adapter_in_down,
    adapter_in_up,
    adapter_out_down,
    adapter_out_up,
):
    planes = lax.axis_size("tensor")
    seqs = lax.axis_size("dp")
    place = lax.axis_index("tensor")
    mine = lax.axis_index("dp")
    length = tokens.shape[1]
    width = tokens.shape[2]
    rows_here = in_inner.shape[0]
    ch = in_inner.shape[2]
    inner = ch * planes
    hs = in_steps.shape[1]
    heads = hs * planes
    rank = adapter_in_down.shape[2]
    adapters = adapter_in_down.shape[0]
    state_w = in_maps.shape[1] // 2
    hb = CB // HEAD
    ncb = ch // CB
    nblk = planes * ncb
    nsub = length // SUB
    quick = seqs == 8 and planes == 4

    def from_plane(v, j):
        return lax.ppermute(v, "tensor", [((s + j) % planes, s) for s in range(planes)])

    def flip(v, bit):
        return lax.ppermute(v, "dp", [(i, i ^ bit) for i in range(seqs)])

    def slot_order(v, first=0, at=place):
        return [
            lax.dynamic_index_in_dim(v, (at + j) % planes, 0, keepdims=False)
            for j in range(first, planes)
        ]

    def by_slot(v):
        return jnp.stack(slot_order(lax.all_gather(v, "tensor", axis=0)))

    def to_slots(rows, whole):
        total = jnp.concatenate([rows[0], whole], axis=1)
        for j in range(1, planes):
            part = jnp.concatenate([rows[j], whole], axis=1).astype(bf16)
            total = total + lax.ppermute(
                part, "tensor", [(s, (s + j) % planes) for s in range(planes)]
            ).astype(f32)
        return total

    flat = [0, 2, 4, 6, 1, 3, 5, 7] if quick else list(range(width // CB))
    if quick:
        picks = [
            [(0, 0), (0, 1), (1, 0), (1, 1), (2, 0), (2, 1), (3, 0), (3, 1)],
            [(0, 0), (1, 0), (0, 1), (1, 1), (2, 0), (3, 0), (2, 1), (3, 1)],
        ]
    else:
        picks = [[(0, 0)]]
    half = planes // 2

    def halves(parts, more=((), ())):
        cut = ch // 2
        return [
            jnp.concatenate([v[:cut] for v in parts] + list(more[0]), axis=0),
            jnp.concatenate([v[cut:] for v in parts] + list(more[1]), axis=0),
        ]

    def pass_one(ab):
        return [flip(ab[0], 2), flip(ab[1], 4)]

    def pass_two(ab):
        return [flip(ab[0], 4), flip(ab[1], 2)]

    def pass_core(arrays):
        return [flip(v, 1) for v in arrays]

    def as_paths(arrays, swapped):
        return [[arrays[k], arrays[k + 2], swapped[k], swapped[k + 2]] for k in range(2)]

    pick = adapter_ids[0]
    down_in = lax.dynamic_index_in_dim(adapter_in_down, pick, 0, keepdims=False)
    up_here = lax.dynamic_index_in_dim(adapter_in_up, pick, 0, keepdims=False)
    down_here = lax.dynamic_index_in_dim(adapter_out_down, pick, 0, keepdims=False)
    up_out = lax.dynamic_index_in_dim(adapter_out_up, pick, 0, keepdims=False)
    numbers = jnp.concatenate(
        [
            conv_inner,
            jnp.repeat(skip_gain, HEAD)[None],
            norm_gain[None],
            jnp.pad(jnp.stack([step_bias, decay_log]), ((0, 0), (0, ch - hs))),
        ],
        axis=0,
    )
    coarse = lax.optimization_barrier(numbers.astype(bf16))
    fine = lax.optimization_barrier((numbers - coarse.astype(f32)).astype(bf16))
    packed = jnp.concatenate(
        [jnp.transpose(up_here, (1, 0, 2)).reshape(2 * rank, ch), down_here.T, coarse, fine],
        axis=0,
    )
    packed = jnp.swapaxes(packed.reshape(64, ncb, CB), 0, 1).reshape(64 * ncb, CB)
    last_rows = tokens[0, -16:].reshape(16 * width // CB, CB)
    halo = [(s, s + 1) for s in range(planes - 1)]
    wt = jnp.transpose(in_inner, (1, 2, 0))
    maps_w = in_maps.T
    steps_w = in_steps.T
    own_rows = 3 * ch // 2
    if quick:
        own = halves(
            [wt[0], wt[1], out_weight],
            ([maps_w[:state_w], steps_w], [maps_w[state_w:]]),
        )
        got = pass_one(own)
        all_x = lax.all_gather(
            jnp.concatenate([wt[1], packed, steps_w, last_rows], axis=0), "tensor", axis=0
        )
        all_z = lax.all_gather(wt[0], "tensor", axis=0)
        all_o = lax.all_gather(out_weight, "tensor", axis=0)
        token, _, own = hold([], [], zip(own, got))
        two = pass_two(own)
        swapped = pass_core(own)
        marks = [ch, ch + 64 * ncb, ch + 64 * ncb + hs]
        all_x = slot_order(all_x)
        pk = jnp.stack([v[marks[0] : marks[1]] for v in all_x])
        last_rows = all_x[planes - 1][marks[2] :]
        far_x = halves(
            [v[:ch] for v in all_x[1:]], ([v[marks[1] : marks[2]] for v in all_x[1:]], ())
        )
        token, passed, _ = hold(swapped, two + far_x)
        two, far_x = passed[:2], passed[2:]
        own = own + two
        swapped = swapped + pass_core(two)
        got = pass_one(far_x)
        held = [token]
    else:
        pk = by_slot(packed)
        last_rows = by_slot(last_rows)[planes - 1]
        steps_w = by_slot(steps_w)
        held = []
    before = last_rows.reshape(16, width)
    before = jnp.where(place > 0, before, jnp.zeros_like(before))
    sc = jnp.stack([mine, lengths[0] - place * length]).astype(jnp.int32)
    normed, masked, root, low2, back2, nt, gt = turn_call(
        sc, tokens[0], before, cotangent[0], pre_gain[None], down_in, up_out, flat, quick, held
    )
    if quick:
        own = as_paths(own, swapped)
        token, _, far_x = hold([nt, pk] + own[0] + own[1], [], zip(far_x, got))
        two = pass_two(far_x)
        swapped = pass_core(far_x)
        held = [token]
        all_maps, all_steps = own, own[0]
        maps_at, maps_rows = own_rows, state_w
        steps_at, mine_slots = own_rows + state_w, 1
    else:
        all_maps = [[lax.all_gather(maps_w, "dp", axis=1, tiled=True)[None]]]
        all_steps = steps_w.reshape(heads, rows_here)
        all_steps = [lax.all_gather(all_steps, "dp", axis=1, tiled=True)[None]]
        maps_at, maps_rows = 0, 2 * state_w
        steps_at, mine_slots = 0, planes
    bt, ct, b_low, c_low, cbt, maps_pre, maps_w = maps_call(
        all_maps, maps_at, maps_rows, picks, nt, conv_maps, length, held
    )
    hp, step_sig, speed, mine_w = steps_call(
        all_steps, steps_at, picks[0], nt, pk, 0, mine_slots, hs, length, held
    )
    small_w = [maps_w, mine_w]

    x_args = (picks, nt, low2, pk, ch)
    z_args = (picks, nt, low2, pk, ch, HALO, False)
    o_args = (picks, gt, back2, pk, ch, 0, True)
    if quick:
        empty = [None] * 4
        bufs, _ = scan_call(
            0, 1, (own, 1), 0, *x_args, hp, ct, b_low, cbt, empty + [None], held
        )
        sent_a = bufs[4]
        bufs, done = scan_call(
            0, 1, (own, 1), 1, *x_args, hp, ct, b_low, cbt, bufs[:4] + [None], held
        )
        sent_b = bufs[4]
        far_z = halves(slot_order(all_z, 1, place + token[0, 0].astype(jnp.int32)))

        token, passed, _ = hold([done] + swapped, two + far_z)
        two, far_z = passed[:2], passed[2:]
        far_x = as_paths(far_x + two, swapped + pass_core(two))
        got = pass_one(far_z)
        z, beside = proj_call(0, 1, (own, 0), *z_args, None, [token])
        wgt, beside = proj_call(0, 1, (own, 2), *o_args, None, [beside])
        far_o = halves(slot_order(all_o, 1, place + beside[0, 0].astype(jnp.int32)))

        token, far_o, far_z = hold([beside] + far_x[0] + far_x[1], far_o, zip(far_z, got))
        two = pass_two(far_z)
        swapped = pass_core(far_z)
        hp_far, sig_far, speed_far, far_w = steps_call(
            far_x[0], own_rows, picks[0], nt, pk, 1, planes, hs, length, [token]
        )
        hp = jnp.concatenate([hp, hp_far], axis=0)
        step_sig = jnp.concatenate([step_sig, sig_far], axis=0)
        speed = jnp.concatenate([speed, speed_far], axis=0)
        small_w.append(far_w)
        bufs, _ = scan_call(
            1, planes, (far_x, 0), 0, *x_args, hp, ct, b_low, cbt, bufs[:4] + [sent_a], [token]
        )
        ent_a = lax.ppermute(bufs[4], "tensor", halo)
        bufs, done = scan_call(
            1, planes, (far_x, 0), 1, *x_args, hp, ct, b_low, cbt, bufs[:4] + [sent_b], [token]
        )
        sent_b = bufs[4]
        token, passed, _ = hold([done] + swapped, two + far_o + [ent_a, sent_b])
        two, far_o, (ent_a, sent_b) = passed[:2], passed[2:4], passed[4:]
        far_z = as_paths(far_z + two, swapped + pass_core(two))
        got = pass_one(far_o)
        ent_b = lax.ppermute(sent_b, "tensor", halo)
        ent_a = lax.ppermute(hop_call(ent_a, 1, bufs[3], hp, 0, [token]), "tensor", halo)

        token, passed, far_o = hold(far_z[0] + far_z[1], [ent_a, ent_b], zip(far_o, got))
        ent_a, ent_b = passed
        two = pass_two(far_o)
        send_b = hop_call(ent_b, 1, bufs[3], hp, 1, [token])
        ent_b = lax.ppermute(send_b, "tensor", halo)
        send_a = hop_call(ent_a, 1, bufs[3], hp, 0, [token])
        ent_a = lax.ppermute(send_a, "tensor", halo)
        z, done = proj_call(1, planes, (far_z, 0), *z_args, z, [send_a, send_b])

        token, passed, _ = hold([done], two + far_o + [ent_a, ent_b])
        two, far_o, (ent_a, ent_b) = passed[:2], passed[2:4], passed[4:]
        far_o = as_paths(far_o + two, pass_core(far_o + two))
        send_b = hop_call(ent_b, 1, bufs[3], hp, 1, [token])
        ent_b = lax.ppermute(send_b, "tensor", halo)
        wgt, done = proj_call(1, planes, (far_o, 0), *o_args, wgt, [send_b])
        _, ent, _ = hold([done], [ent_a, ent_b])
        ent = jnp.stack(ent)
        z_sets = [((0, 1), own, 0), ((1, planes), far_z, 0)]
        x_sets = [((0, 1), own, 1), ((1, planes), far_x, 0)]
        o_sets = [((0, 1), own, 2), ((1, planes), far_o, 0)]
    else:
        w = lax.all_gather(wt, "dp", axis=2, tiled=True)
        w = by_slot(w)
        o = lax.all_gather(out_weight, "dp", axis=1, tiled=True)
        flat_rows = lambda v: [[v.reshape(1, inner, width)]]
        wz, wx = flat_rows(w[:, 0]), flat_rows(w[:, 1])
        o = flat_rows(by_slot(o))
        bufs, _ = scan_call(
            0, planes, (wx, 0), 0, *x_args, hp, ct, b_low, cbt, [None] * 5
        )
        z, _ = proj_call(0, planes, (wz, 0), *z_args, None)
        wgt, _ = proj_call(0, planes, (o, 0), *o_args, None)
        ent = lax.ppermute(bufs[4], "tensor", halo)
        for _ in range(planes - 2):
            ent = lax.ppermute(hop_call(ent, 1, bufs[3], hp), "tensor", halo)
        ent = ent[None]
        z_sets = [((0, planes), wz, 0)]
        x_sets = [((0, planes), wx, 0)]
        o_sets = [((0, planes), o, 0)]
    xc, mix, loc, s_end, _ = bufs
    left = [(s + 1, s) for s in range(planes - 1)]

    nout, dy, dz, sl, sl_sent = gate_call(z, mix, wgt, ent, pk, hp, ct, c_low, inner)

    adj = lax.ppermute(sl_sent, "tensor", left)
    mixed, grad_down_out, grad_up_out = output_call(
        sc, nout, pk, back2, up_out, tokens[0], masked, o_sets, picks, flat, quick
    )
    send = hop_call(adj, planes - 1, sl, hp, 0, [mixed])
    adj = lax.ppermute(send, "tensor", left)
    d_normed, grad_z = gate_back_call(dz, low2, z_sets, picks, width, [send])
    send = hop_call(adj, planes - 1, sl, hp, 0, [d_normed])
    adj = lax.ppermute(send, "tensor", left)
    for _ in range(planes - 4):
        adj = lax.ppermute(hop_call(adj, planes - 1, sl, hp), "tensor", left)
    dxs, u1, u2, kl, dcb, db1, dc1 = back_call(
        dy, xc, hp, ent, loc, ct, c_low, bt, cbt, [send]
    )

    early = to_slots(
        [jnp.concatenate([grad_z[j], grad_down_out[j]], axis=1) for j in range(planes)],
        grad_up_out,
    )
    (dx, tail, head, grad_x, d_low, ddelta, u2f, kf, db3) = finish_call(
        dxs, dy, xc, dz, pk, hp, ent, adj, bt, low2, [mixed, early]
    )
    small_left, maps_tail, maps_head, grad_down = glue_call(
        [dcb, db1, db3, dc1, bt, ct, maps_pre, u1, u2, kl, ddelta, u2f, kf, step_sig, speed]
        + [conv_maps],
        sc, d_low, nt, state_w, length, heads, flat, quick,
    )

    to_left = jnp.concatenate(
        [
            head.reshape(8 * planes, ch),
            jnp.pad(maps_head, ((0, 0), (0, ch - 2 * state_w))),
            jnp.zeros((-(8 * planes + 8) % rank, ch), f32),
            jnp.pad(d_low[:, :HALO], ((0, 0), (0, ch - HALO))),
        ],
        axis=0,
    )
    near = lax.ppermute(to_left, "tensor", left)
    late = to_slots([grad_x[j] for j in range(planes)], grad_down)
    sent = jnp.concatenate(
        [
            early[:, :ch],
            late[:, :ch],
            early[:, ch : 2 * ch],
            late[:, ch:],
            early[:, 2 * ch :],
            jnp.full((rank, 128), pick).astype(f32),
        ],
        axis=1,
    ).astype(bf16)[None]
    if quick:
        both = jnp.concatenate([sent, flip(sent, 1)], axis=0)
        _, (both,), _ = hold([near], [both])
        by_seq = [both] + [flip(both, bit) for bit in (2, 4, 6)]
    else:
        by_seq = [lax.all_gather(sent[0], "dp", axis=0)]

    tokens_grad = input_call(
        sc, dx, tail, near, pk, small_left, maps_tail, conv_maps, d_low, down_in, root,
        pre_gain[None], tokens[0], masked, d_normed, small_w, x_sets, picks, flat, quick,
    )
    if quick:
        _, by_seq, _ = hold([tokens_grad], by_seq)
    g_down, g_up, g_down_out, g_up_out = assemble_call(by_seq, adapters, planes, ch, width)
    g_down = jnp.swapaxes(g_down, 1, 2)
    g_down_out = jnp.swapaxes(g_down_out, 1, 2)
    return (mixed[None], tokens_grad[None], g_down, g_up, g_down_out, g_up_out)


def solution(mesh):
    placed = (
        P("dp", "tensor", None),
        P("dp", "tensor", None),
        P("dp"),
        P("dp"),
        P(),
        P("dp", None, "tensor"),
        P("dp", None),
        P("dp", "tensor"),
        P(None, "tensor"),
        P(),
        P("tensor"),
        P("tensor"),
        P("tensor"),
        P("tensor"),
        P("tensor", "dp"),
        P(),
        P(None, None, None, "tensor"),
        P(None, "tensor", None),
        P(),
    )
    return jax.shard_map(
        body,
        mesh=mesh,
        in_specs=placed,
        out_specs=(
            P("dp", "tensor", None),
            P("dp", "tensor", None),
            P(),
            P(None, None, None, "tensor"),
            P(None, "tensor", None),
            P(),
        ),
        check_vma=False,
    )
```

```python
import functools

import jax
import jax.numpy as jnp
from jax import lax
from jax.experimental import pallas as pl
from jax.experimental.pallas import tpu as pltpu
from jax.sharding import PartitionSpec as P

f32 = jnp.float32
bf16 = jnp.bfloat16
epsilon = 1e-05
highest = lax.Precision.HIGHEST
LOG2E = 1.4426950408889634
HEAD = 64
HALO = 128
SUB = 256
CB = 256
ROWS = 32

NN = ((1,), (0,))
NT = ((1,), (1,))
TN = ((0,), (0,))


def dot(a, b, dims=NN):
    return lax.dot_general(a, b, (dims, ((), ())), preferred_element_type=f32)


def compiler_params(grid_rank):
    return pltpu.CompilerParams(
        dimension_semantics=("arbitrary",) * grid_rank, vmem_limit_bytes=60 * 2**20
    )


def cost(flops, size):
    return pl.CostEstimate(
        flops=int(flops) // 8, bytes_accessed=int(size) // 8, transcendentals=0
    )


def entering(refs, b):
    per = refs[0].shape[0] // CB
    rows = pl.ds(pl.multiple_of(b % per * CB, CB), CB)
    out = refs[0][rows, :]
    for p in range(1, len(refs)):
        out = jnp.where(b // per == p, refs[p][rows, :], out)
    return out


def kind_rows(packed, b, kind):
    return packed.at[pl.ds(pl.multiple_of(b * 64 + kind * 16, 16), 16)]


def block_rows(ref, b):
    return ref.at[pl.ds(pl.multiple_of(b * CB, CB), CB)]


def sigmoid(v):
    return 0.5 + 0.5 * jnp.tanh(0.5 * v)


def columns(numbers):
    v = numbers[...].astype(f32)
    return jnp.transpose(v[:8] + v[8:])


def spread(numbers, which):
    row = lax.broadcasted_iota(jnp.int32, (16, 128 * len(which)), 0) % 8
    col = lax.broadcasted_iota(jnp.int32, (16, 128 * len(which)), 1) // 128
    pick = jnp.zeros(row.shape, f32)
    for k, n in enumerate(which):
        pick = jnp.where((row == n) & (col == k), 1.0, pick)
    return dot(numbers[...], pick.astype(bf16), TN)


def lanes_of(values, width):
    return jnp.concatenate([values] * (width // 128), axis=1)


def tall(rows):
    return jnp.transpose(jnp.concatenate([rows, rows], axis=0))


def conv_values(raw, chan):
    out = raw * chan[:, 3:4]
    for k in range(3):
        out = out + pltpu.roll(raw, 3 - k, 1) * chan[:, k : k + 1]
    return out[:, HALO:]


def conv_rows(raw, taps, shift):
    width = raw.shape[1]
    out = raw * lanes_of(taps[3], width)
    for k in range(3):
        out = out + pltpu.roll(raw, shift(k), 1) * lanes_of(taps[k], width)
    return out


def per_head(values, rows):
    hb = rows.shape[0]
    parts = [values[h * HEAD : (h + 1) * HEAD] * rows[h : h + 1] for h in range(hb)]
    return jnp.concatenate(parts, axis=0)


def head_sums(values, hb):
    parts = [
        jnp.sum(values[h * HEAD : (h + 1) * HEAD], axis=0, keepdims=True) for h in range(hb)
    ]
    return jnp.concatenate(parts, axis=0)


def joined(refs, picks, rows=slice(None)):
    parts = [refs[k][b, rows] for k, b in picks]
    return parts[0] if len(parts) == 1 else jnp.concatenate(parts, axis=1)


def block_at(mine, m, quick):
    return pl.multiple_of((mine ^ m) * CB, CB) if quick else m * CB


def turn_kernel(flat, quick, *refs):
    (sc, tok_r, bef_r, cot_r, gain, down, up) = refs[:7]
    normed_o, masked_o, root_o, low_o, back_o, nt_o, gt_o, halo_sc = refs[-8:]
    width = tok_r.shape[1]
    length = tok_r.shape[0]

    def norm(v):
        v = v.astype(f32)
        root = lax.rsqrt(jnp.sum(v * v, axis=1, keepdims=True) * (1.0 / width) + epsilon)
        return (v * root * gain[...]).astype(bf16), root

    normed, root = norm(tok_r[...])
    normed_o[...] = normed
    root_o[...] = root
    halo_sc[...] = jnp.zeros_like(halo_sc)
    halo_sc[HALO - 16 :, :] = norm(bef_r[...])[0]
    rows = lax.broadcasted_iota(jnp.int32, (length, 1), 0)
    masked_o[...] = jnp.where(rows < sc[1], cot_r[...].astype(f32), 0.0).astype(bf16)
    low = back = None
    for i, m in enumerate(flat):
        at = pl.ds(block_at(sc[0], m, quick), CB)
        nt = jnp.concatenate(
            [jnp.transpose(halo_sc[:, at]), jnp.transpose(normed_o[:, at])], axis=1
        )
        gt = jnp.transpose(masked_o[:, at])
        nt_o[i * CB : (i + 1) * CB, :] = nt
        gt_o[i * CB : (i + 1) * CB, :] = gt
        low_m = dot(down[at, :], nt, TN)
        back_m = dot(up[:, at], gt)
        low = low_m if low is None else low + low_m
        back = back_m if back is None else back + back_m
    low_o[...] = low.astype(bf16)
    back_o[...] = back.astype(bf16)


def turn_call(sc, tokens, before, cot, gain, down, up, flat, quick, later):
    length, width = tokens.shape
    rank = up.shape[0]
    ext = length + HALO
    vm = pl.BlockSpec(memory_space=pltpu.VMEM)
    return pl.pallas_call(
        functools.partial(turn_kernel, flat, quick),
        in_specs=[pl.BlockSpec(memory_space=pltpu.SMEM)] + [vm] * 6
        + [pl.BlockSpec(memory_space=pl.ANY)] * len(later),
        out_specs=[vm] * 7,
        out_shape=[
            jax.ShapeDtypeStruct((length, width), bf16),
            jax.ShapeDtypeStruct((length, width), bf16),
            jax.ShapeDtypeStruct((length, 1), f32),
            jax.ShapeDtypeStruct((rank, ext), bf16),
            jax.ShapeDtypeStruct((rank, length), bf16),
            jax.ShapeDtypeStruct((width, ext), bf16),
            jax.ShapeDtypeStruct((width, length), bf16),
        ],
        scratch_shapes=[pltpu.VMEM((HALO, width), bf16)],
        compiler_params=compiler_params(0),
        cost_estimate=cost(length * width * 200, length * width * 16),
        name="turn",
    )(sc, tokens, before, cot, gain, down, up, *later)


def row_specs(paths, first, rows):
    ops, specs = [], []
    for arrays in paths:
        for a in arrays:
            ops.append(a)
            specs.append(
                pl.BlockSpec((a.shape[0], rows, a.shape[2]), lambda i: (0, first // rows, 0))
            )
    return ops, specs


def maps_kernel(n_w, picks, sub, *refs):
    nt, taps = refs[n_w : n_w + 2]
    bt_o, ct_o, bn_o, cn_o, cbt_o, pre_o, w_o = refs[-7:]
    length = bt_o.shape[1]
    state_w = bt_o.shape[0]
    per = n_w // len(picks)
    w = jnp.concatenate(
        [joined(refs[p * per : (p + 1) * per], order) for p, order in enumerate(picks)], axis=0
    )
    w_o[...] = w
    maps_pre = conv_values(dot(w, nt[...]), tall(taps[...]))
    pre_o[...] = maps_pre
    maps = (maps_pre * sigmoid(maps_pre)).astype(bf16)
    bt, ct = maps[:state_w], maps[state_w:]
    bt_o[...] = bt
    ct_o[...] = ct
    bn = jnp.transpose(bt)
    bn_o[...] = bn
    cn_o[...] = jnp.transpose(ct)
    row = lax.broadcasted_iota(jnp.int32, (sub, sub), 0)
    col = lax.broadcasted_iota(jnp.int32, (sub, sub), 1)
    upto = jnp.where(row <= col, 1.0, 0.0)
    for s in range(length // sub):
        cols = slice(s * sub, (s + 1) * sub)
        cbt_o[s] = upto * dot(bn[cols, :], ct[:, cols])


def maps_call(paths, first, rows, picks, nt, taps, length, later):
    ops, specs = row_specs(paths, first, rows)
    state_w = rows * len(picks) // 2
    vm = pl.BlockSpec(memory_space=pltpu.VMEM)
    n_w = len(ops)
    return pl.pallas_call(
        functools.partial(maps_kernel, n_w, picks, SUB),
        grid=(1,),
        in_specs=specs + [vm, vm] + [pl.BlockSpec(memory_space=pl.ANY)] * len(later),
        out_specs=[vm] * 7,
        out_shape=[
            jax.ShapeDtypeStruct((state_w, length), bf16),
            jax.ShapeDtypeStruct((state_w, length), bf16),
            jax.ShapeDtypeStruct((length, state_w), bf16),
            jax.ShapeDtypeStruct((length, state_w), bf16),
            jax.ShapeDtypeStruct((length // SUB, SUB, SUB), f32),
            jax.ShapeDtypeStruct((2 * state_w, length), f32),
            jax.ShapeDtypeStruct((2 * state_w, nt.shape[0]), bf16),
        ],
        compiler_params=compiler_params(1),
        cost_estimate=cost(nt.shape[0] * nt.shape[1] * 512, nt.size * 2 + nt.shape[0] * 1024),
        name="maps",
    )(*ops, nt, taps, *later)


def steps_kernel(n_w, order, hb, sub, lo, hi, hs, flat, *refs):
    nt, numbers = refs[n_w : n_w + 2]
    hp_o, sig_o, speed_o, w_o, ids_o = refs[-5:]
    if flat is None:
        ids_o[...] = jnp.zeros_like(ids_o)
    else:
        marks = joined(refs[n_w + 2 : 2 * n_w + 2], order).astype(f32)
        spots = [flat.index(m) * CB for m in range(len(flat))]
        ids_o[...] = jnp.concatenate([marks[:1, v : v + 128] for v in spots], axis=0)
    length = sig_o.shape[1]
    heads = sig_o.shape[0]
    w = joined(refs[:n_w], order)
    w_o[...] = w
    cols = [columns(numbers.at[j])[:hs] for j in range(lo, hi)]
    bias = jnp.concatenate([v[:, 6:7] for v in cols], axis=0)
    speed = jnp.exp(jnp.concatenate([v[:, 7:8] for v in cols], axis=0))
    speed_o[...] = jnp.broadcast_to(speed, (heads, 128))
    steps = dot(w, nt[:, HALO:]) + bias
    sig_o[...] = sigmoid(steps)
    delta = jnp.maximum(steps, 0.0) + jnp.log1p(jnp.exp(-jnp.abs(steps)))
    rates = -delta * speed
    row = lax.broadcasted_iota(jnp.int32, (sub, sub), 0)
    col = lax.broadcasted_iota(jnp.int32, (sub, sub), 1)
    upto = jnp.where(row <= col, 1.0, 0.0)
    before = None
    for s in range(length // sub):
        cols = slice(s * sub, (s + 1) * sub)
        cum = (
            lax.dot_general(
                rates[:, cols], upto, (NN, ((), ())), precision=highest,
                preferred_element_type=f32,
            )
            * LOG2E
        )
        cum_all = cum if before is None else cum + before
        before = cum_all[:, sub - 1 : sub]
        for b in range(heads // hb):
            mine = slice(b * hb, (b + 1) * hb)
            hp_o[b, :hb, cols] = cum[mine]
            hp_o[b, hb : 2 * hb, cols] = cum_all[mine]
            hp_o[b, 2 * hb :, cols] = delta[mine, cols]


def steps_call(arrays, first, order, nt, pk, lo, hi, hs, length, later, flat=None):
    heads = (hi - lo) * hs
    hb = CB // HEAD
    ops, specs = row_specs([arrays], first, heads)
    n_w = len(ops)
    marks = ([], []) if flat is None else row_specs([arrays], first + heads, 16)
    vm = pl.BlockSpec(memory_space=pltpu.VMEM)
    return pl.pallas_call(
        functools.partial(steps_kernel, n_w, order, hb, SUB, lo, hi, hs, flat),
        grid=(1,),
        in_specs=specs
        + [vm, pl.BlockSpec((pk.shape[0], 16, CB), lambda i: (0, 3, 0))]
        + marks[1]
        + [pl.BlockSpec(memory_space=pl.ANY)] * len(later),
        out_specs=[vm] * 5,
        out_shape=[
            jax.ShapeDtypeStruct((heads // hb, 3 * hb, length), f32),
            jax.ShapeDtypeStruct((heads, length), f32),
            jax.ShapeDtypeStruct((heads, 128), f32),
            jax.ShapeDtypeStruct((heads, nt.shape[0]), bf16),
            jax.ShapeDtypeStruct((8, 128), f32),
        ],
        compiler_params=compiler_params(1),
        cost_estimate=cost(nt.shape[0] * nt.shape[1] * 128, nt.size * 2),
        name="steps",
    )(*ops, nt, pk, *marks[0], *later)


def far_kernel(ch, first, hs, place, src, a_o, b_o):
    j = pl.program_id(0)
    half = ch // 2
    at = pl.ds(pl.multiple_of(j * half, half), half)
    a_o[at, :] = src[:half, :]
    b_o[at, :] = src[half:ch, :]
    steps = pl.ds(pl.multiple_of(pl.num_programs(0) * half + j * hs, hs), hs)
    a_o[steps, :] = src[first : first + hs, :]


def far_call(place, gathered, ch, first, hs):
    planes, rows, depth = gathered.shape
    n = planes - 1
    shapes = [(n * (ch // 2 + hs), depth), (n * ch // 2, depth)]
    return pl.pallas_call(
        functools.partial(far_kernel, ch, first, hs),
        grid_spec=pltpu.PrefetchScalarGridSpec(
            num_scalar_prefetch=1,
            grid=(n,),
            in_specs=[
                pl.BlockSpec((None, rows, depth), lambda j, p: ((p[0] + j + 1) % planes, 0, 0))
            ],
            out_specs=[pl.BlockSpec(v, lambda j, p: (0, 0)) for v in shapes],
        ),
        out_shape=[jax.ShapeDtypeStruct(v, bf16) for v in shapes],
        compiler_params=compiler_params(1),
        cost_estimate=cost(8, gathered.size * 4),
        name="far",
    )(place, gathered)


def hop_kernel(hb, shift, got, own, hp, *rest):
    out = rest[-1]
    slots, per, length = hp.shape[0], hp.shape[1], hp.shape[3]
    for s in range(slots):
        for c in range(per):
            rows = slice(c * CB, (c + 1) * CB)
            total = jnp.exp2(hp[s, c, hb : 2 * hb, length - 1 : length])
            came = got[(s + shift) % slots, rows, :].astype(f32)
            out[s, rows, :] = (per_head(came, total) + own[s, rows, :]).astype(bf16)


def hop_call(got, shift, own, hp, part=0, later=()):
    slots, rows, state_w = got.shape
    per = rows // CB
    by_slot = hp.reshape((slots, hp.shape[0] // slots) + hp.shape[1:])
    whole = lambda shape: pl.BlockSpec(shape, lambda i: (0,) * len(shape))
    return pl.pallas_call(
        functools.partial(hop_kernel, CB // HEAD, shift),
        grid=(1,),
        in_specs=[
            whole(got.shape),
            pl.BlockSpec((slots, rows, state_w), lambda i: (0, part, 0)),
            pl.BlockSpec((slots, per) + hp.shape[1:], lambda i: (0, part, 0, 0)),
        ]
        + [pl.BlockSpec(memory_space=pl.ANY)] * len(later),
        out_specs=whole(got.shape),
        out_shape=jax.ShapeDtypeStruct(got.shape, bf16),
        compiler_params=compiler_params(1),
        cost_estimate=cost(got.size * 4, got.size * 8),
        name="hop",
    )(got, own, by_slot, *later)


def hold_kernel(n_joined, *refs):
    outs = refs[-1 - n_joined :]
    for k in range(n_joined):
        outs[k][0] = refs[2 * k][...]
        outs[k][1] = refs[2 * k + 1][...]
    outs[-1][...] = jnp.zeros((1, 1), bf16)


def hold(deps, passed=(), pairs=()):
    anywhere = pl.BlockSpec(memory_space=pl.ANY)
    deps, passed, pairs = list(deps), list(passed), list(pairs)
    parts = [v for pair in pairs for v in pair]
    whole = lambda shape: pl.BlockSpec(shape, lambda i: (0,) * len(shape))
    first = len(parts) + len(deps)
    joined_shapes = [(2,) + pair[0].shape for pair in pairs]
    out = pl.pallas_call(
        functools.partial(hold_kernel, len(joined_shapes)),
        grid=(1,),
        in_specs=[whole(a.shape) for a in parts] + [anywhere] * (len(deps) + len(passed)),
        out_specs=[anywhere] * len(passed) + [whole(v) for v in joined_shapes] + [whole((1, 1))],
        out_shape=[jax.ShapeDtypeStruct(v.shape, v.dtype) for v in passed]
        + [jax.ShapeDtypeStruct(v, bf16) for v in joined_shapes]
        + [jax.ShapeDtypeStruct((1, 1), bf16)],
        input_output_aliases={first + k: k for k in range(len(passed))},
        compiler_params=compiler_params(1),
        cost_estimate=cost(8, 8),
        name="hold",
    )(*parts, *deps, *passed)
    n = len(passed)
    return out[-1], list(out[:n]), list(out[n:-1])


def decay_weights(out, cum, col, cbt, s, then=None):
    sub = out.shape[0]
    for r in range(0, sub, ROWS):
        part = slice(r, r + ROWS)
        first = r // 128 * 128
        decay = jnp.exp2(jnp.minimum(cum[:, first:] - col[part], 0.0))
        out[part, first:] = (decay * cbt[s, part, first:]).astype(bf16)
        if then is not None:
            then(part, first, decay)


def scan_kernel(nx, order, hb, sub, *refs):
    xrefs = refs[:nx]
    (nt, low, pk, hp_r, ct, bn, cbt) = refs[nx : nx + 7]
    xc_all, mix_all, ent_all, st_all, sent_all, tok_out = refs[-12:-6]
    raw_sc, x_sc, xs_sc, turn_sc, w_sc, tap_sc = refs[-6:]
    tok_out[...] = jnp.zeros_like(tok_out)
    length = ct.shape[1]
    w_sc[...] = jnp.zeros_like(w_sc)

    @pl.loop(0, xc_all.shape[0] // CB)
    def _(b):
        rows = pl.ds(pl.multiple_of(b * CB, CB), CB)
        mix_out = block_rows(mix_all, b)
        tap_sc[...] = spread(kind_rows(pk, b, 3), range(5))
        hp = hp_r[b]
        raw_sc[...] = dot(joined(xrefs, order, rows), nt[...]) + dot(
            kind_rows(pk, b, 1)[...], low[...], TN
        )
        for r in range(0, CB, ROWS):
            part = slice(r, r + ROWS)
            h = r // HEAD
            taps = [tap_sc[part, k * 128 : (k + 1) * 128] for k in range(4)]
            xc = conv_rows(raw_sc[part, :], taps, lambda k: 3 - k)[:, HALO:]
            xc_all[pl.ds(pl.multiple_of(b * CB + r, ROWS), ROWS), :] = xc.astype(bf16)
            x = xc * sigmoid(xc)
            x_sc[part, :] = x
            xs_sc[part, :] = (x * hp[2 * hb + h : 2 * hb + h + 1]).astype(bf16)
        state = None
        for s in range(length // sub):
            cols = slice(s * sub, (s + 1) * sub)
            cum = hp[:hb, cols]
            rows_n = jnp.transpose(jnp.concatenate([cum, cum], axis=0))
            last = cum[:, sub - 1 : sub]
            ends = jnp.exp2(last - cum)
            add = dot(per_head(xs_sc[:, cols].astype(f32), ends).astype(bf16), bn[cols, :])
            if s > 0:
                ent_all[s - 1, rows, :] = state
                grown = jnp.exp2(cum)
                turn_sc[...] = dot(state.astype(bf16), ct[:, cols])
            for h in range(hb):
                mine = slice(h * HEAD, (h + 1) * HEAD)
                decay_weights(w_sc, cum[h : h + 1], rows_n[:, h : h + 1], cbt, s)
                y = dot(xs_sc[mine, cols], w_sc[...])
                y = y + x_sc[mine, cols] * lanes_of(tap_sc[mine, 512:640], sub)
                if s > 0:
                    y = y + turn_sc[mine, :] * grown[h : h + 1]
                mix_out[mine, cols] = y
            state = add if state is None else per_head(state, jnp.exp2(last)) + add
        if length // sub == 1:
            ent_all[0, rows, :] = state
        st_all[rows, :] = state
        sent_all[rows, :] = state.astype(bf16)


def scan_call(lo, hi, xw, part, picks, nt, low, pk, ch, hp, ct, bn, cbt, bufs, later=()):
    slots = pk.shape[0]
    length = ct.shape[1]
    hb = CB // HEAD
    paths, base = xw
    n_paths = len(paths)
    per = ch // CB // n_paths
    width = per * CB
    nsub = length // SUB
    full = lambda a: pl.BlockSpec(a.shape, lambda s: (0,) * a.ndim)
    per_chan = lambda w: pl.BlockSpec((None, width, w), lambda s: (s + lo, part, 0))
    ops = list(paths[part])
    specs = [
        pl.BlockSpec((a.shape[0], width, a.shape[2]), lambda s: (0, s + base, 0)) for a in ops
    ]
    nx = len(ops)
    ops += [nt, low, pk, hp, ct, bn, cbt]
    specs += [full(nt), full(low)]
    specs += [pl.BlockSpec((None, per * 64, CB), lambda s: (s + lo, part, 0))]
    specs += [
        pl.BlockSpec((per,) + hp.shape[1:], lambda s: ((s + lo) * n_paths + part, 0, 0)),
        full(ct), full(bn), full(cbt),
    ]
    inner_states = max(nsub - 1, 1)
    shapes = [
        jax.ShapeDtypeStruct((slots, ch, length), bf16),
        jax.ShapeDtypeStruct((slots, ch, length), f32),
        jax.ShapeDtypeStruct((slots, inner_states, ch, 128), f32),
        jax.ShapeDtypeStruct((slots, ch, 128), f32),
        jax.ShapeDtypeStruct((slots, width, 128), bf16),
        jax.ShapeDtypeStruct((1, 1), bf16),
    ]
    outs = [
        per_chan(length),
        per_chan(length),
        pl.BlockSpec((None, inner_states, width, 128), lambda s: (s + lo, 0, part, 0)),
        per_chan(128),
        pl.BlockSpec((None, width, 128), lambda s: (s + lo, 0, 0)),
        pl.BlockSpec((1, 1), lambda s: (0, 0)),
    ]
    given = [v for v in bufs if v is not None]
    aliases = {len(ops) + i: k for i, k in enumerate(k for k in range(5) if bufs[k] is not None)}
    ops += given + list(later)
    specs += [pl.BlockSpec(memory_space=pl.ANY)] * (len(given) + len(later))
    n = hi - lo
    out = pl.pallas_call(
        functools.partial(scan_kernel, nx, picks[part], hb, SUB),
        grid=(n,),
        in_specs=specs,
        out_specs=outs,
        out_shape=shapes,
        scratch_shapes=[
            pltpu.VMEM((CB, HALO + length), f32),
            pltpu.VMEM((CB, length), f32),
            pltpu.VMEM((CB, length), bf16),
            pltpu.VMEM((CB, SUB), f32),
            pltpu.VMEM((SUB, SUB), bf16),
            pltpu.VMEM((CB, 640), f32),
        ],
        input_output_aliases=aliases,
        compiler_params=compiler_params(1),
        cost_estimate=cost(
            4 * n * per * CB * 2048 * length, n * per * CB * (4096 + length * 8)
        ),
        name="scan_slots",
    )(*ops)
    return list(out[:5]), out[5]


def proj_kernel(picks, n, cut, gain, *refs):
    (right, low, pk) = refs[n : n + 3]
    out, tok_o = refs[-2:]
    tok_o[...] = jnp.zeros_like(tok_o)
    per = n // len(picks)
    blocks = out.shape[0] // CB // len(picks)
    for p, order in enumerate(picks):
        mine = refs[p * per : (p + 1) * per]
        for k in range(blocks):
            b = p * blocks + k
            value = dot(joined(mine, order, slice(k * CB, (k + 1) * CB)), right[:, cut:])
            value = value + dot(kind_rows(pk, b, 2 if gain else 0)[...], low[:, cut:], TN)
            if gain:
                value = value * lanes_of(spread(kind_rows(pk, b, 3), [5]), value.shape[1])
            out[b * CB : (b + 1) * CB, :] = value.astype(bf16)


def proj_call(lo, hi, weight, picks, right, low, pk, ch, cut, gain, buf, later=()):
    slots = pk.shape[0]
    length = right.shape[1] - cut
    paths, base = weight
    share = ch // len(paths)
    full = lambda a: pl.BlockSpec(a.shape, lambda s: (0,) * a.ndim)
    ops = [a for arrays in paths for a in arrays]
    specs = [
        pl.BlockSpec((a.shape[0], share, a.shape[2]), lambda s: (0, s + base, 0)) for a in ops
    ]
    n_w = len(ops)
    ops += [right, low, pk]
    specs += [full(right), full(low)]
    specs += [pl.BlockSpec((None, ch // 4, CB), lambda s: (s + lo, 0, 0))]
    aliases = {}
    if buf is not None:
        aliases = {len(ops): 0}
        ops.append(buf)
        specs.append(pl.BlockSpec(memory_space=pl.ANY))
    ops += list(later)
    specs += [pl.BlockSpec(memory_space=pl.ANY)] * len(later)
    n = hi - lo
    return pl.pallas_call(
        functools.partial(proj_kernel, picks, n_w, cut, gain),
        grid=(n,),
        in_specs=specs,
        out_specs=[
            pl.BlockSpec((None, ch, length), lambda s: (s + lo, 0, 0)),
            pl.BlockSpec((1, 1), lambda s: (0, 0)),
        ],
        out_shape=[
            jax.ShapeDtypeStruct((slots, ch, length), bf16),
            jax.ShapeDtypeStruct((1, 1), bf16),
        ],
        input_output_aliases=aliases,
        compiler_params=compiler_params(1),
        cost_estimate=cost(2 * n * ch * 2048 * length, n * ch * (4096 + length * 2)),
        name="proj_slots",
    )(*ops)


def fold(values):
    total = values[:8]
    for r in range(8, values.shape[0], 8):
        total = total + values[r : r + 8]
    return total


def gate_kernel(hb, inner, paths, *refs):
    (z_all, mix_all, wgt_all, pk, hp_r, ct, cn) = refs[:7]
    ent_all = refs[7 : 7 + paths]
    nout_all, dmix_all, dz_all, sl_all, sent_all = refs[7 + paths : 12 + paths]
    mix_sc, turn_sc, sq_sc, dot_sc, gain_sc = refs[12 + paths :]
    phase, slot = pl.program_id(0), pl.program_id(1)
    blocks = z_all.shape[0] // CB

    def gates(ref, rows):
        z = ref[rows, :].astype(f32)
        sig = sigmoid(z)
        return sig, z * sig

    @pl.when((phase == 0) & (slot == 0))
    def _():
        sq_sc[...] = jnp.zeros_like(sq_sc)
        dot_sc[...] = jnp.zeros_like(dot_sc)

    @pl.when(phase == 0)
    def _():
        @pl.loop(0, blocks)
        def _(b):
            z_r, mix_r, wgt_r = [block_rows(v, b) for v in (z_all, mix_all, wgt_all)]
            cum = jnp.exp2(hp_r[b, hb : 2 * hb])
            turn_sc[...] = dot(entering(ent_all, b), ct[...])
            sq, dots = sq_sc[...], dot_sc[...]
            for r in range(0, CB, ROWS):
                rows = slice(r, r + ROWS)
                h = r // HEAD
                _, silu = gates(z_r, rows)
                mix = mix_r[rows, :] + turn_sc[rows, :] * cum[h : h + 1]
                mix_sc[slot * blocks + b, rows, :] = mix
                gated = mix * silu
                sq = sq + fold(gated * gated)
                dots = dots + fold(gated * wgt_r[rows, :].astype(f32))
            sq_sc[...] = sq
            dot_sc[...] = dots

    @pl.when(phase == 1)
    def _():
        r_all = lax.rsqrt(jnp.sum(sq_sc[...], axis=0, keepdims=True) * (1.0 / inner) + epsilon)
        coef = r_all * r_all * r_all * (
            jnp.sum(dot_sc[...], axis=0, keepdims=True) * (1.0 / inner)
        )

        @pl.loop(0, blocks)
        def _(b):
            z_r, wgt_r = block_rows(z_all, b), block_rows(wgt_all, b)
            nout_o, dmix_o, dz_o = [block_rows(v, b) for v in (nout_all, dmix_all, dz_all)]
            cum = jnp.exp2(hp_r[b, hb : 2 * hb])
            gain_sc[...] = spread(kind_rows(pk, b, 3), [5])
            for r in range(0, CB, ROWS):
                rows = slice(r, r + ROWS)
                h = r // HEAD
                sig, silu = gates(z_r, rows)
                mix = mix_sc[slot * blocks + b, rows, :]
                gated = mix * silu
                gain = lanes_of(gain_sc[rows, :], gated.shape[1])
                nout_o[rows, :] = (gated * r_all * gain).astype(bf16)
                d_gated = r_all * wgt_r[rows, :].astype(f32) - gated * coef
                d_mix = d_gated * silu
                dmix_o[rows, :] = d_mix.astype(bf16)
                dz_o[rows, :] = (d_gated * mix * (sig + silu * (1.0 - sig))).astype(bf16)
                turn_sc[rows, :] = d_mix * cum[h : h + 1]
            adj = dot(turn_sc[...].astype(bf16), cn[...])
            here = pl.ds(pl.multiple_of(b * CB, CB), CB)
            sl_all[here, :] = adj
            sent_all[here, :] = adj.astype(bf16)


def gate_call(z, mix, wgt, ent, pk, hp, ct, cn, inner):
    slots, ch, length = mix.shape
    ncb = ch // CB
    hb = CB // HEAD
    full = lambda a: pl.BlockSpec(a.shape, lambda p, s: (0,) * a.ndim)
    per_chan = lambda a: pl.BlockSpec((None, ch, a.shape[2]), lambda p, s: (s, 0, 0))
    held = lambda p, s: jnp.where(p == 0, s, slots - 1)
    later = lambda w: pl.BlockSpec((None, ch, w), lambda p, s: (jnp.where(p == 1, s, 0), 0, 0))
    return pl.pallas_call(
        functools.partial(gate_kernel, hb, inner, len(ent)),
        grid=(2, slots),
        in_specs=[
            per_chan(z),
            pl.BlockSpec((None, ch, length), lambda p, s: (held(p, s), 0, 0)),
            per_chan(wgt),
            pl.BlockSpec((None, ch // 4, CB), lambda p, s: (s, 0, 0)),
            pl.BlockSpec((ncb,) + hp.shape[1:], lambda p, s: (s, 0, 0)),
            full(ct),
            full(cn),
        ]
        + [
            pl.BlockSpec((None,) + v.shape[1:], lambda p, s: ((held(p, s) + 1) % slots, 0, 0))
            for v in ent
        ],
        out_specs=[later(length), later(length), later(length), later(128), later(128)],
        out_shape=[
            jax.ShapeDtypeStruct((slots, ch, length), bf16),
            jax.ShapeDtypeStruct((slots, ch, length), bf16),
            jax.ShapeDtypeStruct((slots, ch, length), bf16),
            jax.ShapeDtypeStruct((slots, ch, 128), f32),
            jax.ShapeDtypeStruct((slots, ch, 128), bf16),
        ],
        scratch_shapes=[
            pltpu.VMEM((slots * ncb, CB, length), f32),
            pltpu.VMEM((CB, length), f32),
            pltpu.VMEM((8, length), f32),
            pltpu.VMEM((8, length), f32),
            pltpu.VMEM((CB, 128), f32),
        ],
        compiler_params=compiler_params(2),
        cost_estimate=cost(slots * ch * length * 600, slots * ch * length * 22),
        name="gate",
    )(z, mix, wgt, pk, hp, ct, cn, *ent)


def back_kernel(hb, sub, paths, *refs):
    (dy_all, xc_all, hp_r, loc_all, ct, cn, bt, cbt) = refs[:8]
    ent_all = refs[8 : 8 + paths]
    dxs_all, u1_all, u2_all, kl_all, dcb_o, db_o, dc_o = refs[-12:-5]
    xs_sc, turn_sc, dxi_sc, dm_sc, w_sc = refs[-5:]
    w_sc[...] = jnp.zeros_like(w_sc)
    length = ct.shape[1]
    nsub = length // sub

    @pl.when(pl.program_id(0) == 0)
    def _():
        dcb_o[...] = jnp.zeros_like(dcb_o)
        db_o[...] = jnp.zeros_like(db_o)
        dc_o[...] = jnp.zeros_like(dc_o)

    @pl.loop(0, dy_all.shape[0] // CB)
    def _(b):
        rows = pl.ds(pl.multiple_of(b * CB, CB), CB)
        dy_r, dxs_o = block_rows(dy_all, b), block_rows(dxs_all, b)
        u1_o, u2_o, kl_o = u1_all.at[b], u2_all.at[b], kl_all.at[b]
        hp = hp_r[b]
        for r in range(0, CB, ROWS):
            part = slice(r, r + ROWS)
            h = r // HEAD
            xc = xc_all[pl.ds(pl.multiple_of(b * CB + r, ROWS), ROWS), :].astype(f32)
            x = xc * sigmoid(xc)
            xs_sc[part, :] = (x * hp[2 * hb + h : 2 * hb + h + 1]).astype(bf16)
        adj = None
        kl = []
        for s in reversed(range(nsub)):
            cols = slice(s * sub, (s + 1) * sub)
            cum = hp[:hb, cols]
            rows_n = jnp.transpose(jnp.concatenate([cum, cum], axis=0))
            ecum = jnp.exp2(cum)
            last = cum[:, sub - 1 : sub]
            ends = jnp.exp2(last - cum)
            state = entering(ent_all, b).astype(f32)
            if s > 0:
                before = hp[hb : 2 * hb, s * sub - 1 : s * sub]
                state = loc_all[s - 1, rows, :] + per_head(state, jnp.exp2(before))
            state_low = state.astype(bf16)
            turn_sc[...] = dot(state_low, ct[:, cols])
            ed = per_head(dy_r[:, cols].astype(f32), ecum).astype(bf16)
            dc_o[:, cols] += dot(state_low, ed, TN)
            add = dot(ed, cn[cols, :])
            if adj is not None:
                adj_low = adj.astype(bf16)
                dxi_sc[...] = dot(adj_low, bt[:, cols])
                db_o[:, cols] += dot(
                    adj_low, per_head(xs_sc[:, cols].astype(f32), ends).astype(bf16), TN
                )
            u1, u2 = [], []
            for h in range(hb):
                mine = slice(h * HEAD, (h + 1) * HEAD)
                dy_low, xs_low = dy_r[mine, cols], xs_sc[mine, cols]
                dm_sc[...] = dot(xs_low, dy_low, TN)

                def gather(part, first, decay):
                    dcb_o[s, part, first:] += decay * dm_sc[part, first:]

                decay_weights(w_sc, cum[h : h + 1], rows_n[:, h : h + 1], cbt, s, gather)
                xs = xs_low.astype(f32)
                y = dot(xs_low, w_sc[...]) + turn_sc[mine, :] * ecum[h : h + 1]
                dxs = dot(dy_low, w_sc[...], NT)
                u1.append(
                    jnp.sum(dy_low.astype(f32) * y - xs * dxs, axis=0, keepdims=True)
                )
                if adj is not None:
                    dxi = dxi_sc[mine, :] * ends[h : h + 1]
                    u2.append(jnp.sum(xs * dxi, axis=0, keepdims=True))
                    dxs = dxs + dxi
                dxs_o[mine, cols] = dxs
            u1_o[:, cols] = jnp.concatenate(u1, axis=0)
            if adj is None:
                u2_o[:, cols] = jnp.zeros((hb, sub), f32)
                kl.append(jnp.zeros((hb, 128), f32))
                adj = add
            else:
                u2_o[:, cols] = jnp.concatenate(u2, axis=0)
                kl.append(head_sums(adj * state, hb) * jnp.exp2(last))
                adj = per_head(adj, jnp.exp2(last)) + add
        for s in range(nsub):
            kl_o[:, s * 128 : (s + 1) * 128] = kl[nsub - 1 - s]


def back_call(dy, xc, hp, ent, loc, ct, cn, bt, cbt, later=()):
    slots, ch, length = dy.shape
    ncb = ch // CB
    hb = CB // HEAD
    nsub = length // SUB
    full = lambda a: pl.BlockSpec(a.shape, lambda s: (0,) * a.ndim)
    per_chan = lambda w: pl.BlockSpec((None, ch, w), lambda s: (s, 0, 0))
    blk_out = lambda w: pl.BlockSpec((ncb, hb, w), lambda s: (s, 0, 0))
    blocks = slots * ncb
    return pl.pallas_call(
        functools.partial(back_kernel, hb, SUB, len(ent)),
        grid=(slots,),
        in_specs=[
            per_chan(length),
            per_chan(length),
            pl.BlockSpec((ncb,) + hp.shape[1:], lambda s: (s, 0, 0)),
            pl.BlockSpec((None,) + loc.shape[1:], lambda s: (s, 0, 0, 0)),
            full(ct),
            full(cn),
            full(bt),
            full(cbt),
        ]
        + [pl.BlockSpec((None,) + v.shape[1:], lambda s: ((s + 1) % slots, 0, 0)) for v in ent]
        + [pl.BlockSpec(memory_space=pl.ANY)] * len(later),
        out_specs=[
            per_chan(length),
            blk_out(length),
            blk_out(length),
            blk_out(128 * nsub),
            pl.BlockSpec((nsub, SUB, SUB), lambda s: (0, 0, 0)),
            pl.BlockSpec((128, length), lambda s: (0, 0)),
            pl.BlockSpec((128, length), lambda s: (0, 0)),
        ],
        out_shape=[
            jax.ShapeDtypeStruct((slots, ch, length), f32),
            jax.ShapeDtypeStruct((blocks, hb, length), f32),
            jax.ShapeDtypeStruct((blocks, hb, length), f32),
            jax.ShapeDtypeStruct((blocks, hb, 128 * nsub), f32),
            jax.ShapeDtypeStruct((nsub, SUB, SUB), f32),
            jax.ShapeDtypeStruct((128, length), f32),
            jax.ShapeDtypeStruct((128, length), f32),
        ],
        scratch_shapes=[
            pltpu.VMEM((CB, length), bf16),
            pltpu.VMEM((CB, SUB), f32),
            pltpu.VMEM((CB, SUB), f32),
            pltpu.VMEM((SUB, SUB), f32),
            pltpu.VMEM((SUB, SUB), bf16),
        ],
        compiler_params=compiler_params(1),
        cost_estimate=cost(slots * ch * length * SUB * 20, slots * ch * length * 8),
        name="state_back",
    )(dy, xc, hp, loc, ct, cn, bt, cbt, *ent, *later)


def finish_kernel(hb, paths, *refs):
    (dxs_all, dy_all, xc_all, dz_all, pk, hp_r, adj_all, bt, low) = refs[:9]
    ent_all = refs[9 : 9 + paths]
    dx_all, tail_all, head_all, gx_all, dl_o, dd_all, u2_all, kf_all, db_o = refs[-14:-5]
    turn_sc, xs_sc, head_sc, all_sc, tap_sc = refs[-5:]
    length = bt.shape[1]

    @pl.when(pl.program_id(0) == 0)
    def _():
        db_o[...] = jnp.zeros_like(db_o)
        dl_o[...] = jnp.zeros_like(dl_o)

    for b in range(dx_all.shape[0] // CB):
        rows = slice(b * CB, (b + 1) * CB)
        tap_sc[...] = spread(kind_rows(pk, b, 3), range(5))
        hp = hp_r[b]
        delta = hp[2 * hb : 3 * hb]
        total = hp[hb : 2 * hb]
        last = total[:, length - 1 : length]
        ends = jnp.exp2(last - total)
        adj_low = adj_all[rows, :]
        per = ent_all[0].shape[0] // CB
        ent = ent_all[b // per][b % per * CB : (b % per + 1) * CB, :]
        turn_sc[...] = dot(adj_low, bt[...])
        kf_all[b] = head_sums(adj_low.astype(f32) * ent.astype(f32), hb) * jnp.exp2(last)
        u2, dd = [], []
        for h in range(hb):
            u2_h = jnp.zeros((8, length), f32)
            dd_h = jnp.zeros((8, length), f32)
            for r in range(h * HEAD, (h + 1) * HEAD, ROWS):
                part = slice(r, r + ROWS)
                whole = slice(b * CB + r, b * CB + r + ROWS)
                xc = xc_all[whole, :].astype(f32)
                sig = sigmoid(xc)
                x = xc * sig
                xs = x * delta[h : h + 1]
                extra = turn_sc[part, :] * ends[h : h + 1]
                u2_h = u2_h + fold(xs * extra)
                xs_sc[part, :] = (xs * ends[h : h + 1]).astype(bf16)
                dxs = dxs_all[whole, :] + extra
                dd_h = dd_h + fold(x * dxs)
                skip = lanes_of(tap_sc[part, 512:640], length)
                dx = dxs * delta[h : h + 1] + dy_all[whole, :].astype(f32) * skip
                dconv = dx * (sig + x * (1.0 - sig))
                head_sc[part, :] = dconv[:, :HALO]
                none = jnp.zeros((ROWS, HALO), f32)
                ext = jnp.concatenate([none, dconv, none], axis=1)
                taps = [tap_sc[part, k * 128 : (k + 1) * 128] for k in range(4)]
                out = conv_rows(ext, taps, lambda k: ext.shape[1] - (3 - k))
                tail_all[whole, :] = out[:, length : HALO + length]
                all_low = out[:, : HALO + length].astype(bf16)
                all_sc[part, :] = all_low
                dx_all[whole, :] = all_low[:, HALO:]
            u2.append(jnp.sum(u2_h, axis=0, keepdims=True))
            dd.append(jnp.sum(dd_h, axis=0, keepdims=True))
        u2_all[b] = jnp.concatenate(u2, axis=0)
        dd_all[b] = jnp.concatenate(dd, axis=0)
        db_o[...] += dot(adj_low, xs_sc[...], TN)
        head_all[:, rows] = jnp.transpose(head_sc[...])[:8]
        all_low = all_sc[...]
        gx_all[:, rows] = dot(low[...], all_low, NT)
        dl_o[...] += dot(kind_rows(pk, b, 1)[...], all_low)
        dl_o[:, HALO:] += dot(kind_rows(pk, b, 0)[...], dz_all[rows, :])


def finish_call(dxs, dy, xc, dz, pk, hp, ent, adj, bt, low, later):
    slots, ch, length = dy.shape
    ncb = ch // CB
    hb = CB // HEAD
    rank = low.shape[0]
    full = lambda a: pl.BlockSpec(a.shape, lambda s: (0,) * a.ndim)
    chan = lambda w: pl.BlockSpec((None, ch, w), lambda s: (s, 0, 0))
    blk_out = lambda w: pl.BlockSpec((ncb, hb, w), lambda s: (s, 0, 0))
    turned = lambda w: pl.BlockSpec((None, w, ch), lambda s: (s, 0, 0))
    blocks = slots * ncb
    return pl.pallas_call(
        functools.partial(finish_kernel, hb, len(ent)),
        grid=(slots,),
        in_specs=[
            chan(length),
            chan(length),
            chan(length),
            chan(length),
            pl.BlockSpec((None, ch // 4, CB), lambda s: (s, 0, 0)),
            pl.BlockSpec((ncb,) + hp.shape[1:], lambda s: (s, 0, 0)),
            pl.BlockSpec((None, ch, 128), lambda s: ((s + slots - 1) % slots, 0, 0)),
            full(bt),
            full(low),
        ]
        + [pl.BlockSpec((None,) + v.shape[1:], lambda s: ((s + 1) % slots, 0, 0)) for v in ent]
        + [pl.BlockSpec(memory_space=pl.ANY)] * len(later),
        out_specs=[
            chan(length),
            chan(HALO),
            turned(8),
            turned(rank),
            pl.BlockSpec((rank, HALO + length), lambda s: (0, 0)),
            blk_out(length),
            blk_out(length),
            blk_out(128),
            pl.BlockSpec((128, length), lambda s: (0, 0)),
        ],
        out_shape=[
            jax.ShapeDtypeStruct((slots, ch, length), bf16),
            jax.ShapeDtypeStruct((slots, ch, HALO), f32),
            jax.ShapeDtypeStruct((slots, 8, ch), f32),
            jax.ShapeDtypeStruct((slots, rank, ch), f32),
            jax.ShapeDtypeStruct((rank, HALO + length), f32),
            jax.ShapeDtypeStruct((blocks, hb, length), f32),
            jax.ShapeDtypeStruct((blocks, hb, length), f32),
            jax.ShapeDtypeStruct((blocks, hb, 128), f32),
            jax.ShapeDtypeStruct((128, length), f32),
        ],
        scratch_shapes=[
            pltpu.VMEM((CB, length), f32),
            pltpu.VMEM((CB, length), bf16),
            pltpu.VMEM((CB, HALO), f32),
            pltpu.VMEM((CB, HALO + length), bf16),
            pltpu.VMEM((CB, 640), f32),
        ],
        compiler_params=compiler_params(1),
        cost_estimate=cost(slots * ch * length * 700, slots * ch * length * 14),
        name="finish_back",
    )(dxs, dy, xc, dz, pk, hp, adj, bt, low, *ent, *later)


def glue_kernel(flat_order, quick, sub, *refs):
    (dcb_r, db1, db2, dc1, bt, ct, pre_r, u1, u2, kl, dd, u2f, kf) = refs[:13]
    (sig_r, speed, taps_r, sc, dl, nt) = refs[13:19]
    left_o, tail_o, head_o, gd_o = refs[19:]
    taps = tall(taps_r[...])
    low = dl[...].astype(bf16)
    for i, m in enumerate(flat_order):
        at = pl.ds(block_at(sc[0], m, quick), CB)
        gd_o[:, at] = dot(low, nt[i * CB : (i + 1) * CB, :], NT)
    state_w, length = bt.shape
    nsub = length // sub
    blocks = u1.shape[0]
    row = lax.broadcasted_iota(jnp.int32, (sub, sub), 0)
    col = lax.broadcasted_iota(jnp.int32, (sub, sub), 1)
    below = jnp.where(row >= col, 1.0, 0.0)
    keep = jnp.where(row <= col, 1.0, 0.0)

    def exact(p, q):
        return lax.dot_general(
            p, q, (NN, ((), ())), precision=highest, preferred_element_type=f32
        )

    def flat(ref, cols=slice(None)):
        return jnp.concatenate([ref[b, :, cols] for b in range(blocks)], axis=0)

    d_b, d_c, rate_in = [], [], []
    for s in range(nsub):
        cols = slice(s * sub, (s + 1) * sub)
        dcb = (dcb_r[s] * keep).astype(bf16)
        d_b.append(dot(ct[:, cols], dcb, NT))
        d_c.append(dot(bt[:, cols], dcb))
        lane = slice(s * 128, (s + 1) * 128)
        rate_in.append(
            exact(flat(u1, cols), below)
            + exact(flat(u2, cols), 1.0 - below)
            + jnp.sum(flat(kl, lane), axis=1, keepdims=True)
        )
    d_b = jnp.concatenate(d_b, axis=1) + db1[...] + db2[...]
    d_c = jnp.concatenate(d_c, axis=1) + dc1[...]
    pre = pre_r[...]
    sig = sigmoid(pre)
    d_pre = jnp.concatenate([d_b, d_c], axis=0) * (sig + pre * sig * (1.0 - sig))
    head_o[...] = jnp.transpose(d_pre[:, :HALO])[:8]
    ext = jnp.concatenate([d_pre, jnp.zeros((2 * state_w, HALO), f32)], axis=1)
    out = ext * taps[:, 3:4]
    for k in range(3):
        out = out + pltpu.roll(ext, ext.shape[1] - (3 - k), 1) * taps[:, k : k + 1]
    tail_o[...] = out[:, length - HALO : length]
    left_o[: 2 * state_w, :] = out[:, :length].astype(bf16)
    rate = jnp.concatenate(rate_in, axis=1) + jnp.sum(flat(kf), axis=1, keepdims=True)
    first = flat(u2f)
    run = None
    parts = []
    for s in range(nsub):
        piece = first[:, s * sub : (s + 1) * sub]
        here = exact(piece, 1.0 - below)
        parts.append(here if run is None else here + run)
        ends = jnp.sum(piece, axis=1, keepdims=True)
        run = ends if run is None else run + ends
    rate = rate + jnp.concatenate(parts, axis=1)
    left_o[2 * state_w :, :] = ((flat(dd) - speed[:, :1] * rate) * sig_r[...]).astype(bf16)


def glue_call(args, sc, dl, nt, state_w, length, heads, flat, quick):
    vm = pl.BlockSpec(memory_space=pltpu.VMEM)
    return pl.pallas_call(
        functools.partial(glue_kernel, flat, quick, SUB),
        in_specs=[vm] * len(args) + [pl.BlockSpec(memory_space=pltpu.SMEM), vm, vm],
        out_specs=[vm] * 4,
        out_shape=[
            jax.ShapeDtypeStruct((2 * state_w + heads, length), bf16),
            jax.ShapeDtypeStruct((2 * state_w, HALO), f32),
            jax.ShapeDtypeStruct((8, 2 * state_w), f32),
            jax.ShapeDtypeStruct((dl.shape[0], nt.shape[0]), f32),
        ],
        compiler_params=compiler_params(0),
        cost_estimate=cost(1e8, 4e6),
        name="glue",
    )(*args, sc, dl, nt)


def add_products(acc, turned, sets, picks, refs, slot):
    at = 0
    for lo, hi, per in sets:
        groups = [refs[at + p * per : at + (p + 1) * per] for p in range(len(picks))]
        at += len(picks) * per

        @pl.when((slot >= lo) & (slot < hi))
        def _(groups=groups):
            off = 0
            for i in range(len(picks[0])):
                parts = []
                for group, order in zip(groups, picks):
                    k, b = order[i]
                    parts.append(group[k][b])
                w = parts[0] if len(parts) == 1 else jnp.concatenate(parts, axis=0)
                acc[:, off : off + w.shape[1]] += dot(turned, w)
                off += w.shape[1]


def product_specs(weights, share):
    ops, specs, sets = [], [], []
    for (lo, hi), paths, base in weights:
        sets.append((lo, hi, len(paths[0])))
        for arrays in paths:
            for a in arrays:
                ops.append(a)
                index = lambda s, lo=lo, hi=hi, base=base: (0, base + jnp.clip(s, lo, hi - 1) - lo, 0)
                specs.append(pl.BlockSpec((a.shape[0], share, a.shape[2]), index))
    return ops, specs, sets


def output_kernel(sets, picks, flat, quick, n_w, *refs):
    (sc, nout, dn, bh, up, tok, masked) = refs[:7]
    wrefs = refs[7 : 7 + n_w]
    mixed_o, gdo_o, guo_o, acc, hid = refs[-5:]
    slot = pl.program_id(0)
    rank = up.shape[0]
    length, width = tok.shape

    @pl.when(slot == 0)
    def _():
        acc[...] = jnp.zeros_like(acc)
        hid[...] = jnp.zeros_like(hid)

    values = nout[...]
    gdo_o[...] = dot(bh[...], values, NT)
    for part in range(dn.shape[0] // 64):
        mine = slice(part * CB, (part + 1) * CB)
        hid[...] += dot(dn[part * 64 + 32 : part * 64 + 48, :], values[mine])
    add_products(acc, jnp.transpose(values), sets, picks, wrefs, slot)

    @pl.when(slot == pl.num_programs(0) - 1)
    def _():
        low = hid[...].astype(bf16)
        guo_o[...] = dot(low, masked[...])
        rows = lax.broadcasted_iota(jnp.int32, (length, 1), 0) < sc[1]
        for i, m in enumerate(flat):
            at = pl.ds(block_at(sc[0], m, quick), CB)
            total = acc[:, i * CB : (i + 1) * CB] + dot(low, up[:, at], TN)
            total = total + tok[:, at].astype(f32)
            mixed_o[:, at] = jnp.where(rows, total, 0.0).astype(bf16)


def output_call(sc, nout, pk, bh, up, tok, masked, weights, picks, flat, quick):
    slots, ch, length = nout.shape
    rank, width = up.shape
    block = ch
    full = lambda a: pl.BlockSpec(a.shape, lambda s: (0,) * a.ndim)
    chan = lambda a: pl.BlockSpec((None, block, a.shape[2]), lambda s: (s, 0, 0))
    w_ops, w_specs, sets = product_specs(weights, ch // len(picks))
    return pl.pallas_call(
        functools.partial(output_kernel, sets, picks, flat, quick, len(w_ops)),
        grid=(slots,),
        in_specs=[pl.BlockSpec(memory_space=pltpu.SMEM), chan(nout)]
        + [pl.BlockSpec((None, block // 4, CB), lambda s: (s, 0, 0)), full(bh)]
        + [full(up), full(tok), full(masked)] + w_specs,
        out_specs=[
            pl.BlockSpec((length, width), lambda s: (0, 0)),
            pl.BlockSpec((None, rank, block), lambda s: (s, 0, 0)),
            pl.BlockSpec((rank, width), lambda s: (0, 0)),
        ],
        out_shape=[
            jax.ShapeDtypeStruct((length, width), bf16),
            jax.ShapeDtypeStruct((slots, rank, ch), f32),
            jax.ShapeDtypeStruct((rank, width), f32),
        ],
        scratch_shapes=[pltpu.VMEM((length, width), f32), pltpu.VMEM((rank, length), f32)],
        compiler_params=compiler_params(1),
        cost_estimate=cost(2 * slots * ch * length * width, slots * ch * width * 2),
        name="output",
    )(sc, nout, pk, bh, up, tok, masked, *w_ops)


def gate_back_kernel(sets, picks, n_w, *refs):
    dz, low = refs[:2]
    acc, gz_o = refs[-2:]
    slot = pl.program_id(0)

    @pl.when(slot == 0)
    def _():
        acc[...] = jnp.zeros_like(acc)

    gz_o[...] = dot(low[:, HALO:], dz[...], NT)
    add_products(acc, jnp.transpose(dz[...]), sets, picks, refs[2 : 2 + n_w], slot)


def gate_back_call(dz, low, weights, picks, width, later=()):
    slots, ch, length = dz.shape
    rank = low.shape[0]
    block = ch
    w_ops, w_specs, sets = product_specs(weights, ch // len(picks))
    return pl.pallas_call(
        functools.partial(gate_back_kernel, sets, picks, len(w_ops)),
        grid=(slots,),
        in_specs=[
            pl.BlockSpec((None, block, length), lambda s: (s, 0, 0)),
            pl.BlockSpec(low.shape, lambda s: (0, 0)),
        ]
        + w_specs
        + [pl.BlockSpec(memory_space=pl.ANY)] * len(later),
        out_specs=[
            pl.BlockSpec((length, width), lambda s: (0, 0)),
            pl.BlockSpec((None, rank, block), lambda s: (s, 0, 0)),
        ],
        out_shape=[
            jax.ShapeDtypeStruct((length, width), f32),
            jax.ShapeDtypeStruct((slots, rank, ch), f32),
        ],
        compiler_params=compiler_params(1),
        cost_estimate=cost(2 * slots * ch * length * width, 2 * slots * ch * width),
        name="gate_back",
    )(dz, low, *w_ops, *later)


def beyond(near, taps, rows):
    parts = [jnp.zeros((HALO - 3, rows), f32)]
    for i in range(3):
        total = near[i : i + 1] * taps[0:1]
        for k in range(1, i + 1):
            total = total + near[i - k : i - k + 1] * taps[k : k + 1]
        parts.append(total)
    return jnp.transpose(jnp.concatenate(parts, axis=0))


def input_kernel(sets, picks, flat, quick, n_w, n_small, *refs):
    (sc, dx, tail, near, num, left, maps_tail, maps_near, maps_taps) = refs[:9]
    (dl, near_dl, down, root_r, gain, tok, masked, start) = refs[9:17]
    smalls = refs[17 : 17 + n_small]
    wrefs = refs[17 + n_small : 17 + n_small + n_w]
    out, acc = refs[-2:]
    slot = pl.program_id(0)
    length, width = tok.shape
    cut = length - HALO

    @pl.when(slot == 0)
    def _():
        d_low = jnp.concatenate(
            [dl[:, HALO:length], dl[:, length:] + near_dl[:, :HALO]], axis=1
        ).astype(bf16)
        low = jnp.transpose(d_low)
        n_maps = maps_tail.shape[0]
        maps_last = maps_tail[...] + beyond(maps_near[:, :n_maps], maps_taps, n_maps)
        maps_left = jnp.concatenate([left[:n_maps, :cut], maps_last.astype(bf16)], axis=1)
        total = start[...] + dot(maps_left, smalls[0][...], TN)
        row = n_maps
        for w in smalls[1:]:
            total = total + dot(left[row : row + w.shape[0], :], w[...], TN)
            row += w.shape[0]
        acc[...] = total
        for i, m in enumerate(flat):
            at = pl.ds(block_at(sc[0], m, quick), CB)
            acc[:, i * CB : (i + 1) * CB] += dot(low, down[at, :], NT)

    block = dx.shape[0]
    taps = jnp.concatenate(
        [
            num[b * 64 + 48 : b * 64 + 56, :].astype(f32)
            + num[b * 64 + 56 : b * 64 + 64, :].astype(f32)
            for b in range(block // CB)
        ],
        axis=1,
    )
    last = tail[...] + beyond(near[...], taps, block)
    dx_all = jnp.concatenate([dx[:, :cut], last.astype(bf16)], axis=1)
    add_products(acc, jnp.transpose(dx_all), sets, picks, wrefs, slot)

    @pl.when(slot == pl.num_programs(0) - 1)
    def _():
        root = root_r[...]
        mean = None
        for i, m in enumerate(flat):
            at = pl.ds(block_at(sc[0], m, quick), CB)
            cols = slice(i * CB, (i + 1) * CB)
            scaled = acc[:, cols] * gain[:, at]
            acc[:, cols] = scaled
            part = jnp.sum(scaled * tok[:, at].astype(f32), axis=1, keepdims=True)
            mean = part if mean is None else mean + part
        coef = root * root * root * (mean * (1.0 / width))
        for i, m in enumerate(flat):
            at = pl.ds(block_at(sc[0], m, quick), CB)
            d_resid = root * acc[:, i * CB : (i + 1) * CB] - tok[:, at].astype(f32) * coef
            out[:, at] = (masked[:, at].astype(f32) + d_resid).astype(bf16)


def input_call(
    sc, dx, tail, near, pk, left, maps_tail, maps_taps, dl, down, root, gain, tok, masked, start,
    smalls, weights, picks, flat, quick, later=(),
):
    slots, ch, length = dx.shape
    width = tok.shape[1]
    block = ch
    rank = dl.shape[0]
    once = pl.Buffered(1)
    full = lambda a: pl.BlockSpec(a.shape, lambda s: (0,) * a.ndim, pipeline_mode=once)
    chan = lambda a: pl.BlockSpec((None, block, a.shape[2]), lambda s: (s, 0, 0))
    w_ops, w_specs, sets = product_specs(weights, ch // len(picks))
    near_rows = pl.BlockSpec((8, block), lambda s: ((s + slots - 1) % slots, 0))
    near_maps = pl.BlockSpec((8, ch), lambda s: (slots, 0), pipeline_mode=once)
    near_low = pl.BlockSpec(
        (rank, ch), lambda s: (((slots + 1) * 8 + rank - 1) // rank, 0), pipeline_mode=once
    )
    return pl.pallas_call(
        functools.partial(input_kernel, sets, picks, flat, quick, len(w_ops), len(smalls)),
        grid=(slots,),
        in_specs=[pl.BlockSpec(memory_space=pltpu.SMEM), chan(dx), chan(tail), near_rows]
        + [pl.BlockSpec((None, block // 4, CB), lambda s: (s, 0, 0))]
        + [full(left), full(maps_tail), near_maps, full(maps_taps), full(dl), near_low]
        + [full(a) for a in [down, root, gain, tok, masked, start] + list(smalls)]
        + w_specs
        + [pl.BlockSpec(memory_space=pl.ANY)] * len(later),
        out_specs=pl.BlockSpec((length, width), lambda s: (0, 0)),
        out_shape=jax.ShapeDtypeStruct((length, width), bf16),
        scratch_shapes=[pltpu.VMEM((length, width), f32)],
        compiler_params=compiler_params(1),
        cost_estimate=cost(2 * slots * ch * length * width, 2 * slots * ch * width),
        name="input_back",
    )(
        sc, dx, tail, near, pk, left, maps_tail, near, maps_taps, dl, near, down, root, gain, tok,
        masked, start, *smalls, *w_ops, *later
    )


def assemble_kernel(n, single, ch, ids, *refs):
    parts = refs[:n]
    down_o, up_o, down_out_o, up_out_o = refs[n:]
    here = down_o.shape[0]
    width = down_o.shape[2]
    first = pl.program_id(0) * here
    blocks = [(ref, b) for ref in parts for b in range(ref.shape[0])]

    def put(a, total):
        up_o[a, :, 0, :] = total[:, :ch]
        up_o[a, :, 1, :] = total[:, ch : 2 * ch]
        down_out_o[a] = total[:, 2 * ch : 3 * ch]
        down_o[a] = total[:, 3 * ch : 3 * ch + width]
        up_out_o[a] = total[:, 3 * ch + width :]

    for a in range(here):
        if single:
            for m, (ref, b) in enumerate(blocks):

                @pl.when(ids[m] == first + a)
                def _(ref=ref, b=b, a=a):
                    put(a, ref[b].astype(f32))

        else:
            total = None
            for m, (ref, b) in enumerate(blocks):
                chosen = jnp.where(ids[m] == first + a, 1.0, 0.0)
                term = ref[b].astype(f32) * chosen
                total = term if total is None else total + term
            put(a, total)


def assemble_call(ids, parts, adapters, ch, width):
    rank = parts[0].shape[1]
    each = adapters // 2 if adapters % 2 == 0 else adapters
    single = ids.shape[0] == adapters
    return pl.pallas_call(
        functools.partial(assemble_kernel, len(parts), single, ch),
        grid=(adapters // each,),
        in_specs=[pl.BlockSpec(memory_space=pltpu.SMEM)]
        + [pl.BlockSpec(a.shape, lambda i: (0, 0, 0)) for a in parts],
        out_specs=[
            pl.BlockSpec((each, rank, width), lambda i: (i, 0, 0)),
            pl.BlockSpec((each, rank, 2, ch), lambda i: (i, 0, 0, 0)),
            pl.BlockSpec((each, rank, ch), lambda i: (i, 0, 0)),
            pl.BlockSpec((each, rank, width), lambda i: (i, 0, 0)),
        ],
        out_shape=[
            jax.ShapeDtypeStruct((adapters, rank, width), f32),
            jax.ShapeDtypeStruct((adapters, rank, 2, ch), f32),
            jax.ShapeDtypeStruct((adapters, rank, ch), f32),
            jax.ShapeDtypeStruct((adapters, rank, width), f32),
        ],
        compiler_params=compiler_params(1),
        cost_estimate=cost(1e7, 2e7),
        name="assemble",
    )(ids, *parts)


def body(
    tokens,
    cotangent,
    lengths,
    adapter_ids,
    pre_gain,
    in_inner,
    in_maps,
    in_steps,
    conv_inner,
    conv_maps,
    step_bias,
    decay_log,
    skip_gain,
    norm_gain,
    out_weight,
    adapter_in_down,
    adapter_in_up,
    adapter_out_down,
    adapter_out_up,
):
    planes = lax.axis_size("tensor")
    seqs = lax.axis_size("dp")
    place = lax.axis_index("tensor")
    mine = lax.axis_index("dp")
    length = tokens.shape[1]
    width = tokens.shape[2]
    rows_here = in_inner.shape[0]
    ch = in_inner.shape[2]
    inner = ch * planes
    hs = in_steps.shape[1]
    heads = hs * planes
    rank = adapter_in_down.shape[2]
    adapters = adapter_in_down.shape[0]
    state_w = in_maps.shape[1] // 2
    hb = CB // HEAD
    ncb = ch // CB
    nblk = planes * ncb
    nsub = length // SUB
    quick = seqs == 8 and planes == 4

    def from_plane(v, j):
        return lax.ppermute(v, "tensor", [((s + j) % planes, s) for s in range(planes)])

    def flip(v, bit):
        return lax.ppermute(v, "dp", [(i, i ^ bit) for i in range(seqs)])

    def slot_order(v, first=0, at=place):
        return [
            lax.dynamic_index_in_dim(v, (at + j) % planes, 0, keepdims=False)
            for j in range(first, planes)
        ]

    def by_slot(v):
        return jnp.stack(slot_order(lax.all_gather(v, "tensor", axis=0)))

    def to_slots(rows, whole):
        total = jnp.concatenate([rows[0], whole], axis=1)
        for j in range(1, planes):
            part = jnp.concatenate([rows[j], whole], axis=1).astype(bf16)
            total = total + lax.ppermute(
                part, "tensor", [(s, (s + j) % planes) for s in range(planes)]
            ).astype(f32)
        return total

    flat = [0, 2, 4, 6, 1, 3, 5, 7] if quick else list(range(width // CB))
    if quick:
        picks = [
            [(0, 0), (0, 1), (1, 0), (1, 1), (2, 0), (2, 1), (3, 0), (3, 1)],
            [(0, 0), (1, 0), (0, 1), (1, 1), (2, 0), (3, 0), (2, 1), (3, 1)],
        ]
    else:
        picks = [[(0, 0)]]
    half = planes // 2

    def halves(parts, more=((), ())):
        cut = ch // 2
        return [
            jnp.concatenate([v[:cut] for v in parts] + list(more[0]), axis=0),
            jnp.concatenate([v[cut:] for v in parts] + list(more[1]), axis=0),
        ]

    def pass_one(ab):
        return [flip(ab[0], 2), flip(ab[1], 4)]

    def pass_two(ab):
        return [flip(ab[0], 4), flip(ab[1], 2)]

    def pass_core(arrays):
        return [flip(v, 1) for v in arrays]

    def as_paths(arrays, swapped):
        return [[arrays[k], arrays[k + 2], swapped[k], swapped[k + 2]] for k in range(2)]

    pick = adapter_ids[0]
    down_in = lax.dynamic_index_in_dim(adapter_in_down, pick, 0, keepdims=False)
    up_here = lax.dynamic_index_in_dim(adapter_in_up, pick, 0, keepdims=False)
    down_here = lax.dynamic_index_in_dim(adapter_out_down, pick, 0, keepdims=False)
    up_out = lax.dynamic_index_in_dim(adapter_out_up, pick, 0, keepdims=False)
    numbers = jnp.concatenate(
        [
            conv_inner,
            jnp.repeat(skip_gain, HEAD)[None],
            norm_gain[None],
            jnp.pad(jnp.stack([step_bias, decay_log]), ((0, 0), (0, ch - hs))),
        ],
        axis=0,
    )
    coarse = lax.optimization_barrier(numbers.astype(bf16))
    fine = lax.optimization_barrier((numbers - coarse.astype(f32)).astype(bf16))
    packed = jnp.concatenate(
        [jnp.transpose(up_here, (1, 0, 2)).reshape(2 * rank, ch), down_here.T, coarse, fine],
        axis=0,
    )
    packed = jnp.swapaxes(packed.reshape(64, ncb, CB), 0, 1).reshape(64 * ncb, CB)
    last_rows = tokens[0, -16:].reshape(16 * width // CB, CB)
    halo = [(s, s + 1) for s in range(planes - 1)]
    wt = jnp.transpose(in_inner, (1, 2, 0))
    maps_w = in_maps.T
    steps_w = in_steps.T
    own_rows = 3 * ch // 2
    if quick:
        own = halves(
            [wt[0], wt[1], out_weight],
            (
                [maps_w[:state_w], steps_w, jnp.full((16, rows_here), pick).astype(bf16)],
                [maps_w[state_w:]],
            ),
        )
        got = pass_one(own)
        all_x = lax.all_gather(
            jnp.concatenate([wt[1], packed, steps_w, last_rows], axis=0), "tensor", axis=0
        )
        all_z = lax.all_gather(wt[0], "tensor", axis=0)
        all_o = lax.all_gather(out_weight, "tensor", axis=0)
        token, _, own = hold([], [], zip(own, got))
        two = pass_two(own)
        swapped = pass_core(own)
        marks = [ch, ch + 64 * ncb, ch + 64 * ncb + hs]
        ends = all_x.shape[1]

        def rows_of(j, lo, hi):
            start = ((place + j) % planes, lo, 0)
            return lax.dynamic_slice(all_x, start, (1, hi - lo, rows_here))[0]

        pk = jnp.stack([rows_of(j, marks[0], marks[1]) for j in range(planes)])
        last_rows = rows_of(planes - 1, marks[2], ends)
        far_x = list(
            far_call(jnp.reshape(place, (1,)).astype(jnp.int32), all_x, ch, marks[1], hs)
        )
        token, passed, _ = hold(swapped, two + far_x)
        two, far_x = passed[:2], passed[2:]
        own = own + two
        swapped = swapped + pass_core(two)
        got = pass_one(far_x)
        held = [token]
    else:
        pk = by_slot(packed)
        last_rows = by_slot(last_rows)[planes - 1]
        steps_w = by_slot(steps_w)
        held = []
    before = last_rows.reshape(16, width)
    before = jnp.where(place > 0, before, jnp.zeros_like(before))
    sc = jnp.stack([mine, lengths[0] - place * length]).astype(jnp.int32)
    normed, masked, root, low2, back2, nt, gt = turn_call(
        sc, tokens[0], before, cotangent[0], pre_gain[None], down_in, up_out, flat, quick, held
    )
    if quick:
        own = as_paths(own, swapped)
        token, _, far_x = hold([nt, pk] + own[0] + own[1], [], zip(far_x, got))
        two = pass_two(far_x)
        swapped = pass_core(far_x)
        held = [token]
        all_maps, all_steps = own, own[0]
        maps_at, maps_rows = own_rows, state_w
        steps_at, mine_slots = own_rows + state_w, 1
    else:
        all_maps = [[lax.all_gather(maps_w, "dp", axis=1, tiled=True)[None]]]
        all_steps = steps_w.reshape(heads, rows_here)
        all_steps = [lax.all_gather(all_steps, "dp", axis=1, tiled=True)[None]]
        maps_at, maps_rows = 0, 2 * state_w
        steps_at, mine_slots = 0, planes
    bt, ct, b_low, c_low, cbt, maps_pre, maps_w = maps_call(
        all_maps, maps_at, maps_rows, picks, nt, conv_maps, length, held
    )
    hp, step_sig, speed, mine_w, found = steps_call(
        all_steps, steps_at, picks[0], nt, pk, 0, mine_slots, hs, length, held,
        tuple(flat) if quick else None,
    )
    small_w = [maps_w, mine_w]
    if quick:
        ids = found[:, 0].astype(jnp.int32)
    else:
        ids = lax.all_gather(adapter_ids, "dp", axis=0, tiled=True)

    x_args = (picks, nt, low2, pk, ch)
    z_args = (picks, nt, low2, pk, ch, HALO, False)
    o_args = (picks, gt, back2, pk, ch, 0, True)
    if quick:
        empty = [None] * 4
        bufs, _ = scan_call(
            0, 1, (own, 1), 0, *x_args, hp, ct, b_low, cbt, empty + [None], held
        )
        sent_a = bufs[4]
        bufs, done = scan_call(
            0, 1, (own, 1), 1, *x_args, hp, ct, b_low, cbt, bufs[:4] + [None], held
        )
        sent_b = bufs[4]
        far_z = halves(slot_order(all_z, 1, place + token[0, 0].astype(jnp.int32)))

        token, passed, _ = hold([done] + swapped, two + far_z)
        two, far_z = passed[:2], passed[2:]
        far_x = as_paths(far_x + two, swapped + pass_core(two))
        got = pass_one(far_z)
        z, beside = proj_call(0, 1, (own, 0), *z_args, None, [token])
        wgt, beside = proj_call(0, 1, (own, 2), *o_args, None, [beside])
        far_o = halves(slot_order(all_o, 1, place + beside[0, 0].astype(jnp.int32)))

        token, far_o, far_z = hold([beside] + far_x[0] + far_x[1], far_o, zip(far_z, got))
        two = pass_two(far_z)
        swapped = pass_core(far_z)
        hp_far, sig_far, speed_far, far_w, _ = steps_call(
            far_x[0], own_rows, picks[0], nt, pk, 1, planes, hs, length, [token]
        )
        hp = jnp.concatenate([hp, hp_far], axis=0)
        step_sig = jnp.concatenate([step_sig, sig_far], axis=0)
        speed = jnp.concatenate([speed, speed_far], axis=0)
        small_w.append(far_w)
        bufs, _ = scan_call(
            1, planes, (far_x, 0), 0, *x_args, hp, ct, b_low, cbt, bufs[:4] + [sent_a], [token]
        )
        ent_a = lax.ppermute(bufs[4], "tensor", halo)
        bufs, done = scan_call(
            1, planes, (far_x, 0), 1, *x_args, hp, ct, b_low, cbt, bufs[:4] + [sent_b], [token]
        )
        ent_b = lax.ppermute(bufs[4], "tensor", halo)
        token, passed, _ = hold([done] + swapped, two + far_o + [ent_a])
        two, far_o, (ent_a,) = passed[:2], passed[2:4], passed[4:]
        far_z = as_paths(far_z + two, swapped + pass_core(two))
        got = pass_one(far_o)
        ent_a = lax.ppermute(hop_call(ent_a, 1, bufs[3], hp, 0, [token]), "tensor", halo)

        token, passed, far_o = hold(far_z[0] + far_z[1], [ent_a, ent_b], zip(far_o, got))
        ent_a, ent_b = passed
        two = pass_two(far_o)
        send_b = hop_call(ent_b, 1, bufs[3], hp, 1, [token])
        ent_b = lax.ppermute(send_b, "tensor", halo)
        send_a = hop_call(ent_a, 1, bufs[3], hp, 0, [token])
        ent_a = lax.ppermute(send_a, "tensor", halo)
        z, done = proj_call(1, planes, (far_z, 0), *z_args, z, [send_a, send_b])

        token, passed, _ = hold([done], two + far_o + [ent_a, ent_b])
        two, far_o, (ent_a, ent_b) = passed[:2], passed[2:4], passed[4:]
        far_o = as_paths(far_o + two, pass_core(far_o + two))
        send_b = hop_call(ent_b, 1, bufs[3], hp, 1, [token])
        ent_b = lax.ppermute(send_b, "tensor", halo)
        wgt, done = proj_call(1, planes, (far_o, 0), *o_args, wgt, [send_b])
        _, ent, _ = hold([done], [ent_a, ent_b])
        z_sets = [((0, 1), own, 0), ((1, planes), far_z, 0)]
        x_sets = [((0, 1), own, 1), ((1, planes), far_x, 0)]
        o_sets = [((0, 1), own, 2), ((1, planes), far_o, 0)]
    else:
        w = lax.all_gather(wt, "dp", axis=2, tiled=True)
        w = by_slot(w)
        o = lax.all_gather(out_weight, "dp", axis=1, tiled=True)
        flat_rows = lambda v: [[v.reshape(1, inner, width)]]
        wz, wx = flat_rows(w[:, 0]), flat_rows(w[:, 1])
        o = flat_rows(by_slot(o))
        bufs, _ = scan_call(
            0, planes, (wx, 0), 0, *x_args, hp, ct, b_low, cbt, [None] * 5
        )
        z, _ = proj_call(0, planes, (wz, 0), *z_args, None)
        wgt, _ = proj_call(0, planes, (o, 0), *o_args, None)
        ent = lax.ppermute(bufs[4], "tensor", halo)
        for _ in range(planes - 2):
            ent = lax.ppermute(hop_call(ent, 1, bufs[3], hp), "tensor", halo)
        ent = [ent]
        z_sets = [((0, planes), wz, 0)]
        x_sets = [((0, planes), wx, 0)]
        o_sets = [((0, planes), o, 0)]
    xc, mix, loc, s_end, _ = bufs
    left = [(s + 1, s) for s in range(planes - 1)]

    nout, dy, dz, sl, sl_sent = gate_call(z, mix, wgt, ent, pk, hp, ct, c_low, inner)

    adj = lax.ppermute(sl_sent, "tensor", left)
    mixed, grad_down_out, grad_up_out = output_call(
        sc, nout, pk, back2, up_out, tokens[0], masked, o_sets, picks, flat, quick
    )
    send = hop_call(adj, planes - 1, sl, hp, 0, [mixed])
    adj = lax.ppermute(send, "tensor", left)
    d_normed, grad_z = gate_back_call(dz, low2, z_sets, picks, width, [send])
    send = hop_call(adj, planes - 1, sl, hp, 0, [d_normed])
    adj = lax.ppermute(send, "tensor", left)
    for _ in range(planes - 4):
        adj = lax.ppermute(hop_call(adj, planes - 1, sl, hp), "tensor", left)
    dxs, u1, u2, kl, dcb, db1, dc1 = back_call(
        dy, xc, hp, ent, loc, ct, c_low, bt, cbt, [send]
    )

    early = to_slots(
        [jnp.concatenate([grad_z[j], grad_down_out[j]], axis=1) for j in range(planes)],
        grad_up_out,
    )
    (dx, tail, head, grad_x, d_low, ddelta, u2f, kf, db3) = finish_call(
        dxs, dy, xc, dz, pk, hp, ent, adj, bt, low2, [mixed, early]
    )
    small_left, maps_tail, maps_head, grad_down = glue_call(
        [dcb, db1, db3, dc1, bt, ct, maps_pre, u1, u2, kl, ddelta, u2f, kf, step_sig, speed]
        + [conv_maps],
        sc, d_low, nt, state_w, length, heads, flat, quick,
    )

    to_left = jnp.concatenate(
        [
            head.reshape(8 * planes, ch),
            jnp.pad(maps_head, ((0, 0), (0, ch - 2 * state_w))),
            jnp.zeros((-(8 * planes + 8) % rank, ch), f32),
            jnp.pad(d_low[:, :HALO], ((0, 0), (0, ch - HALO))),
        ],
        axis=0,
    )
    near = lax.ppermute(to_left, "tensor", left)
    late = to_slots([grad_x[j] for j in range(planes)], grad_down)
    sent = jnp.concatenate(
        [
            early[:, :ch],
            late[:, :ch],
            early[:, ch : 2 * ch],
            late[:, ch:],
            early[:, 2 * ch :],
        ],
        axis=1,
    ).astype(bf16)[None]
    if quick:
        _, (sent,), _ = hold([near], [sent])
        both = jnp.concatenate([sent, flip(sent, 1)], axis=0)
        by_seq = [both] + [flip(both, bit) for bit in (2, 4, 6)]
    else:
        by_seq = [lax.all_gather(sent[0], "dp", axis=0)]

    tokens_grad = input_call(
        sc, dx, tail, near, pk, small_left, maps_tail, conv_maps, d_low, down_in, root,
        pre_gain[None], tokens[0], masked, d_normed, small_w, x_sets, picks, flat, quick,
    )
    if quick:
        _, by_seq, _ = hold([tokens_grad], by_seq)
    g_down, g_up, g_down_out, g_up_out = assemble_call(ids, by_seq, adapters, ch, width)
    g_down = jnp.swapaxes(g_down, 1, 2)
    g_down_out = jnp.swapaxes(g_down_out, 1, 2)
    return (mixed[None], tokens_grad[None], g_down, g_up, g_down_out, g_up_out)


def solution(mesh):
    placed = (
        P("dp", "tensor", None),
        P("dp", "tensor", None),
        P("dp"),
        P("dp"),
        P(),
        P("dp", None, "tensor"),
        P("dp", None),
        P("dp", "tensor"),
        P(None, "tensor"),
        P(),
        P("tensor"),
        P("tensor"),
        P("tensor"),
        P("tensor"),
        P("tensor", "dp"),
        P(),
        P(None, None, None, "tensor"),
        P(None, "tensor", None),
        P(),
    )
    return jax.shard_map(
        body,
        mesh=mesh,
        in_specs=placed,
        out_specs=(
            P("dp", "tensor", None),
            P("dp", "tensor", None),
            P(),
            P(None, None, None, "tensor"),
            P(None, "tensor", None),
            P(),
        ),
        check_vma=False,
    )
```

```python
import functools

import jax
import jax.numpy as jnp
from jax import lax
from jax.experimental import pallas as pl
from jax.experimental.pallas import tpu as pltpu
from jax.sharding import PartitionSpec as P

f32 = jnp.float32
bf16 = jnp.bfloat16
epsilon = 1e-05
highest = lax.Precision.HIGHEST
LOG2E = 1.4426950408889634
HEAD = 64
HALO = 128
SUB = 256
CB = 256
ROWS = 32

NN = ((1,), (0,))
NT = ((1,), (1,))
TN = ((0,), (0,))


def dot(a, b, dims=NN):
    return lax.dot_general(a, b, (dims, ((), ())), preferred_element_type=f32)


def compiler_params(grid_rank):
    return pltpu.CompilerParams(
        dimension_semantics=("arbitrary",) * grid_rank, vmem_limit_bytes=60 * 2**20
    )


def cost(flops, size):
    return pl.CostEstimate(
        flops=int(flops) // 8, bytes_accessed=int(size) // 8, transcendentals=0
    )


def entering(refs, b):
    per = refs[0].shape[0] // CB
    rows = pl.ds(pl.multiple_of(b % per * CB, CB), CB)
    out = refs[0][rows, :]
    for p in range(1, len(refs)):
        out = jnp.where(b // per == p, refs[p][rows, :], out)
    return out


def kind_rows(packed, b, kind):
    return packed.at[pl.ds(pl.multiple_of(b * 64 + kind * 16, 16), 16)]


def block_rows(ref, b):
    return ref.at[pl.ds(pl.multiple_of(b * CB, CB), CB)]


def sigmoid(v):
    return 0.5 + 0.5 * jnp.tanh(0.5 * v)


def columns(numbers):
    v = numbers[...].astype(f32)
    return jnp.transpose(v[:8] + v[8:])


def spread(numbers, which):
    row = lax.broadcasted_iota(jnp.int32, (16, 128 * len(which)), 0) % 8
    col = lax.broadcasted_iota(jnp.int32, (16, 128 * len(which)), 1) // 128
    pick = jnp.zeros(row.shape, f32)
    for k, n in enumerate(which):
        pick = jnp.where((row == n) & (col == k), 1.0, pick)
    return dot(numbers[...], pick.astype(bf16), TN)


def lanes_of(values, width):
    return jnp.concatenate([values] * (width // 128), axis=1)


def tall(rows):
    return jnp.transpose(jnp.concatenate([rows, rows], axis=0))


def conv_values(raw, chan):
    out = raw * chan[:, 3:4]
    for k in range(3):
        out = out + pltpu.roll(raw, 3 - k, 1) * chan[:, k : k + 1]
    return out[:, HALO:]


def conv_rows(raw, taps, shift):
    width = raw.shape[1]
    out = raw * lanes_of(taps[3], width)
    for k in range(3):
        out = out + pltpu.roll(raw, shift(k), 1) * lanes_of(taps[k], width)
    return out


def per_head(values, rows):
    hb = rows.shape[0]
    parts = [values[h * HEAD : (h + 1) * HEAD] * rows[h : h + 1] for h in range(hb)]
    return jnp.concatenate(parts, axis=0)


def head_sums(values, hb):
    parts = [
        jnp.sum(values[h * HEAD : (h + 1) * HEAD], axis=0, keepdims=True) for h in range(hb)
    ]
    return jnp.concatenate(parts, axis=0)


def joined(refs, picks, rows=slice(None)):
    parts = [refs[k][b, rows] for k, b in picks]
    return parts[0] if len(parts) == 1 else jnp.concatenate(parts, axis=1)


def block_at(mine, m, quick):
    return pl.multiple_of((mine ^ m) * CB, CB) if quick else m * CB


def turn_kernel(flat, quick, *refs):
    (sc, tok_r, bef_r, cot_r, gain, down, up) = refs[:7]
    normed_o, masked_o, root_o, low_o, back_o, nt_o, gt_o, halo_sc = refs[-8:]
    width = tok_r.shape[1]
    length = tok_r.shape[0]

    def norm(v):
        v = v.astype(f32)
        root = lax.rsqrt(jnp.sum(v * v, axis=1, keepdims=True) * (1.0 / width) + epsilon)
        return (v * root * gain[...]).astype(bf16), root

    normed, root = norm(tok_r[...])
    normed_o[...] = normed
    root_o[...] = root
    halo_sc[...] = jnp.zeros_like(halo_sc)
    halo_sc[HALO - 16 :, :] = norm(bef_r[...])[0]
    rows = lax.broadcasted_iota(jnp.int32, (length, 1), 0)
    masked_o[...] = jnp.where(rows < sc[1], cot_r[...].astype(f32), 0.0).astype(bf16)
    low = back = None
    for i, m in enumerate(flat):
        at = pl.ds(block_at(sc[0], m, quick), CB)
        nt = jnp.concatenate(
            [jnp.transpose(halo_sc[:, at]), jnp.transpose(normed_o[:, at])], axis=1
        )
        gt = jnp.transpose(masked_o[:, at])
        nt_o[i * CB : (i + 1) * CB, :] = nt
        gt_o[i * CB : (i + 1) * CB, :] = gt
        low_m = dot(down[at, :], nt, TN)
        back_m = dot(up[:, at], gt)
        low = low_m if low is None else low + low_m
        back = back_m if back is None else back + back_m
    low_o[...] = low.astype(bf16)
    back_o[...] = back.astype(bf16)


def turn_call(sc, tokens, before, cot, gain, down, up, flat, quick, later):
    length, width = tokens.shape
    rank = up.shape[0]
    ext = length + HALO
    vm = pl.BlockSpec(memory_space=pltpu.VMEM)
    return pl.pallas_call(
        functools.partial(turn_kernel, flat, quick),
        in_specs=[pl.BlockSpec(memory_space=pltpu.SMEM)] + [vm] * 6
        + [pl.BlockSpec(memory_space=pl.ANY)] * len(later),
        out_specs=[vm] * 7,
        out_shape=[
            jax.ShapeDtypeStruct((length, width), bf16),
            jax.ShapeDtypeStruct((length, width), bf16),
            jax.ShapeDtypeStruct((length, 1), f32),
            jax.ShapeDtypeStruct((rank, ext), bf16),
            jax.ShapeDtypeStruct((rank, length), bf16),
            jax.ShapeDtypeStruct((width, ext), bf16),
            jax.ShapeDtypeStruct((width, length), bf16),
        ],
        scratch_shapes=[pltpu.VMEM((HALO, width), bf16)],
        compiler_params=compiler_params(0),
        cost_estimate=cost(length * width * 200, length * width * 16),
        name="turn",
    )(sc, tokens, before, cot, gain, down, up, *later)


def row_specs(paths, first, rows):
    ops, specs = [], []
    for arrays in paths:
        for a in arrays:
            ops.append(a)
            specs.append(
                pl.BlockSpec((a.shape[0], rows, a.shape[2]), lambda i: (0, first // rows, 0))
            )
    return ops, specs


def maps_kernel(n_w, picks, sub, *refs):
    nt, taps = refs[n_w : n_w + 2]
    bt_o, ct_o, bn_o, cn_o, cbt_o, pre_o, w_o = refs[-7:]
    length = bt_o.shape[1]
    state_w = bt_o.shape[0]
    per = n_w // len(picks)
    w = jnp.concatenate(
        [joined(refs[p * per : (p + 1) * per], order) for p, order in enumerate(picks)], axis=0
    )
    w_o[...] = w
    maps_pre = conv_values(dot(w, nt[...]), tall(taps[...]))
    pre_o[...] = maps_pre
    maps = (maps_pre * sigmoid(maps_pre)).astype(bf16)
    bt, ct = maps[:state_w], maps[state_w:]
    bt_o[...] = bt
    ct_o[...] = ct
    bn = jnp.transpose(bt)
    bn_o[...] = bn
    cn_o[...] = jnp.transpose(ct)
    row = lax.broadcasted_iota(jnp.int32, (sub, sub), 0)
    col = lax.broadcasted_iota(jnp.int32, (sub, sub), 1)
    upto = jnp.where(row <= col, 1.0, 0.0)
    for s in range(length // sub):
        cols = slice(s * sub, (s + 1) * sub)
        cbt_o[s] = upto * dot(bn[cols, :], ct[:, cols])


def maps_call(paths, first, rows, picks, nt, taps, length, later):
    ops, specs = row_specs(paths, first, rows)
    state_w = rows * len(picks) // 2
    vm = pl.BlockSpec(memory_space=pltpu.VMEM)
    n_w = len(ops)
    return pl.pallas_call(
        functools.partial(maps_kernel, n_w, picks, SUB),
        grid=(1,),
        in_specs=specs + [vm, vm] + [pl.BlockSpec(memory_space=pl.ANY)] * len(later),
        out_specs=[vm] * 7,
        out_shape=[
            jax.ShapeDtypeStruct((state_w, length), bf16),
            jax.ShapeDtypeStruct((state_w, length), bf16),
            jax.ShapeDtypeStruct((length, state_w), bf16),
            jax.ShapeDtypeStruct((length, state_w), bf16),
            jax.ShapeDtypeStruct((length // SUB, SUB, SUB), f32),
            jax.ShapeDtypeStruct((2 * state_w, length), f32),
            jax.ShapeDtypeStruct((2 * state_w, nt.shape[0]), bf16),
        ],
        compiler_params=compiler_params(1),
        cost_estimate=cost(nt.shape[0] * nt.shape[1] * 512, nt.size * 2 + nt.shape[0] * 1024),
        name="maps",
    )(*ops, nt, taps, *later)


def steps_kernel(n_w, order, hb, sub, lo, hi, hs, flat, *refs):
    nt, numbers = refs[n_w : n_w + 2]
    hp_o, sig_o, speed_o, w_o, ids_o = refs[-5:]
    if flat is None:
        ids_o[...] = jnp.zeros_like(ids_o)
    else:
        marks = joined(refs[n_w + 2 : 2 * n_w + 2], order).astype(f32)
        spots = [flat.index(m) * CB for m in range(len(flat))]
        ids_o[...] = jnp.concatenate([marks[:1, v : v + 128] for v in spots], axis=0)
    length = sig_o.shape[1]
    heads = sig_o.shape[0]
    w = joined(refs[:n_w], order)
    w_o[...] = w
    cols = [columns(numbers.at[j])[:hs] for j in range(lo, hi)]
    bias = jnp.concatenate([v[:, 6:7] for v in cols], axis=0)
    speed = jnp.exp(jnp.concatenate([v[:, 7:8] for v in cols], axis=0))
    speed_o[...] = jnp.broadcast_to(speed, (heads, 128))
    steps = dot(w, nt[:, HALO:]) + bias
    sig_o[...] = sigmoid(steps)
    delta = jnp.maximum(steps, 0.0) + jnp.log1p(jnp.exp(-jnp.abs(steps)))
    rates = -delta * speed
    row = lax.broadcasted_iota(jnp.int32, (sub, sub), 0)
    col = lax.broadcasted_iota(jnp.int32, (sub, sub), 1)
    upto = jnp.where(row <= col, 1.0, 0.0)
    before = None
    for s in range(length // sub):
        cols = slice(s * sub, (s + 1) * sub)
        cum = (
            lax.dot_general(
                rates[:, cols], upto, (NN, ((), ())), precision=highest,
                preferred_element_type=f32,
            )
            * LOG2E
        )
        cum_all = cum if before is None else cum + before
        before = cum_all[:, sub - 1 : sub]
        for b in range(heads // hb):
            mine = slice(b * hb, (b + 1) * hb)
            hp_o[b, :hb, cols] = cum[mine]
            hp_o[b, hb : 2 * hb, cols] = cum_all[mine]
            hp_o[b, 2 * hb :, cols] = delta[mine, cols]


def steps_call(arrays, first, order, nt, pk, lo, hi, hs, length, later, flat=None):
    heads = (hi - lo) * hs
    hb = CB // HEAD
    ops, specs = row_specs([arrays], first, heads)
    n_w = len(ops)
    marks = ([], []) if flat is None else row_specs([arrays], first + heads, 16)
    vm = pl.BlockSpec(memory_space=pltpu.VMEM)
    return pl.pallas_call(
        functools.partial(steps_kernel, n_w, order, hb, SUB, lo, hi, hs, flat),
        grid=(1,),
        in_specs=specs
        + [vm, pl.BlockSpec((pk.shape[0], 16, CB), lambda i: (0, 3, 0))]
        + marks[1]
        + [pl.BlockSpec(memory_space=pl.ANY)] * len(later),
        out_specs=[vm] * 5,
        out_shape=[
            jax.ShapeDtypeStruct((heads // hb, 3 * hb, length), f32),
            jax.ShapeDtypeStruct((heads, length), f32),
            jax.ShapeDtypeStruct((heads, 128), f32),
            jax.ShapeDtypeStruct((heads, nt.shape[0]), bf16),
            jax.ShapeDtypeStruct((8, 128), f32),
        ],
        compiler_params=compiler_params(1),
        cost_estimate=cost(nt.shape[0] * nt.shape[1] * 128, nt.size * 2),
        name="steps",
    )(*ops, nt, pk, *marks[0], *later)


def far_kernel(ch, first, hs, place, src, a_o, b_o):
    j = pl.program_id(0)
    half = ch // 2
    at = pl.ds(pl.multiple_of(j * half, half), half)
    a_o[at, :] = src[:half, :]
    b_o[at, :] = src[half:ch, :]
    steps = pl.ds(pl.multiple_of(pl.num_programs(0) * half + j * hs, hs), hs)
    a_o[steps, :] = src[first : first + hs, :]


def far_call(place, gathered, ch, first, hs):
    planes, rows, depth = gathered.shape
    n = planes - 1
    shapes = [(n * (ch // 2 + hs), depth), (n * ch // 2, depth)]
    return pl.pallas_call(
        functools.partial(far_kernel, ch, first, hs),
        grid_spec=pltpu.PrefetchScalarGridSpec(
            num_scalar_prefetch=1,
            grid=(n,),
            in_specs=[
                pl.BlockSpec((None, rows, depth), lambda j, p: ((p[0] + j + 1) % planes, 0, 0))
            ],
            out_specs=[pl.BlockSpec(v, lambda j, p: (0, 0)) for v in shapes],
        ),
        out_shape=[jax.ShapeDtypeStruct(v, bf16) for v in shapes],
        compiler_params=compiler_params(1),
        cost_estimate=cost(8, gathered.size * 4),
        name="far",
    )(place, gathered)


def hop_kernel(hb, shift, got, own, hp, *rest):
    out = rest[-1]
    slots, per, length = hp.shape[0], hp.shape[1], hp.shape[3]
    for s in range(slots):
        for c in range(per):
            rows = slice(c * CB, (c + 1) * CB)
            total = jnp.exp2(hp[s, c, hb : 2 * hb, length - 1 : length])
            came = got[(s + shift) % slots, rows, :].astype(f32)
            total = per_head(came, total) + own[s, rows, :].astype(f32)
            out[s, rows, :] = total.astype(bf16)


def hop_call(got, shift, own, hp, part=0, later=()):
    slots, rows, state_w = got.shape
    per = rows // CB
    by_slot = hp.reshape((slots, hp.shape[0] // slots) + hp.shape[1:])
    whole = lambda shape: pl.BlockSpec(shape, lambda i: (0,) * len(shape))
    return pl.pallas_call(
        functools.partial(hop_kernel, CB // HEAD, shift),
        grid=(1,),
        in_specs=[
            whole(got.shape),
            whole(own.shape),
            pl.BlockSpec((slots, per) + hp.shape[1:], lambda i: (0, part, 0, 0)),
        ]
        + [pl.BlockSpec(memory_space=pl.ANY)] * len(later),
        out_specs=whole(got.shape),
        out_shape=jax.ShapeDtypeStruct(got.shape, bf16),
        compiler_params=compiler_params(1),
        cost_estimate=cost(got.size * 4, got.size * 8),
        name="hop",
    )(got, own, by_slot, *later)


def hold_kernel(n_joined, *refs):
    outs = refs[-1 - n_joined :]
    for k in range(n_joined):
        outs[k][0] = refs[2 * k][...]
        outs[k][1] = refs[2 * k + 1][...]
    outs[-1][...] = jnp.zeros((1, 1), bf16)


def hold(deps, passed=(), pairs=()):
    anywhere = pl.BlockSpec(memory_space=pl.ANY)
    deps, passed, pairs = list(deps), list(passed), list(pairs)
    parts = [v for pair in pairs for v in pair]
    whole = lambda shape: pl.BlockSpec(shape, lambda i: (0,) * len(shape))
    first = len(parts) + len(deps)
    joined_shapes = [(2,) + pair[0].shape for pair in pairs]
    out = pl.pallas_call(
        functools.partial(hold_kernel, len(joined_shapes)),
        grid=(1,),
        in_specs=[whole(a.shape) for a in parts] + [anywhere] * (len(deps) + len(passed)),
        out_specs=[anywhere] * len(passed) + [whole(v) for v in joined_shapes] + [whole((1, 1))],
        out_shape=[jax.ShapeDtypeStruct(v.shape, v.dtype) for v in passed]
        + [jax.ShapeDtypeStruct(v, bf16) for v in joined_shapes]
        + [jax.ShapeDtypeStruct((1, 1), bf16)],
        input_output_aliases={first + k: k for k in range(len(passed))},
        compiler_params=compiler_params(1),
        cost_estimate=cost(8, 8),
        name="hold",
    )(*parts, *deps, *passed)
    n = len(passed)
    return out[-1], list(out[:n]), list(out[n:-1])


def decay_weights(out, cum, col, cbt, s, then=None):
    sub = out.shape[0]
    for r in range(0, sub, ROWS):
        part = slice(r, r + ROWS)
        first = r // 128 * 128
        decay = jnp.exp2(jnp.minimum(cum[:, first:] - col[part], 0.0))
        out[part, first:] = (decay * cbt[s, part, first:]).astype(bf16)
        if then is not None:
            then(part, first, decay)


def scan_kernel(nx, order, hb, sub, *refs):
    xrefs = refs[:nx]
    (nt, low, pk, hp_r, ct, bn, cbt) = refs[nx : nx + 7]
    xc_all, mix_all, ent_all, sent_all, tok_out = refs[-11:-6]
    raw_sc, x_sc, xs_sc, turn_sc, w_sc, tap_sc = refs[-6:]
    tok_out[...] = jnp.zeros_like(tok_out)
    length = ct.shape[1]
    w_sc[...] = jnp.zeros_like(w_sc)

    @pl.loop(0, xc_all.shape[0] // CB)
    def _(b):
        rows = pl.ds(pl.multiple_of(b * CB, CB), CB)
        mix_out = block_rows(mix_all, b)
        tap_sc[...] = spread(kind_rows(pk, b, 3), range(5))
        hp = hp_r[b]
        raw_sc[...] = dot(joined(xrefs, order, rows), nt[...]) + dot(
            kind_rows(pk, b, 1)[...], low[...], TN
        )
        for r in range(0, CB, ROWS):
            part = slice(r, r + ROWS)
            h = r // HEAD
            taps = [tap_sc[part, k * 128 : (k + 1) * 128] for k in range(4)]
            xc = conv_rows(raw_sc[part, :], taps, lambda k: 3 - k)[:, HALO:]
            xc_all[pl.ds(pl.multiple_of(b * CB + r, ROWS), ROWS), :] = xc.astype(bf16)
            x = xc * sigmoid(xc)
            x_sc[part, :] = x
            xs_sc[part, :] = (x * hp[2 * hb + h : 2 * hb + h + 1]).astype(bf16)
        state = None
        for s in range(length // sub):
            cols = slice(s * sub, (s + 1) * sub)
            cum = hp[:hb, cols]
            rows_n = jnp.transpose(jnp.concatenate([cum, cum], axis=0))
            last = cum[:, sub - 1 : sub]
            ends = jnp.exp2(last - cum)
            add = dot(per_head(xs_sc[:, cols].astype(f32), ends).astype(bf16), bn[cols, :])
            if s > 0:
                ent_all[s - 1, rows, :] = state
                grown = jnp.exp2(cum)
                turn_sc[...] = dot(state.astype(bf16), ct[:, cols])
            for h in range(hb):
                mine = slice(h * HEAD, (h + 1) * HEAD)
                decay_weights(w_sc, cum[h : h + 1], rows_n[:, h : h + 1], cbt, s)
                y = dot(xs_sc[mine, cols], w_sc[...])
                y = y + x_sc[mine, cols] * lanes_of(tap_sc[mine, 512:640], sub)
                if s > 0:
                    y = y + turn_sc[mine, :] * grown[h : h + 1]
                mix_out[mine, cols] = y
            state = add if state is None else per_head(state, jnp.exp2(last)) + add
        if length // sub == 1:
            ent_all[0, rows, :] = state
        sent_all[rows, :] = state.astype(bf16)


def scan_call(lo, hi, xw, part, picks, nt, low, pk, ch, hp, ct, bn, cbt, bufs, later=()):
    slots = pk.shape[0]
    length = ct.shape[1]
    hb = CB // HEAD
    paths, base = xw
    n_paths = len(paths)
    per = ch // CB // n_paths
    width = per * CB
    nsub = length // SUB
    full = lambda a: pl.BlockSpec(a.shape, lambda s: (0,) * a.ndim)
    per_chan = lambda w: pl.BlockSpec((None, width, w), lambda s: (s + lo, part, 0))
    ops = list(paths[part])
    specs = [
        pl.BlockSpec((a.shape[0], width, a.shape[2]), lambda s: (0, s + base, 0)) for a in ops
    ]
    nx = len(ops)
    ops += [nt, low, pk, hp, ct, bn, cbt]
    specs += [full(nt), full(low)]
    specs += [pl.BlockSpec((None, per * 64, CB), lambda s: (s + lo, part, 0))]
    specs += [
        pl.BlockSpec((per,) + hp.shape[1:], lambda s: ((s + lo) * n_paths + part, 0, 0)),
        full(ct), full(bn), full(cbt),
    ]
    inner_states = max(nsub - 1, 1)
    shapes = [
        jax.ShapeDtypeStruct((slots, ch, length), bf16),
        jax.ShapeDtypeStruct((slots, ch, length), f32),
        jax.ShapeDtypeStruct((slots, inner_states, ch, 128), f32),
        jax.ShapeDtypeStruct((slots, width, 128), bf16),
        jax.ShapeDtypeStruct((1, 1), bf16),
    ]
    outs = [
        per_chan(length),
        per_chan(length),
        pl.BlockSpec((None, inner_states, width, 128), lambda s: (s + lo, 0, part, 0)),
        pl.BlockSpec((None, width, 128), lambda s: (s + lo, 0, 0)),
        pl.BlockSpec((1, 1), lambda s: (0, 0)),
    ]
    given = [v for v in bufs if v is not None]
    aliases = {len(ops) + i: k for i, k in enumerate(k for k in range(4) if bufs[k] is not None)}
    ops += given + list(later)
    specs += [pl.BlockSpec(memory_space=pl.ANY)] * (len(given) + len(later))
    n = hi - lo
    out = pl.pallas_call(
        functools.partial(scan_kernel, nx, picks[part], hb, SUB),
        grid=(n,),
        in_specs=specs,
        out_specs=outs,
        out_shape=shapes,
        scratch_shapes=[
            pltpu.VMEM((CB, HALO + length), f32),
            pltpu.VMEM((CB, length), f32),
            pltpu.VMEM((CB, length), bf16),
            pltpu.VMEM((CB, SUB), f32),
            pltpu.VMEM((SUB, SUB), bf16),
            pltpu.VMEM((CB, 640), f32),
        ],
        input_output_aliases=aliases,
        compiler_params=compiler_params(1),
        cost_estimate=cost(
            4 * n * per * CB * 2048 * length, n * per * CB * (4096 + length * 8)
        ),
        name="scan_slots",
    )(*ops)
    return list(out[:4]), out[4]


def proj_kernel(picks, n, cut, gain, *refs):
    (right, low, pk) = refs[n : n + 3]
    out, tok_o = refs[-2:]
    tok_o[...] = jnp.zeros_like(tok_o)
    per = n // len(picks)
    blocks = out.shape[0] // CB // len(picks)
    for p, order in enumerate(picks):
        mine = refs[p * per : (p + 1) * per]
        for k in range(blocks):
            b = p * blocks + k
            value = dot(joined(mine, order, slice(k * CB, (k + 1) * CB)), right[:, cut:])
            value = value + dot(kind_rows(pk, b, 2 if gain else 0)[...], low[:, cut:], TN)
            if gain:
                value = value * lanes_of(spread(kind_rows(pk, b, 3), [5]), value.shape[1])
            out[b * CB : (b + 1) * CB, :] = value.astype(bf16)


def proj_call(lo, hi, weight, picks, right, low, pk, ch, cut, gain, buf, later=()):
    slots = pk.shape[0]
    length = right.shape[1] - cut
    paths, base = weight
    share = ch // len(paths)
    full = lambda a: pl.BlockSpec(a.shape, lambda s: (0,) * a.ndim)
    ops = [a for arrays in paths for a in arrays]
    specs = [
        pl.BlockSpec((a.shape[0], share, a.shape[2]), lambda s: (0, s + base, 0)) for a in ops
    ]
    n_w = len(ops)
    ops += [right, low, pk]
    specs += [full(right), full(low)]
    specs += [pl.BlockSpec((None, ch // 4, CB), lambda s: (s + lo, 0, 0))]
    aliases = {}
    if buf is not None:
        aliases = {len(ops): 0}
        ops.append(buf)
        specs.append(pl.BlockSpec(memory_space=pl.ANY))
    ops += list(later)
    specs += [pl.BlockSpec(memory_space=pl.ANY)] * len(later)
    n = hi - lo
    return pl.pallas_call(
        functools.partial(proj_kernel, picks, n_w, cut, gain),
        grid=(n,),
        in_specs=specs,
        out_specs=[
            pl.BlockSpec((None, ch, length), lambda s: (s + lo, 0, 0)),
            pl.BlockSpec((1, 1), lambda s: (0, 0)),
        ],
        out_shape=[
            jax.ShapeDtypeStruct((slots, ch, length), bf16),
            jax.ShapeDtypeStruct((1, 1), bf16),
        ],
        input_output_aliases=aliases,
        compiler_params=compiler_params(1),
        cost_estimate=cost(2 * n * ch * 2048 * length, n * ch * (4096 + length * 2)),
        name="proj_slots",
    )(*ops)


def fold(values):
    total = values[:8]
    for r in range(8, values.shape[0], 8):
        total = total + values[r : r + 8]
    return total


def gate_kernel(hb, inner, paths, *refs):
    (z_all, mix_all, wgt_all, pk, hp_r, ct, cn) = refs[:7]
    ent_all = refs[7 : 7 + paths]
    nout_all, dmix_all, dz_all, sent_all = refs[7 + paths : 11 + paths]
    mix_sc, turn_sc, sq_sc, dot_sc, gain_sc = refs[11 + paths :]
    phase, slot = pl.program_id(0), pl.program_id(1)
    blocks = z_all.shape[0] // CB

    def gates(ref, rows):
        z = ref[rows, :].astype(f32)
        sig = sigmoid(z)
        return sig, z * sig

    @pl.when((phase == 0) & (slot == 0))
    def _():
        sq_sc[...] = jnp.zeros_like(sq_sc)
        dot_sc[...] = jnp.zeros_like(dot_sc)

    @pl.when(phase == 0)
    def _():
        @pl.loop(0, blocks)
        def _(b):
            z_r, mix_r, wgt_r = [block_rows(v, b) for v in (z_all, mix_all, wgt_all)]
            cum = jnp.exp2(hp_r[b, hb : 2 * hb])
            turn_sc[...] = dot(entering(ent_all, b), ct[...])
            sq, dots = sq_sc[...], dot_sc[...]
            for r in range(0, CB, ROWS):
                rows = slice(r, r + ROWS)
                h = r // HEAD
                _, silu = gates(z_r, rows)
                mix = mix_r[rows, :] + turn_sc[rows, :] * cum[h : h + 1]
                mix_sc[slot * blocks + b, rows, :] = mix
                gated = mix * silu
                sq = sq + fold(gated * gated)
                dots = dots + fold(gated * wgt_r[rows, :].astype(f32))
            sq_sc[...] = sq
            dot_sc[...] = dots

    @pl.when(phase == 1)
    def _():
        r_all = lax.rsqrt(jnp.sum(sq_sc[...], axis=0, keepdims=True) * (1.0 / inner) + epsilon)
        coef = r_all * r_all * r_all * (
            jnp.sum(dot_sc[...], axis=0, keepdims=True) * (1.0 / inner)
        )

        @pl.loop(0, blocks)
        def _(b):
            z_r, wgt_r = block_rows(z_all, b), block_rows(wgt_all, b)
            nout_o, dmix_o, dz_o = [block_rows(v, b) for v in (nout_all, dmix_all, dz_all)]
            cum = jnp.exp2(hp_r[b, hb : 2 * hb])
            gain_sc[...] = spread(kind_rows(pk, b, 3), [5])
            for r in range(0, CB, ROWS):
                rows = slice(r, r + ROWS)
                h = r // HEAD
                sig, silu = gates(z_r, rows)
                mix = mix_sc[slot * blocks + b, rows, :]
                gated = mix * silu
                gain = lanes_of(gain_sc[rows, :], gated.shape[1])
                nout_o[rows, :] = (gated * r_all * gain).astype(bf16)
                d_gated = r_all * wgt_r[rows, :].astype(f32) - gated * coef
                d_mix = d_gated * silu
                dmix_o[rows, :] = d_mix.astype(bf16)
                dz_o[rows, :] = (d_gated * mix * (sig + silu * (1.0 - sig))).astype(bf16)
                turn_sc[rows, :] = d_mix * cum[h : h + 1]
            adj = dot(turn_sc[...].astype(bf16), cn[...])
            here = pl.ds(pl.multiple_of(b * CB, CB), CB)
            sent_all[here, :] = adj.astype(bf16)


def gate_call(z, mix, wgt, ent, pk, hp, ct, cn, inner):
    slots, ch, length = mix.shape
    ncb = ch // CB
    hb = CB // HEAD
    full = lambda a: pl.BlockSpec(a.shape, lambda p, s: (0,) * a.ndim)
    per_chan = lambda a: pl.BlockSpec((None, ch, a.shape[2]), lambda p, s: (s, 0, 0))
    held = lambda p, s: jnp.where(p == 0, s, slots - 1)
    later = lambda w: pl.BlockSpec((None, ch, w), lambda p, s: (jnp.where(p == 1, s, 0), 0, 0))
    return pl.pallas_call(
        functools.partial(gate_kernel, hb, inner, len(ent)),
        grid=(2, slots),
        in_specs=[
            per_chan(z),
            pl.BlockSpec((None, ch, length), lambda p, s: (held(p, s), 0, 0)),
            per_chan(wgt),
            pl.BlockSpec((None, ch // 4, CB), lambda p, s: (s, 0, 0)),
            pl.BlockSpec((ncb,) + hp.shape[1:], lambda p, s: (s, 0, 0)),
            full(ct),
            full(cn),
        ]
        + [
            pl.BlockSpec((None,) + v.shape[1:], lambda p, s: ((held(p, s) + 1) % slots, 0, 0))
            for v in ent
        ],
        out_specs=[later(length), later(length), later(length), later(128)],
        out_shape=[
            jax.ShapeDtypeStruct((slots, ch, length), bf16),
            jax.ShapeDtypeStruct((slots, ch, length), bf16),
            jax.ShapeDtypeStruct((slots, ch, length), bf16),
            jax.ShapeDtypeStruct((slots, ch, 128), bf16),
        ],
        scratch_shapes=[
            pltpu.VMEM((slots * ncb, CB, length), f32),
            pltpu.VMEM((CB, length), f32),
            pltpu.VMEM((8, length), f32),
            pltpu.VMEM((8, length), f32),
            pltpu.VMEM((CB, 128), f32),
        ],
        compiler_params=compiler_params(2),
        cost_estimate=cost(slots * ch * length * 600, slots * ch * length * 22),
        name="gate",
    )(z, mix, wgt, pk, hp, ct, cn, *ent)


def back_kernel(hb, sub, paths, *refs):
    (dy_all, xc_all, hp_r, loc_all, ct, cn, bt, cbt) = refs[:8]
    ent_all = refs[8 : 8 + paths]
    dxs_all, u1_all, u2_all, kl_all, dcb_o, db_o, dc_o = refs[-12:-5]
    xs_sc, turn_sc, dxi_sc, dm_sc, w_sc = refs[-5:]
    w_sc[...] = jnp.zeros_like(w_sc)
    length = ct.shape[1]
    nsub = length // sub

    @pl.when(pl.program_id(0) == 0)
    def _():
        dcb_o[...] = jnp.zeros_like(dcb_o)
        db_o[...] = jnp.zeros_like(db_o)
        dc_o[...] = jnp.zeros_like(dc_o)

    @pl.loop(0, dy_all.shape[0] // CB)
    def _(b):
        rows = pl.ds(pl.multiple_of(b * CB, CB), CB)
        dy_r, dxs_o = block_rows(dy_all, b), block_rows(dxs_all, b)
        u1_o, u2_o, kl_o = u1_all.at[b], u2_all.at[b], kl_all.at[b]
        hp = hp_r[b]
        for r in range(0, CB, ROWS):
            part = slice(r, r + ROWS)
            h = r // HEAD
            xc = xc_all[pl.ds(pl.multiple_of(b * CB + r, ROWS), ROWS), :].astype(f32)
            x = xc * sigmoid(xc)
            xs_sc[part, :] = (x * hp[2 * hb + h : 2 * hb + h + 1]).astype(bf16)
        adj = None
        kl = []
        for s in reversed(range(nsub)):
            cols = slice(s * sub, (s + 1) * sub)
            cum = hp[:hb, cols]
            rows_n = jnp.transpose(jnp.concatenate([cum, cum], axis=0))
            ecum = jnp.exp2(cum)
            last = cum[:, sub - 1 : sub]
            ends = jnp.exp2(last - cum)
            state = entering(ent_all, b).astype(f32)
            if s > 0:
                before = hp[hb : 2 * hb, s * sub - 1 : s * sub]
                state = loc_all[s - 1, rows, :] + per_head(state, jnp.exp2(before))
            state_low = state.astype(bf16)
            turn_sc[...] = dot(state_low, ct[:, cols])
            ed = per_head(dy_r[:, cols].astype(f32), ecum).astype(bf16)
            dc_o[:, cols] += dot(state_low, ed, TN)
            add = dot(ed, cn[cols, :])
            if adj is not None:
                adj_low = adj.astype(bf16)
                dxi_sc[...] = dot(adj_low, bt[:, cols])
                db_o[:, cols] += dot(
                    adj_low, per_head(xs_sc[:, cols].astype(f32), ends).astype(bf16), TN
                )
            u1, u2 = [], []
            for h in range(hb):
                mine = slice(h * HEAD, (h + 1) * HEAD)
                dy_low, xs_low = dy_r[mine, cols], xs_sc[mine, cols]
                dm_sc[...] = dot(xs_low, dy_low, TN)

                def gather(part, first, decay):
                    dcb_o[s, part, first:] += decay * dm_sc[part, first:]

                decay_weights(w_sc, cum[h : h + 1], rows_n[:, h : h + 1], cbt, s, gather)
                xs = xs_low.astype(f32)
                y = dot(xs_low, w_sc[...]) + turn_sc[mine, :] * ecum[h : h + 1]
                dxs = dot(dy_low, w_sc[...], NT)
                u1.append(
                    jnp.sum(dy_low.astype(f32) * y - xs * dxs, axis=0, keepdims=True)
                )
                if adj is not None:
                    dxi = dxi_sc[mine, :] * ends[h : h + 1]
                    u2.append(jnp.sum(xs * dxi, axis=0, keepdims=True))
                    dxs = dxs + dxi
                dxs_o[mine, cols] = dxs
            u1_o[:, cols] = jnp.concatenate(u1, axis=0)
            if adj is None:
                u2_o[:, cols] = jnp.zeros((hb, sub), f32)
                kl.append(jnp.zeros((hb, 128), f32))
                adj = add
            else:
                u2_o[:, cols] = jnp.concatenate(u2, axis=0)
                kl.append(head_sums(adj * state, hb) * jnp.exp2(last))
                adj = per_head(adj, jnp.exp2(last)) + add
        for s in range(nsub):
            kl_o[:, s * 128 : (s + 1) * 128] = kl[nsub - 1 - s]


def back_call(dy, xc, hp, ent, loc, ct, cn, bt, cbt, later=()):
    slots, ch, length = dy.shape
    ncb = ch // CB
    hb = CB // HEAD
    nsub = length // SUB
    full = lambda a: pl.BlockSpec(a.shape, lambda s: (0,) * a.ndim)
    per_chan = lambda w: pl.BlockSpec((None, ch, w), lambda s: (s, 0, 0))
    blk_out = lambda w: pl.BlockSpec((ncb, hb, w), lambda s: (s, 0, 0))
    blocks = slots * ncb
    return pl.pallas_call(
        functools.partial(back_kernel, hb, SUB, len(ent)),
        grid=(slots,),
        in_specs=[
            per_chan(length),
            per_chan(length),
            pl.BlockSpec((ncb,) + hp.shape[1:], lambda s: (s, 0, 0)),
            pl.BlockSpec((None,) + loc.shape[1:], lambda s: (s, 0, 0, 0)),
            full(ct),
            full(cn),
            full(bt),
            full(cbt),
        ]
        + [pl.BlockSpec((None,) + v.shape[1:], lambda s: ((s + 1) % slots, 0, 0)) for v in ent]
        + [pl.BlockSpec(memory_space=pl.ANY)] * len(later),
        out_specs=[
            per_chan(length),
            blk_out(length),
            blk_out(length),
            blk_out(128 * nsub),
            pl.BlockSpec((nsub, SUB, SUB), lambda s: (0, 0, 0)),
            pl.BlockSpec((128, length), lambda s: (0, 0)),
            pl.BlockSpec((128, length), lambda s: (0, 0)),
        ],
        out_shape=[
            jax.ShapeDtypeStruct((slots, ch, length), f32),
            jax.ShapeDtypeStruct((blocks, hb, length), f32),
            jax.ShapeDtypeStruct((blocks, hb, length), f32),
            jax.ShapeDtypeStruct((blocks, hb, 128 * nsub), f32),
            jax.ShapeDtypeStruct((nsub, SUB, SUB), f32),
            jax.ShapeDtypeStruct((128, length), f32),
            jax.ShapeDtypeStruct((128, length), f32),
        ],
        scratch_shapes=[
            pltpu.VMEM((CB, length), bf16),
            pltpu.VMEM((CB, SUB), f32),
            pltpu.VMEM((CB, SUB), f32),
            pltpu.VMEM((SUB, SUB), f32),
            pltpu.VMEM((SUB, SUB), bf16),
        ],
        compiler_params=compiler_params(1),
        cost_estimate=cost(slots * ch * length * SUB * 20, slots * ch * length * 8),
        name="state_back",
    )(dy, xc, hp, loc, ct, cn, bt, cbt, *ent, *later)


def finish_kernel(hb, paths, *refs):
    (dxs_all, dy_all, xc_all, dz_all, pk, hp_r, adj_all, bt, low) = refs[:9]
    ent_all = refs[9 : 9 + paths]
    dx_all, tail_all, head_all, gx_all, dl_o, dd_all, u2_all, kf_all, db_o = refs[-14:-5]
    turn_sc, xs_sc, head_sc, all_sc, tap_sc = refs[-5:]
    length = bt.shape[1]

    @pl.when(pl.program_id(0) == 0)
    def _():
        db_o[...] = jnp.zeros_like(db_o)
        dl_o[...] = jnp.zeros_like(dl_o)

    for b in range(dx_all.shape[0] // CB):
        rows = slice(b * CB, (b + 1) * CB)
        tap_sc[...] = spread(kind_rows(pk, b, 3), range(5))
        hp = hp_r[b]
        delta = hp[2 * hb : 3 * hb]
        total = hp[hb : 2 * hb]
        last = total[:, length - 1 : length]
        ends = jnp.exp2(last - total)
        adj_low = adj_all[rows, :]
        per = ent_all[0].shape[0] // CB
        ent = ent_all[b // per][b % per * CB : (b % per + 1) * CB, :]
        turn_sc[...] = dot(adj_low, bt[...])
        kf_all[b] = head_sums(adj_low.astype(f32) * ent.astype(f32), hb) * jnp.exp2(last)
        u2, dd = [], []
        for h in range(hb):
            u2_h = jnp.zeros((8, length), f32)
            dd_h = jnp.zeros((8, length), f32)
            for r in range(h * HEAD, (h + 1) * HEAD, ROWS):
                part = slice(r, r + ROWS)
                whole = slice(b * CB + r, b * CB + r + ROWS)
                xc = xc_all[whole, :].astype(f32)
                sig = sigmoid(xc)
                x = xc * sig
                xs = x * delta[h : h + 1]
                extra = turn_sc[part, :] * ends[h : h + 1]
                u2_h = u2_h + fold(xs * extra)
                xs_sc[part, :] = (xs * ends[h : h + 1]).astype(bf16)
                dxs = dxs_all[whole, :] + extra
                dd_h = dd_h + fold(x * dxs)
                skip = lanes_of(tap_sc[part, 512:640], length)
                dx = dxs * delta[h : h + 1] + dy_all[whole, :].astype(f32) * skip
                dconv = dx * (sig + x * (1.0 - sig))
                head_sc[part, :] = dconv[:, :HALO]
                none = jnp.zeros((ROWS, HALO), f32)
                ext = jnp.concatenate([none, dconv, none], axis=1)
                taps = [tap_sc[part, k * 128 : (k + 1) * 128] for k in range(4)]
                out = conv_rows(ext, taps, lambda k: ext.shape[1] - (3 - k))
                tail_all[whole, :] = out[:, length : HALO + length]
                all_low = out[:, : HALO + length].astype(bf16)
                all_sc[part, :] = all_low
                dx_all[whole, :] = all_low[:, HALO:]
            u2.append(jnp.sum(u2_h, axis=0, keepdims=True))
            dd.append(jnp.sum(dd_h, axis=0, keepdims=True))
        u2_all[b] = jnp.concatenate(u2, axis=0)
        dd_all[b] = jnp.concatenate(dd, axis=0)
        db_o[...] += dot(adj_low, xs_sc[...], TN)
        head_all[:, rows] = jnp.transpose(head_sc[...])[:8]
        all_low = all_sc[...]
        gx_all[:, rows] = dot(low[...], all_low, NT)
        dl_o[...] += dot(kind_rows(pk, b, 1)[...], all_low)
        dl_o[:, HALO:] += dot(kind_rows(pk, b, 0)[...], dz_all[rows, :])


def finish_call(dxs, dy, xc, dz, pk, hp, ent, adj, bt, low, later):
    slots, ch, length = dy.shape
    ncb = ch // CB
    hb = CB // HEAD
    rank = low.shape[0]
    full = lambda a: pl.BlockSpec(a.shape, lambda s: (0,) * a.ndim)
    chan = lambda w: pl.BlockSpec((None, ch, w), lambda s: (s, 0, 0))
    blk_out = lambda w: pl.BlockSpec((ncb, hb, w), lambda s: (s, 0, 0))
    turned = lambda w: pl.BlockSpec((None, w, ch), lambda s: (s, 0, 0))
    blocks = slots * ncb
    return pl.pallas_call(
        functools.partial(finish_kernel, hb, len(ent)),
        grid=(slots,),
        in_specs=[
            chan(length),
            chan(length),
            chan(length),
            chan(length),
            pl.BlockSpec((None, ch // 4, CB), lambda s: (s, 0, 0)),
            pl.BlockSpec((ncb,) + hp.shape[1:], lambda s: (s, 0, 0)),
            pl.BlockSpec((None, ch, 128), lambda s: ((s + slots - 1) % slots, 0, 0)),
            full(bt),
            full(low),
        ]
        + [pl.BlockSpec((None,) + v.shape[1:], lambda s: ((s + 1) % slots, 0, 0)) for v in ent]
        + [pl.BlockSpec(memory_space=pl.ANY)] * len(later),
        out_specs=[
            chan(length),
            chan(HALO),
            turned(8),
            turned(rank),
            pl.BlockSpec((rank, HALO + length), lambda s: (0, 0)),
            blk_out(length),
            blk_out(length),
            blk_out(128),
            pl.BlockSpec((128, length), lambda s: (0, 0)),
        ],
        out_shape=[
            jax.ShapeDtypeStruct((slots, ch, length), bf16),
            jax.ShapeDtypeStruct((slots, ch, HALO), f32),
            jax.ShapeDtypeStruct((slots, 8, ch), f32),
            jax.ShapeDtypeStruct((slots, rank, ch), f32),
            jax.ShapeDtypeStruct((rank, HALO + length), f32),
            jax.ShapeDtypeStruct((blocks, hb, length), f32),
            jax.ShapeDtypeStruct((blocks, hb, length), f32),
            jax.ShapeDtypeStruct((blocks, hb, 128), f32),
            jax.ShapeDtypeStruct((128, length), f32),
        ],
        scratch_shapes=[
            pltpu.VMEM((CB, length), f32),
            pltpu.VMEM((CB, length), bf16),
            pltpu.VMEM((CB, HALO), f32),
            pltpu.VMEM((CB, HALO + length), bf16),
            pltpu.VMEM((CB, 640), f32),
        ],
        compiler_params=compiler_params(1),
        cost_estimate=cost(slots * ch * length * 700, slots * ch * length * 14),
        name="finish_back",
    )(dxs, dy, xc, dz, pk, hp, adj, bt, low, *ent, *later)


def glue_kernel(flat_order, quick, sub, *refs):
    (dcb_r, db1, db2, dc1, bt, ct, pre_r, u1, u2, kl, dd, u2f, kf) = refs[:13]
    (sig_r, speed, taps_r, sc, dl, nt) = refs[13:19]
    left_o, tail_o, head_o, gd_o = refs[19:]
    taps = tall(taps_r[...])
    low = dl[...].astype(bf16)
    for i, m in enumerate(flat_order):
        at = pl.ds(block_at(sc[0], m, quick), CB)
        gd_o[:, at] = dot(low, nt[i * CB : (i + 1) * CB, :], NT)
    state_w, length = bt.shape
    nsub = length // sub
    blocks = u1.shape[0]
    row = lax.broadcasted_iota(jnp.int32, (sub, sub), 0)
    col = lax.broadcasted_iota(jnp.int32, (sub, sub), 1)
    below = jnp.where(row >= col, 1.0, 0.0)
    keep = jnp.where(row <= col, 1.0, 0.0)

    def exact(p, q):
        return lax.dot_general(
            p, q, (NN, ((), ())), precision=highest, preferred_element_type=f32
        )

    def flat(ref, cols=slice(None)):
        return jnp.concatenate([ref[b, :, cols] for b in range(blocks)], axis=0)

    d_b, d_c, rate_in = [], [], []
    for s in range(nsub):
        cols = slice(s * sub, (s + 1) * sub)
        dcb = (dcb_r[s] * keep).astype(bf16)
        d_b.append(dot(ct[:, cols], dcb, NT))
        d_c.append(dot(bt[:, cols], dcb))
        lane = slice(s * 128, (s + 1) * 128)
        rate_in.append(
            exact(flat(u1, cols), below)
            + exact(flat(u2, cols), 1.0 - below)
            + jnp.sum(flat(kl, lane), axis=1, keepdims=True)
        )
    d_b = jnp.concatenate(d_b, axis=1) + db1[...] + db2[...]
    d_c = jnp.concatenate(d_c, axis=1) + dc1[...]
    pre = pre_r[...]
    sig = sigmoid(pre)
    d_pre = jnp.concatenate([d_b, d_c], axis=0) * (sig + pre * sig * (1.0 - sig))
    head_o[...] = jnp.transpose(d_pre[:, :HALO])[:8]
    ext = jnp.concatenate([d_pre, jnp.zeros((2 * state_w, HALO), f32)], axis=1)
    out = ext * taps[:, 3:4]
    for k in range(3):
        out = out + pltpu.roll(ext, ext.shape[1] - (3 - k), 1) * taps[:, k : k + 1]
    tail_o[...] = out[:, length - HALO : length]
    left_o[: 2 * state_w, :] = out[:, :length].astype(bf16)
    rate = jnp.concatenate(rate_in, axis=1) + jnp.sum(flat(kf), axis=1, keepdims=True)
    first = flat(u2f)
    run = None
    parts = []
    for s in range(nsub):
        piece = first[:, s * sub : (s + 1) * sub]
        here = exact(piece, 1.0 - below)
        parts.append(here if run is None else here + run)
        ends = jnp.sum(piece, axis=1, keepdims=True)
        run = ends if run is None else run + ends
    rate = rate + jnp.concatenate(parts, axis=1)
    left_o[2 * state_w :, :] = ((flat(dd) - speed[:, :1] * rate) * sig_r[...]).astype(bf16)


def glue_call(args, sc, dl, nt, state_w, length, heads, flat, quick):
    vm = pl.BlockSpec(memory_space=pltpu.VMEM)
    return pl.pallas_call(
        functools.partial(glue_kernel, flat, quick, SUB),
        in_specs=[vm] * len(args) + [pl.BlockSpec(memory_space=pltpu.SMEM), vm, vm],
        out_specs=[vm] * 4,
        out_shape=[
            jax.ShapeDtypeStruct((2 * state_w + heads, length), bf16),
            jax.ShapeDtypeStruct((2 * state_w, HALO), f32),
            jax.ShapeDtypeStruct((8, 2 * state_w), f32),
            jax.ShapeDtypeStruct((dl.shape[0], nt.shape[0]), f32),
        ],
        compiler_params=compiler_params(0),
        cost_estimate=cost(1e8, 4e6),
        name="glue",
    )(*args, sc, dl, nt)


def add_products(acc, turned, sets, picks, refs, slot):
    at = 0
    for lo, hi, per in sets:
        groups = [refs[at + p * per : at + (p + 1) * per] for p in range(len(picks))]
        at += len(picks) * per

        @pl.when((slot >= lo) & (slot < hi))
        def _(groups=groups):
            off = 0
            for i in range(len(picks[0])):
                parts = []
                for group, order in zip(groups, picks):
                    k, b = order[i]
                    parts.append(group[k][b])
                w = parts[0] if len(parts) == 1 else jnp.concatenate(parts, axis=0)
                acc[:, off : off + w.shape[1]] += dot(turned, w)
                off += w.shape[1]


def product_specs(weights, share):
    ops, specs, sets = [], [], []
    for (lo, hi), paths, base in weights:
        sets.append((lo, hi, len(paths[0])))
        for arrays in paths:
            for a in arrays:
                ops.append(a)
                index = lambda s, lo=lo, hi=hi, base=base: (0, base + jnp.clip(s, lo, hi - 1) - lo, 0)
                specs.append(pl.BlockSpec((a.shape[0], share, a.shape[2]), index))
    return ops, specs, sets


def output_kernel(sets, picks, flat, quick, n_w, *refs):
    (sc, nout, dn, bh, up, tok, masked) = refs[:7]
    wrefs = refs[7 : 7 + n_w]
    mixed_o, gdo_o, guo_o, acc, hid = refs[-5:]
    slot = pl.program_id(0)
    rank = up.shape[0]
    length, width = tok.shape

    @pl.when(slot == 0)
    def _():
        acc[...] = jnp.zeros_like(acc)
        hid[...] = jnp.zeros_like(hid)

    values = nout[...]
    gdo_o[...] = dot(bh[...], values, NT)
    for part in range(dn.shape[0] // 64):
        mine = slice(part * CB, (part + 1) * CB)
        hid[...] += dot(dn[part * 64 + 32 : part * 64 + 48, :], values[mine])
    add_products(acc, jnp.transpose(values), sets, picks, wrefs, slot)

    @pl.when(slot == pl.num_programs(0) - 1)
    def _():
        low = hid[...].astype(bf16)
        guo_o[...] = dot(low, masked[...])
        rows = lax.broadcasted_iota(jnp.int32, (length, 1), 0) < sc[1]
        for i, m in enumerate(flat):
            at = pl.ds(block_at(sc[0], m, quick), CB)
            total = acc[:, i * CB : (i + 1) * CB] + dot(low, up[:, at], TN)
            total = total + tok[:, at].astype(f32)
            mixed_o[:, at] = jnp.where(rows, total, 0.0).astype(bf16)


def output_call(sc, nout, pk, bh, up, tok, masked, weights, picks, flat, quick):
    slots, ch, length = nout.shape
    rank, width = up.shape
    block = ch
    full = lambda a: pl.BlockSpec(a.shape, lambda s: (0,) * a.ndim)
    chan = lambda a: pl.BlockSpec((None, block, a.shape[2]), lambda s: (s, 0, 0))
    w_ops, w_specs, sets = product_specs(weights, ch // len(picks))
    return pl.pallas_call(
        functools.partial(output_kernel, sets, picks, flat, quick, len(w_ops)),
        grid=(slots,),
        in_specs=[pl.BlockSpec(memory_space=pltpu.SMEM), chan(nout)]
        + [pl.BlockSpec((None, block // 4, CB), lambda s: (s, 0, 0)), full(bh)]
        + [full(up), full(tok), full(masked)] + w_specs,
        out_specs=[
            pl.BlockSpec((length, width), lambda s: (0, 0)),
            pl.BlockSpec((None, rank, block), lambda s: (s, 0, 0)),
            pl.BlockSpec((rank, width), lambda s: (0, 0)),
        ],
        out_shape=[
            jax.ShapeDtypeStruct((length, width), bf16),
            jax.ShapeDtypeStruct((slots, rank, ch), f32),
            jax.ShapeDtypeStruct((rank, width), f32),
        ],
        scratch_shapes=[pltpu.VMEM((length, width), f32), pltpu.VMEM((rank, length), f32)],
        compiler_params=compiler_params(1),
        cost_estimate=cost(2 * slots * ch * length * width, slots * ch * width * 2),
        name="output",
    )(sc, nout, pk, bh, up, tok, masked, *w_ops)


def gate_back_kernel(sets, picks, n_w, *refs):
    dz, low = refs[:2]
    acc, gz_o = refs[-2:]
    slot = pl.program_id(0)

    @pl.when(slot == 0)
    def _():
        acc[...] = jnp.zeros_like(acc)

    gz_o[...] = dot(low[:, HALO:], dz[...], NT)
    add_products(acc, jnp.transpose(dz[...]), sets, picks, refs[2 : 2 + n_w], slot)


def gate_back_call(dz, low, weights, picks, width, later=()):
    slots, ch, length = dz.shape
    rank = low.shape[0]
    block = ch
    w_ops, w_specs, sets = product_specs(weights, ch // len(picks))
    return pl.pallas_call(
        functools.partial(gate_back_kernel, sets, picks, len(w_ops)),
        grid=(slots,),
        in_specs=[
            pl.BlockSpec((None, block, length), lambda s: (s, 0, 0)),
            pl.BlockSpec(low.shape, lambda s: (0, 0)),
        ]
        + w_specs
        + [pl.BlockSpec(memory_space=pl.ANY)] * len(later),
        out_specs=[
            pl.BlockSpec((length, width), lambda s: (0, 0)),
            pl.BlockSpec((None, rank, block), lambda s: (s, 0, 0)),
        ],
        out_shape=[
            jax.ShapeDtypeStruct((length, width), f32),
            jax.ShapeDtypeStruct((slots, rank, ch), f32),
        ],
        compiler_params=compiler_params(1),
        cost_estimate=cost(2 * slots * ch * length * width, 2 * slots * ch * width),
        name="gate_back",
    )(dz, low, *w_ops, *later)


def beyond(near, taps, rows):
    parts = [jnp.zeros((HALO - 3, rows), f32)]
    for i in range(3):
        total = near[i : i + 1] * taps[0:1]
        for k in range(1, i + 1):
            total = total + near[i - k : i - k + 1] * taps[k : k + 1]
        parts.append(total)
    return jnp.transpose(jnp.concatenate(parts, axis=0))


def input_kernel(sets, picks, flat, quick, n_w, n_small, *refs):
    (sc, dx, tail, near, num, left, maps_tail, maps_near, maps_taps) = refs[:9]
    (dl, near_dl, down, root_r, gain, tok, masked, start) = refs[9:17]
    smalls = refs[17 : 17 + n_small]
    wrefs = refs[17 + n_small : 17 + n_small + n_w]
    out, acc = refs[-2:]
    slot = pl.program_id(0)
    length, width = tok.shape
    cut = length - HALO

    @pl.when(slot == 0)
    def _():
        d_low = jnp.concatenate(
            [dl[:, HALO:length], dl[:, length:] + near_dl[:, :HALO]], axis=1
        ).astype(bf16)
        low = jnp.transpose(d_low)
        n_maps = maps_tail.shape[0]
        maps_last = maps_tail[...] + beyond(maps_near[:, :n_maps], maps_taps, n_maps)
        maps_left = jnp.concatenate([left[:n_maps, :cut], maps_last.astype(bf16)], axis=1)
        total = start[...] + dot(maps_left, smalls[0][...], TN)
        row = n_maps
        for w in smalls[1:]:
            total = total + dot(left[row : row + w.shape[0], :], w[...], TN)
            row += w.shape[0]
        acc[...] = total
        for i, m in enumerate(flat):
            at = pl.ds(block_at(sc[0], m, quick), CB)
            acc[:, i * CB : (i + 1) * CB] += dot(low, down[at, :], NT)

    block = dx.shape[0]
    taps = jnp.concatenate(
        [
            num[b * 64 + 48 : b * 64 + 64, :].astype(f32)[:8]
            + num[b * 64 + 48 : b * 64 + 64, :].astype(f32)[8:]
            for b in range(block // CB)
        ],
        axis=1,
    )
    last = tail[...] + beyond(near[...], taps, block)
    dx_all = jnp.concatenate([dx[:, :cut], last.astype(bf16)], axis=1)
    add_products(acc, jnp.transpose(dx_all), sets, picks, wrefs, slot)

    @pl.when(slot == pl.num_programs(0) - 1)
    def _():
        root = root_r[...]
        mean = None
        for i, m in enumerate(flat):
            at = pl.ds(block_at(sc[0], m, quick), CB)
            cols = slice(i * CB, (i + 1) * CB)
            scaled = acc[:, cols] * gain[:, at]
            acc[:, cols] = scaled
            part = jnp.sum(scaled * tok[:, at].astype(f32), axis=1, keepdims=True)
            mean = part if mean is None else mean + part
        coef = root * root * root * (mean * (1.0 / width))
        for i, m in enumerate(flat):
            at = pl.ds(block_at(sc[0], m, quick), CB)
            d_resid = root * acc[:, i * CB : (i + 1) * CB] - tok[:, at].astype(f32) * coef
            out[:, at] = (masked[:, at].astype(f32) + d_resid).astype(bf16)


def input_call(
    sc, dx, tail, near, pk, left, maps_tail, maps_taps, dl, down, root, gain, tok, masked, start,
    smalls, weights, picks, flat, quick, later=(),
):
    slots, ch, length = dx.shape
    width = tok.shape[1]
    block = ch
    rank = dl.shape[0]
    once = pl.Buffered(1)
    full = lambda a: pl.BlockSpec(a.shape, lambda s: (0,) * a.ndim, pipeline_mode=once)
    chan = lambda a: pl.BlockSpec((None, block, a.shape[2]), lambda s: (s, 0, 0))
    w_ops, w_specs, sets = product_specs(weights, ch // len(picks))
    near_rows = pl.BlockSpec((8, block), lambda s: ((s + slots - 1) % slots, 0))
    near_maps = pl.BlockSpec((8, ch), lambda s: (slots, 0), pipeline_mode=once)
    near_low = pl.BlockSpec(
        (rank, ch), lambda s: (((slots + 1) * 8 + rank - 1) // rank, 0), pipeline_mode=once
    )
    return pl.pallas_call(
        functools.partial(input_kernel, sets, picks, flat, quick, len(w_ops), len(smalls)),
        grid=(slots,),
        in_specs=[pl.BlockSpec(memory_space=pltpu.SMEM), chan(dx), chan(tail), near_rows]
        + [pl.BlockSpec((None, block // 4, CB), lambda s: (s, 0, 0))]
        + [full(left), full(maps_tail), near_maps, full(maps_taps), full(dl), near_low]
        + [full(a) for a in [down, root, gain, tok, masked, start] + list(smalls)]
        + w_specs
        + [pl.BlockSpec(memory_space=pl.ANY)] * len(later),
        out_specs=pl.BlockSpec((length, width), lambda s: (0, 0)),
        out_shape=jax.ShapeDtypeStruct((length, width), bf16),
        scratch_shapes=[pltpu.VMEM((length, width), f32)],
        compiler_params=compiler_params(1),
        cost_estimate=cost(2 * slots * ch * length * width, 2 * slots * ch * width),
        name="input_back",
    )(
        sc, dx, tail, near, pk, left, maps_tail, near, maps_taps, dl, near, down, root, gain, tok,
        masked, start, *smalls, *w_ops, *later
    )


def assemble_kernel(n, single, ch, ids, *refs):
    parts = refs[:n]
    down_o, up_o, down_out_o, up_out_o = refs[n:]
    here = down_o.shape[0]
    width = down_o.shape[2]
    first = pl.program_id(0) * here
    blocks = [(ref, b) for ref in parts for b in range(ref.shape[0])]

    def put(a, total):
        up_o[a, :, 0, :] = total[:, :ch]
        up_o[a, :, 1, :] = total[:, ch : 2 * ch]
        down_out_o[a] = total[:, 2 * ch : 3 * ch]
        down_o[a] = total[:, 3 * ch : 3 * ch + width]
        up_out_o[a] = total[:, 3 * ch + width :]

    for a in range(here):
        if single:
            for m, (ref, b) in enumerate(blocks):

                @pl.when(ids[m] == first + a)
                def _(ref=ref, b=b, a=a):
                    put(a, ref[b].astype(f32))

        else:
            total = None
            for m, (ref, b) in enumerate(blocks):
                chosen = jnp.where(ids[m] == first + a, 1.0, 0.0)
                term = ref[b].astype(f32) * chosen
                total = term if total is None else total + term
            put(a, total)


def assemble_call(ids, parts, adapters, ch, width):
    rank = parts[0].shape[1]
    each = adapters // 2 if adapters % 2 == 0 else adapters
    single = ids.shape[0] == adapters
    return pl.pallas_call(
        functools.partial(assemble_kernel, len(parts), single, ch),
        grid=(adapters // each,),
        in_specs=[pl.BlockSpec(memory_space=pltpu.SMEM)]
        + [pl.BlockSpec(a.shape, lambda i: (0, 0, 0)) for a in parts],
        out_specs=[
            pl.BlockSpec((each, rank, width), lambda i: (i, 0, 0)),
            pl.BlockSpec((each, rank, 2, ch), lambda i: (i, 0, 0, 0)),
            pl.BlockSpec((each, rank, ch), lambda i: (i, 0, 0)),
            pl.BlockSpec((each, rank, width), lambda i: (i, 0, 0)),
        ],
        out_shape=[
            jax.ShapeDtypeStruct((adapters, rank, width), f32),
            jax.ShapeDtypeStruct((adapters, rank, 2, ch), f32),
            jax.ShapeDtypeStruct((adapters, rank, ch), f32),
            jax.ShapeDtypeStruct((adapters, rank, width), f32),
        ],
        compiler_params=compiler_params(1),
        cost_estimate=cost(1e7, 2e7),
        name="assemble",
    )(ids, *parts)


def body(
    tokens,
    cotangent,
    lengths,
    adapter_ids,
    pre_gain,
    in_inner,
    in_maps,
    in_steps,
    conv_inner,
    conv_maps,
    step_bias,
    decay_log,
    skip_gain,
    norm_gain,
    out_weight,
    adapter_in_down,
    adapter_in_up,
    adapter_out_down,
    adapter_out_up,
):
    planes = lax.axis_size("tensor")
    seqs = lax.axis_size("dp")
    place = lax.axis_index("tensor")
    mine = lax.axis_index("dp")
    length = tokens.shape[1]
    width = tokens.shape[2]
    rows_here = in_inner.shape[0]
    ch = in_inner.shape[2]
    inner = ch * planes
    hs = in_steps.shape[1]
    heads = hs * planes
    rank = adapter_in_down.shape[2]
    adapters = adapter_in_down.shape[0]
    state_w = in_maps.shape[1] // 2
    hb = CB // HEAD
    ncb = ch // CB
    nblk = planes * ncb
    nsub = length // SUB
    quick = seqs == 8 and planes == 4

    def from_plane(v, j):
        return lax.ppermute(v, "tensor", [((s + j) % planes, s) for s in range(planes)])

    def flip(v, bit):
        return lax.ppermute(v, "dp", [(i, i ^ bit) for i in range(seqs)])

    def slot_order(v, first=0, at=place):
        return [
            lax.dynamic_index_in_dim(v, (at + j) % planes, 0, keepdims=False)
            for j in range(first, planes)
        ]

    def by_slot(v):
        return jnp.stack(slot_order(lax.all_gather(v, "tensor", axis=0)))

    def to_slots(rows, whole):
        total = jnp.concatenate([rows[0], whole], axis=1)
        for j in range(1, planes):
            part = jnp.concatenate([rows[j], whole], axis=1).astype(bf16)
            total = total + lax.ppermute(
                part, "tensor", [(s, (s + j) % planes) for s in range(planes)]
            ).astype(f32)
        return total

    flat = [0, 2, 4, 6, 1, 3, 5, 7] if quick else list(range(width // CB))
    if quick:
        picks = [
            [(0, 0), (0, 1), (1, 0), (1, 1), (2, 0), (2, 1), (3, 0), (3, 1)],
            [(0, 0), (1, 0), (0, 1), (1, 1), (2, 0), (3, 0), (2, 1), (3, 1)],
        ]
    else:
        picks = [[(0, 0)]]
    half = planes // 2

    def halves(parts, more=((), ())):
        cut = ch // 2
        return [
            jnp.concatenate([v[:cut] for v in parts] + list(more[0]), axis=0),
            jnp.concatenate([v[cut:] for v in parts] + list(more[1]), axis=0),
        ]

    def pass_one(ab):
        return [flip(ab[0], 2), flip(ab[1], 4)]

    def pass_two(ab):
        return [flip(ab[0], 4), flip(ab[1], 2)]

    def pass_core(arrays):
        return [flip(v, 1) for v in arrays]

    def as_paths(arrays, swapped):
        return [[arrays[k], arrays[k + 2], swapped[k], swapped[k + 2]] for k in range(2)]

    pick = adapter_ids[0]
    down_in = lax.dynamic_index_in_dim(adapter_in_down, pick, 0, keepdims=False)
    up_here = lax.dynamic_index_in_dim(adapter_in_up, pick, 0, keepdims=False)
    down_here = lax.dynamic_index_in_dim(adapter_out_down, pick, 0, keepdims=False)
    up_out = lax.dynamic_index_in_dim(adapter_out_up, pick, 0, keepdims=False)
    numbers = jnp.concatenate(
        [
            conv_inner,
            jnp.repeat(skip_gain, HEAD)[None],
            norm_gain[None],
            jnp.pad(jnp.stack([step_bias, decay_log]), ((0, 0), (0, ch - hs))),
        ],
        axis=0,
    )
    coarse = lax.optimization_barrier(numbers.astype(bf16))
    fine = lax.optimization_barrier((numbers - coarse.astype(f32)).astype(bf16))
    packed = jnp.concatenate(
        [jnp.transpose(up_here, (1, 0, 2)).reshape(2 * rank, ch), down_here.T, coarse, fine],
        axis=0,
    )
    packed = jnp.swapaxes(packed.reshape(64, ncb, CB), 0, 1).reshape(64 * ncb, CB)
    last_rows = tokens[0, -16:].reshape(16 * width // CB, CB)
    halo = [(s, s + 1) for s in range(planes - 1)]
    wt = jnp.transpose(in_inner, (1, 2, 0))
    maps_w = in_maps.T
    steps_w = in_steps.T
    own_rows = 3 * ch // 2
    if quick:
        own = halves(
            [wt[0], wt[1], out_weight],
            (
                [maps_w[:state_w], steps_w, jnp.full((16, rows_here), pick).astype(bf16)],
                [maps_w[state_w:]],
            ),
        )
        got = pass_one(own)
        all_x = lax.all_gather(
            jnp.concatenate([wt[1], packed, steps_w, last_rows], axis=0), "tensor", axis=0
        )
        all_z = lax.all_gather(wt[0], "tensor", axis=0)
        all_o = lax.all_gather(out_weight, "tensor", axis=0)
        token, _, own = hold([], [], zip(own, got))
        two = pass_two(own)
        swapped = pass_core(own)
        marks = [ch, ch + 64 * ncb, ch + 64 * ncb + hs]
        ends = all_x.shape[1]

        def rows_of(j, lo, hi):
            start = ((place + j) % planes, lo, 0)
            return lax.dynamic_slice(all_x, start, (1, hi - lo, rows_here))[0]

        pk = jnp.stack([rows_of(j, marks[0], marks[1]) for j in range(planes)])
        last_rows = rows_of(planes - 1, marks[2], ends)
        far_x = list(
            far_call(jnp.reshape(place, (1,)).astype(jnp.int32), all_x, ch, marks[1], hs)
        )
        token, passed, _ = hold(swapped, two + far_x)
        two, far_x = passed[:2], passed[2:]
        own = own + two
        swapped = swapped + pass_core(two)
        got = pass_one(far_x)
        held = [token]
    else:
        pk = by_slot(packed)
        last_rows = by_slot(last_rows)[planes - 1]
        steps_w = by_slot(steps_w)
        held = []
    before = last_rows.reshape(16, width)
    before = jnp.where(place > 0, before, jnp.zeros_like(before))
    sc = jnp.stack([mine, lengths[0] - place * length]).astype(jnp.int32)
    normed, masked, root, low2, back2, nt, gt = turn_call(
        sc, tokens[0], before, cotangent[0], pre_gain[None], down_in, up_out, flat, quick, held
    )
    if quick:
        own = as_paths(own, swapped)
        token, _, far_x = hold([nt, pk] + own[0] + own[1], [], zip(far_x, got))
        two = pass_two(far_x)
        swapped = pass_core(far_x)
        held = [token]
        all_maps, all_steps = own, own[0]
        maps_at, maps_rows = own_rows, state_w
        steps_at, mine_slots = own_rows + state_w, 1
    else:
        all_maps = [[lax.all_gather(maps_w, "dp", axis=1, tiled=True)[None]]]
        all_steps = steps_w.reshape(heads, rows_here)
        all_steps = [lax.all_gather(all_steps, "dp", axis=1, tiled=True)[None]]
        maps_at, maps_rows = 0, 2 * state_w
        steps_at, mine_slots = 0, planes
    bt, ct, b_low, c_low, cbt, maps_pre, maps_w = maps_call(
        all_maps, maps_at, maps_rows, picks, nt, conv_maps, length, held
    )
    hp, step_sig, speed, mine_w, found = steps_call(
        all_steps, steps_at, picks[0], nt, pk, 0, mine_slots, hs, length, held,
        tuple(flat) if quick else None,
    )
    small_w = [maps_w, mine_w]
    if quick:
        ids = found[:, 0].astype(jnp.int32)
    else:
        ids = lax.all_gather(adapter_ids, "dp", axis=0, tiled=True)

    x_args = (picks, nt, low2, pk, ch)
    z_args = (picks, nt, low2, pk, ch, HALO, False)
    o_args = (picks, gt, back2, pk, ch, 0, True)
    if quick:
        empty = [None] * 3
        bufs, _ = scan_call(
            0, 1, (own, 1), 0, *x_args, hp, ct, b_low, cbt, empty + [None], held
        )
        sent_a = bufs[3]
        bufs, done = scan_call(
            0, 1, (own, 1), 1, *x_args, hp, ct, b_low, cbt, bufs[:3] + [None], held
        )
        sent_b = bufs[3]
        far_z = halves(slot_order(all_z, 1, place + token[0, 0].astype(jnp.int32)))

        token, passed, _ = hold([done] + swapped, two + far_z)
        two, far_z = passed[:2], passed[2:]
        far_x = as_paths(far_x + two, swapped + pass_core(two))
        got = pass_one(far_z)
        z, beside = proj_call(0, 1, (own, 0), *z_args, None, [token])
        wgt, beside = proj_call(0, 1, (own, 2), *o_args, None, [beside])
        far_o = halves(slot_order(all_o, 1, place + beside[0, 0].astype(jnp.int32)))

        token, far_o, far_z = hold([beside] + far_x[0] + far_x[1], far_o, zip(far_z, got))
        two = pass_two(far_z)
        swapped = pass_core(far_z)
        hp_far, sig_far, speed_far, far_w, _ = steps_call(
            far_x[0], own_rows, picks[0], nt, pk, 1, planes, hs, length, [token]
        )
        hp = jnp.concatenate([hp, hp_far], axis=0)
        step_sig = jnp.concatenate([step_sig, sig_far], axis=0)
        speed = jnp.concatenate([speed, speed_far], axis=0)
        small_w.append(far_w)
        bufs, _ = scan_call(
            1, planes, (far_x, 0), 0, *x_args, hp, ct, b_low, cbt, bufs[:3] + [sent_a], [token]
        )
        sent_a = bufs[3]
        ent_a = lax.ppermute(sent_a, "tensor", halo)
        bufs, done = scan_call(
            1, planes, (far_x, 0), 1, *x_args, hp, ct, b_low, cbt, bufs[:3] + [sent_b], [token]
        )
        sent_b = bufs[3]
        ent_b = lax.ppermute(sent_b, "tensor", halo)
        token, passed, _ = hold([done] + swapped, two + far_o + [ent_a])
        two, far_o, (ent_a,) = passed[:2], passed[2:4], passed[4:]
        far_z = as_paths(far_z + two, swapped + pass_core(two))
        got = pass_one(far_o)
        ent_a = lax.ppermute(hop_call(ent_a, 1, sent_a, hp, 0, [token]), "tensor", halo)

        token, passed, far_o = hold(far_z[0] + far_z[1], [ent_a, ent_b], zip(far_o, got))
        ent_a, ent_b = passed
        two = pass_two(far_o)
        send_b = hop_call(ent_b, 1, sent_b, hp, 1, [token])
        ent_b = lax.ppermute(send_b, "tensor", halo)
        send_a = hop_call(ent_a, 1, sent_a, hp, 0, [token])
        ent_a = lax.ppermute(send_a, "tensor", halo)
        z, done = proj_call(1, planes, (far_z, 0), *z_args, z, [send_a, send_b])

        token, passed, _ = hold([done], two + far_o + [ent_a, ent_b])
        two, far_o, (ent_a, ent_b) = passed[:2], passed[2:4], passed[4:]
        far_o = as_paths(far_o + two, pass_core(far_o + two))
        send_b = hop_call(ent_b, 1, sent_b, hp, 1, [token])
        ent_b = lax.ppermute(send_b, "tensor", halo)
        wgt, done = proj_call(1, planes, (far_o, 0), *o_args, wgt, [send_b])
        _, ent, _ = hold([done], [ent_a, ent_b])
        z_sets = [((0, 1), own, 0), ((1, planes), far_z, 0)]
        x_sets = [((0, 1), own, 1), ((1, planes), far_x, 0)]
        o_sets = [((0, 1), own, 2), ((1, planes), far_o, 0)]
    else:
        w = lax.all_gather(wt, "dp", axis=2, tiled=True)
        w = by_slot(w)
        o = lax.all_gather(out_weight, "dp", axis=1, tiled=True)
        flat_rows = lambda v: [[v.reshape(1, inner, width)]]
        wz, wx = flat_rows(w[:, 0]), flat_rows(w[:, 1])
        o = flat_rows(by_slot(o))
        bufs, _ = scan_call(
            0, planes, (wx, 0), 0, *x_args, hp, ct, b_low, cbt, [None] * 4
        )
        z, _ = proj_call(0, planes, (wz, 0), *z_args, None)
        wgt, _ = proj_call(0, planes, (o, 0), *o_args, None)
        ent = lax.ppermute(bufs[3], "tensor", halo)
        for _ in range(planes - 2):
            ent = lax.ppermute(hop_call(ent, 1, bufs[3], hp), "tensor", halo)
        ent = [ent]
        z_sets = [((0, planes), wz, 0)]
        x_sets = [((0, planes), wx, 0)]
        o_sets = [((0, planes), o, 0)]
    xc, mix, loc, _ = bufs
    left = [(s + 1, s) for s in range(planes - 1)]

    nout, dy, dz, sl = gate_call(z, mix, wgt, ent, pk, hp, ct, c_low, inner)

    adj = lax.ppermute(sl, "tensor", left)
    mixed, grad_down_out, grad_up_out = output_call(
        sc, nout, pk, back2, up_out, tokens[0], masked, o_sets, picks, flat, quick
    )
    send = hop_call(adj, planes - 1, sl, hp, 0, [mixed])
    adj = lax.ppermute(send, "tensor", left)
    d_normed, grad_z = gate_back_call(dz, low2, z_sets, picks, width, [send])
    send = hop_call(adj, planes - 1, sl, hp, 0, [d_normed])
    adj = lax.ppermute(send, "tensor", left)
    for _ in range(planes - 4):
        adj = lax.ppermute(hop_call(adj, planes - 1, sl, hp), "tensor", left)
    dxs, u1, u2, kl, dcb, db1, dc1 = back_call(
        dy, xc, hp, ent, loc, ct, c_low, bt, cbt, [send]
    )

    early = to_slots(
        [jnp.concatenate([grad_z[j], grad_down_out[j]], axis=1) for j in range(planes)],
        grad_up_out,
    )
    (dx, tail, head, grad_x, d_low, ddelta, u2f, kf, db3) = finish_call(
        dxs, dy, xc, dz, pk, hp, ent, adj, bt, low2, [mixed, early]
    )
    small_left, maps_tail, maps_head, grad_down = glue_call(
        [dcb, db1, db3, dc1, bt, ct, maps_pre, u1, u2, kl, ddelta, u2f, kf, step_sig, speed]
        + [conv_maps],
        sc, d_low, nt, state_w, length, heads, flat, quick,
    )

    to_left = jnp.concatenate(
        [
            head.reshape(8 * planes, ch),
            jnp.pad(maps_head, ((0, 0), (0, ch - 2 * state_w))),
            jnp.zeros((-(8 * planes + 8) % rank, ch), f32),
            jnp.pad(d_low[:, :HALO], ((0, 0), (0, ch - HALO))),
        ],
        axis=0,
    )
    near = lax.ppermute(to_left, "tensor", left)
    late = to_slots([grad_x[j] for j in range(planes)], grad_down)
    sent = jnp.concatenate(
        [
            early[:, :ch],
            late[:, :ch],
            early[:, ch : 2 * ch],
            late[:, ch:],
            early[:, 2 * ch :],
        ],
        axis=1,
    ).astype(bf16)[None]
    if quick:
        _, (sent,), _ = hold([near], [sent])
        both = jnp.concatenate([sent, flip(sent, 1)], axis=0)
        by_seq = [both] + [flip(both, bit) for bit in (2, 4, 6)]
    else:
        by_seq = [lax.all_gather(sent[0], "dp", axis=0)]

    tokens_grad = input_call(
        sc, dx, tail, near, pk, small_left, maps_tail, conv_maps, d_low, down_in, root,
        pre_gain[None], tokens[0], masked, d_normed, small_w, x_sets, picks, flat, quick,
    )
    if quick:
        _, by_seq, _ = hold([tokens_grad], by_seq)
    g_down, g_up, g_down_out, g_up_out = assemble_call(ids, by_seq, adapters, ch, width)
    g_down = jnp.swapaxes(g_down, 1, 2)
    g_down_out = jnp.swapaxes(g_down_out, 1, 2)
    return (mixed[None], tokens_grad[None], g_down, g_up, g_down_out, g_up_out)


def solution(mesh):
    placed = (
        P("dp", "tensor", None),
        P("dp", "tensor", None),
        P("dp"),
        P("dp"),
        P(),
        P("dp", None, "tensor"),
        P("dp", None),
        P("dp", "tensor"),
        P(None, "tensor"),
        P(),
        P("tensor"),
        P("tensor"),
        P("tensor"),
        P("tensor"),
        P("tensor", "dp"),
        P(),
        P(None, None, None, "tensor"),
        P(None, "tensor", None),
        P(),
    )
    return jax.shard_map(
        body,
        mesh=mesh,
        in_specs=placed,
        out_specs=(
            P("dp", "tensor", None),
            P("dp", "tensor", None),
            P(),
            P(None, None, None, "tensor"),
            P(None, "tensor", None),
            P(),
        ),
        check_vma=False,
    )
```
